32 devices in a mesh: dp: 8 (over z, core), ctx: 2 (over y), exp: 2 (over x).
Axes of the slice: x: 2, y: 2, z: 4, core: 2. Of those that a mesh axis runs over, the one named last changes fastest.
Arguments:
- residual_in: bfloat16 [16, 1024, 768], P(('dp', 'exp'), 'ctx'), may hold values from -6 to 6
- lengths: int32 [16], P(('dp', 'exp')), may hold values from 256 to 1024, as said below
- routes: int32 [16, 1024, 2], P(('dp', 'exp'), 'ctx'), may hold values from 0 to 11, all different within a row; in each aligned block of 512 rows (0 to 511, 512 to 1023, ..., all dimensions but the last counted through in order) at most 128 rows name the same one
- prev_logits: float32 [16, 1024, 12], P(('dp', 'exp'), 'ctx'), may hold values from -4 to 4
- cotangent: float32 [16, 1024, 768], P(('dp', 'exp'), 'ctx'), may hold values from -6 to 6
- w_qkv: bfloat16 [768, 2304], P(('dp', 'ctx', 'exp')), may hold values from -0.21875 to 0.21875
- w_out: bfloat16 [768, 768], P(('dp', 'ctx', 'exp')), may hold values from -0.875 to 0.875
- attn_gain: bfloat16 [768], P(('dp', 'ctx', 'exp')), may hold values from 0.5 to 1.5
- ffn_gain: bfloat16 [768], P(('dp', 'ctx', 'exp')), may hold values from 0.5 to 1.5
- router: bfloat16 [768, 12], P(('dp', 'ctx', 'exp')), may hold values from -0.15625 to 0.15625
- const_gate: bfloat16 [768, 4], P(('dp', 'ctx', 'exp')), may hold values from -0.21875 to 0.21875
- const_vec: bfloat16 [768, 2], P(('dp', 'ctx', 'exp')), may hold values from -24 to 24
- w_gate: bfloat16 [8, 768, 2048], P('exp', None, ('dp', 'ctx')), may hold values from -0.21875 to 0.21875
- w_up: bfloat16 [8, 768, 2048], P('exp', None, ('dp', 'ctx')), may hold values from -0.21875 to 0.21875
- w_down: bfloat16 [8, 2048, 768], P('exp', ('dp', 'ctx')), may hold values from -1 to 1
Outputs:
- output: float32 [16, 1024, 768], P(('dp', 'exp'), 'ctx')
- grad_x: float32 [16, 1024, 768], P(('dp', 'exp'), 'ctx')
- grad_w_qkv: float32 [768, 2304], P(('dp', 'ctx', 'exp'))
- grad_w_out: float32 [768, 768], P(('dp', 'ctx', 'exp'))
- grad_attn_gain: float32 [768], P(('dp', 'ctx', 'exp'))
- grad_ffn_gain: float32 [768], P(('dp', 'ctx', 'exp'))
- grad_router: float32 [768, 12], P(('dp', 'ctx', 'exp'))
- grad_const_gate: float32 [768, 4], P(('dp', 'ctx', 'exp'))
- grad_const_vec: float32 [768, 2], P(('dp', 'ctx', 'exp'))
- grad_w_gate: float32 [8, 768, 2048], P('exp', None, ('dp', 'ctx'))
- grad_w_up: float32 [8, 768, 2048], P('exp', None, ('dp', 'ctx'))
- grad_w_down: float32 [8, 2048, 768], P('exp', ('dp', 'ctx'))
The draws below stay inside these ranges and needn't reach their ends.
Inputs may be any that keep to these rules, and one draw needn't show every extreme that they name: `lengths`: one sequence has all 1024 slots used in every draw. `routes`: the two ids of a token differ; among the 512 rows of one device no id is named more than 128 times, a bound that some block reaches.
All inputs are finite; a program needn't handle non-finite values.
Results may differ from the reference program's by a relative error of at most 0.015.
Values may be sent and summed in bfloat16 or wider, within the bound.
No kernel may reach another device: no remote copies, remote signals or barrier semaphores. Data moves between devices by JAX's collectives and lax.ppermute only.
A program may use at most 256 MiB of HBM per device.

```python
import math
import jax
import jax.numpy as jnp
import numpy as np
from jax import lax

D = 768
HEADS = 12
HEAD_DIM = 64
FF = 2048
TOK_DEV = 512
KBLK = 512
FFN_EXP = 8
NE = 12
SEQ_LEN = 1024
SEQS = 16
CAP = 128
N_CTX = 2


def draw_lengths(key, part):
    key = jax.random.fold_in(key, 11)
    key_lengths, key_full = jax.random.split(key)
    drawn_lengths = jax.random.randint(key_lengths, (SEQS,), SEQ_LEN // 4, SEQ_LEN + 1)
    full_index = jax.random.randint(key_full, (), 0, SEQS)
    return jnp.where(jnp.arange(SEQS) == full_index, SEQ_LEN, drawn_lengths).astype(jnp.int32)


def block_levels(stream_key, dims, pieces, smallest, top_value):
    level = 1.0
    for position, blocks in pieces:
        draws = jax.random.uniform(jax.random.fold_in(jax.random.fold_in(stream_key, 6), position), (blocks,), jnp.float32, smallest / len(pieces), top_value / len(pieces))
        level = level * jnp.repeat(jnp.exp(draws), dims[position] // blocks).reshape((-1,) + (1,) * (len(dims) - 1 - position))
    return level


def shared_out(key, own, number, rows, amount, top, bound, lean):
    sequence = jax.random.permutation(key, amount)
    packed, ordinary = load_shares(amount, rows * top, bound, lean, True), load_shares(amount, rows * top, bound, lean, False)
    places = jnp.arange(amount)

    def named(sizes, offset_by):
        used = int((sizes > 0).sum())
        fixed = max(1, used // 4)
        shifted = fixed + (places - fixed + offset_by * (used - fixed)) % max(1, amount - fixed)
        return jnp.zeros((amount,), jnp.int32).at[sequence[jnp.where(places < fixed, places, shifted)]].set(jnp.asarray(sizes, jnp.int32))

    sizes = jnp.where(number % 4 == 0, named(packed, number // 4), named(ordinary, number - number // 4 - 1))
    mixed = jax.random.permutation(jax.random.fold_in(own, 3), amount)
    giver, sink = mixed[0:amount // 2 * 2:2], mixed[1:amount // 2 * 2:2]
    room = jnp.minimum(sizes[giver] - 1, bound - sizes[sink]) // 2
    room = jnp.where((giver == sequence[0]) | (sink == sequence[0]) | (sizes[sink] == 0), 0, jnp.maximum(room, 0))
    shifted = jax.random.randint(jax.random.fold_in(own, 4), (amount // 2,), 0, 1 << 20) % (room + 1)
    sizes = sizes.at[giver].add(-shifted).at[sink].add(shifted)
    labels = jnp.searchsorted(jnp.cumsum(sizes), jnp.arange(rows * top), side="right").astype(jnp.int32)
    grid = labels.reshape(top, rows).T
    grid = grid[jax.random.permutation(jax.random.fold_in(own, 1), rows)]
    offset_by = jax.random.randint(jax.random.fold_in(own, 2), (rows, 1), 0, top)
    return jnp.take_along_axis(grid, (jnp.arange(top)[None, :] + offset_by) % top, axis=1)


def load_shares(amount, total, reach, lean, full):
    loads = [(1 << 20) // math.isqrt(grade ** lean) + 1 for grade in range(1, amount + 1)]
    largest = reach if full else min(reach, max(-(-total // amount), total * loads[0] // sum(loads)))
    least = 1 if total - largest >= amount - 1 else 0
    counts, spare = [largest] + [least] * (amount - 1), total - largest - least * (amount - 1)
    while spare > 0:
        candidates = [i for i in range(1, amount) if counts[i] < largest] or [i for i in range(1, amount) if counts[i] < reach]
        pool, left = sum([loads[i] for i in candidates]), spare
        for i in candidates:
            more = min(reach - counts[i], max(1, left * loads[i] // pool), spare)
            counts[i] = counts[i] + more
            spare = spare - more
    return np.array(counts)


def normal_values(stream_key, dims, scale, most, shards=(), kind=jnp.bfloat16):
    factor_of = block_levels(stream_key, dims, shards, -0.22, 0.18) if shards else 1.0
    drawn = jax.random.normal(stream_key, dims, jnp.float32) * scale * factor_of
    return jnp.minimum(jnp.maximum(drawn, -most), most).astype(kind)


def setup_inputs(seed: int = 0) -> dict:
    arg_keys = jax.random.split(jax.random.key(seed), 16)
    residual_in = normal_values(arg_keys[0], (SEQS, SEQ_LEN, D), 1.0, 6.0, ((0, 16), (1, 2)))
    lengths = draw_lengths(jax.random.fold_in(arg_keys[15], 71), 0)
    routes_keys = jax.random.split(jax.random.fold_in(arg_keys[2], 1), SEQS * SEQ_LEN // TOK_DEV)
    routes_turns = jax.random.permutation(jax.random.fold_in(arg_keys[2], 3), SEQS * SEQ_LEN // TOK_DEV)
    routes = jax.vmap(lambda own, number: shared_out(jax.random.fold_in(arg_keys[2], 2), own, number, TOK_DEV, NE, 2, CAP, 1))(routes_keys, routes_turns).reshape((SEQS, SEQ_LEN, 2))
    prev_logits = normal_values(arg_keys[3], (SEQS, SEQ_LEN, NE), 0.3, 4.0, ((0, 16), (1, 2)), jnp.float32)
    cotangent = normal_values(arg_keys[4], (SEQS, SEQ_LEN, D), 1.0, 6.0, ((0, 16), (1, 2)), jnp.float32)
    w_qkv = normal_values(arg_keys[5], (D, 3 * D), D ** -0.5, 0.21875, ((0, 32),))
    w_out = normal_values(arg_keys[6], (D, D), (D // 16) ** -0.5, 0.875, ((0, 32),))
    attn_gain = jnp.clip(1.0 + 0.1 * jax.random.normal(arg_keys[7], (D,), jnp.float32), 0.5, 1.5).astype(jnp.bfloat16)
    ffn_gain = jnp.clip(1.0 + 0.1 * jax.random.normal(arg_keys[8], (D,), jnp.float32), 0.5, 1.5).astype(jnp.bfloat16)
    router = normal_values(arg_keys[9], (D, NE), (2 * D) ** -0.5, 0.15625, ((0, 32),))
    const_gate = normal_values(arg_keys[10], (D, 4), D ** -0.5, 0.21875, ((0, 32),))
    const_vec = normal_values(arg_keys[11], (D, 2), 4.0, 24.0, ((0, 32),))
    w_gate = normal_values(arg_keys[12], (FFN_EXP, D, FF), D ** -0.5, 0.21875, ((0, 2), (2, 16)))
    w_up = normal_values(arg_keys[13], (FFN_EXP, D, FF), D ** -0.5, 0.21875, ((0, 2), (2, 16)))
    w_down = normal_values(arg_keys[14], (FFN_EXP, FF, D), (FF // 64) ** -0.5, 1.0, ((0, 2), (1, 16)))
    return {"residual_in": residual_in, "lengths": lengths, "routes": routes, "prev_logits": prev_logits, "cotangent": cotangent, "w_qkv": w_qkv, "w_out": w_out, "attn_gain": attn_gain, "ffn_gain": ffn_gain, "router": router, "const_gate": const_gate, "const_vec": const_vec, "w_gate": w_gate, "w_up": w_up, "w_down": w_down}


@jax.custom_vjp
def low(v):
    return lax.optimization_barrier(v.astype(jnp.bfloat16)).astype(jnp.float32)

@jax.custom_vjp
def low_back(v):
    return v

def low_keep(v):
    return (low(v), None)

def low_pass(kept, grad):
    return (grad,)

def back_keep(v):
    return (v, None)

def back_low(kept, grad):
    return (low(grad),)
low.defvjp(low_keep, low_pass)
low_back.defvjp(back_keep, back_low)
norm_eps = 1e-06
top_precision = lax.Precision.HIGHEST

def rms_norm(in_rows, gain_vec):
    return in_rows * lax.rsqrt(lax.optimization_barrier(jnp.mean(in_rows * in_rows, axis=-1, keepdims=True)) + norm_eps) * gain_vec

def rotate(in_rows, positions, sign_value):
    half_size = in_rows.shape[-1] // 2
    inv_freq = 10000.0 ** (-2.0 * jnp.arange(half_size, dtype=jnp.float32) / in_rows.shape[-1])
    angles = positions.astype(jnp.float32)[:, None] * inv_freq[None, :]
    cosine = jnp.cos(angles)[:, None, :]
    sine_part = sign_value * jnp.sin(angles)[:, None, :]
    first_half = in_rows[..., :half_size]
    second_half = in_rows[..., half_size:]
    return jnp.concatenate([first_half * cosine - second_half * sine_part, second_half * cosine + first_half * sine_part], axis=-1)

def slot_rank(route_ids):
    flat_ids = route_ids.reshape(-1)
    onehot = (flat_ids[:, None] == jnp.arange(NE, dtype=jnp.int32)[None, :]).astype(jnp.int32)
    earlier = jnp.cumsum(onehot, axis=0) - onehot
    return lax.optimization_barrier(jnp.sum(earlier * onehot, axis=1)).reshape(route_ids.shape)

def attend(queries, keys, values, length):
    seq_rows = queries.shape[0]
    score_scale = HEAD_DIM ** (-0.5)
    key_pos = jnp.arange(seq_rows, dtype=jnp.int32)
    blk_queries = queries.reshape(seq_rows // KBLK, KBLK, HEADS, HEAD_DIM)
    blk_starts = jnp.arange(seq_rows // KBLK, dtype=jnp.int32) * KBLK

    def one_block(pair):
        query_rows, blk_start = pair
        blk_scores = low_back(jnp.einsum('qhd,khd->hqk', query_rows, keys, precision=top_precision) * score_scale)
        query_pos = blk_start + jnp.arange(KBLK, dtype=jnp.int32)
        allowed = (key_pos[None, :] <= query_pos[:, None]) & (key_pos[None, :] < length)
        blk_scores = jnp.where(allowed[None], blk_scores, -1e+30)
        row_max = lax.optimization_barrier(jnp.max(blk_scores, axis=-1, keepdims=True))
        expo_vals = jnp.exp(blk_scores - row_max)
        summed = jnp.einsum('hqk,khd->qhd', low(expo_vals), values, precision=top_precision)
        return summed / jnp.transpose(lax.optimization_barrier(jnp.sum(expo_vals, axis=-1)))[:, :, None]
    attended = lax.map(jax.checkpoint(one_block), (blk_queries, blk_starts))
    return attended.reshape(seq_rows, HEADS * HEAD_DIM)

def expert_ffn(buffer, w_gate, w_up, w_down):
    gate_pre = low_back(jnp.einsum('becd,edf->becf', buffer, w_gate, precision=top_precision))
    up_pre = low_back(jnp.einsum('becd,edf->becf', buffer, w_up, precision=top_precision))
    act_vals = low(jax.nn.silu(gate_pre) * up_pre)
    return low_back(low(jnp.einsum('becf,efd->becd', act_vals, w_down, precision=top_precision)))

def one_sequence(weights, inputs):
    w_qkv, w_out, attn_gain, ffn_gain, router, const_gate, const_vec, w_gate, w_up, w_down = weights
    in_rows, prev_rows, route_ids, length = inputs
    seq_rows = in_rows.shape[0]
    positions = jnp.arange(seq_rows, dtype=jnp.int32)
    hidden_one = low(rms_norm(in_rows, attn_gain))
    qkv_rows = low_back(jnp.dot(hidden_one, w_qkv, precision=top_precision)).reshape(seq_rows, 3, HEADS, HEAD_DIM)
    queries = low(rotate(qkv_rows[:, 0], positions, 1.0))
    keys = low(rotate(qkv_rows[:, 1], positions, 1.0))
    values = low(qkv_rows[:, 2])
    attended = low(low_back(attend(queries, keys, values, length)))
    mid_rows = in_rows + low_back(jnp.dot(attended, w_out, precision=top_precision))
    hidden = low(rms_norm(mid_rows, ffn_gain))
    logits = jnp.dot(hidden, router, precision=top_precision) + prev_rows
    gate_probs = jax.nn.softmax(logits, axis=-1)
    gate_vals = jnp.take_along_axis(gate_probs, route_ids, axis=1)
    block_routes = route_ids.reshape(N_CTX, TOK_DEV, 2)
    slot_ids = jax.vmap(slot_rank)(block_routes)
    is_ffn = block_routes < FFN_EXP
    expert_index = jnp.where(is_ffn, block_routes, FFN_EXP)
    block_ids = jnp.broadcast_to(jnp.arange(N_CTX, dtype=jnp.int32)[:, None, None], block_routes.shape)
    sent_rows = low_back(jnp.broadcast_to(hidden.reshape(N_CTX, TOK_DEV, 1, D), (N_CTX, TOK_DEV, 2, D)))
    buffer = jnp.zeros((N_CTX, FFN_EXP, CAP, D), jnp.float32).at[block_ids, expert_index, slot_ids].set(sent_rows, mode='drop')
    expert_out = expert_ffn(buffer, w_gate, w_up, w_down)
    safe_index = jnp.where(is_ffn, block_routes, 0)
    ffn_rows = (expert_out[block_ids, safe_index, slot_ids] * is_ffn[..., None].astype(jnp.float32)).reshape(seq_rows, 2, D)
    const_mix = jax.nn.softmax(jnp.dot(hidden, const_gate, precision=top_precision).reshape(seq_rows, 2, 2), axis=-1)
    const_rows = const_mix[..., 0:1] * hidden[:, None, :] + const_mix[..., 1:2] * jnp.transpose(const_vec)[None]
    is_copy = (route_ids == FFN_EXP + 1).astype(jnp.float32)
    pick_const = (route_ids[:, :, None] == FFN_EXP + 2 + jnp.arange(2, dtype=jnp.int32)[None, None, :]).astype(jnp.float32)
    chosen = ffn_rows + is_copy[..., None] * hidden[:, None, :] + lax.optimization_barrier(jnp.sum(pick_const[..., None] * const_rows[:, None, :, :], axis=2))
    moe_out = lax.optimization_barrier(jnp.sum(gate_vals[..., None] * chosen, axis=1))
    valid_rows = (positions < length).astype(jnp.float32)[:, None]
    return (mid_rows + moe_out) * valid_rows

def forward(weights, in_rows, prev_logits, routes, lengths):

    def per_sequence(inputs):
        return jax.checkpoint(one_sequence)(weights, inputs)
    return lax.map(per_sequence, (in_rows, prev_logits, routes, lengths))

def reference(residual_in, lengths, routes, prev_logits, cotangent, w_qkv, w_out, attn_gain, ffn_gain, router, const_gate, const_vec, w_gate, w_up, w_down):
    weights = tuple((w.astype(jnp.float32) for w in (w_qkv, w_out, attn_gain, ffn_gain, router, const_gate, const_vec, w_gate, w_up, w_down)))
    in_rows = residual_in.astype(jnp.float32)
    prev_rows = prev_logits.astype(jnp.float32)

    def run(weight_set, layer_in):
        return forward(weight_set, layer_in, prev_rows, routes, lengths)
    output, pull_back = jax.vjp(run, weights, in_rows)
    weight_grads, grad_x = pull_back(cotangent.astype(jnp.float32))
    return (output, grad_x, weight_grads[0], weight_grads[1], weight_grads[2], weight_grads[3], weight_grads[4], weight_grads[5], weight_grads[6], weight_grads[7], weight_grads[8], weight_grads[9])
```

```python
import jax
import jax.numpy as jnp
from jax import lax
from jax.sharding import PartitionSpec as P

HEADS = 12
KBLK = 512

norm_eps = 1e-06
top_precision = lax.Precision.HIGHEST
f32 = jnp.float32
bf16 = jnp.bfloat16


def dot32(a, b, dims=((1,), (0,)), precision=None):
    return lax.dot_general(a, b, (dims, ((), ())), precision=precision, preferred_element_type=f32)


def swap(block, axis, bit):
    return lax.ppermute(block, axis, [(i, i ^ bit) for i in range(lax.axis_size(axis))])


def bits_of(axis, low=1, high=None):
    high = lax.axis_size(axis) if high is None else high
    found = []
    while low < high:
        found.append(low)
        low *= 2
    return found[::-1]


def row_weight(axis):
    x = lax.axis_size("exp")
    c = lax.axis_size("ctx")
    return {"exp": 1, "ctx": x, "dp": x * c}[axis]


def plan_steps(middle):
    far = [("dp", bit) for bit in bits_of("dp", 2)]
    mid = [(axis, bit) for axis in middle for bit in bits_of(axis)]
    near = [("dp", bit) for bit in bits_of("dp", 1, 2)]
    return far + mid + near


def gather_rows(block, steps):
    placed = []
    shape = block.shape
    whole = block
    for axis, bit in steps:
        other = swap(whole, axis, bit)
        upper = (lax.axis_index(axis) & bit) != 0
        weight = row_weight(axis) * bit
        pos = sum(1 for w in placed if w > weight)
        whole = jnp.stack(
            [jnp.where(upper, other, whole), jnp.where(upper, whole, other)], axis=pos
        )
        placed.insert(pos, weight)
    return whole.reshape((-1,) + shape[1:])


def scatter_rows(whole, steps):
    placed = sorted([row_weight(axis) * bit for axis, bit in steps], reverse=True)
    part = whole.reshape((2,) * len(placed) + (-1,) + whole.shape[1:])
    for axis, bit in reversed(steps):
        pos = placed.index(row_weight(axis) * bit)
        upper = (lax.axis_index(axis) & bit) != 0
        low = lax.index_in_dim(part, 0, pos, keepdims=False)
        high = lax.index_in_dim(part, 1, pos, keepdims=False)
        sent = jnp.where(upper, low, high).astype(bf16)
        part = jnp.where(upper, high, low).astype(f32) + swap(sent, axis, bit).astype(f32)
        placed.pop(pos)
    return part


def gather_expert(shards, ff_axis):
    n_own = shards.shape[0]
    reps = lax.axis_size("dp") // n_own
    mine = lax.axis_index("dp") // reps
    pieces = [lax.dynamic_index_in_dim(shards, mine, 0, keepdims=False)]
    for k in range(1, n_own):
        sent = lax.dynamic_index_in_dim(shards, mine ^ k, 0, keepdims=False)
        pieces.append(swap(sent, "dp", reps * k))
    whole = jnp.concatenate(pieces, axis=ff_axis)
    for bit in bits_of("ctx"):
        whole = jnp.concatenate([whole, swap(whole, "ctx", bit)], axis=ff_axis)
    for bit in bits_of("dp", 1, reps):
        whole = jnp.concatenate([whole, swap(whole, "dp", bit)], axis=ff_axis)
    return whole


def scatter_expert(grad, n_own, ff_axis):
    reps = lax.axis_size("dp") // n_own
    mine = lax.axis_index("dp") // reps
    steps = [("ctx", bit) for bit in bits_of("ctx")] + [("dp", bit) for bit in bits_of("dp", 1, reps)]
    for axis, bit in reversed(steps):
        keep, sent = jnp.split(grad, 2, axis=ff_axis)
        grad = keep.astype(f32) + swap(sent.astype(bf16), axis, bit).astype(f32)
    pieces = jnp.split(grad, n_own, axis=ff_axis)
    back = [pieces[0].astype(f32)]
    for k in range(1, n_own):
        back.append(swap(pieces[k].astype(bf16), "dp", reps * k).astype(f32))
    bit = 1
    while bit < n_own:
        flip = (mine & bit) != 0
        back = [jnp.where(flip, back[i ^ bit], back[i]) for i in range(n_own)]
        bit *= 2
    return jnp.stack(back)


def rms_scale(rows):
    return lax.rsqrt(jnp.mean(rows * rows, axis=-1, keepdims=True) + norm_eps)


def rms_backward(in_rows, inv_scale, gain_vec, grad_rows):
    normed = in_rows * inv_scale
    gain_grad = jnp.sum(grad_rows * normed, axis=0)
    inner_grad = grad_rows * gain_vec
    back_rows = inv_scale * (
        inner_grad - normed * jnp.mean(inner_grad * normed, axis=-1, keepdims=True)
    )
    return (back_rows, gain_grad)


def rotate(in_rows, positions, sign_value):
    half_size = in_rows.shape[-1] // 2
    inv_freq = 10000.0 ** (-2.0 * jnp.arange(half_size, dtype=f32) / in_rows.shape[-1])
    angles = positions.astype(f32)[:, None] * inv_freq[None, :]
    cosine = jnp.cos(angles)[:, None, :]
    sine_part = sign_value * jnp.sin(angles)[:, None, :]
    first_half = in_rows[..., :half_size]
    second_half = in_rows[..., half_size:]
    return jnp.concatenate(
        [
            first_half * cosine - second_half * sine_part,
            second_half * cosine + first_half * sine_part,
        ],
        axis=-1,
    )


def local(
    residual_in,
    lengths,
    routes,
    prev_logits,
    cotangent,
    w_qkv,
    w_out,
    attn_gain,
    ffn_gain,
    router,
    const_gate,
    const_vec,
    w_gate,
    w_up,
    w_down,
):
    tok_rows = residual_in.shape[1]
    feat = residual_in.shape[2]
    head_size = feat // HEADS
    score_scale = head_size ** (-0.5)
    n_dp = lax.axis_size("dp")
    n_ctx = lax.axis_size("ctx")
    n_exp = lax.axis_size("exp")
    own_exp = w_gate.shape[0]
    reps = n_dp // own_exp
    n_all = router.shape[1]
    n_ffn = n_all - 4
    cap_rows = tok_rows // 4
    sub_rows = cap_rows // reps
    n_slots = n_ffn * cap_rows
    ctx_rank = lax.axis_index("ctx")
    positions = ctx_rank * tok_rows + jnp.arange(tok_rows, dtype=jnp.int32)
    length = lengths[0]
    valid_rows = (positions < length).astype(f32)[:, None]
    in_rows = residual_in[0].astype(f32)
    grad_out = cotangent[0] * valid_rows

    steps_a = plan_steps(("ctx", "exp"))
    steps_b = plan_steps(("exp", "ctx"))
    small = jnp.concatenate(
        [router, const_gate, const_vec, attn_gain[:, None], ffn_gain[:, None]], axis=1
    )
    small = jnp.pad(small, ((0, 0), (0, 128 - small.shape[1])))
    key_pack = gather_rows(jnp.concatenate([w_qkv[:, feat : 2 * feat], small], axis=1), steps_a)
    full_v = gather_rows(w_qkv[:, 2 * feat :], steps_b)
    full_q = gather_rows(w_qkv[:, :feat], steps_a)
    full_out = gather_rows(w_out, steps_b)
    full_k = key_pack[:, :feat]
    small = key_pack[:, feat:]
    full_router = small[:, :n_all]
    full_cg = small[:, n_all : n_all + 4]
    full_cv = small[:, n_all + 4 : n_all + 6]
    gain_attn = small[:, n_all + 6].astype(f32)
    gain_ffn = small[:, n_all + 7].astype(f32)

    route_ids = routes[0]
    choose = (route_ids[:, :, None] == jnp.arange(n_all, dtype=jnp.int32)[None, None, :]).astype(f32)
    both = jnp.sum(choose, axis=1)
    before = jnp.arange(tok_rows)
    before = (before[None, :] < before[:, None]).astype(bf16)
    counts = dot32(before, both.astype(bf16))
    slot_ids = jnp.sum(choose * counts[:, None, :], axis=-1).astype(jnp.int32)
    is_ffn = route_ids < n_ffn
    place = (
        ((route_ids % own_exp) * reps + slot_ids // sub_rows) * n_exp + route_ids // own_exp
    ) * sub_rows + slot_ids % sub_rows
    place = jnp.where(is_ffn, place, -1)
    row_ids = jnp.arange(n_slots, dtype=jnp.int32)
    hit = [row_ids[:, None] == place[None, :, j] for j in range(2)]
    spread = (hit[0] | hit[1]).astype(bf16)
    pick = [(place[:, j][:, None] == row_ids[None, :]).astype(bf16) for j in range(2)]

    def to_experts(rows):
        return lax.all_to_all(
            rows.reshape(n_dp * n_exp, sub_rows, -1),
            ("dp", "exp"),
            split_axis=0,
            concat_axis=0,
            tiled=True,
        ).reshape(n_slots, -1)

    grad_rows_in = to_experts(dot32(spread, grad_out.astype(bf16)).astype(bf16))

    scale_one = rms_scale(in_rows)
    hidden_one = (in_rows * scale_one * gain_attn).astype(bf16)

    def heads_of(rows):
        return rows.reshape(tok_rows, HEADS, head_size)

    own_keys = (
        rotate(heads_of(dot32(hidden_one, full_k)), positions, 1.0)
        .astype(bf16)
        .reshape(tok_rows, feat)
    )
    own_values = dot32(hidden_one, full_v).astype(bf16)
    queries = rotate(heads_of(dot32(hidden_one, full_q)), positions, 1.0).astype(bf16)

    def gather_ctx(rows):
        for bit in reversed(bits_of("ctx")):
            other = swap(rows, "ctx", bit)
            upper = (ctx_rank & bit) != 0
            rows = jnp.concatenate([jnp.where(upper, other, rows), jnp.where(upper, rows, other)], axis=0)
        return rows

    def scatter_ctx(rows):
        for bit in bits_of("ctx"):
            low, high = jnp.split(rows, 2, axis=0)
            upper = (ctx_rank & bit) != 0
            sent = jnp.where(upper, low, high).astype(bf16)
            rows = jnp.where(upper, high, low) + swap(sent, "ctx", bit).astype(f32)
        return rows

    all_keys = gather_ctx(own_keys)
    all_values = gather_ctx(own_values)
    key_count = jnp.minimum((ctx_rank + 1) * tok_rows, length)
    blk_count = (key_count + KBLK - 1) // KBLK

    def block_scores(blk_index):
        blk_start = blk_index * KBLK
        key_rows = lax.dynamic_slice_in_dim(all_keys, blk_start, KBLK, 0).reshape(
            KBLK, HEADS, head_size
        )
        value_rows = lax.dynamic_slice_in_dim(all_values, blk_start, KBLK, 0).reshape(
            KBLK, HEADS, head_size
        )
        key_pos = blk_start + jnp.arange(KBLK, dtype=jnp.int32)
        allowed = (key_pos[None, :] <= positions[:, None]) & (key_pos[None, :] < length)
        raw_scores = (
            jnp.einsum("qhd,khd->hqk", queries, key_rows, preferred_element_type=f32) * score_scale
        )
        return (jnp.where(allowed[None], raw_scores, -1e30), key_rows, value_rows)

    def forward_step(blk_index, loop_state):
        run_max, run_total, run_acc = loop_state
        blk_scores, key_rows, value_rows = block_scores(blk_index)
        new_max = jnp.maximum(run_max, jnp.max(blk_scores, axis=-1))
        expo_vals = jnp.exp(blk_scores - new_max[..., None])
        factor = jnp.exp(run_max - new_max)
        run_total = run_total * factor + jnp.sum(expo_vals, axis=-1)
        run_acc = run_acc * jnp.transpose(factor)[:, :, None] + jnp.einsum(
            "hqk,khd->qhd", expo_vals.astype(bf16), value_rows, preferred_element_type=f32
        )
        return (new_max, run_total, run_acc)

    start_state = (
        jnp.full((HEADS, tok_rows), -1e30, f32),
        jnp.zeros((HEADS, tok_rows), f32),
        jnp.zeros((tok_rows, HEADS, head_size), f32),
    )
    run_max, run_total, run_acc = lax.fori_loop(0, blk_count, forward_step, start_state)
    attended = run_acc / jnp.transpose(run_total)[:, :, None]
    log_total = run_max + jnp.log(run_total)
    attended_low = attended.reshape(tok_rows, feat).astype(bf16)

    mid_rows = in_rows + dot32(attended_low, full_out)
    scale_two = rms_scale(mid_rows)
    hidden = (mid_rows * scale_two * gain_ffn).astype(bf16)
    hidden_f = hidden.astype(f32)
    logits = dot32(hidden, full_router) + prev_logits[0]
    gate_probs = jax.nn.softmax(logits, axis=-1)
    gate_vals = jnp.sum(choose * gate_probs[:, None, :], axis=-1)
    rows_in = to_experts(dot32(spread, hidden).astype(bf16))
    gate_rows = jnp.sum(
        jnp.where(hit[0], gate_vals[None, :, 0], 0.0) + jnp.where(hit[1], gate_vals[None, :, 1], 0.0),
        axis=1,
    )
    gates_in = to_experts(gate_rows)

    w_g = gather_expert(w_gate, 1)
    w_u = gather_expert(w_up, 1)
    w_d = gather_expert(w_down, 0)
    gate_pre = dot32(rows_in, w_g)
    up_pre = dot32(rows_in, w_u)
    sig = jax.nn.sigmoid(gate_pre)
    silu_gate = gate_pre * sig
    act = (silu_gate * up_pre).astype(bf16)
    expert_out = dot32(act, w_d).astype(bf16)
    grad_rows_f = grad_rows_in.astype(f32)
    gate_grad_rows = jnp.sum(grad_rows_f * expert_out.astype(f32), axis=1)
    grad_expert_out = (grad_rows_f * gates_in).astype(bf16)
    grad_act = dot32(grad_expert_out, w_d, ((1,), (1,)))
    grad_gate_pre = (grad_act * up_pre * sig * (1.0 + gate_pre * (1.0 - sig))).astype(bf16)
    grad_up_pre = (grad_act * silu_gate).astype(bf16)
    grad_in = (
        dot32(grad_gate_pre, w_g, ((1,), (1,))) + dot32(grad_up_pre, w_u, ((1,), (1,)))
    ).astype(bf16)
    back_gates = to_experts(gate_grad_rows)
    back_grads = to_experts(grad_in)
    back_rows = to_experts(expert_out)
    grad_down = dot32(act, grad_expert_out, ((0,), (0,)))
    grad_gate = dot32(rows_in, grad_gate_pre, ((0,), (0,)))
    grad_up = dot32(rows_in, grad_up_pre, ((0,), (0,)))
    expert_grads = (
        scatter_expert(grad_gate, own_exp, 1),
        scatter_expert(grad_up, own_exp, 1),
        scatter_expert(grad_down, own_exp, 0),
    )

    const_mix = jax.nn.softmax(dot32(hidden, full_cg).reshape(tok_rows, 2, 2), axis=-1)
    vectors = jnp.transpose(full_cv.astype(f32))
    copy_gate = jnp.sum(jnp.where(route_ids == n_ffn + 1, gate_vals, 0.0), axis=1)
    const_sel = choose[:, :, n_ffn + 2 :]
    const_gates = jnp.sum(const_sel * gate_vals[:, :, None], axis=1)
    hidden_coef = copy_gate + jnp.sum(const_mix[..., 0] * const_gates, axis=1)
    vec_coef = const_mix[..., 1] * const_gates
    picked = [dot32(pick[j], back_rows) for j in range(2)]
    moe_out = (
        gate_vals[:, 0:1] * picked[0]
        + gate_vals[:, 1:2] * picked[1]
        + hidden_coef[:, None] * hidden_f
        + dot32(vec_coef, vectors, precision=top_precision)
    )
    output = (mid_rows + moe_out) * valid_rows

    g_hidden = jnp.sum(grad_out * hidden_f, axis=1)
    g_vec = dot32(grad_out, vectors, ((1,), (1,)), precision=top_precision)
    const_dots = const_mix[..., 0] * g_hidden[:, None] + const_mix[..., 1] * g_vec
    ffn_dots = jnp.stack(
        [
            jnp.sum(jnp.where(jnp.transpose(hit[j]), jnp.transpose(back_gates), 0.0), axis=1)
            for j in range(2)
        ],
        axis=1,
    )
    grad_gates = (
        ffn_dots
        + jnp.where(route_ids == n_ffn + 1, g_hidden[:, None], 0.0)
        + jnp.sum(const_sel * const_dots[:, None, :], axis=2)
    )
    grad_mix = jnp.stack([const_gates * g_hidden[:, None], const_gates * g_vec], axis=-1)
    grad_mix_logits = (
        const_mix * (grad_mix - jnp.sum(const_mix * grad_mix, axis=-1, keepdims=True))
    ).reshape(tok_rows, 4)
    grad_vectors = dot32(vec_coef, grad_out, ((0,), (0,)), precision=top_precision)
    grad_probs = jnp.sum(choose * grad_gates[:, :, None], axis=1)
    grad_logits = gate_probs * (
        grad_probs - jnp.sum(gate_probs * grad_probs, axis=-1, keepdims=True)
    )
    grad_hidden = (
        dot32(pick[0], back_grads)
        + dot32(pick[1], back_grads)
        + hidden_coef[:, None] * grad_out
        + dot32(grad_mix_logits, full_cg.astype(f32), ((1,), (1,)), precision=top_precision)
        + dot32(grad_logits, full_router.astype(f32), ((1,), (1,)), precision=top_precision)
    )
    grad_router = dot32(hidden_f, grad_logits, ((0,), (0,)), precision=top_precision)
    grad_cg = dot32(hidden_f, grad_mix_logits, ((0,), (0,)), precision=top_precision)
    grad_mid_norm, grad_gain_two = rms_backward(mid_rows, scale_two, gain_ffn, grad_hidden)
    grad_mid = grad_out + grad_mid_norm
    grad_attn = grad_mid.astype(bf16)
    grad_w_out = dot32(attended_low, grad_attn, ((0,), (0,)))
    grad_attended = dot32(grad_attn, full_out, ((1,), (1,))).astype(bf16)
    grad_attended = grad_attended.reshape(tok_rows, HEADS, head_size)
    row_delta = jnp.transpose(jnp.sum(grad_attended.astype(f32) * attended, axis=-1))

    def backward_step(blk_index, loop_state):
        grad_queries, grad_key_rows, grad_value_rows = loop_state
        blk_scores, key_rows, value_rows = block_scores(blk_index)
        blk_probs = jnp.exp(blk_scores - log_total[..., None])
        grad_probs_blk = jnp.einsum(
            "qhd,khd->hqk", grad_attended, value_rows, preferred_element_type=f32
        )
        grad_scores = (blk_probs * (grad_probs_blk - row_delta[..., None])).astype(bf16)
        grad_queries = grad_queries + jnp.einsum(
            "hqk,khd->qhd", grad_scores, key_rows, preferred_element_type=f32
        )
        key_part = jnp.einsum(
            "hqk,qhd->khd", grad_scores, queries, preferred_element_type=f32
        ).reshape(KBLK, feat)
        value_part = jnp.einsum(
            "hqk,qhd->khd", blk_probs.astype(bf16), grad_attended, preferred_element_type=f32
        ).reshape(KBLK, feat)
        blk_start = blk_index * KBLK
        grad_key_rows = lax.dynamic_update_slice_in_dim(grad_key_rows, key_part, blk_start, 0)
        grad_value_rows = lax.dynamic_update_slice_in_dim(grad_value_rows, value_part, blk_start, 0)
        return (grad_queries, grad_key_rows, grad_value_rows)

    back_state = (
        jnp.zeros((tok_rows, HEADS, head_size), f32),
        jnp.zeros((tok_rows * n_ctx, feat), f32),
        jnp.zeros((tok_rows * n_ctx, feat), f32),
    )
    grad_queries, grad_key_rows, grad_value_rows = lax.fori_loop(
        0, blk_count, backward_step, back_state
    )
    own_key_grads = scatter_ctx(grad_key_rows)
    own_value_grads = scatter_ctx(grad_value_rows)
    grad_q = (
        rotate(grad_queries * score_scale, positions, -1.0).reshape(tok_rows, feat).astype(bf16)
    )
    grad_k = (
        rotate(heads_of(own_key_grads * score_scale), positions, -1.0)
        .reshape(tok_rows, feat)
        .astype(bf16)
    )
    grad_v = own_value_grads.astype(bf16)
    grad_hidden_one = (
        dot32(grad_q, full_q, ((1,), (1,)))
        + dot32(grad_k, full_k, ((1,), (1,)))
        + dot32(grad_v, full_v, ((1,), (1,)))
    )
    grad_in_norm, grad_gain_one = rms_backward(in_rows, scale_one, gain_attn, grad_hidden_one)
    grad_x = grad_mid + grad_in_norm
    small_grads = jnp.concatenate(
        [
            grad_router,
            grad_cg,
            jnp.transpose(grad_vectors),
            grad_gain_one[:, None],
            grad_gain_two[:, None],
        ],
        axis=1,
    )
    small_grads = jnp.pad(small_grads, ((0, 0), (0, 128 - small_grads.shape[1])))
    out_out = scatter_rows(grad_w_out, steps_b)
    q_out = scatter_rows(dot32(hidden_one, grad_q, ((0,), (0,))), steps_a)
    v_out = scatter_rows(dot32(hidden_one, grad_v, ((0,), (0,))), steps_b)
    k_out = scatter_rows(
        jnp.concatenate([dot32(hidden_one, grad_k, ((0,), (0,))), small_grads], axis=1), steps_a
    )
    small_out = k_out[:, feat:]
    return (
        output[None],
        grad_x[None],
        jnp.concatenate([q_out, k_out[:, :feat], v_out], axis=1),
        out_out,
        small_out[:, n_all + 6],
        small_out[:, n_all + 7],
        small_out[:, :n_all],
        small_out[:, n_all : n_all + 4],
        small_out[:, n_all + 4 : n_all + 6],
        expert_grads[0],
        expert_grads[1],
        expert_grads[2],
    )


def solution(mesh):
    in_specs = (
        P(("dp", "exp"), "ctx", None),
        P(("dp", "exp")),
        P(("dp", "exp"), "ctx", None),
        P(("dp", "exp"), "ctx", None),
        P(("dp", "exp"), "ctx", None),
        P(("dp", "ctx", "exp"), None),
        P(("dp", "ctx", "exp"), None),
        P(("dp", "ctx", "exp")),
        P(("dp", "ctx", "exp")),
        P(("dp", "ctx", "exp"), None),
        P(("dp", "ctx", "exp"), None),
        P(("dp", "ctx", "exp"), None),
        P("exp", None, ("dp", "ctx")),
        P("exp", None, ("dp", "ctx")),
        P("exp", ("dp", "ctx"), None),
    )
    out_specs = (
        P(("dp", "exp"), "ctx", None),
        P(("dp", "exp"), "ctx", None),
        P(("dp", "ctx", "exp"), None),
        P(("dp", "ctx", "exp"), None),
        P(("dp", "ctx", "exp")),
        P(("dp", "ctx", "exp")),
        P(("dp", "ctx", "exp"), None),
        P(("dp", "ctx", "exp"), None),
        P(("dp", "ctx", "exp"), None),
        P("exp", None, ("dp", "ctx")),
        P("exp", None, ("dp", "ctx")),
        P("exp", ("dp", "ctx"), None),
    )
    return jax.shard_map(local, mesh=mesh, in_specs=in_specs, out_specs=out_specs, check_vma=False)
```

```python
import functools

import jax
import jax.numpy as jnp
from jax import lax
from jax.experimental import pallas as pl
from jax.experimental.pallas import tpu as pltpu
from jax.sharding import PartitionSpec as P

HEADS = 12

norm_eps = 1e-06
top_precision = lax.Precision.HIGHEST
f32 = jnp.float32
bf16 = jnp.bfloat16


CHUNK = 256
BLOCK = 512
PAIR = 128
NEG = -1e30
SCALE = 48
MICROS = {
    "project": 6, "project_other": 5, "spread": 4, "attend": 17, "mid": 9, "expert": 30, "weights_far": 10,
    "weights_near": 8, "weights_kept": 8, "weights_sum": 4, "gates_back": 11, "grads_other": 17, "back_other": 8, "grads_own": 13,
    "back_own": 13, "out_grads": 7, "output": 6, "first_norm": 4, "weights_all": 26, "pack": 3, "unpack": 4, "combine": 3,
}


def cost(name):
    return pl.CostEstimate(flops=MICROS[name] * 1000000000 // SCALE, bytes_accessed=1, transcendentals=0)


def mul_nt(a, b):
    return lax.dot_general(a, b, (((1,), (1,)), ((), ())), preferred_element_type=f32)


def mul_nn(a, b):
    return lax.dot_general(a, b, (((1,), (0,)), ((), ())), preferred_element_type=f32)


def mul_tn(a, b):
    return lax.dot_general(a, b, (((0,), (0,)), ((), ())), preferred_element_type=f32)


def head_part(rows, head):
    lane = lax.broadcasted_iota(jnp.int32, rows.shape, 1)
    return jnp.where((lane >= PAIR // 2) == (head == 1), rows, jnp.zeros_like(rows))


def key_allowed(shape, key_start, length, query_start=None):
    key = key_start + lax.broadcasted_iota(jnp.int32, shape, 0)
    allowed = key < length
    if query_start is not None:
        allowed &= key <= query_start + lax.broadcasted_iota(jnp.int32, shape, 1)
    return allowed


def attend_kernel(info, q_ref, k_ref, v_ref, ok_ref, ov_ref, out_ref, low_ref, log_ref):
    base, length, blocks = info[0], info[1], info[2]
    queries = q_ref[...]
    rows = queries.shape[0]
    half = PAIR // 2
    parts = [head_part(queries, head) for head in range(2)]
    lows = [slice(head * half, (head + 1) * half) for head in range(2)]

    def padded(first, some):
        if first == 0:
            return some
        return jnp.concatenate([jnp.zeros((some.shape[0], first), f32), some], axis=1)

    states = []
    for head in range(2):
        scores = []
        for first in range(0, rows, CHUNK):
            part = mul_nt(k_ref[first : first + CHUNK, :], parts[head][first:])
            allowed = key_allowed(part.shape, base + first, length, base + first)
            scores.append(jnp.where(allowed, part, NEG))
        top = jnp.max(scores[0], axis=0, keepdims=True)
        for i, part in enumerate(scores[1:], 1):
            more = jnp.max(part, axis=0, keepdims=True)
            first = i * CHUNK
            top = jnp.concatenate([top[:, :first], jnp.maximum(top[:, first:], more)], axis=1)
        total = jnp.zeros((1, rows), f32)
        acc = jnp.zeros((half, rows), f32)
        for i, part in enumerate(scores):
            first = i * CHUNK
            expo = jnp.exp(part - top[:, first:])
            total += padded(first, jnp.sum(expo, axis=0, keepdims=True))
            acc += padded(first, mul_tn(v_ref[first : first + CHUNK, :], expo.astype(bf16))[lows[head]])
        states.append((top, total, acc))

    def step(c, states):
        first = pl.multiple_of(c * BLOCK, BLOCK)
        keys = ok_ref[pl.ds(first, BLOCK), :]
        vals = ov_ref[pl.ds(first, BLOCK), :]
        new = []
        for head in range(2):
            top, total, acc = states[head]
            scores = mul_nt(keys, parts[head])
            scores = jnp.where(key_allowed(scores.shape, first, length), scores, NEG)
            new_top = jnp.maximum(top, jnp.max(scores, axis=0, keepdims=True))
            expo = jnp.exp(scores - new_top)
            factor = jnp.exp(top - new_top)
            total = total * factor + jnp.sum(expo, axis=0, keepdims=True)
            acc = acc * factor + mul_tn(vals, expo.astype(bf16))[lows[head]]
            new.append((new_top, total, acc))
        return tuple(new)

    states = lax.fori_loop(0, blocks, step, tuple(states))
    full = jnp.concatenate([s[2] / s[1] for s in states], axis=0)
    out = jnp.transpose(full)
    out_ref[...] = out
    low_ref[...] = out.astype(bf16)
    for head in range(2):
        log_ref[0, head : head + 1, :] = states[head][0] + jnp.log(states[head][1])


def pair_grads(keys, vals, part, grad_part, log_row, delta_row, allowed):
    probs = jnp.exp(mul_nt(keys, part) - log_row)
    probs = jnp.where(allowed, probs, 0.0)
    grad_probs = mul_nt(vals, grad_part)
    grad_scores = (probs * (grad_probs - delta_row)).astype(bf16)
    return (
        mul_nn(grad_scores, part),
        mul_nn(probs.astype(bf16), grad_part),
        mul_tn(keys, grad_scores),
    )


def other_backward(
    info, q_ref, k_ref, v_ref, grad_ref, out_ref, log_ref, dq_ref, dk_ref, dv_ref, delta_ref
):
    length, chunks = info[1], info[2] * (BLOCK // CHUNK)
    half = PAIR // 2
    queries, grads = q_ref[...], grad_ref[...]
    rows = queries.shape[0]
    product = jnp.transpose(grads.astype(f32) * out_ref[...])
    parts = [head_part(queries, head) for head in range(2)]
    grad_parts = [head_part(grads, head) for head in range(2)]
    deltas = [
        jnp.sum(product[head * half : (head + 1) * half], axis=0, keepdims=True) for head in range(2)
    ]
    for head in range(2):
        delta_ref[0, head : head + 1, :] = deltas[head]

    def step(c, dq):
        first = pl.multiple_of(c * CHUNK, CHUNK)
        keys = k_ref[pl.ds(first, CHUNK), :]
        vals = v_ref[pl.ds(first, CHUNK), :]
        allowed = key_allowed((CHUNK, rows), first, length)
        both = [
            pair_grads(
                keys, vals, parts[h], grad_parts[h], log_ref[0, h : h + 1, :], deltas[h], allowed
            )
            for h in range(2)
        ]
        dk_ref[pl.ds(first, CHUNK), :] = (both[0][0] + both[1][0]).astype(dk_ref.dtype)
        dv_ref[pl.ds(first, CHUNK), :] = (both[0][1] + both[1][1]).astype(dv_ref.dtype)
        return dq + jnp.concatenate([both[0][2][:half], both[1][2][half:]], axis=0)

    dq = lax.fori_loop(0, chunks, step, jnp.zeros((PAIR, rows), f32))
    dq_ref[...] = dq

    def clear(c, none):
        first = pl.multiple_of(c * CHUNK, CHUNK)
        dk_ref[pl.ds(first, CHUNK), :] = jnp.zeros((CHUNK, PAIR), dk_ref.dtype)
        dv_ref[pl.ds(first, CHUNK), :] = jnp.zeros((CHUNK, PAIR), dv_ref.dtype)
        return none

    lax.fori_loop(chunks, k_ref.shape[0] // CHUNK, clear, 0)


def own_backward(
    info, q_ref, k_ref, v_ref, grad_ref, log_ref, delta_ref, before_ref, dq_ref, dk_ref, dv_ref
):
    base, length = info[0], info[1]
    half = PAIR // 2
    queries, grads = q_ref[...], grad_ref[...]
    rows = queries.shape[0]
    parts = [head_part(queries, head) for head in range(2)]
    grad_parts = [head_part(grads, head) for head in range(2)]
    dq = before_ref[...]
    for first in range(0, rows, CHUNK):
        keys = k_ref[first : first + CHUNK, :]
        vals = v_ref[first : first + CHUNK, :]
        allowed = key_allowed((CHUNK, rows - first), base + first, length, base + first)
        both = [
            pair_grads(
                keys,
                vals,
                parts[h][first:],
                grad_parts[h][first:],
                log_ref[0, h : h + 1, first:],
                delta_ref[0, h : h + 1, first:],
                allowed,
            )
            for h in range(2)
        ]
        dk_ref[first : first + CHUNK, :] = both[0][0] + both[1][0]
        dv_ref[first : first + CHUNK, :] = both[0][1] + both[1][1]
        more = jnp.concatenate([both[0][2][:half], both[1][2][half:]], axis=0)
        if first:
            more = jnp.concatenate([jnp.zeros((PAIR, first), f32), more], axis=1)
        dq = dq + more
    dq_ref[...] = jnp.transpose(dq)


def per_pair(rows):
    return pl.BlockSpec((rows, PAIR), lambda i, info: (0, i))


def turned(cols):
    return pl.BlockSpec((PAIR, cols), lambda i, info: (i, 0))


def stats(cols):
    return pl.BlockSpec((1, 2, cols), lambda i, info: (i, 0, 0))


def ordered(kernel, n_in, n_deps):
    if not n_deps:
        return kernel

    def run(*refs):
        kernel(*refs[:n_in], *refs[n_in + n_deps :])

    return run


def waits(deps):
    return [pl.BlockSpec(memory_space=pl.ANY)] * len(deps)


def attn_call(kernel, info, args, in_specs, outs, out_specs, flops, name, deps=()):
    return pl.pallas_call(
        ordered(kernel, 1 + len(args), len(deps)),
        grid_spec=pltpu.PrefetchScalarGridSpec(
            num_scalar_prefetch=1,
            grid=(HEADS // 2,),
            in_specs=in_specs + waits(deps),
            out_specs=out_specs,
        ),
        out_shape=[jax.ShapeDtypeStruct(s, d) for s, d in outs],
        compiler_params=pltpu.CompilerParams(vmem_limit_bytes=48 << 20),
        cost_estimate=cost(name),
        name=name,
    )(info, *args, *deps)


def attend(info, q, k, v, other_k, other_v, deps):
    t, d = q.shape
    st = (HEADS // 2, 2, t)
    n = other_k.shape[0]
    return attn_call(
        attend_kernel, info, (q, k, v, other_k, other_v),
        [per_pair(t)] * 3 + [per_pair(n)] * 2,
        [((t, d), f32), ((t, d), bf16), (st, f32)], [per_pair(t), per_pair(t), stats(t)], 8 * t * t * d, "attend", deps,
    )


def grads_other(info, q, k, v, grad, out, log_total, deps):
    t, d = q.shape
    n = k.shape[0]
    return attn_call(
        other_backward, info, (q, k, v, grad, out, log_total),
        [per_pair(t), per_pair(n), per_pair(n), per_pair(t), per_pair(t), stats(t)],
        [((d, t), f32), ((n, d), bf16), ((n, d), bf16), ((HEADS // 2, 2, t), f32)],
        [turned(t), per_pair(n), per_pair(n), stats(t)], 10 * t * t * d, "grads_other", deps,
    )


def grads_own(info, q, k, v, grad, log_total, delta, before, deps):
    t, d = q.shape
    return attn_call(
        own_backward, info, (q, k, v, grad, log_total, delta, before),
        [per_pair(t)] * 4 + [stats(t)] * 2 + [turned(t)],
        [((t, d), f32)] * 3, [per_pair(t)] * 3, 10 * t * t * d, "grads_own", deps,
    )


def dot32(a, b, dims=((1,), (0,)), precision=None):
    return lax.dot_general(a, b, (dims, ((), ())), precision=precision, preferred_element_type=f32)


def swap(block, axis, bit):
    return lax.ppermute(block, axis, [(i, i ^ bit) for i in range(lax.axis_size(axis))])


def bits_of(axis, low=1, high=None):
    high = lax.axis_size(axis) if high is None else high
    found = []
    while low < high:
        found.append(low)
        low *= 2
    return found[::-1]


def row_weight(axis):
    x = lax.axis_size("exp")
    c = lax.axis_size("ctx")
    return {"exp": 1, "ctx": x, "dp": x * c}[axis]


def plan_steps(middle):
    far = [("dp", bit) for bit in bits_of("dp", 2)]
    mid = [(axis, bit) for axis in middle for bit in bits_of(axis)]
    near = [("dp", bit) for bit in bits_of("dp", 1, 2)]
    return far, mid, near


def row_bits(steps):
    return sorted([row_weight(axis) * bit for axis, bit in steps], reverse=True)


def nothing(*refs):
    pass


def hold(value, *others):
    return pl.pallas_call(
        nothing,
        in_specs=waits((value,) + others),
        out_specs=waits((value,))[0],
        out_shape=jax.ShapeDtypeStruct(value.shape, value.dtype),
        input_output_aliases={0: 0},
        cost_estimate=pl.CostEstimate(flops=0, bytes_accessed=0, transcendentals=0),
        name="hold",
    )(value, *others)


def gather_step(whole, placed, axis, bit, meanwhile=()):
    other = swap(whole, axis, bit)
    if meanwhile:
        whole = hold(whole, *meanwhile)
    upper = (lax.axis_index(axis) & bit) != 0
    weight = row_weight(axis) * bit
    pos = sum(1 for w in placed if w > weight)
    both = [jnp.where(upper, other, whole), jnp.where(upper, whole, other)]
    return jnp.stack(both, axis=pos), placed[:pos] + [weight] + placed[pos:]


def gather_steps(whole, placed, steps):
    for axis, bit in steps:
        whole, placed = gather_step(whole, placed, axis, bit)
    return whole, placed


def scatter_split(part, placed, axis, bit):
    pos = placed.index(row_weight(axis) * bit)
    upper = (lax.axis_index(axis) & bit) != 0
    low = lax.index_in_dim(part, 0, pos, keepdims=False)
    high = lax.index_in_dim(part, 1, pos, keepdims=False)
    sent = jnp.where(upper, low, high).astype(bf16)
    kept = jnp.where(upper, high, low).astype(f32)
    return sent, kept, placed[:pos] + placed[pos + 1 :]


def scatter_step(part, placed, axis, bit):
    sent, kept, placed = scatter_split(part, placed, axis, bit)
    return kept + swap(sent, axis, bit).astype(f32), placed


def combine_kernel(block, up_ref, kept_ref, came_ref, keep_ref, give_ref):
    total = kept_ref[...] + came_ref[...].astype(f32)
    keep_ref[...], give_ref[...] = split_rows(up_ref[0] == 1, total, block)


def combine(kept, came, placed, axis, bit, rows):
    weight = row_weight(axis) * bit
    block = rows * 2 ** sum(1 for w in placed if w < weight)
    upper = ((lax.axis_index(axis) & bit) != 0).astype(jnp.int32).reshape(1)
    shape = (kept.shape[0] // 2, kept.shape[1])
    keep, give = simple_call(
        functools.partial(combine_kernel, block), (kept, came), [(shape, f32), (shape, bf16)], 0, "combine", (), (upper,)
    )
    placed = [w for w in placed if w != weight]
    whole = (2,) * len(placed) + (-1, shape[1])
    return give.reshape(whole), keep.reshape(whole), placed


def scatter_parts(pairs, orders, far, near, rows, meanwhile):
    places = [row_bits(far + orders[0])] * len(pairs)
    parts = pairs
    for i, steps in enumerate(zip(*[reversed(order) for order in orders])):
        if i == 0:
            splits = [
                combine(keep, swap(give, *near[0]), where, *step, rows)
                for (keep, give), where, step in zip(parts, places, steps)
            ]
        else:
            splits = [scatter_split(part, where, *step) for part, where, step in zip(parts, places, steps)]
        sent, kept, places = [list(column) for column in zip(*splits)]
        came = [swap(part, *step) for part, step in zip(sent, steps)]
        if i == 0:
            kept[-1] = hold(kept[-1], *meanwhile(sent[-1]))
        parts = [a + b.astype(f32) for a, b in zip(kept, came)]
    placed = places[0]
    part = jnp.concatenate(parts, axis=-1)
    for axis, bit in reversed(far):
        part, placed = scatter_step(part, placed, axis, bit)
    return part


def pack_kernel(gate_ref, up_ref, down_ref, out_ref):
    out_ref[0, 0] = gate_ref[0]
    out_ref[0, 1] = up_ref[0]
    out_ref[0, 2] = jnp.transpose(down_ref[0])


def unpack_kernel(back_ref, gate_ref, up_ref, down_ref):
    gate_ref[0] = back_ref[0, 0].astype(f32)
    up_ref[0] = back_ref[0, 1].astype(f32)
    down_ref[0] = jnp.transpose(back_ref[0, 2].astype(f32))


def one_of(*shape):
    return pl.BlockSpec((1,) + shape, lambda i: (i,) + (0,) * len(shape))


def pack_expert(w_gate, w_up, w_down, deps):
    n, d, f = w_gate.shape
    return pl.pallas_call(
        ordered(pack_kernel, 3, len(deps)),
        grid=(n,),
        in_specs=[one_of(d, f), one_of(d, f), one_of(f, d)] + waits(deps),
        out_specs=one_of(3, d, f),
        out_shape=jax.ShapeDtypeStruct((n, 3, d, f), w_gate.dtype),
        cost_estimate=cost("pack"),
        name="pack",
    )(w_gate, w_up, w_down, *deps)


def unpack_expert(back, deps):
    n, _, d, f = back.shape
    return pl.pallas_call(
        ordered(unpack_kernel, 1, len(deps)),
        grid=(n,),
        in_specs=[one_of(3, d, f)] + waits(deps),
        out_specs=[one_of(d, f), one_of(d, f), one_of(f, d)],
        out_shape=[jax.ShapeDtypeStruct(shape, f32) for shape in ((n, d, f), (n, d, f), (n, f, d))],
        cost_estimate=cost("unpack"),
        name="unpack",
    )(back, *deps)


def trade_far(parts):
    n_own = parts.shape[0]
    reps = lax.axis_size("dp") // n_own
    groups = [[i * reps + r for i in range(n_own)] for r in range(reps)]
    return lax.all_to_all(parts, "dp", 0, 0, axis_index_groups=groups, tiled=True)


def near_steps(n_own):
    reps = lax.axis_size("dp") // n_own
    return [("ctx", bit) for bit in bits_of("ctx")] + [("dp", bit) for bit in bits_of("dp", 1, reps)]


def gather_expert_near(groups, steps):
    for axis, bit in steps:
        groups = groups + [swap(group, axis, bit) for group in groups]
    return groups


def scatter_expert_near(groups, steps):
    for axis, bit in reversed(steps):
        n = len(groups) // 2
        came = [swap(group.astype(bf16), axis, bit) for group in groups[n:]]
        groups = [a.astype(f32) + b.astype(f32) for a, b in zip(groups[:n], came)]
    return groups[0]


def weights_sum_kernel(kept_ref, came_ref, out_ref):
    out_ref[...] = (kept_ref[...] + came_ref[...].astype(f32)).astype(bf16)


def rms_scale(rows):
    return lax.rsqrt(jnp.mean(rows * rows, axis=-1, keepdims=True) + norm_eps)


def rms_backward(in_rows, inv_scale, gain_vec, grad_rows):
    normed = in_rows * inv_scale
    gain_grad = jnp.sum(grad_rows * normed, axis=0, keepdims=True)
    inner_grad = grad_rows * gain_vec
    back_rows = inv_scale * (
        inner_grad - normed * jnp.mean(inner_grad * normed, axis=-1, keepdims=True)
    )
    return (back_rows, gain_grad)


def rope(rows, cos, sin):
    lane = lax.broadcasted_iota(jnp.int32, (rows.shape[0], PAIR), 1)
    low = lane % (PAIR // 2) < PAIR // 4
    parts = []
    for first in range(0, rows.shape[1], PAIR):
        part = rows[:, first : first + PAIR]
        other = jnp.where(low, pltpu.roll(part, PAIR - PAIR // 4, 1), pltpu.roll(part, PAIR // 4, 1))
        parts.append(part * cos + other * sin)
    return jnp.concatenate(parts, axis=1)


def gain_row(first_ref, lane):
    small = first_ref[:, first_ref.shape[1] - PAIR :].astype(f32)
    return jnp.transpose(small)[lane : lane + 1]


def project_kernel(scale, lane, x_ref, first_ref, second_ref, cos_ref, sin_ref, h_ref, q_ref, k_ref, v_ref):
    rows = x_ref[...].astype(f32)
    d = rows.shape[1]
    hidden = (rows * rms_scale(rows) * gain_row(first_ref, lane)).astype(bf16)
    h_ref[...] = hidden
    cos, sin = cos_ref[...], sin_ref[...]
    k_ref[...] = rope(mul_nn(hidden, first_ref[:, d : 2 * d]), cos, sin).astype(bf16)
    v_ref[...] = mul_nn(hidden, second_ref[:, :d]).astype(bf16)
    q_ref[...] = (rope(mul_nn(hidden, first_ref[:, :d]), cos, sin) * scale).astype(bf16)


def other_project_kernel(lane, x_ref, first_ref, second_ref, cos_ref, sin_ref, h_ref, k_ref, v_ref):
    rows = x_ref[...].astype(f32)
    d = rows.shape[1]
    hidden = (rows * rms_scale(rows) * gain_row(first_ref, lane)).astype(bf16)
    h_ref[...] = hidden
    k_ref[...] = rope(mul_nn(hidden, first_ref[:, d : 2 * d]), cos_ref[...], sin_ref[...]).astype(bf16)
    v_ref[...] = mul_nn(hidden, second_ref[:, :d]).astype(bf16)


def other_back_kernel(
    dk_ref, dv_ref, h_ref, first_ref, second_ref, cos_ref, sin_ref, x_ref, dwk_ref, dwv_ref, dh_ref, dgain_ref
):
    first = pl.program_id(0) == 0
    d = x_ref.shape[1]
    grad_k = rope(dk_ref[...].astype(f32), cos_ref[...], -sin_ref[...]).astype(bf16)
    grad_v = dv_ref[...]
    hidden = h_ref[...]
    rows = x_ref[...].astype(f32)
    dh = mul_nt(grad_k, first_ref[:, d : 2 * d]) + mul_nt(grad_v, second_ref[:, :d])
    dh_ref[...] = dh.astype(bf16)
    dwk, dwv = mul_tn(hidden, grad_k), mul_tn(hidden, grad_v)
    dgain = jnp.sum(dh * rows * rms_scale(rows), axis=0, keepdims=True)

    @pl.when(first)
    def _():
        dwk_ref[...] = dwk
        dwv_ref[...] = dwv
        dgain_ref[...] = dgain

    @pl.when(jnp.logical_not(first))
    def _():
        dwk_ref[...] += dwk
        dwv_ref[...] += dwv
        dgain_ref[...] += dgain


def split_rows(upper, rows, block):
    keep, give = [], []
    for first in range(0, rows.shape[0], 2 * block):
        low, high = rows[first : first + block], rows[first + block : first + 2 * block]
        keep.append(jnp.where(upper, high, low))
        give.append(jnp.where(upper, low, high))
    return jnp.concatenate(keep, axis=0), jnp.concatenate(give, axis=0).astype(bf16)


def own_back_kernel(
    scale, block, core_ref, dq_ref, dk_ref, dv_ref, h_ref, first_ref, second_ref, cos_ref, sin_ref, x_ref, mwk_ref, mwv_ref, mgain_ref,
    keep_ref, give_ref, rest_ref, dh_ref,
):
    d = h_ref.shape[1]
    upper = core_ref[0] == 1
    cos, sin = cos_ref[...], -sin_ref[...]
    hidden = h_ref[...]
    grad_q = rope(dq_ref[...] * scale, cos, sin).astype(bf16)
    keep_ref[:, :d], give_ref[:, :d] = split_rows(upper, mul_tn(hidden, grad_q), block)
    dh = mul_nt(grad_q, first_ref[:, :d])
    grad_k = rope(dk_ref[...], cos, sin).astype(bf16)
    dw_k = mul_tn(hidden, grad_k) + mwk_ref[...]
    keep_ref[:, d : 2 * d], give_ref[:, d : 2 * d] = split_rows(upper, dw_k, block)
    dh += mul_nt(grad_k, first_ref[:, d : 2 * d])
    grad_v = dv_ref[...].astype(bf16)
    rest_ref[...] = mul_tn(hidden, grad_v) + mwv_ref[...]
    dh += mul_nt(grad_v, second_ref[:, :d])
    dh_ref[...] = dh
    rows = x_ref[...].astype(f32)
    dgain = jnp.sum(dh * rows * rms_scale(rows), axis=0, keepdims=True) + mgain_ref[...]
    lane = lax.broadcasted_iota(jnp.int32, (d, PAIR), 1)
    column = jnp.transpose(jnp.broadcast_to(dgain, (8, d)))[:, :1]
    tail = jnp.where(lane == 0, column, 0.0)
    keep_ref[:, 2 * d :], give_ref[:, 2 * d :] = split_rows(upper, tail, block)


def first_norm_kernel(lane, dh_ref, more_ref, x_ref, first_ref, mid_ref, dx_ref):
    rows = x_ref[...].astype(f32)
    grad = dh_ref[...] + more_ref[...].astype(f32)
    back, _ = rms_backward(rows, rms_scale(rows), gain_row(first_ref, lane), grad)
    dx_ref[...] = mid_ref[...] + back


def simple_call(kernel, args, outs, flops, name, deps=(), scalars=()):
    whole = pl.BlockSpec(memory_space=pltpu.VMEM)
    small = pl.BlockSpec(memory_space=pltpu.SMEM)
    return pl.pallas_call(
        ordered(kernel, len(scalars) + len(args), len(deps)),
        in_specs=[small] * len(scalars) + [whole] * len(args) + waits(deps),
        out_shape=[jax.ShapeDtypeStruct(s, d) for s, d in outs],
        compiler_params=pltpu.CompilerParams(vmem_limit_bytes=56 << 20),
        cost_estimate=cost(name),
        name=name,
    )(*scalars, *args, *deps)


def expert_kernel(n_groups, *refs):
    x_ref, g_ref = refs[:2]
    w_refs = refs[2 : 2 + n_groups]
    out_ref, dx_ref, act_ref, dg_ref, du_ref, gx_ref, gg_ref = refs[2 + n_groups :]
    grads = g_ref[...]
    n, d = grads.shape
    rows = x_ref[:, :d]
    gates = x_ref[:, d : d + 1].astype(f32) + x_ref[:, d + 1 : d + 2].astype(f32)
    gx_ref[...] = jnp.transpose((rows.astype(f32) * gates).astype(bf16))
    gg_ref[...] = jnp.transpose((grads.astype(f32) * gates).astype(bf16))
    out = jnp.zeros((n, d), f32)
    back = jnp.zeros((n, d), f32)
    col = 0
    for w_ref in w_refs:
        wg, wu, wd = [
            jnp.concatenate([w_ref[p, m] for p in range(w_ref.shape[0])], axis=1) for m in range(3)
        ]
        width = wg.shape[1]
        gate_pre = mul_nn(rows, wg)
        up_pre = mul_nn(rows, wu)
        sig = 1.0 / (1.0 + jnp.exp(-gate_pre))
        silu = gate_pre * sig
        act = (silu * up_pre).astype(bf16)
        act_ref[:, col : col + width] = act
        out += mul_nt(act, wd)
        grad_act = mul_nn(grads, wd)
        grad_gate = (grad_act * up_pre * sig * (1.0 + gate_pre * (1.0 - sig))).astype(bf16)
        grad_up = (grad_act * silu).astype(bf16)
        dg_ref[:, col : col + width] = grad_gate
        du_ref[:, col : col + width] = grad_up
        back += mul_nt(grad_gate, wg) + mul_nt(grad_up, wu)
        col += width
    low = out.astype(bf16)
    out_ref[...] = low
    dx_ref[:, :d] = back.astype(bf16)
    dots = jnp.sum(grads.astype(f32) * low.astype(f32), axis=1, keepdims=True)
    high, rest = halves(dots)
    lane = lax.broadcasted_iota(jnp.int32, (n, PAIR), 1)
    pair = jnp.where(lane == 0, high.astype(f32), jnp.where(lane == 1, rest.astype(f32), 0.0))
    dx_ref[:, d:] = pair.astype(bf16)


def expert_call(x, g, groups):
    n, d = g.shape
    wide = x.shape[1]
    ff = sum(group.shape[0] * group.shape[3] for group in groups)
    blk = min(512, n)

    def rows(cols):
        return pl.BlockSpec((blk, cols), lambda i: (i, 0))

    widths = [d, wide, ff, ff, ff]
    across = pl.BlockSpec((d, blk), lambda i: (0, i))
    return pl.pallas_call(
        functools.partial(expert_kernel, len(groups)),
        grid=(n // blk,),
        in_specs=[rows(wide), rows(d)] + [pl.BlockSpec(group.shape, lambda i: (0, 0, 0, 0)) for group in groups],
        out_specs=[rows(cols) for cols in widths] + [across] * 2,
        out_shape=[jax.ShapeDtypeStruct((n, cols), bf16) for cols in widths]
        + [jax.ShapeDtypeStruct((d, n), bf16)] * 2,
        compiler_params=pltpu.CompilerParams(vmem_limit_bytes=60 << 20),
        cost_estimate=cost("expert"),
        name="expert",
    )(x, g, *groups)


def expert_weights_kernel(n_came, n_through, x_ref, gg_ref, act_ref, dg_ref, du_ref, *refs):
    out_ref = refs[n_came + n_through]
    pieces, _, _, width = out_ref.shape
    for m, (left, right) in enumerate([(x_ref, dg_ref), (x_ref, du_ref), (gg_ref, act_ref)]):
        grad = mul_nn(left[...], right[...])
        for p in range(pieces):
            part = grad[:, p * width : (p + 1) * width]
            if n_came:
                part += refs[0][p, m].astype(f32)
            out_ref[p, m] = part.astype(out_ref.dtype)


def expert_weights(x, gg, act, dg, du, start, pieces, width, kind, name, came=None, came_start=0, through=None, deps=()):
    d, n = x.shape
    step = min(4, pieces)
    cols = step * width
    rows = pl.BlockSpec((d, n), lambda i: (0, 0))
    part = pl.BlockSpec((n, cols), lambda i: (0, start // cols + i))
    more = [] if came is None else [came]
    passed = [] if through is None else [through]
    block = (step, 3, d, width)
    return pl.pallas_call(
        ordered(functools.partial(expert_weights_kernel, len(more), len(passed)), 5 + len(more) + len(passed), len(deps)),
        grid=(pieces // step,),
        in_specs=[rows, rows, part, part, part]
        + [pl.BlockSpec(block, lambda i: (came_start // step + i, 0, 0, 0))] * len(more)
        + waits(passed)
        + waits(deps),
        out_specs=[pl.BlockSpec(block, lambda i: (i, 0, 0, 0))] + waits(passed),
        out_shape=[jax.ShapeDtypeStruct((pieces, 3, d, width), kind)]
        + [jax.ShapeDtypeStruct(p.shape, p.dtype) for p in passed],
        input_output_aliases={5 + len(more): 1} if passed else {},
        compiler_params=pltpu.CompilerParams(vmem_limit_bytes=60 << 20),
        cost_estimate=cost(name),
        name=name,
    )(x, gg, act, dg, du, *more, *passed, *deps)


def lane_of(rows):
    return lax.broadcasted_iota(jnp.int32, (rows, PAIR), 1)


def col(rows, i):
    return rows[:, i : i + 1]


def halves(rows):
    high = rows.astype(bf16)
    return high, (rows - high.astype(f32)).astype(bf16)


VEC, COEF, GATE, CONST = 0, 2, 3, 5


def mid_kernel(
    n_all, att_ref, first_ref, second_ref, x_ref, prev_ref, routes_ref, place_ref,
    mid_ref, hidden_ref, scal_ref, send_ref,
):
    n_ffn = n_all - 4
    d = x_ref.shape[1]
    mid = x_ref[...].astype(f32) + mul_nn(att_ref[...], second_ref[:, d:])
    mid_ref[...] = mid
    hidden = (mid * rms_scale(mid) * gain_row(first_ref, n_all + 7)).astype(bf16)
    hidden_ref[...] = hidden
    rows, d = hidden.shape
    lane = lane_of(rows)
    raw = mul_nn(hidden, first_ref[:, 2 * d :])
    logits = jnp.where(lane < n_all, raw + prev_ref[...], NEG)
    expo = jnp.exp(logits - jnp.max(logits, axis=1, keepdims=True))
    probs = jnp.where(lane < n_all, expo / jnp.sum(expo, axis=1, keepdims=True), 0.0)
    ids = [col(routes_ref[...], j) for j in range(2)]
    gates = [jnp.sum(jnp.where(lane == r, probs, 0.0), axis=1, keepdims=True) for r in ids]
    scal = probs
    coef = sum(jnp.where(r == n_ffn + 1, g, 0.0) for r, g in zip(ids, gates))
    base = n_all + 4
    for c in range(2):
        gap = col(raw, n_all + 2 * c + 1) - col(raw, n_all + 2 * c)
        first, second = 1.0 / (1.0 + jnp.exp(gap)), 1.0 / (1.0 + jnp.exp(-gap))
        const = sum(jnp.where(r == n_ffn + 2 + c, g, 0.0) for r, g in zip(ids, gates))
        coef += first * const
        scal = jnp.where(lane == n_all + 2 * c, first, scal)
        scal = jnp.where(lane == n_all + 2 * c + 1, second, scal)
        scal = jnp.where(lane == base + VEC + c, second * const, scal)
        scal = jnp.where(lane == base + CONST + c, const, scal)
        scal = jnp.where(lane == base + GATE + c, gates[c], scal)
    scal_ref[...] = jnp.where(lane == base + COEF, coef, scal)
    slots = send_ref.shape[0]
    row = lax.broadcasted_iota(jnp.int32, (slots, rows), 0)
    hits = [(row == place_ref[j : j + 1, :]) for j in range(2)]
    both = jnp.where(hits[0] | hits[1], 1.0, 0.0).astype(bf16)
    send_ref[:, :d] = mul_nn(both, hidden).astype(bf16)
    extra = jnp.zeros((slots, PAIR), f32)
    for j in range(2):
        high, low = halves(gates[j])
        pair = jnp.where(lane == 0, high.astype(f32), jnp.where(lane == 1, low.astype(f32), 0.0))
        extra += mul_nn(jnp.where(hits[j], 1.0, 0.0).astype(bf16), pair.astype(bf16))
    send_ref[:, d:] = extra.astype(bf16)


def spread_kernel(cot_ref, valid_ref, place_ref, send_ref):
    grads = (cot_ref[...] * valid_ref[...]).astype(bf16)
    row = lax.broadcasted_iota(jnp.int32, (send_ref.shape[0], grads.shape[0]), 0)
    hit = (row == place_ref[0:1, :]) | (row == place_ref[1:2, :])
    send_ref[...] = mul_nn(jnp.where(hit, 1.0, 0.0).astype(bf16), grads).astype(bf16)


def picked_rows(place_ref, j, table):
    rows, slots = place_ref.shape[0], table.shape[0]
    slot = lax.broadcasted_iota(jnp.int32, (rows, slots), 1)
    pick = jnp.where(slot == col(place_ref[...], j), 1.0, 0.0).astype(bf16)
    return mul_nn(pick, table)


def gates_back_kernel(
    n_all, back_ref, place_ref, routes_ref, scal_ref, hidden_ref, mid_ref, cot_ref, valid_ref, first_ref, second_ref,
    gmid_ref, gatt_ref, mix_ref, dgain_ref,
):
    n_ffn = n_all - 4
    base = n_all + 4
    scal = scal_ref[...]
    grads = cot_ref[...] * valid_ref[...]
    rows, d = grads.shape
    lane = lane_of(rows)
    hidden = hidden_ref[...].astype(f32)
    small = first_ref[:, 2 * d :]
    g_hidden = jnp.sum(grads * hidden, axis=1, keepdims=True)
    high, low = halves(grads)
    g_small = mul_nn(high, small) + mul_nn(low, small)
    table = back_ref[...]
    grad_hidden = col(scal, base + COEF) * grads
    grad_probs = jnp.zeros((rows, PAIR), f32)
    for j in range(2):
        r = col(routes_ref[...], j)
        came = picked_rows(place_ref, j, table)
        grad_hidden += col(scal, base + GATE + j) * came[:, :d]
        dots = came[:, d : d + 1] + came[:, d + 1 : d + 2]
        dots += jnp.where(r == n_ffn + 1, g_hidden, 0.0)
        for c in range(2):
            whole = col(scal, n_all + 2 * c) * g_hidden + col(scal, n_all + 2 * c + 1) * col(g_small, base + c)
            dots += jnp.where(r == n_ffn + 2 + c, whole, 0.0)
        grad_probs += jnp.where(lane == r, dots, 0.0)
    probs = jnp.where(lane < n_all, scal, 0.0)
    mix = probs * (grad_probs - jnp.sum(probs * grad_probs, axis=1, keepdims=True))
    for c in range(2):
        first, second = col(scal, n_all + 2 * c), col(scal, n_all + 2 * c + 1)
        const = col(scal, base + CONST + c)
        a, b = const * g_hidden, const * col(g_small, base + c)
        inner = first * a + second * b
        mix = jnp.where(lane == n_all + 2 * c, first * (a - inner), mix)
        mix = jnp.where(lane == n_all + 2 * c + 1, second * (b - inner), mix)
    mix_ref[...] = mix
    high, low = halves(mix)
    grad_hidden += mul_nt(high, small) + mul_nt(low, small)
    mid = mid_ref[...]
    back, dgain = rms_backward(mid, rms_scale(mid), gain_row(first_ref, n_all + 7), grad_hidden)
    dgain_ref[...] = dgain
    grad_mid = grads + back
    gmid_ref[...] = grad_mid
    gatt_ref[...] = mul_nt(grad_mid.astype(bf16), second_ref[:, d:]).astype(bf16)


def out_grads_kernel(
    n_all, block, core_ref, att_ref, gmid_ref, hidden_ref, mix_ref, scal_ref, cot_ref, valid_ref, dgain_ref, rest_ref,
    keep_ref, give_ref,
):
    d = att_ref.shape[1]
    base = n_all + 4
    first = rest_ref.shape[1]
    upper = core_ref[0] == 1
    keep_ref[:, :first], give_ref[:, :first] = split_rows(upper, rest_ref[...], block)
    dw_out = mul_tn(att_ref[...], gmid_ref[...].astype(bf16))
    keep_ref[:, first : first + d], give_ref[:, first : first + d] = split_rows(upper, dw_out, block)
    hidden = hidden_ref[...]
    high, low = halves(mix_ref[...])
    grads = mul_tn(hidden, high) + mul_tn(hidden, low)
    scal = scal_ref[...]
    lane = lane_of(scal.shape[0])
    vec = jnp.where((lane >= base + VEC) & (lane < base + VEC + 2), scal, 0.0)
    vec_high, vec_low = halves(vec)
    g_high, g_low = halves(cot_ref[...] * valid_ref[...])
    grads += mul_tn(g_high, vec_high) + mul_tn(g_high, vec_low) + mul_tn(g_low, vec_high)
    column = jnp.transpose(jnp.broadcast_to(dgain_ref[...], (8, d)))[:, :1]
    lane = lane_of(d)
    tail = jnp.where(lane == base + 2, column, grads)
    keep_ref[:, first + d :], give_ref[:, first + d :] = split_rows(upper, tail, block)


def output_kernel(n_all, back_ref, place_ref, scal_ref, hidden_ref, mid_ref, valid_ref, first_ref, out_ref):
    base = n_all + 4
    scal = scal_ref[...]
    lane = lane_of(scal.shape[0])
    vec = jnp.where((lane >= base + VEC) & (lane < base + VEC + 2), scal, 0.0)
    high, low = halves(vec)
    small = first_ref[:, first_ref.shape[1] - PAIR :]
    total = mid_ref[...] + mul_nt(high, small) + mul_nt(low, small)
    total += col(scal, base + COEF) * hidden_ref[...].astype(f32)
    table = back_ref[...]
    for j in range(2):
        total += col(scal, base + GATE + j) * picked_rows(place_ref, j, table)
    out_ref[...] = total * valid_ref[...]


def local(
    residual_in,
    lengths,
    routes,
    prev_logits,
    cotangent,
    w_qkv,
    w_out,
    attn_gain,
    ffn_gain,
    router,
    const_gate,
    const_vec,
    w_gate,
    w_up,
    w_down,
):
    tok_rows = residual_in.shape[1]
    feat = residual_in.shape[2]
    head_size = feat // HEADS
    score_scale = head_size ** (-0.5)
    n_dp = lax.axis_size("dp")
    n_ctx = lax.axis_size("ctx")
    n_exp = lax.axis_size("exp")
    own_exp = w_gate.shape[0]
    reps = n_dp // own_exp
    n_all = router.shape[1]
    n_ffn = n_all - 4
    cap_rows = tok_rows // 4
    sub_rows = cap_rows // reps
    n_slots = n_ffn * cap_rows
    ctx_rank = lax.axis_index("ctx")
    positions = ctx_rank * tok_rows + jnp.arange(tok_rows, dtype=jnp.int32)
    length = lengths[0]
    valid_rows = (positions < length).astype(f32)[:, None]

    def gather_ctx(rows):
        if n_ctx == 2:
            return swap(rows, "ctx", 1)
        for bit in reversed(bits_of("ctx")):
            other = swap(rows, "ctx", bit)
            upper = (ctx_rank & bit) != 0
            rows = jnp.concatenate([jnp.where(upper, other, rows), jnp.where(upper, rows, other)], axis=0)
        return rows

    def scatter_ctx(rows):
        if n_ctx == 2:
            return swap(rows, "ctx", 1)
        for bit in bits_of("ctx"):
            low, high = jnp.split(rows, 2, axis=0)
            upper = (ctx_rank & bit) != 0
            sent = jnp.where(upper, low, high).astype(bf16)
            rows = jnp.where(upper, high, low).astype(f32) + swap(sent, "ctx", bit).astype(f32)
        return rows

    route_ids = routes[0]
    choose = (route_ids[:, :, None] == jnp.arange(n_all, dtype=jnp.int32)[None, None, :]).astype(f32)
    both = jnp.sum(choose, axis=1)
    before = jnp.arange(tok_rows)
    before = (before[None, :] < before[:, None]).astype(bf16)
    counts = dot32(before, both.astype(bf16))
    slot_ids = jnp.sum(choose * counts[:, None, :], axis=-1).astype(jnp.int32)
    is_ffn = route_ids < n_ffn
    place = (
        ((route_ids % own_exp) * reps + slot_ids // sub_rows) * n_exp + route_ids // own_exp
    ) * sub_rows + slot_ids % sub_rows
    place = jnp.where(is_ffn, place, -1)
    row_ids = jnp.arange(n_slots, dtype=jnp.int32)
    place_rows = jnp.transpose(place)

    def to_experts(rows):
        return lax.all_to_all(
            rows.reshape(n_dp * n_exp, sub_rows, -1),
            ("dp", "exp"),
            split_axis=0,
            concat_axis=0,
            tiled=True,
        ).reshape(n_slots, -1)

    (grad_sent,) = simple_call(
        spread_kernel, (cotangent[0], valid_rows, place_rows), [((n_slots, feat), bf16)], 0, "spread"
    )

    small = jnp.concatenate(
        [router, const_gate, const_vec, attn_gain[:, None], ffn_gain[:, None]], axis=1
    )
    small = jnp.pad(small, ((0, 0), (0, PAIR - small.shape[1])))
    width = 2 * feat + PAIR
    far, mid_a, near = plan_steps(("ctx", "exp"))
    _, mid_b, _ = plan_steps(("exp", "ctx"))
    lane = jnp.arange(PAIR, dtype=jnp.int32)
    half = head_size // 2
    inv_freq = 10000.0 ** (-2.0 * (lane % half).astype(f32) / head_size)
    sign = jnp.where(lane % head_size < half, -1.0, 1.0)

    def turns(where):
        angles = where.astype(f32)[:, None] * inv_freq[None, :]
        return jnp.cos(angles), jnp.sin(angles) * sign[None, :]

    cosine, sine = turns(positions)
    other_start = (1 - ctx_rank) * tok_rows if n_ctx == 2 else 0
    n_other = tok_rows if n_ctx == 2 else tok_rows * n_ctx
    other_cos, other_sin = turns(other_start + jnp.arange(n_other, dtype=jnp.int32))
    other_in = gather_ctx(residual_in[0])
    rows = jnp.concatenate([w_qkv[:, : 2 * feat], small, w_qkv[:, 2 * feat :], w_out], axis=1)
    packed = pack_expert(w_gate, w_up, w_down, ())
    windows = [()] * (len(far) - 2) + [(packed,), (other_in, cosine, sine, other_cos, other_sin)]
    whole, placed = rows, []
    for step, meanwhile in zip(far, windows):
        whole, placed = gather_step(whole, placed, *step, meanwhile)
    group = trade_far(hold(packed, whole))
    part_a, part_b = whole[..., :width], whole[..., width:]
    placed_a, placed_b = placed, placed
    for i, (step_a, step_b) in enumerate(zip(mid_a, mid_b)):
        part_a, placed_a = gather_step(part_a, placed_a, *step_a)
        part_b, placed_b = gather_step(part_b, placed_b, *step_b, () if i else (grad_sent,))
    first_part, _ = gather_steps(part_a, placed_a, near)
    second_part, _ = gather_steps(part_b, placed_b, near)
    first_part = first_part.reshape(feat, width)
    second_part = second_part.reshape(feat, 2 * feat)

    rows_low = ((tok_rows, feat), bf16)
    rows_full = ((tok_rows, feat), f32)
    square = 2 * tok_rows * feat * feat
    hidden_one, queries, own_keys, own_values = simple_call(
        functools.partial(project_kernel, score_scale, n_all + 6),
        (residual_in[0], first_part, second_part, cosine, sine), [rows_low] * 4, 3 * square, "project",
    )
    tok_spec = pl.BlockSpec((tok_rows, feat), lambda i: (i, 0))
    turn_spec = pl.BlockSpec((tok_rows, PAIR), lambda i: (i, 0))

    def fixed(rows, cols):
        return pl.BlockSpec((rows, cols), lambda i: (0, 0))

    other_hidden, other_keys, other_values = pl.pallas_call(
        functools.partial(other_project_kernel, n_all + 6),
        grid=(n_other // tok_rows,),
        in_specs=[tok_spec, fixed(feat, width), fixed(feat, 2 * feat), turn_spec, turn_spec],
        out_specs=[tok_spec] * 3,
        out_shape=[jax.ShapeDtypeStruct((n_other, feat), bf16)] * 3,
        compiler_params=pltpu.CompilerParams(vmem_limit_bytes=56 << 20),
        cost_estimate=cost("project_other"),
        name="project_other",
    )(other_in, first_part, second_part, other_cos, other_sin)
    grad_rows_in = to_experts(hold(grad_sent, group, hidden_one, other_keys))
    info = jnp.stack([ctx_rank * tok_rows, length, ctx_rank]).astype(jnp.int32)
    prev = jnp.pad(prev_logits[0], ((0, 0), (0, PAIR - n_all)))
    attended, attended_low, log_total = attend(
        info, queries, own_keys, own_values, other_keys, other_values, (group, prev, place)
    )

    mid_rows, hidden, scalars, sent_rows = simple_call(
        functools.partial(mid_kernel, n_all),
        (attended_low, first_part, second_part, residual_in[0], prev, route_ids, place_rows),
        [rows_full, rows_low, ((tok_rows, PAIR), f32), ((n_slots, feat + PAIR), bf16)], 0, "mid",
    )
    rows_in = to_experts(sent_rows)

    steps_near = near_steps(own_exp)
    groups = gather_expert_near([group], steps_near)
    piece_width = group.shape[3]
    if piece_width < PAIR:
        merge = PAIR // piece_width
        whole = jnp.concatenate(groups).reshape(-1, merge, 3, feat, piece_width)
        groups = [jnp.moveaxis(whole, 1, 3).reshape(-1, 3, feat, PAIR)]
    expert_out, grad_in, act, grad_gate_pre, grad_up_pre, gated_rows, grad_expert_out = expert_call(
        rows_in, grad_rows_in, groups
    )
    back_grads = to_experts(grad_in)
    n_groups = 2 ** len(steps_near)
    flows = (gated_rows, grad_expert_out, act, grad_gate_pre, grad_up_pre)
    if piece_width < PAIR or len(steps_near) != 2:
        step = max(piece_width, PAIR)
        (whole,) = expert_weights(*flows, 0, act.shape[1] // step, step, f32, "weights_all")
        if piece_width < PAIR:
            whole = jnp.moveaxis(whole.reshape(-1, 3, feat, merge, piece_width), 3, 1)
        whole = whole.reshape(n_groups, own_exp, 3, feat, piece_width)
        expert_sum = scatter_expert_near([whole[i] for i in range(n_groups)], steps_near)
        weights_done = ()
    else:
        group_cols = own_exp * piece_width
        (far_sent,) = expert_weights(*flows, 2 * group_cols, 2 * own_exp, piece_width, bf16, "weights_far")
        far_came = swap(far_sent, *steps_near[1])
        (near_sent,) = expert_weights(
            *flows, group_cols, own_exp, piece_width, bf16, "weights_near", far_came, own_exp
        )
        near_came = swap(near_sent, *steps_near[0])
        kept, expert_out = expert_weights(
            *flows, 0, own_exp, piece_width, f32, "weights_kept", far_came, 0, expert_out, (near_sent,)
        )
        weights_done = (near_sent, kept)
    back_rows = to_experts(expert_out)
    small_shape = ((tok_rows, PAIR), f32)
    grad_mid, grad_attended, grad_mix, grad_gain_two = simple_call(
        functools.partial(gates_back_kernel, n_all),
        (
            back_grads, place, route_ids, scalars, hidden, mid_rows, cotangent[0], valid_rows, first_part, second_part,
        ),
        [rows_full, rows_low, small_shape, ((1, feat), f32)], 0, "gates_back", weights_done,
    )
    grad_queries, other_dk, other_dv, delta = grads_other(
        info, queries, other_keys, other_values, grad_attended, attended, log_total, ()
    )
    half_cols = (4 * feat + 2 * PAIR) // 2
    core = (lax.axis_index("dp") & 1).astype(jnp.int32).reshape(1)
    core_block = feat // (n_dp * n_ctx * n_exp) * row_weight("dp")
    more_wk, more_wv, other_dh, more_gain = pl.pallas_call(
        other_back_kernel,
        grid=(n_other // tok_rows,),
        in_specs=[
            tok_spec, tok_spec, tok_spec, fixed(feat, width), fixed(feat, 2 * feat), turn_spec, turn_spec, tok_spec,
        ],
        out_specs=[fixed(feat, feat), fixed(feat, feat), tok_spec, fixed(1, feat)],
        out_shape=[
            jax.ShapeDtypeStruct((feat, feat), f32), jax.ShapeDtypeStruct((feat, feat), f32),
            jax.ShapeDtypeStruct((n_other, feat), bf16), jax.ShapeDtypeStruct((1, feat), f32),
        ],
        compiler_params=pltpu.CompilerParams(vmem_limit_bytes=56 << 20),
        cost_estimate=cost("back_other"),
        name="back_other",
    )(other_dk, other_dv, other_hidden, first_part, second_part, other_cos, other_sin, other_in)
    more_dh = scatter_ctx(other_dh)
    grad_queries, own_dk, own_dv = grads_own(
        info, queries, own_keys, own_values, grad_attended, log_total, delta, grad_queries, (back_rows, other_dh)
    )
    if weights_done:
        (expert_sum,) = simple_call(
            weights_sum_kernel, (kept, near_came), [(kept.shape, bf16)], 0, "weights_sum", (own_dk,)
        )
    else:
        expert_sum = expert_sum.astype(bf16)
    expert_back = trade_far(expert_sum)
    first_keep, first_give, dw_rest, grad_hidden_one = simple_call(
        functools.partial(own_back_kernel, score_scale, core_block),
        (
            grad_queries, own_dk, own_dv, hidden_one, first_part, second_part, cosine, sine, residual_in[0],
            more_wk, more_wv, more_gain,
        ),
        [((feat // 2, half_cols), f32), ((feat // 2, half_cols), bf16), ((feat, feat), f32), rows_full],
        6 * square, "back_own", (expert_sum,), (core,),
    )
    out_keep, out_give = simple_call(
        functools.partial(out_grads_kernel, n_all, core_block),
        (attended_low, grad_mid, hidden, grad_mix, scalars, cotangent[0], valid_rows, grad_gain_two, dw_rest),
        [((feat // 2, half_cols), f32), ((feat // 2, half_cols), bf16)], 0, "out_grads", (more_dh,), (core,),
    )

    def last_rows(sent):
        (output,) = simple_call(
            functools.partial(output_kernel, n_all),
            (back_rows, place, scalars, hidden, mid_rows, valid_rows, first_part), [rows_full], 0, "output", (sent,),
        )
        (grad_x,) = simple_call(
            functools.partial(first_norm_kernel, n_all + 6),
            (grad_hidden_one, more_dh, residual_in[0], first_part, grad_mid), [rows_full], 0, "first_norm", (sent,),
        )
        results.extend([output, grad_x, *unpack_expert(expert_back, (output, grad_x))])
        return results

    results = []
    sums = scatter_parts(
        [(first_keep, first_give), (out_keep, out_give)], [mid_a, mid_b], far, near, w_out.shape[0], last_rows
    )
    output, grad_x, *expert_grads = results
    small_out = sums[:, 4 * feat + PAIR :]
    return (
        output[None],
        grad_x[None],
        jnp.concatenate([sums[:, : 2 * feat], sums[:, width : width + feat]], axis=1),
        sums[:, width + feat : width + 2 * feat],
        sums[:, 2 * feat],
        small_out[:, n_all + 6],
        small_out[:, :n_all],
        small_out[:, n_all : n_all + 4],
        small_out[:, n_all + 4 : n_all + 6],
        expert_grads[0],
        expert_grads[1],
        expert_grads[2],
    )


def solution(mesh):
    in_specs = (
        P(("dp", "exp"), "ctx", None),
        P(("dp", "exp")),
        P(("dp", "exp"), "ctx", None),
        P(("dp", "exp"), "ctx", None),
        P(("dp", "exp"), "ctx", None),
        P(("dp", "ctx", "exp"), None),
        P(("dp", "ctx", "exp"), None),
        P(("dp", "ctx", "exp")),
        P(("dp", "ctx", "exp")),
        P(("dp", "ctx", "exp"), None),
        P(("dp", "ctx", "exp"), None),
        P(("dp", "ctx", "exp"), None),
        P("exp", None, ("dp", "ctx")),
        P("exp", None, ("dp", "ctx")),
        P("exp", ("dp", "ctx"), None),
    )
    out_specs = (
        P(("dp", "exp"), "ctx", None),
        P(("dp", "exp"), "ctx", None),
        P(("dp", "ctx", "exp"), None),
        P(("dp", "ctx", "exp"), None),
        P(("dp", "ctx", "exp")),
        P(("dp", "ctx", "exp")),
        P(("dp", "ctx", "exp"), None),
        P(("dp", "ctx", "exp"), None),
        P(("dp", "ctx", "exp"), None),
        P("exp", None, ("dp", "ctx")),
        P("exp", None, ("dp", "ctx")),
        P("exp", ("dp", "ctx"), None),
    )
    return jax.shard_map(local, mesh=mesh, in_specs=in_specs, out_specs=out_specs, check_vma=False)
```

```python
import functools

import jax
import jax.numpy as jnp
from jax import lax
from jax.experimental import pallas as pl
from jax.experimental.pallas import tpu as pltpu
from jax.sharding import PartitionSpec as P

HEADS = 12

norm_eps = 1e-06
top_precision = lax.Precision.HIGHEST
f32 = jnp.float32
bf16 = jnp.bfloat16


CHUNK = 256
BLOCK = 512
OCHUNK = 512
QCHUNK = 128
PAIR = 128
NEG = -1e30
SCALE = 48
VMEM = 62 << 20
MICROS = {
    "project": 6, "project_other": 5, "spread": 4, "attend": 17, "mid": 9, "expert": 30, "weights_sent": 1,
    "weights_near": 0, "weights_kept": 0, "weights_sum": 4, "gates_back": 11, "grads_other": 17, "back_other": 8, "grads_own": 13,
    "back_own": 13, "out_grads": 7, "output": 6, "first_norm": 4, "weights_all": 26, "pack": 3, "unpack": 4, "combine": 1, "rows": 2, "sums": 1,
}


def cost(name):
    return pl.CostEstimate(flops=MICROS[name] * 1000000000 // SCALE, bytes_accessed=1, transcendentals=0)


def mul_nt(a, b):
    return lax.dot_general(a, b, (((1,), (1,)), ((), ())), preferred_element_type=f32)


def mul_nn(a, b):
    return lax.dot_general(a, b, (((1,), (0,)), ((), ())), preferred_element_type=f32)


def mul_tn(a, b):
    return lax.dot_general(a, b, (((0,), (0,)), ((), ())), preferred_element_type=f32)


def head_part(rows, head):
    lane = lax.broadcasted_iota(jnp.int32, rows.shape, 1)
    return jnp.where((lane >= PAIR // 2) == (head == 1), rows, jnp.zeros_like(rows))


def key_allowed(shape, key_start, length, query_start=None):
    key = key_start + lax.broadcasted_iota(jnp.int32, shape, 0)
    allowed = key < length
    if query_start is not None:
        allowed &= key <= query_start + lax.broadcasted_iota(jnp.int32, shape, 1)
    return allowed


def both_heads(rows, first=0):
    return jnp.concatenate([head_part(rows[first:], head) for head in range(2)], axis=0)


def beside(row_pair):
    return jnp.concatenate([row_pair[0:1], row_pair[1:2]], axis=1)


def split_heads(wide):
    half, t = PAIR // 2, wide.shape[1] // 2
    return jnp.concatenate([wide[:half, :t], wide[half:, t:]], axis=0)


def attend_kernel(info, q_ref, k_ref, v_ref, ok_ref, ov_ref, out_ref, low_ref, log_ref):
    base, length, blocks = info[0], info[1], info[2]
    queries = q_ref[...]
    rows = queries.shape[0]
    half = PAIR // 2
    starts = list(range(0, rows, QCHUNK))
    twice = [both_heads(queries[first : first + QCHUNK]) for first in starts]

    def spread(row):
        n = row.shape[1] // 2
        return jnp.concatenate(
            [jnp.broadcast_to(row[:, :n], (half, n)), jnp.broadcast_to(row[:, n:], (half, n))], axis=0
        )

    scores, tops, states = [], [], []
    for first, part in zip(starts, twice):
        end = first + QCHUNK
        some = mul_nt(k_ref[:end, :], part)
        allowed = key_allowed((end, QCHUNK), base, length, base + first)
        scores.append(jnp.where(jnp.concatenate([allowed, allowed], axis=1), some, NEG))
    for some in scores:
        tops.append(jnp.max(some, axis=0, keepdims=True))
    for first, some, top in zip(starts, scores, tops):
        expo = jnp.exp(some - top)
        total = jnp.sum(expo, axis=0, keepdims=True)
        acc = split_heads(mul_tn(v_ref[: first + QCHUNK, :], expo.astype(bf16)))
        states.append((top, total, acc))

    def step(c, states):
        first = pl.multiple_of(c * BLOCK, BLOCK)
        keys = ok_ref[pl.ds(first, BLOCK), :]
        vals = ov_ref[pl.ds(first, BLOCK), :]
        allowed = key_allowed((BLOCK, 2 * QCHUNK), first, length)
        scores = [jnp.where(allowed, mul_nt(keys, part), NEG) for part in twice]
        new = []
        for some, (top, total, acc) in zip(scores, states):
            new_top = jnp.maximum(top, jnp.max(some, axis=0, keepdims=True))
            expo = jnp.exp(some - new_top)
            factor = jnp.exp(top - new_top)
            total = total * factor + jnp.sum(expo, axis=0, keepdims=True)
            acc = acc * spread(factor) + split_heads(mul_tn(vals, expo.astype(bf16)))
            new.append((new_top, total, acc))
        return tuple(new)

    states = lax.fori_loop(0, blocks, step, tuple(states))
    for first, (top, total, acc) in zip(starts, states):
        there = slice(first, first + QCHUNK)
        out = jnp.transpose(acc / spread(total))
        out_ref[there, :] = out
        low_ref[there, :] = out.astype(bf16)
        log = top + jnp.log(total)
        log_ref[0, 0:1, there] = log[:, :QCHUNK]
        log_ref[0, 1:2, there] = log[:, QCHUNK:]


def pair_grads(keys, vals, twice, grad_twice, log_row, delta_row, allowed):
    probs = jnp.where(allowed, jnp.exp(mul_nt(keys, twice) - log_row), 0.0)
    grad_probs = mul_nt(vals, grad_twice)
    grad_scores = (probs * (grad_probs - delta_row)).astype(bf16)
    return (
        mul_nn(grad_scores, twice),
        mul_nn(probs.astype(bf16), grad_twice),
        split_heads(mul_tn(keys, grad_scores)),
    )


def other_backward(
    info, q_ref, k_ref, v_ref, grad_ref, out_ref, log_ref, dq_ref, dk_ref, dv_ref, delta_ref
):
    length, chunks = info[1], info[2] * (BLOCK // OCHUNK)
    half = PAIR // 2
    queries, grads = q_ref[...], grad_ref[...]
    rows = queries.shape[0]
    product = jnp.transpose(grads.astype(f32) * out_ref[...])
    twice, grad_twice = both_heads(queries), both_heads(grads)
    for head in range(2):
        delta_ref[0, head : head + 1, :] = jnp.sum(
            product[head * half : (head + 1) * half], axis=0, keepdims=True
        )
    log_row, delta_row = beside(log_ref[0]), beside(delta_ref[0])

    def step(c, dq):
        first = pl.multiple_of(c * OCHUNK, OCHUNK)
        keys = k_ref[pl.ds(first, OCHUNK), :]
        vals = v_ref[pl.ds(first, OCHUNK), :]
        allowed = key_allowed((OCHUNK, 2 * rows), first, length)
        dk, dv, more = pair_grads(keys, vals, twice, grad_twice, log_row, delta_row, allowed)
        dk_ref[pl.ds(first, OCHUNK), :] = dk.astype(dk_ref.dtype)
        dv_ref[pl.ds(first, OCHUNK), :] = dv.astype(dv_ref.dtype)
        return dq + more

    dq_ref[...] = lax.fori_loop(0, chunks, step, jnp.zeros((PAIR, rows), f32))

    def clear(c, none):
        first = pl.multiple_of(c * OCHUNK, OCHUNK)
        dk_ref[pl.ds(first, OCHUNK), :] = jnp.zeros((OCHUNK, PAIR), dk_ref.dtype)
        dv_ref[pl.ds(first, OCHUNK), :] = jnp.zeros((OCHUNK, PAIR), dv_ref.dtype)
        return none

    lax.fori_loop(chunks, k_ref.shape[0] // OCHUNK, clear, 0)


def own_backward(
    info, q_ref, k_ref, v_ref, grad_ref, log_ref, delta_ref, before_ref, dq_ref, dk_ref, dv_ref
):
    base, length = info[0], info[1]
    queries, grads = q_ref[...], grad_ref[...]
    rows = queries.shape[0]
    dq = before_ref[...]
    for first in range(0, rows, CHUNK):
        keys = k_ref[first : first + CHUNK, :]
        vals = v_ref[first : first + CHUNK, :]
        allowed = key_allowed((CHUNK, rows - first), base + first, length, base + first)
        dk, dv, more = pair_grads(
            keys,
            vals,
            both_heads(queries, first),
            both_heads(grads, first),
            beside(log_ref[0, :, first:]),
            beside(delta_ref[0, :, first:]),
            jnp.concatenate([allowed, allowed], axis=1),
        )
        dk_ref[first : first + CHUNK, :] = dk.astype(dk_ref.dtype)
        dv_ref[first : first + CHUNK, :] = dv.astype(dv_ref.dtype)
        if first:
            more = jnp.concatenate([jnp.zeros((PAIR, first), f32), more], axis=1)
        dq = dq + more
    dq_ref[...] = jnp.transpose(dq).astype(dq_ref.dtype)


def per_pair(rows):
    return pl.BlockSpec((rows, PAIR), lambda i, info: (0, i))


def turned(cols):
    return pl.BlockSpec((PAIR, cols), lambda i, info: (i, 0))


def stats(cols):
    return pl.BlockSpec((1, 2, cols), lambda i, info: (i, 0, 0))


def ordered(kernel, n_in, n_deps):
    if not n_deps:
        return kernel

    def run(*refs):
        kernel(*refs[:n_in], *refs[n_in + n_deps :])

    return run


def waits(deps):
    return [pl.BlockSpec(memory_space=pl.ANY)] * len(deps)


def attn_call(kernel, info, args, in_specs, outs, out_specs, flops, name, deps=()):
    return pl.pallas_call(
        ordered(kernel, 1 + len(args), len(deps)),
        grid_spec=pltpu.PrefetchScalarGridSpec(
            num_scalar_prefetch=1,
            grid=(HEADS // 2,),
            in_specs=in_specs + waits(deps),
            out_specs=out_specs,
        ),
        out_shape=[jax.ShapeDtypeStruct(s, d) for s, d in outs],
        compiler_params=pltpu.CompilerParams(vmem_limit_bytes=VMEM),
        cost_estimate=cost(name),
        name=name,
    )(info, *args, *deps)


def attend(info, q, k, v, other_k, other_v, deps):
    t, d = q.shape
    st = (HEADS // 2, 2, t)
    n = other_k.shape[0]
    return attn_call(
        attend_kernel, info, (q, k, v, other_k, other_v),
        [per_pair(t)] * 3 + [per_pair(n)] * 2,
        [((t, d), f32), ((t, d), bf16), (st, f32)], [per_pair(t), per_pair(t), stats(t)], 8 * t * t * d, "attend", deps,
    )


def grads_other(info, q, k, v, grad, out, log_total, deps):
    t, d = q.shape
    n = k.shape[0]
    return attn_call(
        other_backward, info, (q, k, v, grad, out, log_total),
        [per_pair(t), per_pair(n), per_pair(n), per_pair(t), per_pair(t), stats(t)],
        [((d, t), f32), ((n, d), bf16), ((n, d), bf16), ((HEADS // 2, 2, t), f32)],
        [turned(t), per_pair(n), per_pair(n), stats(t)], 10 * t * t * d, "grads_other", deps,
    )


def grads_own(info, q, k, v, grad, log_total, delta, before, deps):
    t, d = q.shape
    return attn_call(
        own_backward, info, (q, k, v, grad, log_total, delta, before),
        [per_pair(t)] * 4 + [stats(t)] * 2 + [turned(t)],
        [((t, d), bf16)] * 3, [per_pair(t)] * 3, 10 * t * t * d, "grads_own", deps,
    )


def dot32(a, b, dims=((1,), (0,)), precision=None):
    return lax.dot_general(a, b, (dims, ((), ())), precision=precision, preferred_element_type=f32)


def swap(block, axis, bit):
    return lax.ppermute(block, axis, [(i, i ^ bit) for i in range(lax.axis_size(axis))])


def bits_of(axis, low=1, high=None):
    high = lax.axis_size(axis) if high is None else high
    found = []
    while low < high:
        found.append(low)
        low *= 2
    return found[::-1]


def row_weight(axis):
    x = lax.axis_size("exp")
    c = lax.axis_size("ctx")
    return {"exp": 1, "ctx": x, "dp": x * c}[axis]


def plan_steps(middle):
    far = [("dp", bit) for bit in bits_of("dp", 2)]
    mid = [(axis, bit) for axis in middle for bit in bits_of(axis)]
    near = [("dp", bit) for bit in bits_of("dp", 1, 2)]
    return far, mid, near


def row_bits(steps):
    return sorted([row_weight(axis) * bit for axis, bit in steps], reverse=True)


def nothing(*refs):
    pass


def hold(value, *others):
    return pl.pallas_call(
        nothing,
        in_specs=waits((value,) + others),
        out_specs=waits((value,))[0],
        out_shape=jax.ShapeDtypeStruct(value.shape, value.dtype),
        input_output_aliases={0: 0},
        cost_estimate=pl.CostEstimate(flops=0, bytes_accessed=0, transcendentals=0),
        name="hold",
    )(value, *others)


def rows_kernel(wqkv_ref, wout_ref, *refs):
    out_ref = refs[-1]
    d = wout_ref.shape[1]
    out_ref[:, : 3 * d] = wqkv_ref[...]
    out_ref[:, 3 * d : 4 * d] = wout_ref[...]
    small = jnp.zeros((wout_ref.shape[0], PAIR), f32)
    first = 0
    for ref in refs[:-1]:
        shape = (ref.shape[0], PAIR)
        here = lax.broadcasted_iota(jnp.int32, shape, 0) + first == lax.broadcasted_iota(jnp.int32, shape, 1)
        small += mul_tn(ref[...], jnp.where(here, 1.0, 0.0).astype(bf16))
        first += ref.shape[0]
    out_ref[:, 4 * d :] = small.astype(bf16)


def gather_step(whole, placed, axis, bit, meanwhile=()):
    other = swap(whole, axis, bit)
    if meanwhile:
        whole = hold(whole, *meanwhile)
    upper = (lax.axis_index(axis) & bit) != 0
    weight = row_weight(axis) * bit
    pos = sum(1 for w in placed if w > weight)
    both = [jnp.where(upper, other, whole), jnp.where(upper, whole, other)]
    return jnp.stack(both, axis=pos), placed[:pos] + [weight] + placed[pos:]


def gather_steps(whole, placed, steps):
    for axis, bit in steps:
        whole, placed = gather_step(whole, placed, axis, bit)
    return whole, placed


def gather_far(rows, steps, meanwhile):
    axis = steps[0][0]
    bits = [bit for _, bit in steps]
    parts = [rows] + [swap(rows, axis, mask) for mask in (bits[1], bits[0], bits[0] + bits[1])]
    parts[0] = hold(rows, *meanwhile)
    low, high = [(lax.axis_index(axis) & bit) != 0 for bit in (bits[1], bits[0])]
    parts = [jnp.where(low, parts[i ^ 1], parts[i]) for i in range(4)]
    parts = [jnp.where(high, parts[i ^ 2], parts[i]) for i in range(4)]
    whole = jnp.stack(parts).reshape((2, 2) + rows.shape)
    return whole, [row_weight(axis) * bit for bit in bits]


def scatter_split(part, placed, axis, bit):
    pos = placed.index(row_weight(axis) * bit)
    upper = (lax.axis_index(axis) & bit) != 0
    low = lax.index_in_dim(part, 0, pos, keepdims=False)
    high = lax.index_in_dim(part, 1, pos, keepdims=False)
    sent = jnp.where(upper, low, high).astype(bf16)
    kept = jnp.where(upper, high, low).astype(f32)
    return sent, kept, placed[:pos] + placed[pos + 1 :]


def scatter_step(part, placed, axis, bit):
    sent, kept, placed = scatter_split(part, placed, axis, bit)
    return kept + swap(sent, axis, bit).astype(f32), placed


def combine_kernel(n, block, up_ref, *refs):
    keep_ref, give_ref = refs[2 * n :]
    first = 0
    for kept, came in zip(refs[:n], refs[n : 2 * n]):
        cols = slice(first, first + kept.shape[1])
        total = kept[...] + came[...].astype(f32)
        keep_ref[:, cols], give_ref[:, cols] = split_rows(up_ref[0] == 1, total, block)
        first += kept.shape[1]


def combine(kept, came, placed, axis, bit, rows, deps, steps=1):
    weight = row_weight(axis) * bit
    placed = [w for w in placed if w != weight]
    block = rows * 2 ** sum(1 for w in placed if w < weight)
    upper = ((lax.axis_index(axis) & bit) != 0).astype(jnp.int32).reshape(1)
    n_rows = kept[0][0].shape[0] // steps
    args = [*kept, *came]
    out = pl.BlockSpec((n_rows // 2, sum(arg[1][1] for arg in kept)), lambda i: (i, 0))
    shape = (n_rows // 2 * steps, out.block_shape[1])
    keep, give = pl.pallas_call(
        ordered(functools.partial(combine_kernel, len(kept), block), 1 + len(args), len(deps)),
        grid=(steps,),
        in_specs=[pl.BlockSpec(memory_space=pltpu.SMEM)]
        + [pl.BlockSpec((n_rows, arg[1][1]), lambda i, index=arg[2]: (i, index)) for arg in args]
        + waits(deps),
        out_specs=[out, out],
        out_shape=[jax.ShapeDtypeStruct(shape, f32), jax.ShapeDtypeStruct(shape, bf16)],
        compiler_params=pltpu.CompilerParams(vmem_limit_bytes=VMEM),
        cost_estimate=cost("combine"),
        name="combine",
    )(upper, *[arg[0] for arg in args], *deps)
    return keep, give, placed


def whole_of(array):
    return column(array, array.shape[1], 0)


def scatter_split(part, placed, axis, bit):
    pos = placed.index(row_weight(axis) * bit)
    upper = (lax.axis_index(axis) & bit) != 0
    low = lax.index_in_dim(part, 0, pos, keepdims=False)
    high = lax.index_in_dim(part, 1, pos, keepdims=False)
    sent = jnp.where(upper, low, high).astype(bf16)
    kept = jnp.where(upper, high, low).astype(f32)
    return sent, kept, placed[:pos] + placed[pos + 1 :]


def scatter_parts(parts, orders, far, near, rows, deps, meanwhile):
    swapped = {}
    for blocks in parts:
        for _, give, _, _ in blocks:
            if id(give) not in swapped:
                swapped[id(give)] = swap(give, *near[0])
    sums, places = [], []
    for i, (blocks, order) in enumerate(zip(parts, orders)):
        step, late = order[-1], i == len(parts) - 1
        keep, give, placed = combine(
            [column(keep, width, index) for keep, _, width, index in blocks],
            [column(swapped[id(give)], width, index) for _, give, width, index in blocks],
            row_bits(far + order), *step, rows, deps if late else (),
        )
        came = swap(give, *step)
        if late:
            keep = hold(keep, *meanwhile(give))
        sums.append((keep + came.astype(f32)).reshape((2,) * len(placed) + (-1, keep.shape[1])))
        places.append(placed)
    for steps in zip(*[reversed(order[:-1]) for order in orders]):
        splits = [scatter_split(part, where, *step) for part, where, step in zip(sums, places, steps)]
        places = [split[2] for split in splits]
        sums = [kept + swap(sent, *step).astype(f32) for (sent, kept, _), step in zip(splits, steps)]
    total, placed = jnp.concatenate(sums, axis=-1), places[0]
    for step in reversed(far):
        sent, kept, placed = scatter_split(total, placed, *step)
        total = kept + swap(sent, *step).astype(f32)
    return total


def pack_kernel(gate_ref, up_ref, down_ref, out_ref):
    out_ref[0, 0] = gate_ref[0]
    out_ref[0, 1] = up_ref[0]
    out_ref[0, 2] = jnp.transpose(down_ref[0])


def unpack_kernel(first_ref, rest_ref, gate_ref, up_ref, down_ref):
    gate_ref[0] = first_ref[0, 0].astype(f32)
    up_ref[0] = rest_ref[0, 0].astype(f32)
    down_ref[0] = jnp.transpose(rest_ref[0, 1].astype(f32))


def one_of(*shape):
    return pl.BlockSpec((1,) + shape, lambda i: (i,) + (0,) * len(shape))


def pack_expert(w_gate, w_up, w_down, deps):
    n, d, f = w_gate.shape
    return pl.pallas_call(
        ordered(pack_kernel, 3, len(deps)),
        grid=(n,),
        in_specs=[one_of(d, f), one_of(d, f), one_of(f, d)] + waits(deps),
        out_specs=one_of(3, d, f),
        out_shape=jax.ShapeDtypeStruct((n, 3, d, f), w_gate.dtype),
        compiler_params=pltpu.CompilerParams(vmem_limit_bytes=VMEM),
        cost_estimate=cost("pack"),
        name="pack",
    )(w_gate, w_up, w_down, *deps)


def unpack_expert(first, rest, deps):
    n, _, d, f = first.shape
    return pl.pallas_call(
        ordered(unpack_kernel, 2, len(deps)),
        grid=(n,),
        in_specs=[one_of(1, d, f), one_of(2, d, f)] + waits(deps),
        out_specs=[one_of(d, f), one_of(d, f), one_of(f, d)],
        out_shape=[jax.ShapeDtypeStruct(shape, f32) for shape in ((n, d, f), (n, d, f), (n, f, d))],
        compiler_params=pltpu.CompilerParams(vmem_limit_bytes=VMEM),
        cost_estimate=cost("unpack"),
        name="unpack",
    )(first, rest, *deps)


def trade_far(parts):
    n_own = parts.shape[0]
    reps = lax.axis_size("dp") // n_own
    groups = [[i * reps + r for i in range(n_own)] for r in range(reps)]
    return lax.all_to_all(parts, "dp", 0, 0, axis_index_groups=groups, tiled=True)


def near_steps(n_own):
    reps = lax.axis_size("dp") // n_own
    return [("ctx", bit) for bit in bits_of("ctx")] + [("dp", bit) for bit in bits_of("dp", 1, reps)]


def gather_expert_near(groups, steps):
    for axis, bit in steps:
        groups = groups + [swap(group, axis, bit) for group in groups]
    return groups


def scatter_expert_near(groups, steps):
    for axis, bit in reversed(steps):
        n = len(groups) // 2
        came = [swap(group.astype(bf16), axis, bit) for group in groups[n:]]
        groups = [a.astype(f32) + b.astype(f32) for a, b in zip(groups[:n], came)]
    return groups[0]


def rms_scale(rows):
    return lax.rsqrt(jnp.mean(rows * rows, axis=-1, keepdims=True) + norm_eps)


def rms_backward(in_rows, inv_scale, gain_vec, grad_rows):
    normed = in_rows * inv_scale
    gain_grad = jnp.sum(grad_rows * normed, axis=0, keepdims=True)
    inner_grad = grad_rows * gain_vec
    back_rows = inv_scale * (
        inner_grad - normed * jnp.mean(inner_grad * normed, axis=-1, keepdims=True)
    )
    return (back_rows, gain_grad)


def rope(rows, cos, sin):
    lane = lax.broadcasted_iota(jnp.int32, (rows.shape[0], PAIR), 1)
    low = lane % (PAIR // 2) < PAIR // 4
    parts = []
    for first in range(0, rows.shape[1], PAIR):
        part = rows[:, first : first + PAIR]
        other = jnp.where(low, pltpu.roll(part, PAIR - PAIR // 4, 1), pltpu.roll(part, PAIR // 4, 1))
        parts.append(part * cos + other * sin)
    return jnp.concatenate(parts, axis=1)


def gain_row(small_ref, lane):
    return jnp.transpose(small_ref[...].astype(f32))[lane : lane + 1]


def project_kernel(scale, lane, x_ref, first_ref, wv_ref, small_ref, cos_ref, sin_ref, h_ref, q_ref, k_ref, v_ref):
    rows = x_ref[...].astype(f32)
    d = rows.shape[1]
    hidden = (rows * rms_scale(rows) * gain_row(small_ref, lane)).astype(bf16)
    h_ref[...] = hidden
    cos, sin = cos_ref[...], sin_ref[...]
    k_ref[...] = rope(mul_nn(hidden, first_ref[:, d : 2 * d]), cos, sin).astype(bf16)
    v_ref[...] = mul_nn(hidden, wv_ref[...]).astype(bf16)
    q_ref[...] = (rope(mul_nn(hidden, first_ref[:, :d]), cos, sin) * scale).astype(bf16)


def other_project_kernel(lane, x_ref, wk_ref, small_ref, wv_ref, cos_ref, sin_ref, h_ref, k_ref, v_ref):
    rows = x_ref[...].astype(f32)
    d = rows.shape[1]
    hidden = (rows * rms_scale(rows) * gain_row(small_ref, lane)).astype(bf16)
    h_ref[...] = hidden
    k_ref[...] = rope(mul_nn(hidden, wk_ref[...]), cos_ref[...], sin_ref[...]).astype(bf16)
    v_ref[...] = mul_nn(hidden, wv_ref[...]).astype(bf16)


def other_back_kernel(dk_ref, dv_ref, wk_ref, wv_ref, cos_ref, sin_ref, x_ref, gk_ref, dh_ref, dgain_ref):
    first = pl.program_id(0) == 0
    grad_k = rope(dk_ref[...].astype(f32), cos_ref[...], -sin_ref[...]).astype(bf16)
    gk_ref[...] = grad_k
    rows = x_ref[...].astype(f32)
    dh = mul_nt(grad_k, wk_ref[...]) + mul_nt(dv_ref[...], wv_ref[...])
    dh_ref[...] = dh.astype(bf16)
    dgain = jnp.sum(dh * rows * rms_scale(rows), axis=0, keepdims=True)

    @pl.when(first)
    def _():
        dgain_ref[...] = dgain

    @pl.when(jnp.logical_not(first))
    def _():
        dgain_ref[...] += dgain


def split_rows(upper, rows, block):
    keep, give = [], []
    for first in range(0, rows.shape[0], 2 * block):
        low, high = rows[first : first + block], rows[first + block : first + 2 * block]
        keep.append(jnp.where(upper, high, low))
        give.append(jnp.where(upper, low, high))
    return jnp.concatenate(keep, axis=0), jnp.concatenate(give, axis=0).astype(bf16)


def own_back_kernel(
    scale, block, core_ref, dq_ref, dk_ref, dv_ref, h_ref, first_ref, wv_ref, cos_ref, sin_ref, x_ref, oh_ref, ok_ref, ov_ref,
    mgain_ref, keep_ref, give_ref, v_keep_ref, v_give_ref, dh_ref, small_keep_ref, small_give_ref,
):
    step = pl.program_id(0)
    upper = core_ref[0] == 1
    cos, sin = cos_ref[...], -sin_ref[...]

    def finish(grad, weight, other, keep, give):
        dw = mul_tn(h_ref[...], grad)
        if other is not None:
            dw += mul_tn(oh_ref[...], other)
        keep[...], give[...] = split_rows(upper, dw, block)
        return mul_nt(grad, weight)

    @pl.when(step == 0)
    def _():
        grad = rope(dq_ref[...].astype(f32) * scale, cos, sin).astype(bf16)
        dh_ref[...] = finish(grad, first_ref[...], None, keep_ref, give_ref)

    @pl.when(step == 1)
    def _():
        grad = rope(dk_ref[...].astype(f32), cos, sin).astype(bf16)
        dh_ref[...] += finish(grad, first_ref[...], ok_ref[...], keep_ref, give_ref)

    @pl.when(step == 2)
    def _():
        dh = dh_ref[...] + finish(dv_ref[...], wv_ref[...], ov_ref[...], v_keep_ref, v_give_ref)
        dh_ref[...] = dh
        rows = x_ref[...].astype(f32)
        dgain = jnp.sum(dh * rows * rms_scale(rows), axis=0, keepdims=True) + mgain_ref[...]
        d = dgain.shape[1]
        column = jnp.transpose(jnp.broadcast_to(dgain, (8, d)))[:, :1]
        small = jnp.where(lane_of(d) == 0, column, 0.0)
        small_keep_ref[...], small_give_ref[...] = split_rows(upper, small, block)


def first_norm_kernel(lane, dh_ref, more_ref, x_ref, small_ref, mid_ref, dx_ref):
    rows = x_ref[...].astype(f32)
    grad = dh_ref[...] + more_ref[...].astype(f32)
    back, _ = rms_backward(rows, rms_scale(rows), gain_row(small_ref, lane), grad)
    dx_ref[...] = mid_ref[...] + back


def column(array, width, index):
    return array, (array.shape[0], width), index


def simple_call(kernel, args, outs, flops, name, deps=(), scalars=()):
    whole = pl.BlockSpec(memory_space=pltpu.VMEM)
    small = pl.BlockSpec(memory_space=pltpu.SMEM)
    specs, arrays = [], []
    for arg in args:
        if isinstance(arg, tuple):
            array, block, index = arg
            specs.append(pl.BlockSpec(block, lambda i, index=index: (0, index)))
            arrays.append(array)
        else:
            specs.append(whole)
            arrays.append(arg)
    return pl.pallas_call(
        ordered(kernel, len(scalars) + len(args), len(deps)),
        grid=(1,),
        in_specs=[small] * len(scalars) + specs + waits(deps),
        out_shape=[jax.ShapeDtypeStruct(s, d) for s, d in outs],
        compiler_params=pltpu.CompilerParams(vmem_limit_bytes=VMEM),
        cost_estimate=cost(name),
        name=name,
    )(*scalars, *arrays, *deps)


def expert_kernel(n_groups, *refs):
    x_ref, g_ref = refs[:2]
    w_refs = refs[2 : 2 + n_groups]
    out_ref, dx_ref, act_ref, dg_ref, du_ref, gx_ref, gg_ref, store, out_sum, back_sum, done = refs[-11:]
    step = pl.program_id(0)
    n, d = out_sum.shape
    copies = [pltpu.make_async_copy(w, store.at[k], done.at[k]) for k, w in enumerate(w_refs)]

    @pl.when(step == 0)
    def _():
        for copy in copies:
            copy.start()
        out_sum[...] = jnp.zeros((n, d), f32)
        back_sum[...] = jnp.zeros((n, d), f32)

    for k, copy in enumerate(copies):
        pl.when(step == k)(copy.wait)
    grads = g_ref[...].reshape(n, d)
    rows = x_ref[:, :d]
    wg, wu, wd = [
        jnp.concatenate([store[step, p, m] for p in range(store.shape[1])], axis=1) for m in range(3)
    ]
    gate_pre = mul_nn(rows, wg)
    up_pre = mul_nn(rows, wu)
    grad_act = mul_nn(grads, wd)
    sig = 1.0 / (1.0 + jnp.exp(-gate_pre))
    silu = gate_pre * sig
    act = (silu * up_pre).astype(bf16)
    act_ref[...] = act
    grad_gate = (grad_act * up_pre * sig * (1.0 + gate_pre * (1.0 - sig))).astype(bf16)
    grad_up = (grad_act * silu).astype(bf16)
    dg_ref[...] = grad_gate
    du_ref[...] = grad_up
    out_sum[...] += mul_nt(act, wd)
    back_sum[...] += mul_nt(grad_gate, wg) + mul_nt(grad_up, wu)

    @pl.when(step == n_groups - 1)
    def _():
        gates = x_ref[:, d : d + 1].astype(f32) + x_ref[:, d + 1 : d + 2].astype(f32)
        gx_ref[...] = jnp.transpose((rows.astype(f32) * gates).astype(bf16))
        gg_ref[...] = jnp.transpose((grads.astype(f32) * gates).astype(bf16))
        low = out_sum[...].astype(bf16)
        out_ref[...] = low.reshape(out_ref.shape)
        dx_ref[:, :d] = back_sum[...].astype(bf16)
        dots = jnp.sum(grads.astype(f32) * low.astype(f32), axis=1, keepdims=True)
        high, rest = halves(dots)
        lane = lax.broadcasted_iota(jnp.int32, (n, PAIR), 1)
        pair = jnp.where(lane == 0, high.astype(f32), jnp.where(lane == 1, rest.astype(f32), 0.0))
        dx_ref[:, d:] = pair.astype(bf16)


def expert_call(part, x, g, groups, outs, name):
    n, wide = x.shape
    d = g.shape[-1]
    group = groups[0].shape
    cols = group[0] * group[3]
    ff = cols * len(groups)
    block = pl.BlockSpec((g.shape[0], 1) + g.shape[2:], lambda i: (0, part, 0, 0))
    passed = [] if outs is None else [outs]

    def whole(*shape):
        return pl.BlockSpec(shape, lambda i: (0,) * len(shape))

    def column(rows):
        return pl.BlockSpec((rows, cols), lambda i: (0, i))

    shapes = [(n, wide), (n, ff), (n, ff), (n, ff), (d, n), (d, n)]
    return pl.pallas_call(
        functools.partial(expert_kernel, len(groups)),
        grid=(len(groups),),
        in_specs=[whole(n, wide), block] + waits(groups) + waits(passed),
        out_specs=[block, whole(n, wide)] + [column(n)] * 3 + [whole(d, n)] * 2,
        out_shape=[jax.ShapeDtypeStruct(g.shape, bf16)] + [jax.ShapeDtypeStruct(shape, bf16) for shape in shapes],
        input_output_aliases={2 + len(groups): 0} if passed else {},
        scratch_shapes=[
            pltpu.VMEM((len(groups),) + group, bf16), pltpu.VMEM((n, d), f32), pltpu.VMEM((n, d), f32),
            pltpu.SemaphoreType.DMA((len(groups),)),
        ],
        compiler_params=pltpu.CompilerParams(vmem_limit_bytes=VMEM),
        cost_estimate=cost("expert"),
        name=name,
    )(x, g, *groups, *passed)


def expert_weights_kernel(plan, n_through, *refs):
    xs, ggs, acts, dgs, dus = [refs[2 * i : 2 * i + 2] for i in range(5)]
    out_refs = refs[10 + n_through :]
    step = pl.program_id(0)
    pieces, _, d, width = out_refs[0].shape
    for m, (left, right) in enumerate([(xs, dgs), (xs, dus), (ggs, acts)]):
        grad = mul_nn(
            jnp.concatenate([half[...] for half in left], axis=1), jnp.concatenate([half[...] for half in right], axis=0)
        )

        def write(ref):
            for p in range(pieces):
                ref[p, m] = grad[:, p * width : (p + 1) * width].astype(ref.dtype)

        first = 0
        for count, ref in zip(plan, out_refs):
            pl.when((step >= first) & (step < first + count))(functools.partial(write, ref))
            first += count


def expert_weights(flows, order, plan, pieces, width, kinds, name, through=None, deps=()):
    d, n = flows[0][0].shape
    cols = pieces * width
    rows = pl.BlockSpec((d, n), lambda i: (0, 0))
    flip = order[0] != 0

    def group(i):
        return len(order) - 1 - i if flip else i

    part = pl.BlockSpec((n, cols), lambda i: (0, group(i)))
    passed = [] if through is None else [through]
    blocks, first = [], 0
    for count in plan:
        blocks.append(
            pl.BlockSpec(
                (pieces, 3, d, width),
                lambda i, first=first, count=count: (jnp.clip(i - first, 0, count - 1), 0, 0, 0),
            )
        )
        first += count
    return pl.pallas_call(
        ordered(functools.partial(expert_weights_kernel, plan, len(passed)), 10 + len(passed), len(deps)),
        grid=(len(order),),
        in_specs=[rows] * 4 + [part] * 6 + waits(passed) + waits(deps),
        out_specs=blocks + waits(passed),
        out_shape=[
            jax.ShapeDtypeStruct((pieces * count, 3, d, width), kind) for count, kind in zip(plan, kinds)
        ]
        + [jax.ShapeDtypeStruct(p.shape, p.dtype) for p in passed],
        input_output_aliases={10: len(plan)} if passed else {},
        compiler_params=pltpu.CompilerParams(vmem_limit_bytes=VMEM),
        cost_estimate=cost(name),
        name=name,
    )(*[half for flow in flows for half in flow], *passed, *deps)


def weights_sent_kernel(near_ref, came_ref, first_ref, rest_ref):
    total = near_ref[...] + came_ref[...]
    first_ref[...] = total[:, :1]
    rest_ref[...] = total[:, 1:]


def weights_sent(near, came):
    n = near.shape[0]
    tail = near.shape[2:]

    def some(count):
        return pl.BlockSpec((1, count) + tail, lambda i: (i, 0, 0, 0))

    return pl.pallas_call(
        weights_sent_kernel,
        grid=(n,),
        in_specs=[some(3)] * 2,
        out_specs=[some(1), some(2)],
        out_shape=[jax.ShapeDtypeStruct((n, count) + tail, bf16) for count in (1, 2)],
        compiler_params=pltpu.CompilerParams(vmem_limit_bytes=VMEM),
        cost_estimate=cost("weights_sent"),
        name="weights_sent",
    )(near, came)


def weights_sum_kernel(kept_ref, far_ref, near_ref, out_ref):
    out_ref[...] = (kept_ref[...].astype(f32) + far_ref[...].astype(f32) + near_ref[...].astype(f32)).astype(bf16)


def weights_sum(kept, far, near, first, deps):
    n, count = near.shape[:2]
    block = (1, 1) + near.shape[2:]
    own = pl.BlockSpec(block, lambda i, j: (i, j, 0, 0))
    part = pl.BlockSpec(block, lambda i, j: (i, first + j, 0, 0))
    return pl.pallas_call(
        ordered(weights_sum_kernel, 3, len(deps)),
        grid=(n, count),
        in_specs=[part, part, own] + waits(deps),
        out_specs=own,
        out_shape=jax.ShapeDtypeStruct(near.shape, bf16),
        compiler_params=pltpu.CompilerParams(vmem_limit_bytes=VMEM),
        cost_estimate=cost("weights_sum"),
        name="weights_sum",
    )(kept, far, near, *deps)


def lane_of(rows):
    return lax.broadcasted_iota(jnp.int32, (rows, PAIR), 1)


def col(rows, i):
    return rows[:, i : i + 1]


def halves(rows):
    high = rows.astype(bf16)
    return high, (rows - high.astype(f32)).astype(bf16)


VEC, COEF, GATE, CONST = 0, 2, 3, 5


def mid_kernel(
    n_all, att_ref, small_ref, wo_ref, x_ref, prev_ref, routes_ref, place_ref,
    mid_ref, hidden_ref, scal_ref, *send_refs,
):
    n_ffn = n_all - 4
    d = x_ref.shape[1]
    mid = x_ref[...].astype(f32) + mul_nn(att_ref[...], wo_ref[...])
    mid_ref[...] = mid
    hidden = (mid * rms_scale(mid) * gain_row(small_ref, n_all + 7)).astype(bf16)
    hidden_ref[...] = hidden
    rows, d = hidden.shape
    lane = lane_of(rows)
    raw = mul_nn(hidden, small_ref[...])
    logits = jnp.where(lane < n_all, raw + prev_ref[...], NEG)
    expo = jnp.exp(logits - jnp.max(logits, axis=1, keepdims=True))
    probs = jnp.where(lane < n_all, expo / jnp.sum(expo, axis=1, keepdims=True), 0.0)
    ids = [col(routes_ref[...], j) for j in range(2)]
    gates = [jnp.sum(jnp.where(lane == r, probs, 0.0), axis=1, keepdims=True) for r in ids]
    scal = probs
    coef = sum(jnp.where(r == n_ffn + 1, g, 0.0) for r, g in zip(ids, gates))
    base = n_all + 4
    for c in range(2):
        gap = col(raw, n_all + 2 * c + 1) - col(raw, n_all + 2 * c)
        first, second = 1.0 / (1.0 + jnp.exp(gap)), 1.0 / (1.0 + jnp.exp(-gap))
        const = sum(jnp.where(r == n_ffn + 2 + c, g, 0.0) for r, g in zip(ids, gates))
        coef += first * const
        scal = jnp.where(lane == n_all + 2 * c, first, scal)
        scal = jnp.where(lane == n_all + 2 * c + 1, second, scal)
        scal = jnp.where(lane == base + VEC + c, second * const, scal)
        scal = jnp.where(lane == base + CONST + c, const, scal)
        scal = jnp.where(lane == base + GATE + c, gates[c], scal)
    scal_ref[...] = jnp.where(lane == base + COEF, coef, scal)
    n_half = send_refs[0].shape[0]
    slots = n_half * len(send_refs)
    row = lax.broadcasted_iota(jnp.int32, (slots, rows), 0)
    hits = [(row == place_ref[j : j + 1, :]) for j in range(2)]
    both = jnp.where(hits[0] | hits[1], 1.0, 0.0).astype(bf16)
    rows_out = mul_nn(both, hidden).astype(bf16)
    extra = jnp.zeros((slots, PAIR), f32)
    for j in range(2):
        high, low = halves(gates[j])
        pair = jnp.where(lane == 0, high.astype(f32), jnp.where(lane == 1, low.astype(f32), 0.0))
        extra += mul_nn(jnp.where(hits[j], 1.0, 0.0).astype(bf16), pair.astype(bf16))
    for i, ref in enumerate(send_refs):
        ref[:, :d] = rows_out[i * n_half : (i + 1) * n_half]
        ref[:, d:] = extra[i * n_half : (i + 1) * n_half].astype(bf16)


def spread_kernel(cot_ref, valid_ref, place_ref, send_ref):
    grads = (cot_ref[...] * valid_ref[...]).astype(bf16)
    row = lax.broadcasted_iota(jnp.int32, (send_ref.shape[0], grads.shape[0]), 0)
    hit = (row == place_ref[0:1, :]) | (row == place_ref[1:2, :])
    send_ref[...] = mul_nn(jnp.where(hit, 1.0, 0.0).astype(bf16), grads).astype(bf16)


def picked_rows(place_ref, j, table):
    rows, slots = place_ref.shape[0], table.shape[0]
    slot = lax.broadcasted_iota(jnp.int32, (rows, slots), 1)
    pick = jnp.where(slot == col(place_ref[...], j), 1.0, 0.0).astype(bf16)
    return mul_nn(pick, table)


def gates_back_kernel(
    n_all, back_ref, more_ref, place_ref, routes_ref, scal_ref, hidden_ref, mid_ref, cot_ref, valid_ref, small_ref, wo_ref,
    gmid_ref, gatt_ref, mix_ref, dgain_ref,
):
    n_ffn = n_all - 4
    base = n_all + 4
    scal = scal_ref[...]
    grads = cot_ref[...] * valid_ref[...]
    rows, d = grads.shape
    lane = lane_of(rows)
    hidden = hidden_ref[...].astype(f32)
    small = small_ref[...]
    g_hidden = jnp.sum(grads * hidden, axis=1, keepdims=True)
    high, low = halves(grads)
    g_small = mul_nn(high, small) + mul_nn(low, small)
    table = jnp.concatenate([back_ref[...], more_ref[...]], axis=0)
    grad_hidden = col(scal, base + COEF) * grads
    grad_probs = jnp.zeros((rows, PAIR), f32)
    for j in range(2):
        r = col(routes_ref[...], j)
        came = picked_rows(place_ref, j, table)
        grad_hidden += col(scal, base + GATE + j) * came[:, :d]
        dots = came[:, d : d + 1] + came[:, d + 1 : d + 2]
        dots += jnp.where(r == n_ffn + 1, g_hidden, 0.0)
        for c in range(2):
            whole = col(scal, n_all + 2 * c) * g_hidden + col(scal, n_all + 2 * c + 1) * col(g_small, base + c)
            dots += jnp.where(r == n_ffn + 2 + c, whole, 0.0)
        grad_probs += jnp.where(lane == r, dots, 0.0)
    probs = jnp.where(lane < n_all, scal, 0.0)
    mix = probs * (grad_probs - jnp.sum(probs * grad_probs, axis=1, keepdims=True))
    for c in range(2):
        first, second = col(scal, n_all + 2 * c), col(scal, n_all + 2 * c + 1)
        const = col(scal, base + CONST + c)
        a, b = const * g_hidden, const * col(g_small, base + c)
        inner = first * a + second * b
        mix = jnp.where(lane == n_all + 2 * c, first * (a - inner), mix)
        mix = jnp.where(lane == n_all + 2 * c + 1, second * (b - inner), mix)
    mix_ref[...] = mix
    high, low = halves(mix)
    grad_hidden += mul_nt(high, small) + mul_nt(low, small)
    mid = mid_ref[...]
    back, dgain = rms_backward(mid, rms_scale(mid), gain_row(small_ref, n_all + 7), grad_hidden)
    dgain_ref[...] = dgain
    grad_mid = grads + back
    gmid_ref[...] = grad_mid
    gatt_ref[...] = mul_nt(grad_mid.astype(bf16), wo_ref[...]).astype(bf16)


def out_grads_kernel(
    n_all, block, core_ref, att_ref, gmid_ref, hidden_ref, mix_ref, scal_ref, cot_ref, valid_ref, dgain_ref, keep_ref, give_ref,
):
    d = att_ref.shape[1]
    base = n_all + 4
    upper = core_ref[0] == 1
    dw_out = mul_tn(att_ref[...], gmid_ref[...].astype(bf16))
    keep_ref[:, :d], give_ref[:, :d] = split_rows(upper, dw_out, block)
    hidden = hidden_ref[...]
    high, low = halves(mix_ref[...])
    grads = mul_tn(hidden, high) + mul_tn(hidden, low)
    scal = scal_ref[...]
    lane = lane_of(scal.shape[0])
    vec = jnp.where((lane >= base + VEC) & (lane < base + VEC + 2), scal, 0.0)
    vec_high, vec_low = halves(vec)
    g_high, g_low = halves(cot_ref[...] * valid_ref[...])
    grads += mul_tn(g_high, vec_high) + mul_tn(g_high, vec_low) + mul_tn(g_low, vec_high)
    column = jnp.transpose(jnp.broadcast_to(dgain_ref[...], (8, d)))[:, :1]
    tail = jnp.where(lane_of(d) == base + 2, column, grads)
    keep_ref[:, d:], give_ref[:, d:] = split_rows(upper, tail, block)


def output_kernel(n_all, back_ref, place_ref, scal_ref, hidden_ref, mid_ref, valid_ref, small_ref, out_ref):
    base = n_all + 4
    scal = scal_ref[...]
    lane = lane_of(scal.shape[0])
    vec = jnp.where((lane >= base + VEC) & (lane < base + VEC + 2), scal, 0.0)
    high, low = halves(vec)
    small = small_ref[...]
    total = mid_ref[...] + mul_nt(high, small) + mul_nt(low, small)
    total += col(scal, base + COEF) * hidden_ref[...].astype(f32)
    table = back_ref[...]
    for j in range(2):
        total += col(scal, base + GATE + j) * picked_rows(place_ref, j, table)
    out_ref[...] = total * valid_ref[...]


def local(
    residual_in,
    lengths,
    routes,
    prev_logits,
    cotangent,
    w_qkv,
    w_out,
    attn_gain,
    ffn_gain,
    router,
    const_gate,
    const_vec,
    w_gate,
    w_up,
    w_down,
):
    tok_rows = residual_in.shape[1]
    feat = residual_in.shape[2]
    head_size = feat // HEADS
    score_scale = head_size ** (-0.5)
    n_dp = lax.axis_size("dp")
    n_ctx = lax.axis_size("ctx")
    n_exp = lax.axis_size("exp")
    own_exp = w_gate.shape[0]
    reps = n_dp // own_exp
    n_all = router.shape[1]
    n_ffn = n_all - 4
    cap_rows = tok_rows // 4
    sub_rows = cap_rows // reps
    n_slots = n_ffn * cap_rows
    ctx_rank = lax.axis_index("ctx")
    positions = ctx_rank * tok_rows + jnp.arange(tok_rows, dtype=jnp.int32)
    length = lengths[0]
    valid_rows = (positions < length).astype(f32)[:, None]

    def gather_ctx(rows):
        if n_ctx == 2:
            return swap(rows, "ctx", 1)
        for bit in reversed(bits_of("ctx")):
            other = swap(rows, "ctx", bit)
            upper = (ctx_rank & bit) != 0
            rows = jnp.concatenate([jnp.where(upper, other, rows), jnp.where(upper, rows, other)], axis=0)
        return rows

    def scatter_ctx(rows):
        if n_ctx == 2:
            return swap(rows, "ctx", 1)
        for bit in bits_of("ctx"):
            low, high = jnp.split(rows, 2, axis=0)
            upper = (ctx_rank & bit) != 0
            sent = jnp.where(upper, low, high).astype(bf16)
            rows = jnp.where(upper, high, low).astype(f32) + swap(sent, "ctx", bit).astype(f32)
        return rows

    route_ids = routes[0]
    choose = (route_ids[:, :, None] == jnp.arange(n_all, dtype=jnp.int32)[None, None, :]).astype(f32)
    both = jnp.sum(choose, axis=1)
    before = jnp.arange(tok_rows)
    before = (before[None, :] < before[:, None]).astype(bf16)
    counts = dot32(before, both.astype(bf16))
    slot_ids = jnp.sum(choose * counts[:, None, :], axis=-1).astype(jnp.int32)
    is_ffn = route_ids < n_ffn
    place = (
        ((route_ids % own_exp) * reps + slot_ids // sub_rows) * n_exp + route_ids // own_exp
    ) * sub_rows + slot_ids % sub_rows
    half_rows = sub_rows // 2
    place_half = (
        (place // half_rows % 2) * (n_slots // 2) + place // sub_rows * half_rows + place % half_rows
    )
    place = jnp.where(is_ffn, place, -1)
    place_half = jnp.where(is_ffn, place_half, -1)
    row_ids = jnp.arange(n_slots, dtype=jnp.int32)
    place_rows = jnp.transpose(place)

    def to_experts(rows):
        return lax.all_to_all(
            rows.reshape(n_dp * n_exp, rows.shape[0] // (n_dp * n_exp), -1),
            ("dp", "exp"),
            split_axis=0,
            concat_axis=0,
            tiled=True,
        ).reshape(rows.shape[0], -1)

    width = 2 * feat
    far, mid_a, near = plan_steps(("ctx", "exp"))
    _, mid_b, _ = plan_steps(("exp", "ctx"))
    lane = jnp.arange(PAIR, dtype=jnp.int32)
    half = head_size // 2
    inv_freq = 10000.0 ** (-2.0 * (lane % half).astype(f32) / head_size)
    sign = jnp.where(lane % head_size < half, -1.0, 1.0)

    def turns(where):
        angles = where.astype(f32)[:, None] * inv_freq[None, :]
        return jnp.cos(angles), jnp.sin(angles) * sign[None, :]

    cosine, sine = turns(positions)
    other_start = (1 - ctx_rank) * tok_rows if n_ctx == 2 else 0
    n_other = tok_rows if n_ctx == 2 else tok_rows * n_ctx
    other_cos, other_sin = turns(other_start + jnp.arange(n_other, dtype=jnp.int32))
    other_in = gather_ctx(residual_in[0])
    (rows,) = simple_call(
        rows_kernel, (w_qkv, w_out, router.T, const_gate.T, const_vec.T, attn_gain[None], ffn_gain[None]),
        [((w_out.shape[0], 4 * feat + PAIR), bf16)], 0, "rows",
    )
    packed = pack_expert(w_gate, w_up, w_down, ())
    tables = (cosine, sine, other_cos, other_sin)
    if len(far) == 2:
        whole, placed = gather_far(rows, far, (packed,) + tables)
    else:
        whole, placed = gather_steps(rows, [], far)
    group = trade_far(hold(packed, whole))
    part_a, part_b = whole[..., :width], whole[..., width:]
    placed_a, placed_b = placed, placed
    for i, (step_a, step_b) in enumerate(zip(mid_a, mid_b)):
        meanwhile = (other_in,) if i == 0 else ()
        if i + 1 == len(mid_a):
            (grad_sent,) = simple_call(
                spread_kernel, (cotangent[0], valid_rows, place_rows), [((n_slots, feat), bf16)], 0, "spread", (part_b,)
            )
            meanwhile = (grad_sent,)
        part_a, placed_a = gather_step(part_a, placed_a, *step_a)
        part_b, placed_b = gather_step(part_b, placed_b, *step_b, meanwhile)
    first_part, _ = gather_steps(part_a, placed_a, near)
    second_part, _ = gather_steps(part_b, placed_b, near)
    first_part = first_part.reshape(feat, width)
    second_part = second_part.reshape(feat, 2 * feat + PAIR)

    small_at = 2 * feat // PAIR
    w_v, w_o, small = column(second_part, feat, 0), column(second_part, feat, 1), column(second_part, PAIR, small_at)
    rows_low = ((tok_rows, feat), bf16)
    rows_full = ((tok_rows, feat), f32)
    square = 2 * tok_rows * feat * feat
    hidden_one, queries, own_keys, own_values = simple_call(
        functools.partial(project_kernel, score_scale, n_all + 6),
        (residual_in[0], first_part, w_v, small, cosine, sine), [rows_low] * 4, 3 * square, "project",
    )
    tok_spec = pl.BlockSpec((tok_rows, feat), lambda i: (i, 0))
    turn_spec = pl.BlockSpec((tok_rows, PAIR), lambda i: (i, 0))

    def fixed(rows, cols, index=0):
        return pl.BlockSpec((rows, cols), lambda i: (0, index))

    other_hidden, other_keys, other_values = pl.pallas_call(
        functools.partial(other_project_kernel, n_all + 6),
        grid=(n_other // tok_rows,),
        in_specs=[tok_spec, fixed(feat, feat, 1), fixed(feat, PAIR, small_at), fixed(feat, feat), turn_spec, turn_spec],
        out_specs=[tok_spec] * 3,
        out_shape=[jax.ShapeDtypeStruct((n_other, feat), bf16)] * 3,
        compiler_params=pltpu.CompilerParams(vmem_limit_bytes=VMEM),
        cost_estimate=cost("project_other"),
        name="project_other",
    )(other_in, first_part, second_part, second_part, other_cos, other_sin)
    grad_rows_in = to_experts(hold(grad_sent, group, hidden_one, other_keys))
    info = jnp.stack([ctx_rank * tok_rows, length, ctx_rank]).astype(jnp.int32)
    prev = jnp.pad(prev_logits[0], ((0, 0), (0, PAIR - n_all)))
    attended, attended_low, log_total = attend(
        info, queries, own_keys, own_values, other_keys, other_values, (group, prev, place, place_half)
    )

    mid_rows, hidden, scalars, *sent_rows = simple_call(
        functools.partial(mid_kernel, n_all),
        (attended_low, small, w_o, residual_in[0], prev, route_ids, jnp.transpose(place_half)),
        [rows_full, rows_low, ((tok_rows, PAIR), f32)] + [((n_slots // 2, feat + PAIR), bf16)] * 2, 0, "mid",
    )
    rows_in = [to_experts(hold(sent_rows[0], grad_rows_in)), to_experts(sent_rows[1])]

    steps_near = near_steps(own_exp)
    groups = gather_expert_near([group], steps_near)
    piece_width = group.shape[3]
    if piece_width < PAIR:
        merge = PAIR // piece_width
        whole = jnp.concatenate(groups).reshape(-1, merge, 3, feat, piece_width)
        groups = [jnp.moveaxis(whole, 1, 3).reshape(-1, 3, feat, PAIR)]
    grads_in = grad_rows_in.reshape(n_dp * n_exp, 2, half_rows, feat)
    expert_out = None
    flows, back_grads = [], []
    for part in range(2):
        expert_out, grad_in, *flow = expert_call(part, rows_in[part], grads_in, groups, expert_out, f"expert_{part}")
        back_grads.append(to_experts(grad_in))
        flows.append(flow)
    expert_out = expert_out.reshape(n_slots, feat)
    n_groups = 2 ** len(steps_near)
    act, grad_gate_pre, grad_up_pre, gated_rows, grad_expert_out = zip(*flows)
    flows = (gated_rows, grad_expert_out, act, grad_gate_pre, grad_up_pre)
    simple = piece_width >= PAIR and len(steps_near) == 2
    if simple:
        far_near, far_kept, near_own, kept, expert_out = expert_weights(
            flows, (3, 2, 1, 0), (1, 1, 1, 1), own_exp, piece_width, (bf16,) * 4, "weights_all", expert_out,
            (back_grads[0],),
        )
        far_near = swap(hold(far_near, back_grads[1]), *steps_near[1])
        far_kept = swap(hold(far_kept, back_grads[1]), *steps_near[1])
        near_sent = weights_sent(near_own, far_near)
        near_came = [swap(part, *steps_near[0]) for part in near_sent]
    else:
        step = max(piece_width, PAIR)
        n_steps = act[0].shape[1] // step
        (whole,) = expert_weights(flows, tuple(range(n_steps)), (n_steps,), 1, step, (f32,), "weights_all")
        if piece_width < PAIR:
            whole = jnp.moveaxis(whole.reshape(-1, 3, feat, merge, piece_width), 3, 1)
        whole = whole.reshape(n_groups, own_exp, 3, feat, piece_width)
        expert_sum = scatter_expert_near([whole[i] for i in range(n_groups)], steps_near)
    back_rows = to_experts(expert_out)
    small_shape = ((tok_rows, PAIR), f32)
    grad_mid, grad_attended, grad_mix, grad_gain_two = simple_call(
        functools.partial(gates_back_kernel, n_all),
        (
            *back_grads, place_half, route_ids, scalars, hidden, mid_rows, cotangent[0], valid_rows, small, w_o,
        ),
        [rows_full, rows_low, small_shape, ((1, feat), f32)], 0, "gates_back", tuple(near_sent) if simple else (),
    )
    grad_queries, other_dk, other_dv, delta = grads_other(
        info, queries, other_keys, other_values, grad_attended, attended, log_total, ()
    )
    core = (lax.axis_index("dp") & 1).astype(jnp.int32).reshape(1)
    core_block = feat // (n_dp * n_ctx * n_exp) * row_weight("dp")
    other_gk, other_dh, more_gain = pl.pallas_call(
        other_back_kernel,
        grid=(n_other // tok_rows,),
        in_specs=[tok_spec, tok_spec, fixed(feat, feat, 1), fixed(feat, feat), turn_spec, turn_spec, tok_spec],
        out_specs=[tok_spec, tok_spec, fixed(1, feat)],
        out_shape=[
            jax.ShapeDtypeStruct((n_other, feat), bf16), jax.ShapeDtypeStruct((n_other, feat), bf16),
            jax.ShapeDtypeStruct((1, feat), f32),
        ],
        compiler_params=pltpu.CompilerParams(vmem_limit_bytes=VMEM),
        cost_estimate=cost("back_other"),
        name="back_other",
    )(other_dk, other_dv, first_part, second_part, other_cos, other_sin, other_in)
    more_dh = scatter_ctx(other_dh)
    if simple:
        sum_first = weights_sum(kept, far_kept, near_came[0], 0, (other_dh,))
    else:
        sum_first, sum_rest = expert_sum[:, :1].astype(bf16), expert_sum[:, 1:].astype(bf16)
    back_first = trade_far(sum_first)
    grad_queries, own_dk, own_dv = grads_own(
        info, queries, own_keys, own_values, grad_attended, log_total, delta, grad_queries, (back_rows, sum_first)
    )
    half_rows = feat // 2
    out_keep, out_give = simple_call(
        functools.partial(out_grads_kernel, n_all, core_block),
        (attended_low, grad_mid, hidden, grad_mix, scalars, cotangent[0], valid_rows, grad_gain_two),
        [((half_rows, feat + PAIR), f32), ((half_rows, feat + PAIR), bf16)], 0, "out_grads", (own_dk,), (core,),
    )

    if simple:
        sum_rest = weights_sum(kept, far_kept, near_came[1], 1, (out_keep,))
    back_rest = trade_far(sum_rest)
    own_args = (
        core, grad_queries, own_dk, own_dv, hidden_one, first_part, second_part, cosine, sine, residual_in[0], other_hidden,
        other_gk, other_dv, more_gain,
    )
    own_deps = (sum_rest, back_first)
    step_spec = pl.BlockSpec((half_rows, feat), lambda i: (0, jnp.minimum(i, 1)))
    token, turn, other = fixed(tok_rows, feat), fixed(tok_rows, PAIR), fixed(n_other, feat)
    qk_keep, qk_give, v_keep, v_give, grad_hidden_one, gain_keep, gain_give = pl.pallas_call(
        ordered(functools.partial(own_back_kernel, score_scale, core_block), len(own_args), len(own_deps)),
        grid=(3,),
        in_specs=[pl.BlockSpec(memory_space=pltpu.SMEM)] + [token] * 4
        + [pl.BlockSpec((feat, feat), lambda i: (0, jnp.minimum(i, 1))), fixed(feat, feat), turn, turn, token]
        + [other] * 3 + [fixed(1, feat)] + waits(own_deps),
        out_specs=[step_spec] * 2 + [fixed(half_rows, feat)] * 2 + [token] + [fixed(half_rows, PAIR)] * 2,
        out_shape=[
            jax.ShapeDtypeStruct((half_rows, 2 * feat), f32), jax.ShapeDtypeStruct((half_rows, 2 * feat), bf16),
            jax.ShapeDtypeStruct((half_rows, feat), f32), jax.ShapeDtypeStruct((half_rows, feat), bf16),
            jax.ShapeDtypeStruct((tok_rows, feat), f32),
            jax.ShapeDtypeStruct((half_rows, PAIR), f32), jax.ShapeDtypeStruct((half_rows, PAIR), bf16),
        ],
        compiler_params=pltpu.CompilerParams(vmem_limit_bytes=VMEM),
        cost_estimate=cost("back_own"),
        name="back_own",
    )(*own_args, *own_deps)
    def last_rows(sent):
        (output,) = simple_call(
            functools.partial(output_kernel, n_all),
            (back_rows, place, scalars, hidden, mid_rows, valid_rows, small), [rows_full], 0, "output", (sent,),
        )
        (grad_x,) = simple_call(
            functools.partial(first_norm_kernel, n_all + 6),
            (grad_hidden_one, more_dh, residual_in[0], small, grad_mid), [rows_full], 0, "first_norm", (output,),
        )
        results.extend([output, grad_x, *unpack_expert(back_first, back_rest, (output, grad_x))])
        return results

    results = []
    sums = scatter_parts(
        [
            [(qk_keep, qk_give, 2 * feat, 0), (gain_keep, gain_give, PAIR, 0)],
            [(v_keep, v_give, feat, 0), (out_keep, out_give, feat + PAIR, 0)],
        ],
        [mid_a, mid_b], far, near, w_out.shape[0], (), last_rows,
    )
    output, grad_x, *expert_grads = results
    small_out = sums[:, 4 * feat + PAIR :]
    return (
        output[None],
        grad_x[None],
        jnp.concatenate([sums[:, : 2 * feat], sums[:, 2 * feat + PAIR : 3 * feat + PAIR]], axis=1),
        sums[:, 3 * feat + PAIR : 4 * feat + PAIR],
        sums[:, 2 * feat],
        small_out[:, n_all + 6],
        small_out[:, :n_all],
        small_out[:, n_all : n_all + 4],
        small_out[:, n_all + 4 : n_all + 6],
        expert_grads[0],
        expert_grads[1],
        expert_grads[2],
    )


def solution(mesh):
    in_specs = (
        P(("dp", "exp"), "ctx", None),
        P(("dp", "exp")),
        P(("dp", "exp"), "ctx", None),
        P(("dp", "exp"), "ctx", None),
        P(("dp", "exp"), "ctx", None),
        P(("dp", "ctx", "exp"), None),
        P(("dp", "ctx", "exp"), None),
        P(("dp", "ctx", "exp")),
        P(("dp", "ctx", "exp")),
        P(("dp", "ctx", "exp"), None),
        P(("dp", "ctx", "exp"), None),
        P(("dp", "ctx", "exp"), None),
        P("exp", None, ("dp", "ctx")),
        P("exp", None, ("dp", "ctx")),
        P("exp", ("dp", "ctx"), None),
    )
    out_specs = (
        P(("dp", "exp"), "ctx", None),
        P(("dp", "exp"), "ctx", None),
        P(("dp", "ctx", "exp"), None),
        P(("dp", "ctx", "exp"), None),
        P(("dp", "ctx", "exp")),
        P(("dp", "ctx", "exp")),
        P(("dp", "ctx", "exp"), None),
        P(("dp", "ctx", "exp"), None),
        P(("dp", "ctx", "exp"), None),
        P("exp", None, ("dp", "ctx")),
        P("exp", None, ("dp", "ctx")),
        P("exp", ("dp", "ctx"), None),
    )
    return jax.shard_map(local, mesh=mesh, in_specs=in_specs, out_specs=out_specs, check_vma=False)
```

```python
import functools

import jax
import jax.numpy as jnp
from jax import lax
from jax.experimental import pallas as pl
from jax.experimental.pallas import tpu as pltpu
from jax.sharding import PartitionSpec as P

HEADS = 12

norm_eps = 1e-06
top_precision = lax.Precision.HIGHEST
f32 = jnp.float32
bf16 = jnp.bfloat16


CHUNK = 256
BLOCK = 512
OCHUNK = 512
QCHUNK = 128
PAIR = 128
NEG = -1e30
SCALE = 48
VMEM = 62 << 20
MICROS = {
    "project": 6, "project_other": 5, "spread": 4, "attend": 17, "mid": 9, "expert": 30, "weights_sent": 0,
    "weights_near": 0, "weights_kept": 0, "weights_sum": 0, "gates_back": 0, "grads_other": 0, "back_other": 0, "grads_own": 0,
    "back_own": 13, "out_grads": 0, "output": 6, "first_norm": 4, "weights_all": 26, "pack": 3, "unpack": 4, "combine": 1, "rows": 2, "sums": 1,
}


def cost(name):
    return pl.CostEstimate(flops=MICROS[name] * 1000000000 // SCALE, bytes_accessed=1, transcendentals=0)


def mul_nt(a, b):
    return lax.dot_general(a, b, (((1,), (1,)), ((), ())), preferred_element_type=f32)


def mul_nn(a, b):
    return lax.dot_general(a, b, (((1,), (0,)), ((), ())), preferred_element_type=f32)


def mul_tn(a, b):
    return lax.dot_general(a, b, (((0,), (0,)), ((), ())), preferred_element_type=f32)


def head_part(rows, head):
    lane = lax.broadcasted_iota(jnp.int32, rows.shape, 1)
    return jnp.where((lane >= PAIR // 2) == (head == 1), rows, jnp.zeros_like(rows))


def key_allowed(shape, key_start, length, query_start=None):
    key = key_start + lax.broadcasted_iota(jnp.int32, shape, 0)
    allowed = key < length
    if query_start is not None:
        allowed &= key <= query_start + lax.broadcasted_iota(jnp.int32, shape, 1)
    return allowed


def both_heads(rows, first=0):
    return jnp.concatenate([head_part(rows[first:], head) for head in range(2)], axis=0)


def beside(row_pair):
    return jnp.concatenate([row_pair[0:1], row_pair[1:2]], axis=1)


def split_heads(wide):
    half, t = PAIR // 2, wide.shape[1] // 2
    return jnp.concatenate([wide[:half, :t], wide[half:, t:]], axis=0)


def attend_kernel(info, q_ref, k_ref, v_ref, ok_ref, ov_ref, out_ref, low_ref, log_ref):
    base, length, blocks = info[0], info[1], info[2]
    queries = q_ref[...]
    rows = queries.shape[0]
    half = PAIR // 2
    starts = list(range(0, rows, QCHUNK))
    twice = [both_heads(queries[first : first + QCHUNK]) for first in starts]

    def spread(row):
        n = row.shape[1] // 2
        return jnp.concatenate(
            [jnp.broadcast_to(row[:, :n], (half, n)), jnp.broadcast_to(row[:, n:], (half, n))], axis=0
        )

    scores, tops, states = [], [], []
    for first, part in zip(starts, twice):
        end = first + QCHUNK
        some = mul_nt(k_ref[:end, :], part)
        allowed = key_allowed((end, QCHUNK), base, length, base + first)
        scores.append(jnp.where(jnp.concatenate([allowed, allowed], axis=1), some, NEG))
    for some in scores:
        tops.append(jnp.max(some, axis=0, keepdims=True))
    for first, some, top in zip(starts, scores, tops):
        expo = jnp.exp(some - top)
        total = jnp.sum(expo, axis=0, keepdims=True)
        acc = split_heads(mul_tn(v_ref[: first + QCHUNK, :], expo.astype(bf16)))
        states.append((top, total, acc))

    def step(c, states):
        first = pl.multiple_of(c * BLOCK, BLOCK)
        keys = ok_ref[pl.ds(first, BLOCK), :]
        vals = ov_ref[pl.ds(first, BLOCK), :]
        allowed = key_allowed((BLOCK, 2 * QCHUNK), first, length)
        scores = [jnp.where(allowed, mul_nt(keys, part), NEG) for part in twice]
        new = []
        for some, (top, total, acc) in zip(scores, states):
            new_top = jnp.maximum(top, jnp.max(some, axis=0, keepdims=True))
            expo = jnp.exp(some - new_top)
            factor = jnp.exp(top - new_top)
            total = total * factor + jnp.sum(expo, axis=0, keepdims=True)
            acc = acc * spread(factor) + split_heads(mul_tn(vals, expo.astype(bf16)))
            new.append((new_top, total, acc))
        return tuple(new)

    states = lax.fori_loop(0, blocks, step, tuple(states))
    for first, (top, total, acc) in zip(starts, states):
        there = slice(first, first + QCHUNK)
        out = jnp.transpose(acc / spread(total))
        out_ref[there, :] = out
        low_ref[there, :] = out.astype(bf16)
        log = top + jnp.log(total)
        log_ref[0, 0:1, there] = log[:, :QCHUNK]
        log_ref[0, 1:2, there] = log[:, QCHUNK:]


def pair_grads(keys, vals, twice, grad_twice, log_row, delta_row, allowed):
    probs = jnp.where(allowed, jnp.exp(mul_nt(keys, twice) - log_row), 0.0)
    grad_probs = mul_nt(vals, grad_twice)
    grad_scores = (probs * (grad_probs - delta_row)).astype(bf16)
    return (
        mul_nn(grad_scores, twice),
        mul_nn(probs.astype(bf16), grad_twice),
        split_heads(mul_tn(keys, grad_scores)),
    )


def other_backward(
    info, q_ref, k_ref, v_ref, grad_ref, out_ref, log_ref, dq_ref, dk_ref, dv_ref, delta_ref
):
    length, chunks = info[1], info[2] * (BLOCK // OCHUNK)
    half = PAIR // 2
    queries, grads = q_ref[...], grad_ref[...]
    rows = queries.shape[0]
    product = jnp.transpose(grads.astype(f32) * out_ref[...])
    twice, grad_twice = both_heads(queries), both_heads(grads)
    for head in range(2):
        delta_ref[0, head : head + 1, :] = jnp.sum(
            product[head * half : (head + 1) * half], axis=0, keepdims=True
        )
    log_row, delta_row = beside(log_ref[0]), beside(delta_ref[0])

    def step(c, dq):
        first = pl.multiple_of(c * OCHUNK, OCHUNK)
        keys = k_ref[pl.ds(first, OCHUNK), :]
        vals = v_ref[pl.ds(first, OCHUNK), :]
        allowed = key_allowed((OCHUNK, 2 * rows), first, length)
        dk, dv, more = pair_grads(keys, vals, twice, grad_twice, log_row, delta_row, allowed)
        dk_ref[pl.ds(first, OCHUNK), :] = dk.astype(dk_ref.dtype)
        dv_ref[pl.ds(first, OCHUNK), :] = dv.astype(dv_ref.dtype)
        return dq + more

    dq_ref[...] = lax.fori_loop(0, chunks, step, jnp.zeros((PAIR, rows), f32))

    def clear(c, none):
        first = pl.multiple_of(c * OCHUNK, OCHUNK)
        dk_ref[pl.ds(first, OCHUNK), :] = jnp.zeros((OCHUNK, PAIR), dk_ref.dtype)
        dv_ref[pl.ds(first, OCHUNK), :] = jnp.zeros((OCHUNK, PAIR), dv_ref.dtype)
        return none

    lax.fori_loop(chunks, k_ref.shape[0] // OCHUNK, clear, 0)


def own_backward(
    info, q_ref, k_ref, v_ref, grad_ref, log_ref, delta_ref, before_ref, dq_ref, dk_ref, dv_ref
):
    base, length = info[0], info[1]
    queries, grads = q_ref[...], grad_ref[...]
    rows = queries.shape[0]
    dq = before_ref[...]
    for first in range(0, rows, CHUNK):
        keys = k_ref[first : first + CHUNK, :]
        vals = v_ref[first : first + CHUNK, :]
        allowed = key_allowed((CHUNK, rows - first), base + first, length, base + first)
        dk, dv, more = pair_grads(
            keys,
            vals,
            both_heads(queries, first),
            both_heads(grads, first),
            beside(log_ref[0, :, first:]),
            beside(delta_ref[0, :, first:]),
            jnp.concatenate([allowed, allowed], axis=1),
        )
        dk_ref[first : first + CHUNK, :] = dk.astype(dk_ref.dtype)
        dv_ref[first : first + CHUNK, :] = dv.astype(dv_ref.dtype)
        if first:
            more = jnp.concatenate([jnp.zeros((PAIR, first), f32), more], axis=1)
        dq = dq + more
    dq_ref[...] = jnp.transpose(dq).astype(dq_ref.dtype)


def per_pair(rows):
    return pl.BlockSpec((rows, PAIR), lambda i, info: (0, i))


def turned(cols):
    return pl.BlockSpec((PAIR, cols), lambda i, info: (i, 0))


def stats(cols):
    return pl.BlockSpec((1, 2, cols), lambda i, info: (i, 0, 0))


def ordered(kernel, n_in, n_deps):
    if not n_deps:
        return kernel

    def run(*refs):
        kernel(*refs[:n_in], *refs[n_in + n_deps :])

    return run


def waits(deps):
    return [pl.BlockSpec(memory_space=pl.ANY)] * len(deps)


def attn_call(kernel, info, args, in_specs, outs, out_specs, flops, name, deps=()):
    return pl.pallas_call(
        ordered(kernel, 1 + len(args), len(deps)),
        grid_spec=pltpu.PrefetchScalarGridSpec(
            num_scalar_prefetch=1,
            grid=(HEADS // 2,),
            in_specs=in_specs + waits(deps),
            out_specs=out_specs,
        ),
        out_shape=[jax.ShapeDtypeStruct(s, d) for s, d in outs],
        compiler_params=pltpu.CompilerParams(vmem_limit_bytes=VMEM),
        cost_estimate=cost(name),
        name=name,
    )(info, *args, *deps)


def attend(info, q, k, v, other_k, other_v, deps):
    t, d = q.shape
    st = (HEADS // 2, 2, t)
    n = other_k.shape[0]
    return attn_call(
        attend_kernel, info, (q, k, v, other_k, other_v),
        [per_pair(t)] * 3 + [per_pair(n)] * 2,
        [((t, d), f32), ((t, d), bf16), (st, f32)], [per_pair(t), per_pair(t), stats(t)], 8 * t * t * d, "attend", deps,
    )


def grads_other(info, q, k, v, grad, out, log_total, deps):
    t, d = q.shape
    n = k.shape[0]
    return attn_call(
        other_backward, info, (q, k, v, grad, out, log_total),
        [per_pair(t), per_pair(n), per_pair(n), per_pair(t), per_pair(t), stats(t)],
        [((d, t), f32), ((n, d), bf16), ((n, d), bf16), ((HEADS // 2, 2, t), f32)],
        [turned(t), per_pair(n), per_pair(n), stats(t)], 10 * t * t * d, "grads_other", deps,
    )


def grads_own(info, q, k, v, grad, log_total, delta, before, deps):
    t, d = q.shape
    return attn_call(
        own_backward, info, (q, k, v, grad, log_total, delta, before),
        [per_pair(t)] * 4 + [stats(t)] * 2 + [turned(t)],
        [((t, d), bf16)] * 3, [per_pair(t)] * 3, 10 * t * t * d, "grads_own", deps,
    )


def dot32(a, b, dims=((1,), (0,)), precision=None):
    return lax.dot_general(a, b, (dims, ((), ())), precision=precision, preferred_element_type=f32)


def swap(block, axis, bit):
    return lax.ppermute(block, axis, [(i, i ^ bit) for i in range(lax.axis_size(axis))])


def bits_of(axis, low=1, high=None):
    high = lax.axis_size(axis) if high is None else high
    found = []
    while low < high:
        found.append(low)
        low *= 2
    return found[::-1]


def row_weight(axis):
    x = lax.axis_size("exp")
    c = lax.axis_size("ctx")
    return {"exp": 1, "ctx": x, "dp": x * c}[axis]


def plan_steps(middle):
    far = [("dp", bit) for bit in bits_of("dp", 2)]
    mid = [(axis, bit) for axis in middle for bit in bits_of(axis)]
    near = [("dp", bit) for bit in bits_of("dp", 1, 2)]
    return far, mid, near


def row_bits(steps):
    return sorted([row_weight(axis) * bit for axis, bit in steps], reverse=True)


def nothing(*refs):
    pass


def hold(value, *others):
    return pl.pallas_call(
        nothing,
        in_specs=waits((value,) + others),
        out_specs=waits((value,))[0],
        out_shape=jax.ShapeDtypeStruct(value.shape, value.dtype),
        input_output_aliases={0: 0},
        cost_estimate=pl.CostEstimate(flops=0, bytes_accessed=0, transcendentals=0),
        name="hold",
    )(value, *others)


def rows_kernel(wqkv_ref, wout_ref, *refs):
    out_ref = refs[-1]
    d = wout_ref.shape[1]
    out_ref[:, : 3 * d] = wqkv_ref[...]
    out_ref[:, 3 * d : 4 * d] = wout_ref[...]
    small = jnp.zeros((wout_ref.shape[0], PAIR), f32)
    first = 0
    for ref in refs[:-1]:
        shape = (ref.shape[0], PAIR)
        here = lax.broadcasted_iota(jnp.int32, shape, 0) + first == lax.broadcasted_iota(jnp.int32, shape, 1)
        small += mul_tn(ref[...], jnp.where(here, 1.0, 0.0).astype(bf16))
        first += ref.shape[0]
    out_ref[:, 4 * d :] = small.astype(bf16)


def gather_step(whole, placed, axis, bit, meanwhile=()):
    other = swap(whole, axis, bit)
    if meanwhile:
        whole = hold(whole, *meanwhile)
    upper = (lax.axis_index(axis) & bit) != 0
    weight = row_weight(axis) * bit
    pos = sum(1 for w in placed if w > weight)
    both = [jnp.where(upper, other, whole), jnp.where(upper, whole, other)]
    return jnp.stack(both, axis=pos), placed[:pos] + [weight] + placed[pos:]


def gather_steps(whole, placed, steps):
    for axis, bit in steps:
        whole, placed = gather_step(whole, placed, axis, bit)
    return whole, placed


def gather_far(rows, steps, meanwhile):
    axis = steps[0][0]
    bits = [bit for _, bit in steps]
    parts = [rows] + [swap(rows, axis, mask) for mask in (bits[1], bits[0], bits[0] + bits[1])]
    parts[0] = hold(rows, *meanwhile)
    low, high = [(lax.axis_index(axis) & bit) != 0 for bit in (bits[1], bits[0])]
    parts = [jnp.where(low, parts[i ^ 1], parts[i]) for i in range(4)]
    parts = [jnp.where(high, parts[i ^ 2], parts[i]) for i in range(4)]
    whole = jnp.stack(parts).reshape((2, 2) + rows.shape)
    return whole, [row_weight(axis) * bit for bit in bits]


def scatter_split(part, placed, axis, bit):
    pos = placed.index(row_weight(axis) * bit)
    upper = (lax.axis_index(axis) & bit) != 0
    low = lax.index_in_dim(part, 0, pos, keepdims=False)
    high = lax.index_in_dim(part, 1, pos, keepdims=False)
    sent = jnp.where(upper, low, high).astype(bf16)
    kept = jnp.where(upper, high, low).astype(f32)
    return sent, kept, placed[:pos] + placed[pos + 1 :]


def scatter_step(part, placed, axis, bit):
    sent, kept, placed = scatter_split(part, placed, axis, bit)
    return kept + swap(sent, axis, bit).astype(f32), placed


def combine_kernel(n, block, up_ref, *refs):
    keep_ref, give_ref = refs[2 * n :]
    first = 0
    for kept, came in zip(refs[:n], refs[n : 2 * n]):
        cols = slice(first, first + kept.shape[1])
        total = kept[...] + came[...].astype(f32)
        keep_ref[:, cols], give_ref[:, cols] = split_rows(up_ref[0] == 1, total, block)
        first += kept.shape[1]


def combine(kept, came, placed, axis, bit, rows, deps, steps=1):
    weight = row_weight(axis) * bit
    placed = [w for w in placed if w != weight]
    block = rows * 2 ** sum(1 for w in placed if w < weight)
    upper = ((lax.axis_index(axis) & bit) != 0).astype(jnp.int32).reshape(1)
    n_rows = kept[0][0].shape[0] // steps
    args = [*kept, *came]
    out = pl.BlockSpec((n_rows // 2, sum(arg[1][1] for arg in kept)), lambda i: (i, 0))
    shape = (n_rows // 2 * steps, out.block_shape[1])
    keep, give = pl.pallas_call(
        ordered(functools.partial(combine_kernel, len(kept), block), 1 + len(args), len(deps)),
        grid=(steps,),
        in_specs=[pl.BlockSpec(memory_space=pltpu.SMEM)]
        + [pl.BlockSpec((n_rows, arg[1][1]), lambda i, index=arg[2]: (i, index)) for arg in args]
        + waits(deps),
        out_specs=[out, out],
        out_shape=[jax.ShapeDtypeStruct(shape, f32), jax.ShapeDtypeStruct(shape, bf16)],
        compiler_params=pltpu.CompilerParams(vmem_limit_bytes=VMEM),
        cost_estimate=cost("combine"),
        name="combine",
    )(upper, *[arg[0] for arg in args], *deps)
    return keep, give, placed


def whole_of(array):
    return column(array, array.shape[1], 0)


def scatter_split(part, placed, axis, bit):
    pos = placed.index(row_weight(axis) * bit)
    upper = (lax.axis_index(axis) & bit) != 0
    low = lax.index_in_dim(part, 0, pos, keepdims=False)
    high = lax.index_in_dim(part, 1, pos, keepdims=False)
    sent = jnp.where(upper, low, high).astype(bf16)
    kept = jnp.where(upper, high, low).astype(f32)
    return sent, kept, placed[:pos] + placed[pos + 1 :]


def scatter_parts(parts, orders, far, near, rows, deps, meanwhile, widths, narrow):
    swapped = {}
    for blocks in parts:
        for _, give, _, _ in blocks:
            if id(give) not in swapped:
                swapped[id(give)] = swap(give, *near[0])
    sums, places, gives = [], [], []
    for i, (blocks, order) in enumerate(zip(parts, orders)):
        step, late = order[-1], i == len(parts) - 1
        keep, give, placed = combine(
            [column(keep, width, index) for keep, _, width, index in blocks],
            [column(swapped[id(give)], width, index) for _, give, width, index in blocks],
            row_bits(far + order), *step, rows, deps if late else (),
        )
        gives.append(give)
        sums.append((keep, swap(give, *step)))
        places.append(placed)
    ready = meanwhile(gives)
    sums = [
        (hold(keep, *ready) + came.astype(f32)).reshape((2,) * len(placed) + (-1, keep.shape[1]))
        for (keep, came), placed in zip(sums, places)
    ]
    for steps in zip(*[reversed(order[:-1]) for order in orders]):
        splits = [scatter_split(part, where, *step) for part, where, step in zip(sums, places, steps)]
        places = [split[2] for split in splits]
        sums = [kept + swap(sent, *step).astype(f32) for (sent, kept, _), step in zip(splits, steps)]
    total, placed = jnp.concatenate(sums, axis=-1), places[0]
    for step in reversed(far):
        sent, kept, placed = scatter_split(total, placed, *step)
        came = swap(sent, *step)
        if placed:
            total = kept + came.astype(f32)
    return simple_call(
        sums_kernel, (kept, came), [((rows, width), f32) for width in widths] + [((n, rows), f32) for n in narrow], 0, "sums"
    )


def sums_kernel(kept_ref, came_ref, qkv_ref, out_ref, *refs):
    d = out_ref.shape[1]
    total = kept_ref[...] + came_ref[...].astype(f32)
    qkv_ref[...] = total[:, : 3 * d]
    out_ref[...] = total[:, 3 * d + PAIR : 4 * d + PAIR]
    gain = jnp.transpose(total[:, 3 * d : 3 * d + PAIR])
    small = jnp.transpose(total[:, 4 * d + PAIR :])
    first = 0
    for ref in refs[:-1]:
        ref[...] = small[first : first + ref.shape[0]]
        first += ref.shape[0]
    refs[-1][...] = gain[:1]


def pack_kernel(gate_ref, up_ref, down_ref, out_ref):
    out_ref[0, 0] = gate_ref[0]
    out_ref[0, 1] = up_ref[0]
    out_ref[0, 2] = jnp.transpose(down_ref[0])


def unpack_kernel(first_ref, rest_ref, gate_ref, up_ref, down_ref):
    rows = first_ref.shape[2]
    for ref, there in ((first_ref, slice(0, rows)), (rest_ref, slice(rows, rows + rest_ref.shape[2]))):
        gate_ref[0, there] = ref[0, 0].astype(f32)
        up_ref[0, there] = ref[0, 1].astype(f32)
        down_ref[0, :, there] = jnp.transpose(ref[0, 2].astype(f32))


def one_of(*shape):
    return pl.BlockSpec((1,) + shape, lambda i: (i,) + (0,) * len(shape))


def pack_expert(w_gate, w_up, w_down, deps):
    n, d, f = w_gate.shape
    return pl.pallas_call(
        ordered(pack_kernel, 3, len(deps)),
        grid=(n,),
        in_specs=[one_of(d, f), one_of(d, f), one_of(f, d)] + waits(deps),
        out_specs=one_of(3, d, f),
        out_shape=jax.ShapeDtypeStruct((n, 3, d, f), w_gate.dtype),
        compiler_params=pltpu.CompilerParams(vmem_limit_bytes=VMEM),
        cost_estimate=cost("pack"),
        name="pack",
    )(w_gate, w_up, w_down, *deps)


def unpack_expert(first, rest, deps):
    n, m, d, f = first.shape
    d = d + rest.shape[2]
    outs = (d, f), (d, f), (f, d)
    return pl.pallas_call(
        ordered(unpack_kernel, 2, len(deps)),
        grid=(n,),
        in_specs=[one_of(*part.shape[1:]) for part in (first, rest)] + waits(deps),
        out_specs=[one_of(*shape) for shape in outs],
        out_shape=[jax.ShapeDtypeStruct((n,) + shape, f32) for shape in outs],
        compiler_params=pltpu.CompilerParams(vmem_limit_bytes=VMEM),
        cost_estimate=cost("unpack"),
        name="unpack",
    )(first, rest, *deps)


def trade_far(parts):
    n_own = parts.shape[0]
    reps = lax.axis_size("dp") // n_own
    groups = [[i * reps + r for i in range(n_own)] for r in range(reps)]
    return lax.all_to_all(parts, "dp", 0, 0, axis_index_groups=groups, tiled=True)


def near_steps(n_own):
    reps = lax.axis_size("dp") // n_own
    return [("ctx", bit) for bit in bits_of("ctx")] + [("dp", bit) for bit in bits_of("dp", 1, reps)]


def gather_expert_near(groups, steps):
    for axis, bit in steps:
        groups = groups + [swap(group, axis, bit) for group in groups]
    return groups


def scatter_expert_near(groups, steps):
    for axis, bit in reversed(steps):
        n = len(groups) // 2
        came = [swap(group.astype(bf16), axis, bit) for group in groups[n:]]
        groups = [a.astype(f32) + b.astype(f32) for a, b in zip(groups[:n], came)]
    return groups[0]


def rms_scale(rows):
    return lax.rsqrt(jnp.mean(rows * rows, axis=-1, keepdims=True) + norm_eps)


def rms_backward(in_rows, inv_scale, gain_vec, grad_rows):
    normed = in_rows * inv_scale
    gain_grad = jnp.sum(grad_rows * normed, axis=0, keepdims=True)
    inner_grad = grad_rows * gain_vec
    back_rows = inv_scale * (
        inner_grad - normed * jnp.mean(inner_grad * normed, axis=-1, keepdims=True)
    )
    return (back_rows, gain_grad)


def rope(rows, cos, sin):
    lane = lax.broadcasted_iota(jnp.int32, (rows.shape[0], PAIR), 1)
    low = lane % (PAIR // 2) < PAIR // 4
    parts = []
    for first in range(0, rows.shape[1], PAIR):
        part = rows[:, first : first + PAIR]
        other = jnp.where(low, pltpu.roll(part, PAIR - PAIR // 4, 1), pltpu.roll(part, PAIR // 4, 1))
        parts.append(part * cos + other * sin)
    return jnp.concatenate(parts, axis=1)


def gain_row(small_ref, lane):
    return jnp.transpose(small_ref[...].astype(f32))[lane : lane + 1]


def project_kernel(scale, lane, x_ref, first_ref, wv_ref, small_ref, cos_ref, sin_ref, h_ref, q_ref, k_ref, v_ref):
    rows = x_ref[...].astype(f32)
    d = rows.shape[1]
    hidden = (rows * rms_scale(rows) * gain_row(small_ref, lane)).astype(bf16)
    h_ref[...] = hidden
    cos, sin = cos_ref[...], sin_ref[...]
    k_ref[...] = rope(mul_nn(hidden, first_ref[:, d : 2 * d]), cos, sin).astype(bf16)
    v_ref[...] = mul_nn(hidden, wv_ref[...]).astype(bf16)
    q_ref[...] = (rope(mul_nn(hidden, first_ref[:, :d]), cos, sin) * scale).astype(bf16)


def other_project_kernel(lane, x_ref, wk_ref, small_ref, wv_ref, cos_ref, sin_ref, h_ref, k_ref, v_ref):
    rows = x_ref[...].astype(f32)
    d = rows.shape[1]
    hidden = (rows * rms_scale(rows) * gain_row(small_ref, lane)).astype(bf16)
    h_ref[...] = hidden
    k_ref[...] = rope(mul_nn(hidden, wk_ref[...]), cos_ref[...], sin_ref[...]).astype(bf16)
    v_ref[...] = mul_nn(hidden, wv_ref[...]).astype(bf16)


def other_back_kernel(dk_ref, dv_ref, wk_ref, wv_ref, cos_ref, sin_ref, x_ref, gk_ref, dh_ref, dgain_ref):
    first = pl.program_id(0) == 0
    grad_k = rope(dk_ref[...].astype(f32), cos_ref[...], -sin_ref[...]).astype(bf16)
    gk_ref[...] = grad_k
    rows = x_ref[...].astype(f32)
    dh = mul_nt(grad_k, wk_ref[...]) + mul_nt(dv_ref[...], wv_ref[...])
    dh_ref[...] = dh.astype(bf16)
    dgain = jnp.sum(dh * rows * rms_scale(rows), axis=0, keepdims=True)

    @pl.when(first)
    def _():
        dgain_ref[...] = dgain

    @pl.when(jnp.logical_not(first))
    def _():
        dgain_ref[...] += dgain


def split_rows(upper, rows, block):
    keep, give = [], []
    for first in range(0, rows.shape[0], 2 * block):
        low, high = rows[first : first + block], rows[first + block : first + 2 * block]
        keep.append(jnp.where(upper, high, low))
        give.append(jnp.where(upper, low, high))
    return jnp.concatenate(keep, axis=0), jnp.concatenate(give, axis=0).astype(bf16)


def own_back_kernel(
    scale, block, core_ref, dq_ref, dk_ref, dv_ref, h_ref, first_ref, wv_ref, cos_ref, sin_ref, x_ref, oh_ref, ok_ref, ov_ref,
    mgain_ref, keep_ref, give_ref, v_keep_ref, v_give_ref, dh_ref,
):
    step = pl.program_id(0)
    upper = core_ref[0] == 1
    cos, sin = cos_ref[...], -sin_ref[...]

    def finish(grad, weight, other, keep, give):
        dw = mul_tn(h_ref[...], grad)
        if other is not None:
            dw += mul_tn(oh_ref[...], other)
        keep[...], give[...] = split_rows(upper, dw, block)
        return mul_nt(grad, weight)

    @pl.when(step == 0)
    def _():
        grad = rope(dq_ref[...].astype(f32) * scale, cos, sin).astype(bf16)
        dh_ref[...] = finish(grad, first_ref[...], None, keep_ref, give_ref)

    @pl.when(step == 1)
    def _():
        grad = rope(dk_ref[...].astype(f32), cos, sin).astype(bf16)
        dh_ref[...] += finish(grad, first_ref[...], ok_ref[...], keep_ref, give_ref)

    @pl.when(step == 2)
    def _():
        d = dh_ref.shape[1]
        dh = dh_ref[...] + finish(dv_ref[...], wv_ref[...], ov_ref[...], v_keep_ref.at[:, :d], v_give_ref.at[:, :d])
        dh_ref[...] = dh
        rows = x_ref[...].astype(f32)
        dgain = jnp.sum(dh * rows * rms_scale(rows), axis=0, keepdims=True) + mgain_ref[...]
        column = jnp.transpose(jnp.broadcast_to(dgain, (8, d)))[:, :1]
        small = jnp.where(lane_of(d) == 0, column, 0.0)
        v_keep_ref[:, d:], v_give_ref[:, d:] = split_rows(upper, small, block)


def first_norm_kernel(lane, dh_ref, more_ref, x_ref, small_ref, mid_ref, dx_ref):
    rows = x_ref[...].astype(f32)
    grad = dh_ref[...] + more_ref[...].astype(f32)
    back, _ = rms_backward(rows, rms_scale(rows), gain_row(small_ref, lane), grad)
    dx_ref[...] = mid_ref[...] + back


def column(array, width, index):
    return array, (array.shape[0], width), index


def simple_call(kernel, args, outs, flops, name, deps=(), scalars=()):
    whole = pl.BlockSpec(memory_space=pltpu.VMEM)
    small = pl.BlockSpec(memory_space=pltpu.SMEM)
    specs, arrays = [], []
    for arg in args:
        if isinstance(arg, tuple):
            array, block, index = arg
            specs.append(pl.BlockSpec(block, lambda i, index=index: (0, index)))
            arrays.append(array)
        else:
            specs.append(whole)
            arrays.append(arg)
    return pl.pallas_call(
        ordered(kernel, len(scalars) + len(args), len(deps)),
        grid=(1,),
        in_specs=[small] * len(scalars) + specs + waits(deps),
        out_shape=[jax.ShapeDtypeStruct(s, d) for s, d in outs],
        compiler_params=pltpu.CompilerParams(vmem_limit_bytes=VMEM),
        cost_estimate=cost(name),
        name=name,
    )(*scalars, *arrays, *deps)


def expert_kernel(n_groups, *refs):
    x_ref, g_ref = refs[:2]
    w_refs = refs[2 : 2 + n_groups]
    out_ref, dx_ref, act_ref, dg_ref, du_ref, gx_ref, gg_ref, store, out_sum, back_sum, done = refs[-11:]
    step = pl.program_id(0)
    n, d = out_sum.shape
    copies = [pltpu.make_async_copy(w, store.at[k], done.at[k]) for k, w in enumerate(w_refs)]

    @pl.when(step == 0)
    def _():
        for copy in copies:
            copy.start()
        out_sum[...] = jnp.zeros((n, d), f32)
        back_sum[...] = jnp.zeros((n, d), f32)

    for k, copy in enumerate(copies):
        pl.when(step == k)(copy.wait)
    grads = g_ref[...].reshape(n, d)
    rows = x_ref[:, :d]
    wg, wu, wd = [
        jnp.concatenate([store[step, p, m] for p in range(store.shape[1])], axis=1) for m in range(3)
    ]
    gate_pre = mul_nn(rows, wg)
    up_pre = mul_nn(rows, wu)
    grad_act = mul_nn(grads, wd)
    sig = 1.0 / (1.0 + jnp.exp(-gate_pre))
    silu = gate_pre * sig
    act = (silu * up_pre).astype(bf16)
    act_ref[...] = act
    grad_gate = (grad_act * up_pre * sig * (1.0 + gate_pre * (1.0 - sig))).astype(bf16)
    grad_up = (grad_act * silu).astype(bf16)
    dg_ref[...] = grad_gate
    du_ref[...] = grad_up
    out_sum[...] += mul_nt(act, wd)
    back_sum[...] += mul_nt(grad_gate, wg) + mul_nt(grad_up, wu)

    @pl.when(step == n_groups - 1)
    def _():
        gates = x_ref[:, d : d + 1].astype(f32) + x_ref[:, d + 1 : d + 2].astype(f32)
        gx_ref[...] = jnp.transpose((rows.astype(f32) * gates).astype(bf16))
        gg_ref[...] = jnp.transpose((grads.astype(f32) * gates).astype(bf16))
        low = out_sum[...].astype(bf16)
        out_ref[...] = low.reshape(out_ref.shape)
        dx_ref[:, :d] = back_sum[...].astype(bf16)
        dots = jnp.sum(grads.astype(f32) * low.astype(f32), axis=1, keepdims=True)
        high, rest = halves(dots)
        lane = lax.broadcasted_iota(jnp.int32, (n, PAIR), 1)
        pair = jnp.where(lane == 0, high.astype(f32), jnp.where(lane == 1, rest.astype(f32), 0.0))
        dx_ref[:, d:] = pair.astype(bf16)


def expert_call(part, x, g, groups, outs, name):
    n, wide = x.shape
    d = g.shape[-1]
    group = groups[0].shape
    cols = group[0] * group[3]
    ff = cols * len(groups)
    block = pl.BlockSpec((g.shape[0], 1) + g.shape[2:], lambda i: (0, part, 0, 0))
    passed = [] if outs is None else [outs]

    def whole(*shape):
        return pl.BlockSpec(shape, lambda i: (0,) * len(shape))

    def column(rows):
        return pl.BlockSpec((rows, cols), lambda i: (0, i))

    shapes = [(n, wide), (n, ff), (n, ff), (n, ff), (d, n), (d, n)]
    return pl.pallas_call(
        functools.partial(expert_kernel, len(groups)),
        grid=(len(groups),),
        in_specs=[whole(n, wide), block] + waits(groups) + waits(passed),
        out_specs=[block, whole(n, wide)] + [column(n)] * 3 + [whole(d, n)] * 2,
        out_shape=[jax.ShapeDtypeStruct(g.shape, bf16)] + [jax.ShapeDtypeStruct(shape, bf16) for shape in shapes],
        input_output_aliases={2 + len(groups): 0} if passed else {},
        scratch_shapes=[
            pltpu.VMEM((len(groups),) + group, bf16), pltpu.VMEM((n, d), f32), pltpu.VMEM((n, d), f32),
            pltpu.SemaphoreType.DMA((len(groups),)),
        ],
        compiler_params=pltpu.CompilerParams(vmem_limit_bytes=VMEM),
        cost_estimate=cost("expert"),
        name=name,
    )(x, g, *groups, *passed)


def expert_weights_kernel(plan, n_through, *refs):
    xs, ggs, acts, dgs, dus = [refs[2 * i : 2 * i + 2] for i in range(5)]
    out_refs = refs[10 + n_through :]
    step = pl.program_id(0)
    pieces, _, d, width = out_refs[0].shape
    for m, (left, right) in enumerate([(xs, dgs), (xs, dus), (ggs, acts)]):
        grad = mul_nn(
            jnp.concatenate([half[...] for half in left], axis=1), jnp.concatenate([half[...] for half in right], axis=0)
        )

        def write(ref):
            for p in range(pieces):
                ref[p, m] = grad[:, p * width : (p + 1) * width].astype(ref.dtype)

        first = 0
        for count, ref in zip(plan, out_refs):
            pl.when((step >= first) & (step < first + count))(functools.partial(write, ref))
            first += count


def expert_weights(flows, order, plan, pieces, width, kinds, name, through=None, deps=()):
    d, n = flows[0][0].shape
    cols = pieces * width
    rows = pl.BlockSpec((d, n), lambda i: (0, 0))
    flip = order[0] != 0

    def group(i):
        return len(order) - 1 - i if flip else i

    part = pl.BlockSpec((n, cols), lambda i: (0, group(i)))
    passed = [] if through is None else [through]
    blocks, first = [], 0
    for count in plan:
        blocks.append(
            pl.BlockSpec(
                (pieces, 3, d, width),
                lambda i, first=first, count=count: (jnp.clip(i - first, 0, count - 1), 0, 0, 0),
            )
        )
        first += count
    return pl.pallas_call(
        ordered(functools.partial(expert_weights_kernel, plan, len(passed)), 10 + len(passed), len(deps)),
        grid=(len(order),),
        in_specs=[rows] * 4 + [part] * 6 + waits(passed) + waits(deps),
        out_specs=blocks + waits(passed),
        out_shape=[
            jax.ShapeDtypeStruct((pieces * count, 3, d, width), kind) for count, kind in zip(plan, kinds)
        ]
        + [jax.ShapeDtypeStruct(p.shape, p.dtype) for p in passed],
        input_output_aliases={10: len(plan)} if passed else {},
        compiler_params=pltpu.CompilerParams(vmem_limit_bytes=VMEM),
        cost_estimate=cost(name),
        name=name,
    )(*[half for flow in flows for half in flow], *passed, *deps)


def weights_sent_kernel(near_ref, came_ref, *out_refs):
    first = 0
    for ref in out_refs:
        there = slice(first, first + ref.shape[2])
        ref[...] = near_ref[:, :, there] + came_ref[:, :, there]
        first += ref.shape[2]


def weights_sent(near, came):
    n, m, d, f = near.shape
    whole = pl.BlockSpec((2, m, d, f), lambda i: (i, 0, 0, 0))
    cuts = (d // 3, d - d // 3)
    return pl.pallas_call(
        weights_sent_kernel,
        grid=(n // 2,),
        in_specs=[whole] * 2,
        out_specs=[pl.BlockSpec((2, m, rows, f), lambda i: (i, 0, 0, 0)) for rows in cuts],
        out_shape=[jax.ShapeDtypeStruct((n, m, rows, f), bf16) for rows in cuts],
        compiler_params=pltpu.CompilerParams(vmem_limit_bytes=VMEM),
        cost_estimate=cost("weights_sent"),
        name="weights_sent",
    )(near, came)


def weights_sum_kernel(kept_ref, far_ref, near_ref, out_ref):
    out_ref[...] = (kept_ref[...].astype(f32) + far_ref[...].astype(f32) + near_ref[...].astype(f32)).astype(bf16)


def weights_sum(kept, far, near, first, deps):
    n, m, d, f = near.shape
    unit = kept.shape[2] // 3
    own = pl.BlockSpec((2, m, unit, f), lambda i, j: (i, 0, j, 0))
    some = pl.BlockSpec((2, m, unit, f), lambda i, j: (i, 0, first // unit + j, 0))
    return pl.pallas_call(
        ordered(weights_sum_kernel, 3, len(deps)),
        grid=(n // 2, d // unit),
        in_specs=[some, some, own] + waits(deps),
        out_specs=own,
        out_shape=jax.ShapeDtypeStruct(near.shape, bf16),
        compiler_params=pltpu.CompilerParams(vmem_limit_bytes=VMEM),
        cost_estimate=cost("weights_sum"),
        name="weights_sum",
    )(kept, far, near, *deps)


def lane_of(rows):
    return lax.broadcasted_iota(jnp.int32, (rows, PAIR), 1)


def col(rows, i):
    return rows[:, i : i + 1]


def halves(rows):
    high = rows.astype(bf16)
    return high, (rows - high.astype(f32)).astype(bf16)


VEC, COEF, GATE, CONST = 0, 2, 3, 5


def mid_kernel(
    n_all, att_ref, small_ref, wo_ref, x_ref, prev_ref, routes_ref, place_ref,
    mid_ref, hidden_ref, scal_ref, *send_refs,
):
    n_ffn = n_all - 4
    d = x_ref.shape[1]
    mid = x_ref[...].astype(f32) + mul_nn(att_ref[...], wo_ref[...])
    mid_ref[...] = mid
    hidden = (mid * rms_scale(mid) * gain_row(small_ref, n_all + 7)).astype(bf16)
    hidden_ref[...] = hidden
    rows, d = hidden.shape
    lane = lane_of(rows)
    raw = mul_nn(hidden, small_ref[...])
    logits = jnp.where(lane < n_all, raw + prev_ref[...], NEG)
    expo = jnp.exp(logits - jnp.max(logits, axis=1, keepdims=True))
    probs = jnp.where(lane < n_all, expo / jnp.sum(expo, axis=1, keepdims=True), 0.0)
    ids = [col(routes_ref[...], j) for j in range(2)]
    gates = [jnp.sum(jnp.where(lane == r, probs, 0.0), axis=1, keepdims=True) for r in ids]
    scal = probs
    coef = sum(jnp.where(r == n_ffn + 1, g, 0.0) for r, g in zip(ids, gates))
    base = n_all + 4
    for c in range(2):
        gap = col(raw, n_all + 2 * c + 1) - col(raw, n_all + 2 * c)
        first, second = 1.0 / (1.0 + jnp.exp(gap)), 1.0 / (1.0 + jnp.exp(-gap))
        const = sum(jnp.where(r == n_ffn + 2 + c, g, 0.0) for r, g in zip(ids, gates))
        coef += first * const
        scal = jnp.where(lane == n_all + 2 * c, first, scal)
        scal = jnp.where(lane == n_all + 2 * c + 1, second, scal)
        scal = jnp.where(lane == base + VEC + c, second * const, scal)
        scal = jnp.where(lane == base + CONST + c, const, scal)
        scal = jnp.where(lane == base + GATE + c, gates[c], scal)
    scal_ref[...] = jnp.where(lane == base + COEF, coef, scal)
    n_half = send_refs[0].shape[0]
    slots = n_half * len(send_refs)
    row = lax.broadcasted_iota(jnp.int32, (slots, rows), 0)
    hits = [(row == place_ref[j : j + 1, :]) for j in range(2)]
    both = jnp.where(hits[0] | hits[1], 1.0, 0.0).astype(bf16)
    rows_out = mul_nn(both, hidden).astype(bf16)
    extra = jnp.zeros((slots, PAIR), f32)
    for j in range(2):
        high, low = halves(gates[j])
        pair = jnp.where(lane == 0, high.astype(f32), jnp.where(lane == 1, low.astype(f32), 0.0))
        extra += mul_nn(jnp.where(hits[j], 1.0, 0.0).astype(bf16), pair.astype(bf16))
    for i, ref in enumerate(send_refs):
        ref[:, :d] = rows_out[i * n_half : (i + 1) * n_half]
        ref[:, d:] = extra[i * n_half : (i + 1) * n_half].astype(bf16)


def spread_kernel(cot_ref, valid_ref, place_ref, send_ref):
    grads = (cot_ref[...] * valid_ref[...]).astype(bf16)
    row = lax.broadcasted_iota(jnp.int32, (send_ref.shape[0], grads.shape[0]), 0)
    hit = (row == place_ref[0:1, :]) | (row == place_ref[1:2, :])
    send_ref[...] = mul_nn(jnp.where(hit, 1.0, 0.0).astype(bf16), grads).astype(bf16)


def picked_rows(place_ref, j, table):
    rows, slots = place_ref.shape[0], table.shape[0]
    slot = lax.broadcasted_iota(jnp.int32, (rows, slots), 1)
    pick = jnp.where(slot == col(place_ref[...], j), 1.0, 0.0).astype(bf16)
    return mul_nn(pick, table)


def gates_back_kernel(
    n_all, back_ref, more_ref, place_ref, routes_ref, scal_ref, hidden_ref, mid_ref, cot_ref, valid_ref, small_ref, wo_ref,
    gmid_ref, gatt_ref, mix_ref, dgain_ref,
):
    n_ffn = n_all - 4
    base = n_all + 4
    scal = scal_ref[...]
    grads = cot_ref[...] * valid_ref[...]
    rows, d = grads.shape
    lane = lane_of(rows)
    hidden = hidden_ref[...].astype(f32)
    small = small_ref[...]
    g_hidden = jnp.sum(grads * hidden, axis=1, keepdims=True)
    high, low = halves(grads)
    g_small = mul_nn(high, small) + mul_nn(low, small)
    table = jnp.concatenate([back_ref[...], more_ref[...]], axis=0)
    grad_hidden = col(scal, base + COEF) * grads
    grad_probs = jnp.zeros((rows, PAIR), f32)
    for j in range(2):
        r = col(routes_ref[...], j)
        came = picked_rows(place_ref, j, table)
        grad_hidden += col(scal, base + GATE + j) * came[:, :d]
        dots = came[:, d : d + 1] + came[:, d + 1 : d + 2]
        dots += jnp.where(r == n_ffn + 1, g_hidden, 0.0)
        for c in range(2):
            whole = col(scal, n_all + 2 * c) * g_hidden + col(scal, n_all + 2 * c + 1) * col(g_small, base + c)
            dots += jnp.where(r == n_ffn + 2 + c, whole, 0.0)
        grad_probs += jnp.where(lane == r, dots, 0.0)
    probs = jnp.where(lane < n_all, scal, 0.0)
    mix = probs * (grad_probs - jnp.sum(probs * grad_probs, axis=1, keepdims=True))
    for c in range(2):
        first, second = col(scal, n_all + 2 * c), col(scal, n_all + 2 * c + 1)
        const = col(scal, base + CONST + c)
        a, b = const * g_hidden, const * col(g_small, base + c)
        inner = first * a + second * b
        mix = jnp.where(lane == n_all + 2 * c, first * (a - inner), mix)
        mix = jnp.where(lane == n_all + 2 * c + 1, second * (b - inner), mix)
    mix_ref[...] = mix
    high, low = halves(mix)
    grad_hidden += mul_nt(high, small) + mul_nt(low, small)
    mid = mid_ref[...]
    back, dgain = rms_backward(mid, rms_scale(mid), gain_row(small_ref, n_all + 7), grad_hidden)
    dgain_ref[...] = dgain
    grad_mid = grads + back
    gmid_ref[...] = grad_mid
    gatt_ref[...] = mul_nt(grad_mid.astype(bf16), wo_ref[...]).astype(bf16)


def out_grads_kernel(
    n_all, block, core_ref, att_ref, gmid_ref, hidden_ref, mix_ref, scal_ref, cot_ref, valid_ref, dgain_ref, keep_ref, give_ref,
):
    d = att_ref.shape[1]
    base = n_all + 4
    upper = core_ref[0] == 1
    dw_out = mul_tn(att_ref[...], gmid_ref[...].astype(bf16))
    keep_ref[:, :d], give_ref[:, :d] = split_rows(upper, dw_out, block)
    hidden = hidden_ref[...]
    high, low = halves(mix_ref[...])
    grads = mul_tn(hidden, high) + mul_tn(hidden, low)
    scal = scal_ref[...]
    lane = lane_of(scal.shape[0])
    vec = jnp.where((lane >= base + VEC) & (lane < base + VEC + 2), scal, 0.0)
    vec_high, vec_low = halves(vec)
    g_high, g_low = halves(cot_ref[...] * valid_ref[...])
    grads += mul_tn(g_high, vec_high) + mul_tn(g_high, vec_low) + mul_tn(g_low, vec_high)
    column = jnp.transpose(jnp.broadcast_to(dgain_ref[...], (8, d)))[:, :1]
    tail = jnp.where(lane_of(d) == base + 2, column, grads)
    keep_ref[:, d:], give_ref[:, d:] = split_rows(upper, tail, block)


def output_kernel(n_all, back_ref, place_ref, scal_ref, hidden_ref, mid_ref, valid_ref, small_ref, out_ref):
    base = n_all + 4
    scal = scal_ref[...]
    lane = lane_of(scal.shape[0])
    vec = jnp.where((lane >= base + VEC) & (lane < base + VEC + 2), scal, 0.0)
    high, low = halves(vec)
    small = small_ref[...]
    total = mid_ref[...] + mul_nt(high, small) + mul_nt(low, small)
    total += col(scal, base + COEF) * hidden_ref[...].astype(f32)
    table = back_ref[...]
    for j in range(2):
        total += col(scal, base + GATE + j) * picked_rows(place_ref, j, table)
    out_ref[...] = total * valid_ref[...]


def local(
    residual_in,
    lengths,
    routes,
    prev_logits,
    cotangent,
    w_qkv,
    w_out,
    attn_gain,
    ffn_gain,
    router,
    const_gate,
    const_vec,
    w_gate,
    w_up,
    w_down,
):
    tok_rows = residual_in.shape[1]
    feat = residual_in.shape[2]
    head_size = feat // HEADS
    score_scale = head_size ** (-0.5)
    n_dp = lax.axis_size("dp")
    n_ctx = lax.axis_size("ctx")
    n_exp = lax.axis_size("exp")
    own_exp = w_gate.shape[0]
    reps = n_dp // own_exp
    n_all = router.shape[1]
    n_ffn = n_all - 4
    cap_rows = tok_rows // 4
    sub_rows = cap_rows // reps
    n_slots = n_ffn * cap_rows
    ctx_rank = lax.axis_index("ctx")
    positions = ctx_rank * tok_rows + jnp.arange(tok_rows, dtype=jnp.int32)
    length = lengths[0]
    valid_rows = (positions < length).astype(f32)[:, None]

    def gather_ctx(rows):
        if n_ctx == 2:
            return swap(rows, "ctx", 1)
        for bit in reversed(bits_of("ctx")):
            other = swap(rows, "ctx", bit)
            upper = (ctx_rank & bit) != 0
            rows = jnp.concatenate([jnp.where(upper, other, rows), jnp.where(upper, rows, other)], axis=0)
        return rows

    def scatter_ctx(rows):
        if n_ctx == 2:
            return swap(rows, "ctx", 1)
        for bit in bits_of("ctx"):
            low, high = jnp.split(rows, 2, axis=0)
            upper = (ctx_rank & bit) != 0
            sent = jnp.where(upper, low, high).astype(bf16)
            rows = jnp.where(upper, high, low).astype(f32) + swap(sent, "ctx", bit).astype(f32)
        return rows

    route_ids = routes[0]
    choose = (route_ids[:, :, None] == jnp.arange(n_all, dtype=jnp.int32)[None, None, :]).astype(f32)
    both = jnp.sum(choose, axis=1)
    before = jnp.arange(tok_rows)
    before = (before[None, :] < before[:, None]).astype(bf16)
    counts = dot32(before, both.astype(bf16))
    slot_ids = jnp.sum(choose * counts[:, None, :], axis=-1).astype(jnp.int32)
    is_ffn = route_ids < n_ffn
    place = (
        ((route_ids % own_exp) * reps + slot_ids // sub_rows) * n_exp + route_ids // own_exp
    ) * sub_rows + slot_ids % sub_rows
    half_rows = sub_rows // 2
    place_half = (
        (place // half_rows % 2) * (n_slots // 2) + place // sub_rows * half_rows + place % half_rows
    )
    place = jnp.where(is_ffn, place, -1)
    place_half = jnp.where(is_ffn, place_half, -1)
    row_ids = jnp.arange(n_slots, dtype=jnp.int32)
    place_rows = jnp.transpose(place)

    def to_experts(rows):
        return lax.all_to_all(
            rows.reshape(n_dp * n_exp, rows.shape[0] // (n_dp * n_exp), -1),
            ("dp", "exp"),
            split_axis=0,
            concat_axis=0,
            tiled=True,
        ).reshape(rows.shape[0], -1)

    width = 2 * feat
    far, mid_a, near = plan_steps(("ctx", "exp"))
    _, mid_b, _ = plan_steps(("exp", "ctx"))
    lane = jnp.arange(PAIR, dtype=jnp.int32)
    half = head_size // 2
    inv_freq = 10000.0 ** (-2.0 * (lane % half).astype(f32) / head_size)
    sign = jnp.where(lane % head_size < half, -1.0, 1.0)

    def turns(where):
        angles = where.astype(f32)[:, None] * inv_freq[None, :]
        return jnp.cos(angles), jnp.sin(angles) * sign[None, :]

    cosine, sine = turns(positions)
    other_start = (1 - ctx_rank) * tok_rows if n_ctx == 2 else 0
    n_other = tok_rows if n_ctx == 2 else tok_rows * n_ctx
    other_cos, other_sin = turns(other_start + jnp.arange(n_other, dtype=jnp.int32))
    other_in = gather_ctx(residual_in[0])
    (rows,) = simple_call(
        rows_kernel, (w_qkv, w_out, router.T, const_gate.T, const_vec.T, attn_gain[None], ffn_gain[None]),
        [((w_out.shape[0], 4 * feat + PAIR), bf16)], 0, "rows",
    )
    packed = pack_expert(w_gate, w_up, w_down, (rows,))
    tables = (cosine, sine, other_cos, other_sin)
    if len(far) == 2:
        whole, placed = gather_far(rows, far, (packed,) + tables)
    else:
        whole, placed = gather_steps(rows, [], far)
    group = trade_far(packed)
    part_a, part_b = whole[..., :width], whole[..., width:]
    placed_a, placed_b = placed, placed
    for i, (step_a, step_b) in enumerate(zip(mid_a, mid_b)):
        meanwhile = (other_in,) if i == 0 else ()
        if i + 1 == len(mid_a):
            (grad_sent,) = simple_call(
                spread_kernel, (cotangent[0], valid_rows, place_rows), [((n_slots, feat), bf16)], 0, "spread", (part_b,)
            )
            meanwhile = (grad_sent,)
        part_a, placed_a = gather_step(part_a, placed_a, *step_a)
        part_b, placed_b = gather_step(part_b, placed_b, *step_b, meanwhile)
    first_part, _ = gather_steps(part_a, placed_a, near)
    second_part, _ = gather_steps(part_b, placed_b, near)
    first_part = first_part.reshape(feat, width)
    second_part = second_part.reshape(feat, 2 * feat + PAIR)

    small_at = 2 * feat // PAIR
    w_v, w_o, small = column(second_part, feat, 0), column(second_part, feat, 1), column(second_part, PAIR, small_at)
    rows_low = ((tok_rows, feat), bf16)
    rows_full = ((tok_rows, feat), f32)
    square = 2 * tok_rows * feat * feat
    hidden_one, queries, own_keys, own_values = simple_call(
        functools.partial(project_kernel, score_scale, n_all + 6),
        (residual_in[0], first_part, w_v, small, cosine, sine), [rows_low] * 4, 3 * square, "project",
    )
    tok_spec = pl.BlockSpec((tok_rows, feat), lambda i: (i, 0))
    turn_spec = pl.BlockSpec((tok_rows, PAIR), lambda i: (i, 0))

    def fixed(rows, cols, index=0):
        return pl.BlockSpec((rows, cols), lambda i: (0, index))

    other_hidden, other_keys, other_values = pl.pallas_call(
        functools.partial(other_project_kernel, n_all + 6),
        grid=(n_other // tok_rows,),
        in_specs=[tok_spec, fixed(feat, feat, 1), fixed(feat, PAIR, small_at), fixed(feat, feat), turn_spec, turn_spec],
        out_specs=[tok_spec] * 3,
        out_shape=[jax.ShapeDtypeStruct((n_other, feat), bf16)] * 3,
        compiler_params=pltpu.CompilerParams(vmem_limit_bytes=VMEM),
        cost_estimate=cost("project_other"),
        name="project_other",
    )(other_in, first_part, second_part, second_part, other_cos, other_sin)
    grad_rows_in = to_experts(hold(grad_sent, group, hidden_one, other_keys))
    info = jnp.stack([ctx_rank * tok_rows, length, ctx_rank]).astype(jnp.int32)
    prev = jnp.pad(prev_logits[0], ((0, 0), (0, PAIR - n_all)))
    attended, attended_low, log_total = attend(
        info, queries, own_keys, own_values, other_keys, other_values, (group, prev, place, place_half)
    )

    mid_rows, hidden, scalars, *sent_rows = simple_call(
        functools.partial(mid_kernel, n_all),
        (attended_low, small, w_o, residual_in[0], prev, route_ids, jnp.transpose(place_half)),
        [rows_full, rows_low, ((tok_rows, PAIR), f32)] + [((n_slots // 2, feat + PAIR), bf16)] * 2, 0, "mid",
    )
    rows_in = [to_experts(hold(sent_rows[0], grad_rows_in)), to_experts(sent_rows[1])]

    steps_near = near_steps(own_exp)
    groups = gather_expert_near([group], steps_near)
    piece_width = group.shape[3]
    if piece_width < PAIR:
        merge = PAIR // piece_width
        whole = jnp.concatenate(groups).reshape(-1, merge, 3, feat, piece_width)
        groups = [jnp.moveaxis(whole, 1, 3).reshape(-1, 3, feat, PAIR)]
    grads_in = grad_rows_in.reshape(n_dp * n_exp, 2, half_rows, feat)
    expert_out = None
    flows, back_grads = [], []
    for part in range(2):
        expert_out, grad_in, *flow = expert_call(part, rows_in[part], grads_in, groups, expert_out, f"expert_{part}")
        back_grads.append(to_experts(grad_in))
        flows.append(flow)
    expert_out = expert_out.reshape(n_slots, feat)
    n_groups = 2 ** len(steps_near)
    act, grad_gate_pre, grad_up_pre, gated_rows, grad_expert_out = zip(*flows)
    flows = (gated_rows, grad_expert_out, act, grad_gate_pre, grad_up_pre)
    simple = piece_width >= PAIR and len(steps_near) == 2
    if simple:
        far_near, far_kept, near_own, kept, expert_out = expert_weights(
            flows, (3, 2, 1, 0), (1, 1, 1, 1), own_exp, piece_width, (bf16,) * 4, "weights_all", expert_out,
            (back_grads[0],),
        )
        far_near = swap(hold(far_near, back_grads[1]), *steps_near[1])
        far_kept = swap(hold(far_kept, back_grads[1]), *steps_near[1])
        near_sent = weights_sent(near_own, far_near)
        near_came = [swap(part, *steps_near[0]) for part in near_sent]
    else:
        step = max(piece_width, PAIR)
        n_steps = act[0].shape[1] // step
        (whole,) = expert_weights(flows, tuple(range(n_steps)), (n_steps,), 1, step, (f32,), "weights_all")
        if piece_width < PAIR:
            whole = jnp.moveaxis(whole.reshape(-1, 3, feat, merge, piece_width), 3, 1)
        whole = whole.reshape(n_groups, own_exp, 3, feat, piece_width)
        expert_sum = scatter_expert_near([whole[i] for i in range(n_groups)], steps_near)
    back_rows = to_experts(expert_out)
    small_shape = ((tok_rows, PAIR), f32)
    grad_mid, grad_attended, grad_mix, grad_gain_two = simple_call(
        functools.partial(gates_back_kernel, n_all),
        (
            *back_grads, place_half, route_ids, scalars, hidden, mid_rows, cotangent[0], valid_rows, small, w_o,
        ),
        [rows_full, rows_low, small_shape, ((1, feat), f32)], 0, "gates_back", tuple(near_sent) if simple else (),
    )
    grad_queries, other_dk, other_dv, delta = grads_other(
        info, queries, other_keys, other_values, grad_attended, attended, log_total, ()
    )
    core = (lax.axis_index("dp") & 1).astype(jnp.int32).reshape(1)
    core_block = feat // (n_dp * n_ctx * n_exp) * row_weight("dp")
    other_gk, other_dh, more_gain = pl.pallas_call(
        other_back_kernel,
        grid=(n_other // tok_rows,),
        in_specs=[tok_spec, tok_spec, fixed(feat, feat, 1), fixed(feat, feat), turn_spec, turn_spec, tok_spec],
        out_specs=[tok_spec, tok_spec, fixed(1, feat)],
        out_shape=[
            jax.ShapeDtypeStruct((n_other, feat), bf16), jax.ShapeDtypeStruct((n_other, feat), bf16),
            jax.ShapeDtypeStruct((1, feat), f32),
        ],
        compiler_params=pltpu.CompilerParams(vmem_limit_bytes=VMEM),
        cost_estimate=cost("back_other"),
        name="back_other",
    )(other_dk, other_dv, first_part, second_part, other_cos, other_sin, other_in)
    more_dh = scatter_ctx(other_dh)
    if simple:
        sum_first = weights_sum(kept, far_kept, near_came[0], 0, (other_dh,))
    else:
        sum_first, sum_rest = jnp.split(expert_sum.astype(bf16), [feat // 3], axis=2)
    back_first = trade_far(sum_first)
    grad_queries, own_dk, own_dv = grads_own(
        info, queries, own_keys, own_values, grad_attended, log_total, delta, grad_queries, (back_rows, sum_first)
    )
    half_rows = feat // 2
    out_keep, out_give = simple_call(
        functools.partial(out_grads_kernel, n_all, core_block),
        (attended_low, grad_mid, hidden, grad_mix, scalars, cotangent[0], valid_rows, grad_gain_two),
        [((half_rows, feat + PAIR), f32), ((half_rows, feat + PAIR), bf16)], 0, "out_grads", (own_dk,), (core,),
    )

    if simple:
        sum_rest = weights_sum(kept, far_kept, near_came[1], feat // 3, (out_keep,))
    back_rest = trade_far(sum_rest)
    own_args = (
        core, grad_queries, own_dk, own_dv, hidden_one, first_part, second_part, cosine, sine, residual_in[0], other_hidden,
        other_gk, other_dv, more_gain,
    )
    own_deps = (sum_rest, back_first)
    step_spec = pl.BlockSpec((half_rows, feat), lambda i: (0, jnp.minimum(i, 1)))
    token, turn, other = fixed(tok_rows, feat), fixed(tok_rows, PAIR), fixed(n_other, feat)
    qk_keep, qk_give, v_keep, v_give, grad_hidden_one = pl.pallas_call(
        ordered(functools.partial(own_back_kernel, score_scale, core_block), len(own_args), len(own_deps)),
        grid=(3,),
        in_specs=[pl.BlockSpec(memory_space=pltpu.SMEM)] + [token] * 4
        + [pl.BlockSpec((feat, feat), lambda i: (0, jnp.minimum(i, 1))), fixed(feat, feat), turn, turn, token]
        + [other] * 3 + [fixed(1, feat)] + waits(own_deps),
        out_specs=[step_spec] * 2 + [fixed(half_rows, feat + PAIR)] * 2 + [token],
        out_shape=[
            jax.ShapeDtypeStruct((half_rows, 2 * feat), f32), jax.ShapeDtypeStruct((half_rows, 2 * feat), bf16),
            jax.ShapeDtypeStruct((half_rows, feat + PAIR), f32), jax.ShapeDtypeStruct((half_rows, feat + PAIR), bf16),
            jax.ShapeDtypeStruct((tok_rows, feat), f32),
        ],
        compiler_params=pltpu.CompilerParams(vmem_limit_bytes=VMEM),
        cost_estimate=cost("back_own"),
        name="back_own",
    )(*own_args, *own_deps)
    def last_rows(sent):
        (output,) = simple_call(
            functools.partial(output_kernel, n_all),
            (back_rows, place, scalars, hidden, mid_rows, valid_rows, small), [rows_full], 0, "output", tuple(sent),
        )
        (grad_x,) = simple_call(
            functools.partial(first_norm_kernel, n_all + 6),
            (grad_hidden_one, more_dh, residual_in[0], small, grad_mid), [rows_full], 0, "first_norm", (output,),
        )
        results.extend([output, grad_x, *unpack_expert(back_first, back_rest, (output, grad_x))])
        return results

    results = []
    dw_qkv, dw_out, *narrow = scatter_parts(
        [
            [(qk_keep, qk_give, 2 * feat, 0)],
            [(v_keep, v_give, feat + PAIR, 0), (out_keep, out_give, feat + PAIR, 0)],
        ],
        [mid_a, mid_b], far, near, w_out.shape[0], (), last_rows, (3 * feat, feat), (n_all, 4, 2, 1, 1),
    )
    output, grad_x, *expert_grads = results
    return (
        output[None],
        grad_x[None],
        dw_qkv,
        dw_out,
        narrow[4][0],
        narrow[3][0],
        narrow[0].T,
        narrow[1].T,
        narrow[2].T,
        expert_grads[0],
        expert_grads[1],
        expert_grads[2],
    )


def solution(mesh):
    in_specs = (
        P(("dp", "exp"), "ctx", None),
        P(("dp", "exp")),
        P(("dp", "exp"), "ctx", None),
        P(("dp", "exp"), "ctx", None),
        P(("dp", "exp"), "ctx", None),
        P(("dp", "ctx", "exp"), None),
        P(("dp", "ctx", "exp"), None),
        P(("dp", "ctx", "exp")),
        P(("dp", "ctx", "exp")),
        P(("dp", "ctx", "exp"), None),
        P(("dp", "ctx", "exp"), None),
        P(("dp", "ctx", "exp"), None),
        P("exp", None, ("dp", "ctx")),
        P("exp", None, ("dp", "ctx")),
        P("exp", ("dp", "ctx"), None),
    )
    out_specs = (
        P(("dp", "exp"), "ctx", None),
        P(("dp", "exp"), "ctx", None),
        P(("dp", "ctx", "exp"), None),
        P(("dp", "ctx", "exp"), None),
        P(("dp", "ctx", "exp")),
        P(("dp", "ctx", "exp")),
        P(("dp", "ctx", "exp"), None),
        P(("dp", "ctx", "exp"), None),
        P(("dp", "ctx", "exp"), None),
        P("exp", None, ("dp", "ctx")),
        P("exp", None, ("dp", "ctx")),
        P("exp", ("dp", "ctx"), None),
    )
    return jax.shard_map(local, mesh=mesh, in_specs=in_specs, out_specs=out_specs, check_vma=False)
```

```python
import functools

import jax
import jax.numpy as jnp
from jax import lax
from jax.experimental import pallas as pl
from jax.experimental.pallas import tpu as pltpu
from jax.sharding import PartitionSpec as P

HEADS = 12

norm_eps = 1e-06
top_precision = lax.Precision.HIGHEST
f32 = jnp.float32
bf16 = jnp.bfloat16


CHUNK = 256
BLOCK = 512
OCHUNK = 512
QCHUNK = 128
PAIR = 128
NEG = -1e30
SCALE = 48
VMEM = 62 << 20
MICROS = {
    "project": 6, "project_other": 5, "spread": 4, "attend": 17, "mid": 9, "expert": 30, "weights_sent": 0,
    "weights_near": 0, "weights_kept": 0, "weights_sum": 0, "gates_back": 0, "grads_other": 0, "back_other": 0, "grads_own": 0,
    "back_own": 0, "out_grads": 0, "output": 6, "first_norm": 4, "weights_all": 26, "pack": 3, "unpack": 4, "combine": 1, "rows": 2, "sums": 1,
}


def cost(name):
    return pl.CostEstimate(flops=MICROS[name] * 1000000000 // SCALE, bytes_accessed=1, transcendentals=0)


def mul_nt(a, b):
    return lax.dot_general(a, b, (((1,), (1,)), ((), ())), preferred_element_type=f32)


def mul_nn(a, b):
    return lax.dot_general(a, b, (((1,), (0,)), ((), ())), preferred_element_type=f32)


def mul_tn(a, b):
    return lax.dot_general(a, b, (((0,), (0,)), ((), ())), preferred_element_type=f32)


def head_part(rows, head):
    lane = lax.broadcasted_iota(jnp.int32, rows.shape, 1)
    return jnp.where((lane >= PAIR // 2) == (head == 1), rows, jnp.zeros_like(rows))


def key_allowed(shape, key_start, length, query_start=None):
    key = key_start + lax.broadcasted_iota(jnp.int32, shape, 0)
    allowed = key < length
    if query_start is not None:
        allowed &= key <= query_start + lax.broadcasted_iota(jnp.int32, shape, 1)
    return allowed


def both_heads(rows, first=0):
    return jnp.concatenate([head_part(rows[first:], head) for head in range(2)], axis=0)


def beside(row_pair):
    return jnp.concatenate([row_pair[0:1], row_pair[1:2]], axis=1)


def split_heads(wide):
    half, t = PAIR // 2, wide.shape[1] // 2
    return jnp.concatenate([wide[:half, :t], wide[half:, t:]], axis=0)


def attend_kernel(info, q_ref, k_ref, v_ref, ok_ref, ov_ref, out_ref, low_ref, log_ref):
    base, length, blocks = info[0], info[1], info[2]
    queries = q_ref[...]
    rows = queries.shape[0]
    half = PAIR // 2
    starts = list(range(0, rows, QCHUNK))
    twice = [both_heads(queries[first : first + QCHUNK]) for first in starts]

    def spread(row):
        n = row.shape[1] // 2
        return jnp.concatenate(
            [jnp.broadcast_to(row[:, :n], (half, n)), jnp.broadcast_to(row[:, n:], (half, n))], axis=0
        )

    scores, tops, states = [], [], []
    for first, part in zip(starts, twice):
        end = first + QCHUNK
        some = mul_nt(k_ref[:end, :], part)
        allowed = key_allowed((end, QCHUNK), base, length, base + first)
        scores.append(jnp.where(jnp.concatenate([allowed, allowed], axis=1), some, NEG))
    for some in scores:
        tops.append(jnp.max(some, axis=0, keepdims=True))
    for first, some, top in zip(starts, scores, tops):
        expo = jnp.exp(some - top)
        total = jnp.sum(expo, axis=0, keepdims=True)
        acc = split_heads(mul_tn(v_ref[: first + QCHUNK, :], expo.astype(bf16)))
        states.append((top, total, acc))

    def step(c, states):
        first = pl.multiple_of(c * BLOCK, BLOCK)
        keys = ok_ref[pl.ds(first, BLOCK), :]
        vals = ov_ref[pl.ds(first, BLOCK), :]
        allowed = key_allowed((BLOCK, 2 * QCHUNK), first, length)
        scores = [jnp.where(allowed, mul_nt(keys, part), NEG) for part in twice]
        new = []
        for some, (top, total, acc) in zip(scores, states):
            new_top = jnp.maximum(top, jnp.max(some, axis=0, keepdims=True))
            expo = jnp.exp(some - new_top)
            factor = jnp.exp(top - new_top)
            total = total * factor + jnp.sum(expo, axis=0, keepdims=True)
            acc = acc * spread(factor) + split_heads(mul_tn(vals, expo.astype(bf16)))
            new.append((new_top, total, acc))
        return tuple(new)

    states = lax.fori_loop(0, blocks, step, tuple(states))
    for first, (top, total, acc) in zip(starts, states):
        there = slice(first, first + QCHUNK)
        out = jnp.transpose(acc / spread(total))
        out_ref[there, :] = out
        low_ref[there, :] = out.astype(bf16)
        log = top + jnp.log(total)
        log_ref[0, 0:1, there] = log[:, :QCHUNK]
        log_ref[0, 1:2, there] = log[:, QCHUNK:]


def pair_grads(keys, vals, twice, grad_twice, log_row, delta_row, allowed):
    probs = jnp.where(allowed, jnp.exp(mul_nt(keys, twice) - log_row), 0.0)
    grad_probs = mul_nt(vals, grad_twice)
    grad_scores = (probs * (grad_probs - delta_row)).astype(bf16)
    return (
        mul_nn(grad_scores, twice),
        mul_nn(probs.astype(bf16), grad_twice),
        split_heads(mul_tn(keys, grad_scores)),
    )


def other_backward(
    info, q_ref, k_ref, v_ref, grad_ref, out_ref, log_ref, dq_ref, dk_ref, dv_ref, delta_ref
):
    length, chunks = info[1], info[2] * (BLOCK // OCHUNK)
    half = PAIR // 2
    queries, grads = q_ref[...], grad_ref[...]
    rows = queries.shape[0]
    product = jnp.transpose(grads.astype(f32) * out_ref[...])
    twice, grad_twice = both_heads(queries), both_heads(grads)
    for head in range(2):
        delta_ref[0, head : head + 1, :] = jnp.sum(
            product[head * half : (head + 1) * half], axis=0, keepdims=True
        )
    log_row, delta_row = beside(log_ref[0]), beside(delta_ref[0])

    def step(c, dq):
        first = pl.multiple_of(c * OCHUNK, OCHUNK)
        keys = k_ref[pl.ds(first, OCHUNK), :]
        vals = v_ref[pl.ds(first, OCHUNK), :]
        allowed = key_allowed((OCHUNK, 2 * rows), first, length)
        dk, dv, more = pair_grads(keys, vals, twice, grad_twice, log_row, delta_row, allowed)
        dk_ref[pl.ds(first, OCHUNK), :] = dk.astype(dk_ref.dtype)
        dv_ref[pl.ds(first, OCHUNK), :] = dv.astype(dv_ref.dtype)
        return dq + more

    dq_ref[...] = lax.fori_loop(0, chunks, step, jnp.zeros((PAIR, rows), f32))

    def clear(c, none):
        first = pl.multiple_of(c * OCHUNK, OCHUNK)
        dk_ref[pl.ds(first, OCHUNK), :] = jnp.zeros((OCHUNK, PAIR), dk_ref.dtype)
        dv_ref[pl.ds(first, OCHUNK), :] = jnp.zeros((OCHUNK, PAIR), dv_ref.dtype)
        return none

    lax.fori_loop(chunks, k_ref.shape[0] // OCHUNK, clear, 0)


def own_backward(
    info, q_ref, k_ref, v_ref, grad_ref, log_ref, delta_ref, before_ref, dq_ref, dk_ref, dv_ref
):
    base, length = info[0], info[1]
    queries, grads = q_ref[...], grad_ref[...]
    rows = queries.shape[0]
    dq = before_ref[...]
    for first in range(0, rows, CHUNK):
        keys = k_ref[first : first + CHUNK, :]
        vals = v_ref[first : first + CHUNK, :]
        allowed = key_allowed((CHUNK, rows - first), base + first, length, base + first)
        dk, dv, more = pair_grads(
            keys,
            vals,
            both_heads(queries, first),
            both_heads(grads, first),
            beside(log_ref[0, :, first:]),
            beside(delta_ref[0, :, first:]),
            jnp.concatenate([allowed, allowed], axis=1),
        )
        dk_ref[first : first + CHUNK, :] = dk.astype(dk_ref.dtype)
        dv_ref[first : first + CHUNK, :] = dv.astype(dv_ref.dtype)
        if first:
            more = jnp.concatenate([jnp.zeros((PAIR, first), f32), more], axis=1)
        dq = dq + more
    dq_ref[...] = jnp.transpose(dq).astype(dq_ref.dtype)


def per_pair(rows):
    return pl.BlockSpec((rows, PAIR), lambda i, info: (0, i))


def turned(cols):
    return pl.BlockSpec((PAIR, cols), lambda i, info: (i, 0))


def stats(cols):
    return pl.BlockSpec((1, 2, cols), lambda i, info: (i, 0, 0))


def ordered(kernel, n_in, n_deps):
    if not n_deps:
        return kernel

    def run(*refs):
        kernel(*refs[:n_in], *refs[n_in + n_deps :])

    return run


def waits(deps):
    return [pl.BlockSpec(memory_space=pl.ANY)] * len(deps)


def attn_call(kernel, info, args, in_specs, outs, out_specs, flops, name, deps=()):
    return pl.pallas_call(
        ordered(kernel, 1 + len(args), len(deps)),
        grid_spec=pltpu.PrefetchScalarGridSpec(
            num_scalar_prefetch=1,
            grid=(HEADS // 2,),
            in_specs=in_specs + waits(deps),
            out_specs=out_specs,
        ),
        out_shape=[jax.ShapeDtypeStruct(s, d) for s, d in outs],
        compiler_params=pltpu.CompilerParams(vmem_limit_bytes=VMEM),
        cost_estimate=cost(name),
        name=name,
    )(info, *args, *deps)


def attend(info, q, k, v, other_k, other_v, deps):
    t, d = q.shape
    st = (HEADS // 2, 2, t)
    n = other_k.shape[0]
    return attn_call(
        attend_kernel, info, (q, k, v, other_k, other_v),
        [per_pair(t)] * 3 + [per_pair(n)] * 2,
        [((t, d), f32), ((t, d), bf16), (st, f32)], [per_pair(t), per_pair(t), stats(t)], 8 * t * t * d, "attend", deps,
    )


def grads_other(info, q, k, v, grad, out, log_total, deps):
    t, d = q.shape
    n = k.shape[0]
    return attn_call(
        other_backward, info, (q, k, v, grad, out, log_total),
        [per_pair(t), per_pair(n), per_pair(n), per_pair(t), per_pair(t), stats(t)],
        [((d, t), f32), ((n, d), bf16), ((n, d), bf16), ((HEADS // 2, 2, t), f32)],
        [turned(t), per_pair(n), per_pair(n), stats(t)], 10 * t * t * d, "grads_other", deps,
    )


def grads_own(info, q, k, v, grad, log_total, delta, before, deps):
    t, d = q.shape
    return attn_call(
        own_backward, info, (q, k, v, grad, log_total, delta, before),
        [per_pair(t)] * 4 + [stats(t)] * 2 + [turned(t)],
        [((t, d), bf16)] * 3, [per_pair(t)] * 3, 10 * t * t * d, "grads_own", deps,
    )


def dot32(a, b, dims=((1,), (0,)), precision=None):
    return lax.dot_general(a, b, (dims, ((), ())), precision=precision, preferred_element_type=f32)


def swap(block, axis, bit):
    return lax.ppermute(block, axis, [(i, i ^ bit) for i in range(lax.axis_size(axis))])


def bits_of(axis, low=1, high=None):
    high = lax.axis_size(axis) if high is None else high
    found = []
    while low < high:
        found.append(low)
        low *= 2
    return found[::-1]


def row_weight(axis):
    x = lax.axis_size("exp")
    c = lax.axis_size("ctx")
    return {"exp": 1, "ctx": x, "dp": x * c}[axis]


def plan_steps(middle):
    far = [("dp", bit) for bit in bits_of("dp", 2)]
    mid = [(axis, bit) for axis in middle for bit in bits_of(axis)]
    near = [("dp", bit) for bit in bits_of("dp", 1, 2)]
    return far, mid, near


def row_bits(steps):
    return sorted([row_weight(axis) * bit for axis, bit in steps], reverse=True)


def nothing(*refs):
    pass


def hold(value, *others):
    return pl.pallas_call(
        nothing,
        in_specs=waits((value,) + others),
        out_specs=waits((value,))[0],
        out_shape=jax.ShapeDtypeStruct(value.shape, value.dtype),
        input_output_aliases={0: 0},
        cost_estimate=pl.CostEstimate(flops=0, bytes_accessed=0, transcendentals=0),
        name="hold",
    )(value, *others)


def rows_kernel(wqkv_ref, wout_ref, *refs):
    out_ref = refs[-1]
    d = wout_ref.shape[1]
    out_ref[:, : 3 * d] = wqkv_ref[...]
    out_ref[:, 3 * d : 4 * d] = wout_ref[...]
    small = jnp.zeros((wout_ref.shape[0], PAIR), f32)
    first = 0
    for ref in refs[:-1]:
        shape = (ref.shape[0], PAIR)
        here = lax.broadcasted_iota(jnp.int32, shape, 0) + first == lax.broadcasted_iota(jnp.int32, shape, 1)
        small += mul_tn(ref[...], jnp.where(here, 1.0, 0.0).astype(bf16))
        first += ref.shape[0]
    out_ref[:, 4 * d :] = small.astype(bf16)


def gather_step(whole, placed, axis, bit, meanwhile=()):
    other = swap(whole, axis, bit)
    if meanwhile:
        whole = hold(whole, *meanwhile)
    upper = (lax.axis_index(axis) & bit) != 0
    weight = row_weight(axis) * bit
    pos = sum(1 for w in placed if w > weight)
    both = [jnp.where(upper, other, whole), jnp.where(upper, whole, other)]
    return jnp.stack(both, axis=pos), placed[:pos] + [weight] + placed[pos:]


def gather_steps(whole, placed, steps):
    for axis, bit in steps:
        whole, placed = gather_step(whole, placed, axis, bit)
    return whole, placed


def gather_far(rows, steps, meanwhile):
    axis = steps[0][0]
    bits = [bit for _, bit in steps]
    parts = [rows] + [swap(rows, axis, mask) for mask in (bits[1], bits[0], bits[0] + bits[1])]
    parts[0] = hold(rows, *meanwhile)
    low, high = [(lax.axis_index(axis) & bit) != 0 for bit in (bits[1], bits[0])]
    parts = [jnp.where(low, parts[i ^ 1], parts[i]) for i in range(4)]
    parts = [jnp.where(high, parts[i ^ 2], parts[i]) for i in range(4)]
    whole = jnp.stack(parts).reshape((2, 2) + rows.shape)
    return whole, [row_weight(axis) * bit for bit in bits]


def scatter_split(part, placed, axis, bit):
    pos = placed.index(row_weight(axis) * bit)
    upper = (lax.axis_index(axis) & bit) != 0
    low = lax.index_in_dim(part, 0, pos, keepdims=False)
    high = lax.index_in_dim(part, 1, pos, keepdims=False)
    sent = jnp.where(upper, low, high).astype(bf16)
    kept = jnp.where(upper, high, low).astype(f32)
    return sent, kept, placed[:pos] + placed[pos + 1 :]


def scatter_step(part, placed, axis, bit):
    sent, kept, placed = scatter_split(part, placed, axis, bit)
    return kept + swap(sent, axis, bit).astype(f32), placed


def combine_kernel(n, block, up_ref, *refs):
    keep_ref, give_ref = refs[2 * n :]
    first = 0
    for kept, came in zip(refs[:n], refs[n : 2 * n]):
        cols = slice(first, first + kept.shape[1])
        total = kept[...] + came[...].astype(f32)
        keep_ref[:, cols], give_ref[:, cols] = split_rows(up_ref[0] == 1, total, block)
        first += kept.shape[1]


def combine(kept, came, placed, axis, bit, rows, deps, steps=2):
    weight = row_weight(axis) * bit
    placed = [w for w in placed if w != weight]
    block = rows * 2 ** sum(1 for w in placed if w < weight)
    upper = ((lax.axis_index(axis) & bit) != 0).astype(jnp.int32).reshape(1)
    n_rows = kept[0][0].shape[0] // steps
    args = [*kept, *came]
    out = pl.BlockSpec((n_rows // 2, sum(arg[1][1] for arg in kept)), lambda i: (i, 0))
    shape = (n_rows // 2 * steps, out.block_shape[1])
    keep, give = pl.pallas_call(
        ordered(functools.partial(combine_kernel, len(kept), block), 1 + len(args), len(deps)),
        grid=(steps,),
        in_specs=[pl.BlockSpec(memory_space=pltpu.SMEM)]
        + [pl.BlockSpec((n_rows, arg[1][1]), lambda i, index=arg[2]: (i, index)) for arg in args]
        + waits(deps),
        out_specs=[out, out],
        out_shape=[jax.ShapeDtypeStruct(shape, f32), jax.ShapeDtypeStruct(shape, bf16)],
        compiler_params=pltpu.CompilerParams(vmem_limit_bytes=VMEM),
        cost_estimate=cost("combine"),
        name="combine",
    )(upper, *[arg[0] for arg in args], *deps)
    return keep, give, placed


def whole_of(array):
    return column(array, array.shape[1], 0)


def scatter_split(part, placed, axis, bit):
    pos = placed.index(row_weight(axis) * bit)
    upper = (lax.axis_index(axis) & bit) != 0
    low = lax.index_in_dim(part, 0, pos, keepdims=False)
    high = lax.index_in_dim(part, 1, pos, keepdims=False)
    sent = jnp.where(upper, low, high).astype(bf16)
    kept = jnp.where(upper, high, low).astype(f32)
    return sent, kept, placed[:pos] + placed[pos + 1 :]


def scatter_parts(parts, orders, far, near, rows, deps, meanwhile, widths, narrow):
    swapped = {}
    for blocks in parts:
        for _, give, _, _ in blocks:
            if id(give) not in swapped:
                swapped[id(give)] = swap(give, *near[0])
    sums, places, gives = [], [], []
    for i, (blocks, order) in enumerate(zip(parts, orders)):
        step, late = order[-1], i == len(parts) - 1
        keep, give, placed = combine(
            [column(keep, width, index) for keep, _, width, index in blocks],
            [column(swapped[id(give)], width, index) for _, give, width, index in blocks],
            row_bits(far + order), *step, rows, () if late else deps,
        )
        gives.append(give)
        sums.append((keep, swap(give, *step)))
        places.append(placed)
    ready = meanwhile(gives)
    sums = [
        (hold(keep, *ready) + came.astype(f32)).reshape((2,) * len(placed) + (-1, keep.shape[1]))
        for (keep, came), placed in zip(sums, places)
    ]
    for steps in zip(*[reversed(order[:-1]) for order in orders]):
        splits = [scatter_split(part, where, *step) for part, where, step in zip(sums, places, steps)]
        places = [split[2] for split in splits]
        sums = [kept + swap(sent, *step).astype(f32) for (sent, kept, _), step in zip(splits, steps)]
    total, placed = jnp.concatenate(sums, axis=-1), places[0]
    for step in reversed(far):
        sent, kept, placed = scatter_split(total, placed, *step)
        came = swap(sent, *step)
        if placed:
            total = kept + came.astype(f32)
    return simple_call(
        sums_kernel, (kept, came), [((rows, width), f32) for width in widths] + [((n, rows), f32) for n in narrow], 0, "sums"
    )


def sums_kernel(kept_ref, came_ref, qkv_ref, out_ref, *refs):
    d = out_ref.shape[1]
    total = kept_ref[...] + came_ref[...].astype(f32)
    qkv_ref[...] = total[:, : 3 * d]
    out_ref[...] = total[:, 3 * d + PAIR : 4 * d + PAIR]
    gain = jnp.transpose(total[:, 3 * d : 3 * d + PAIR])
    small = jnp.transpose(total[:, 4 * d + PAIR :])
    first = 0
    for ref in refs[:-1]:
        ref[...] = small[first : first + ref.shape[0]]
        first += ref.shape[0]
    refs[-1][...] = gain[:1]


def pack_kernel(gate_ref, up_ref, down_ref, out_ref):
    out_ref[0, 0] = gate_ref[0]
    out_ref[0, 1] = up_ref[0]
    out_ref[0, 2] = jnp.transpose(down_ref[0])


def unpack_kernel(first_ref, rest_ref, gate_ref, up_ref, down_ref):
    rows = first_ref.shape[2]
    for ref, there in ((first_ref, slice(0, rows)), (rest_ref, slice(rows, rows + rest_ref.shape[2]))):
        gate_ref[0, there] = ref[0, 0].astype(f32)
        up_ref[0, there] = ref[0, 1].astype(f32)
        down_ref[0, :, there] = jnp.transpose(ref[0, 2].astype(f32))


def one_of(*shape):
    return pl.BlockSpec((1,) + shape, lambda i: (i,) + (0,) * len(shape))


def pack_expert(w_gate, w_up, w_down, deps):
    n, d, f = w_gate.shape
    return pl.pallas_call(
        ordered(pack_kernel, 3, len(deps)),
        grid=(n,),
        in_specs=[one_of(d, f), one_of(d, f), one_of(f, d)] + waits(deps),
        out_specs=one_of(3, d, f),
        out_shape=jax.ShapeDtypeStruct((n, 3, d, f), w_gate.dtype),
        compiler_params=pltpu.CompilerParams(vmem_limit_bytes=VMEM),
        cost_estimate=cost("pack"),
        name="pack",
    )(w_gate, w_up, w_down, *deps)


def unpack_expert(first, rest, deps):
    n, m, d, f = first.shape
    d = d + rest.shape[2]
    outs = (d, f), (d, f), (f, d)
    return pl.pallas_call(
        ordered(unpack_kernel, 2, len(deps)),
        grid=(n,),
        in_specs=[one_of(*part.shape[1:]) for part in (first, rest)] + waits(deps),
        out_specs=[one_of(*shape) for shape in outs],
        out_shape=[jax.ShapeDtypeStruct((n,) + shape, f32) for shape in outs],
        compiler_params=pltpu.CompilerParams(vmem_limit_bytes=VMEM),
        cost_estimate=cost("unpack"),
        name="unpack",
    )(first, rest, *deps)


def trade_far(parts):
    n_own = parts.shape[0]
    reps = lax.axis_size("dp") // n_own
    groups = [[i * reps + r for i in range(n_own)] for r in range(reps)]
    return lax.all_to_all(parts, "dp", 0, 0, axis_index_groups=groups, tiled=True)


def near_steps(n_own):
    reps = lax.axis_size("dp") // n_own
    return [("ctx", bit) for bit in bits_of("ctx")] + [("dp", bit) for bit in bits_of("dp", 1, reps)]


def gather_expert_near(groups, steps):
    for axis, bit in steps:
        groups = groups + [swap(group, axis, bit) for group in groups]
    return groups


def scatter_expert_near(groups, steps):
    for axis, bit in reversed(steps):
        n = len(groups) // 2
        came = [swap(group.astype(bf16), axis, bit) for group in groups[n:]]
        groups = [a.astype(f32) + b.astype(f32) for a, b in zip(groups[:n], came)]
    return groups[0]


def rms_scale(rows):
    return lax.rsqrt(jnp.mean(rows * rows, axis=-1, keepdims=True) + norm_eps)


def rms_backward(in_rows, inv_scale, gain_vec, grad_rows):
    normed = in_rows * inv_scale
    gain_grad = jnp.sum(grad_rows * normed, axis=0, keepdims=True)
    inner_grad = grad_rows * gain_vec
    back_rows = inv_scale * (
        inner_grad - normed * jnp.mean(inner_grad * normed, axis=-1, keepdims=True)
    )
    return (back_rows, gain_grad)


def rope(rows, cos, sin):
    lane = lax.broadcasted_iota(jnp.int32, (rows.shape[0], PAIR), 1)
    low = lane % (PAIR // 2) < PAIR // 4
    parts = []
    for first in range(0, rows.shape[1], PAIR):
        part = rows[:, first : first + PAIR]
        other = jnp.where(low, pltpu.roll(part, PAIR - PAIR // 4, 1), pltpu.roll(part, PAIR // 4, 1))
        parts.append(part * cos + other * sin)
    return jnp.concatenate(parts, axis=1)


def gain_row(small_ref, lane):
    return jnp.transpose(small_ref[...].astype(f32))[lane : lane + 1]


def project_kernel(scale, lane, x_ref, first_ref, wv_ref, small_ref, cos_ref, sin_ref, h_ref, q_ref, k_ref, v_ref):
    rows = x_ref[...].astype(f32)
    d = rows.shape[1]
    hidden = (rows * rms_scale(rows) * gain_row(small_ref, lane)).astype(bf16)
    h_ref[...] = hidden
    cos, sin = cos_ref[...], sin_ref[...]
    k_ref[...] = rope(mul_nn(hidden, first_ref[:, d : 2 * d]), cos, sin).astype(bf16)
    v_ref[...] = mul_nn(hidden, wv_ref[...]).astype(bf16)
    q_ref[...] = (rope(mul_nn(hidden, first_ref[:, :d]), cos, sin) * scale).astype(bf16)


def other_project_kernel(lane, x_ref, wk_ref, small_ref, wv_ref, cos_ref, sin_ref, h_ref, k_ref, v_ref):
    rows = x_ref[...].astype(f32)
    d = rows.shape[1]
    hidden = (rows * rms_scale(rows) * gain_row(small_ref, lane)).astype(bf16)
    h_ref[...] = hidden
    k_ref[...] = rope(mul_nn(hidden, wk_ref[...]), cos_ref[...], sin_ref[...]).astype(bf16)
    v_ref[...] = mul_nn(hidden, wv_ref[...]).astype(bf16)


def other_back_kernel(dk_ref, dv_ref, wk_ref, wv_ref, cos_ref, sin_ref, x_ref, gk_ref, dh_ref, dgain_ref):
    first = pl.program_id(0) == 0
    grad_k = rope(dk_ref[...].astype(f32), cos_ref[...], -sin_ref[...]).astype(bf16)
    gk_ref[...] = grad_k
    rows = x_ref[...].astype(f32)
    dh = mul_nt(grad_k, wk_ref[...]) + mul_nt(dv_ref[...], wv_ref[...])
    dh_ref[...] = dh.astype(bf16)
    dgain = jnp.sum(dh * rows * rms_scale(rows), axis=0, keepdims=True)

    @pl.when(first)
    def _():
        dgain_ref[...] = dgain

    @pl.when(jnp.logical_not(first))
    def _():
        dgain_ref[...] += dgain


def split_rows(upper, rows, block):
    keep, give = [], []
    for first in range(0, rows.shape[0], 2 * block):
        low, high = rows[first : first + block], rows[first + block : first + 2 * block]
        keep.append(jnp.where(upper, high, low))
        give.append(jnp.where(upper, low, high))
    return jnp.concatenate(keep, axis=0), jnp.concatenate(give, axis=0).astype(bf16)


def own_back_kernel(
    scale, block, core_ref, dq_ref, dk_ref, dv_ref, h_ref, first_ref, wv_ref, cos_ref, sin_ref, x_ref, oh_ref, ok_ref, ov_ref,
    mgain_ref, q_keep_ref, q_give_ref, k_keep_ref, k_give_ref, v_keep_ref, v_give_ref, dh_ref,
):
    step = pl.program_id(0)
    upper = core_ref[0] == 1
    cos, sin = cos_ref[...], -sin_ref[...]

    def finish(grad, weight, other, keep, give):
        dw = mul_tn(h_ref[...], grad)
        if other is not None:
            dw += mul_tn(oh_ref[...], other)
        keep[...], give[...] = split_rows(upper, dw, block)
        return mul_nt(grad, weight)

    @pl.when(step == 0)
    def _():
        grad = rope(dq_ref[...].astype(f32) * scale, cos, sin).astype(bf16)
        dh_ref[...] = finish(grad, first_ref[...], None, q_keep_ref, q_give_ref)

    @pl.when(step == 1)
    def _():
        grad = rope(dk_ref[...].astype(f32), cos, sin).astype(bf16)
        dh_ref[...] += finish(grad, first_ref[...], ok_ref[...], k_keep_ref, k_give_ref)

    @pl.when(step == 2)
    def _():
        d = dh_ref.shape[1]
        dh = dh_ref[...] + finish(dv_ref[...], wv_ref[...], ov_ref[...], v_keep_ref.at[:, :d], v_give_ref.at[:, :d])
        dh_ref[...] = dh
        rows = x_ref[...].astype(f32)
        dgain = jnp.sum(dh * rows * rms_scale(rows), axis=0, keepdims=True) + mgain_ref[...]
        column = jnp.transpose(jnp.broadcast_to(dgain, (8, d)))[:, :1]
        small = jnp.where(lane_of(d) == 0, column, 0.0)
        v_keep_ref[:, d:], v_give_ref[:, d:] = split_rows(upper, small, block)


def first_norm_kernel(lane, dh_ref, more_ref, x_ref, small_ref, mid_ref, dx_ref):
    rows = x_ref[...].astype(f32)
    grad = dh_ref[...] + more_ref[...].astype(f32)
    back, _ = rms_backward(rows, rms_scale(rows), gain_row(small_ref, lane), grad)
    dx_ref[...] = mid_ref[...] + back


def column(array, width, index):
    return array, (array.shape[0], width), index


def simple_call(kernel, args, outs, flops, name, deps=(), scalars=()):
    whole = pl.BlockSpec(memory_space=pltpu.VMEM)
    small = pl.BlockSpec(memory_space=pltpu.SMEM)
    specs, arrays = [], []
    for arg in args:
        if isinstance(arg, tuple):
            array, block, index = arg
            specs.append(pl.BlockSpec(block, lambda i, index=index: (0, index)))
            arrays.append(array)
        else:
            specs.append(whole)
            arrays.append(arg)
    return pl.pallas_call(
        ordered(kernel, len(scalars) + len(args), len(deps)),
        grid=(1,),
        in_specs=[small] * len(scalars) + specs + waits(deps),
        out_shape=[jax.ShapeDtypeStruct(s, d) for s, d in outs],
        compiler_params=pltpu.CompilerParams(vmem_limit_bytes=VMEM),
        cost_estimate=cost(name),
        name=name,
    )(*scalars, *arrays, *deps)


def expert_kernel(n_groups, *refs):
    x_ref, g_ref = refs[:2]
    w_refs = refs[2 : 2 + n_groups]
    out_ref, dx_ref, act_ref, dg_ref, du_ref, gx_ref, gg_ref, store, out_sum, back_sum, done = refs[-11:]
    step = pl.program_id(0)
    n, d = out_sum.shape
    copies = [pltpu.make_async_copy(w, store.at[k], done.at[k]) for k, w in enumerate(w_refs)]

    @pl.when(step == 0)
    def _():
        for copy in copies:
            copy.start()
        out_sum[...] = jnp.zeros((n, d), f32)
        back_sum[...] = jnp.zeros((n, d), f32)

    for k, copy in enumerate(copies):
        pl.when(step == k)(copy.wait)
    grads = g_ref[...].reshape(n, d)
    rows = x_ref[:, :d]
    wg, wu, wd = [
        jnp.concatenate([store[step, p, m] for p in range(store.shape[1])], axis=1) for m in range(3)
    ]
    gate_pre = mul_nn(rows, wg)
    up_pre = mul_nn(rows, wu)
    grad_act = mul_nn(grads, wd)
    sig = 1.0 / (1.0 + jnp.exp(-gate_pre))
    silu = gate_pre * sig
    act = (silu * up_pre).astype(bf16)
    act_ref[...] = act
    grad_gate = (grad_act * up_pre * sig * (1.0 + gate_pre * (1.0 - sig))).astype(bf16)
    grad_up = (grad_act * silu).astype(bf16)
    dg_ref[...] = grad_gate
    du_ref[...] = grad_up
    out_sum[...] += mul_nt(act, wd)
    back_sum[...] += mul_nt(grad_gate, wg) + mul_nt(grad_up, wu)

    @pl.when(step == n_groups - 1)
    def _():
        gates = x_ref[:, d : d + 1].astype(f32) + x_ref[:, d + 1 : d + 2].astype(f32)
        gx_ref[...] = jnp.transpose((rows.astype(f32) * gates).astype(bf16))
        gg_ref[...] = jnp.transpose((grads.astype(f32) * gates).astype(bf16))
        low = out_sum[...].astype(bf16)
        out_ref[...] = low.reshape(out_ref.shape)
        dx_ref[:, :d] = back_sum[...].astype(bf16)
        dots = jnp.sum(grads.astype(f32) * low.astype(f32), axis=1, keepdims=True)
        high, rest = halves(dots)
        lane = lax.broadcasted_iota(jnp.int32, (n, PAIR), 1)
        pair = jnp.where(lane == 0, high.astype(f32), jnp.where(lane == 1, rest.astype(f32), 0.0))
        dx_ref[:, d:] = pair.astype(bf16)


def expert_call(part, x, g, groups, outs, name):
    n, wide = x.shape
    d = g.shape[-1]
    group = groups[0].shape
    cols = group[0] * group[3]
    ff = cols * len(groups)
    block = pl.BlockSpec((g.shape[0], 1) + g.shape[2:], lambda i: (0, part, 0, 0))
    passed = [] if outs is None else [outs]

    def whole(*shape):
        return pl.BlockSpec(shape, lambda i: (0,) * len(shape))

    def column(rows):
        return pl.BlockSpec((rows, cols), lambda i: (0, i))

    shapes = [(n, wide), (n, ff), (n, ff), (n, ff), (d, n), (d, n)]
    return pl.pallas_call(
        functools.partial(expert_kernel, len(groups)),
        grid=(len(groups),),
        in_specs=[whole(n, wide), block] + waits(groups) + waits(passed),
        out_specs=[block, whole(n, wide)] + [column(n)] * 3 + [whole(d, n)] * 2,
        out_shape=[jax.ShapeDtypeStruct(g.shape, bf16)] + [jax.ShapeDtypeStruct(shape, bf16) for shape in shapes],
        input_output_aliases={2 + len(groups): 0} if passed else {},
        scratch_shapes=[
            pltpu.VMEM((len(groups),) + group, bf16), pltpu.VMEM((n, d), f32), pltpu.VMEM((n, d), f32),
            pltpu.SemaphoreType.DMA((len(groups),)),
        ],
        compiler_params=pltpu.CompilerParams(vmem_limit_bytes=VMEM),
        cost_estimate=cost("expert"),
        name=name,
    )(x, g, *groups, *passed)


def expert_weights_kernel(plan, n_through, *refs):
    xs, ggs, acts, dgs, dus = [refs[2 * i : 2 * i + 2] for i in range(5)]
    out_refs = refs[10 + n_through :]
    step = pl.program_id(0)
    pieces, _, d, width = out_refs[0].shape
    for m, (left, right) in enumerate([(xs, dgs), (xs, dus), (ggs, acts)]):
        grad = mul_nn(
            jnp.concatenate([half[...] for half in left], axis=1), jnp.concatenate([half[...] for half in right], axis=0)
        )

        def write(ref):
            for p in range(pieces):
                ref[p, m] = grad[:, p * width : (p + 1) * width].astype(ref.dtype)

        first = 0
        for count, ref in zip(plan, out_refs):
            pl.when((step >= first) & (step < first + count))(functools.partial(write, ref))
            first += count


def expert_weights(flows, order, plan, pieces, width, kinds, name, through=None, deps=()):
    d, n = flows[0][0].shape
    cols = pieces * width
    rows = pl.BlockSpec((d, n), lambda i: (0, 0))
    flip = order[0] != 0

    def group(i):
        return len(order) - 1 - i if flip else i

    part = pl.BlockSpec((n, cols), lambda i: (0, group(i)))
    passed = [] if through is None else [through]
    blocks, first = [], 0
    for count in plan:
        blocks.append(
            pl.BlockSpec(
                (pieces, 3, d, width),
                lambda i, first=first, count=count: (jnp.clip(i - first, 0, count - 1), 0, 0, 0),
            )
        )
        first += count
    return pl.pallas_call(
        ordered(functools.partial(expert_weights_kernel, plan, len(passed)), 10 + len(passed), len(deps)),
        grid=(len(order),),
        in_specs=[rows] * 4 + [part] * 6 + waits(passed) + waits(deps),
        out_specs=blocks + waits(passed),
        out_shape=[
            jax.ShapeDtypeStruct((pieces * count, 3, d, width), kind) for count, kind in zip(plan, kinds)
        ]
        + [jax.ShapeDtypeStruct(p.shape, p.dtype) for p in passed],
        input_output_aliases={10: len(plan)} if passed else {},
        compiler_params=pltpu.CompilerParams(vmem_limit_bytes=VMEM),
        cost_estimate=cost(name),
        name=name,
    )(*[half for flow in flows for half in flow], *passed, *deps)


def weights_sent_kernel(near_ref, came_ref, *out_refs):
    first = 0
    for ref in out_refs:
        there = slice(first, first + ref.shape[2])
        ref[...] = near_ref[:, :, there] + came_ref[:, :, there]
        first += ref.shape[2]


def weights_sent(near, came):
    n, m, d, f = near.shape
    whole = pl.BlockSpec((2, m, d, f), lambda i: (i, 0, 0, 0))
    cuts = (d // 3, d - d // 3)
    return pl.pallas_call(
        weights_sent_kernel,
        grid=(n // 2,),
        in_specs=[whole] * 2,
        out_specs=[pl.BlockSpec((2, m, rows, f), lambda i: (i, 0, 0, 0)) for rows in cuts],
        out_shape=[jax.ShapeDtypeStruct((n, m, rows, f), bf16) for rows in cuts],
        compiler_params=pltpu.CompilerParams(vmem_limit_bytes=VMEM),
        cost_estimate=cost("weights_sent"),
        name="weights_sent",
    )(near, came)


def weights_sum_kernel(kept_ref, far_ref, near_ref, out_ref):
    out_ref[...] = (kept_ref[...].astype(f32) + far_ref[...].astype(f32) + near_ref[...].astype(f32)).astype(bf16)


def weights_sum(kept, far, near, first, deps):
    n, m, d, f = near.shape
    unit = kept.shape[2] // 3
    own = pl.BlockSpec((2, m, unit, f), lambda i, j: (i, 0, j, 0))
    some = pl.BlockSpec((2, m, unit, f), lambda i, j: (i, 0, first // unit + j, 0))
    return pl.pallas_call(
        ordered(weights_sum_kernel, 3, len(deps)),
        grid=(n // 2, d // unit),
        in_specs=[some, some, own] + waits(deps),
        out_specs=own,
        out_shape=jax.ShapeDtypeStruct(near.shape, bf16),
        compiler_params=pltpu.CompilerParams(vmem_limit_bytes=VMEM),
        cost_estimate=cost("weights_sum"),
        name="weights_sum",
    )(kept, far, near, *deps)


def lane_of(rows):
    return lax.broadcasted_iota(jnp.int32, (rows, PAIR), 1)


def col(rows, i):
    return rows[:, i : i + 1]


def halves(rows):
    high = rows.astype(bf16)
    return high, (rows - high.astype(f32)).astype(bf16)


VEC, COEF, GATE, CONST = 0, 2, 3, 5


def mid_kernel(
    n_all, att_ref, small_ref, wo_ref, x_ref, prev_ref, routes_ref, place_ref,
    mid_ref, hidden_ref, scal_ref, *send_refs,
):
    n_ffn = n_all - 4
    d = x_ref.shape[1]
    mid = x_ref[...].astype(f32) + mul_nn(att_ref[...], wo_ref[...])
    mid_ref[...] = mid
    hidden = (mid * rms_scale(mid) * gain_row(small_ref, n_all + 7)).astype(bf16)
    hidden_ref[...] = hidden
    rows, d = hidden.shape
    lane = lane_of(rows)
    raw = mul_nn(hidden, small_ref[...])
    logits = jnp.where(lane < n_all, raw + prev_ref[...], NEG)
    expo = jnp.exp(logits - jnp.max(logits, axis=1, keepdims=True))
    probs = jnp.where(lane < n_all, expo / jnp.sum(expo, axis=1, keepdims=True), 0.0)
    ids = [col(routes_ref[...], j) for j in range(2)]
    gates = [jnp.sum(jnp.where(lane == r, probs, 0.0), axis=1, keepdims=True) for r in ids]
    scal = probs
    coef = sum(jnp.where(r == n_ffn + 1, g, 0.0) for r, g in zip(ids, gates))
    base = n_all + 4
    for c in range(2):
        gap = col(raw, n_all + 2 * c + 1) - col(raw, n_all + 2 * c)
        first, second = 1.0 / (1.0 + jnp.exp(gap)), 1.0 / (1.0 + jnp.exp(-gap))
        const = sum(jnp.where(r == n_ffn + 2 + c, g, 0.0) for r, g in zip(ids, gates))
        coef += first * const
        scal = jnp.where(lane == n_all + 2 * c, first, scal)
        scal = jnp.where(lane == n_all + 2 * c + 1, second, scal)
        scal = jnp.where(lane == base + VEC + c, second * const, scal)
        scal = jnp.where(lane == base + CONST + c, const, scal)
        scal = jnp.where(lane == base + GATE + c, gates[c], scal)
    scal_ref[...] = jnp.where(lane == base + COEF, coef, scal)
    n_half = send_refs[0].shape[0]
    slots = n_half * len(send_refs)
    row = lax.broadcasted_iota(jnp.int32, (slots, rows), 0)
    hits = [(row == place_ref[j : j + 1, :]) for j in range(2)]
    both = jnp.where(hits[0] | hits[1], 1.0, 0.0).astype(bf16)
    rows_out = mul_nn(both, hidden).astype(bf16)
    extra = jnp.zeros((slots, PAIR), f32)
    for j in range(2):
        high, low = halves(gates[j])
        pair = jnp.where(lane == 0, high.astype(f32), jnp.where(lane == 1, low.astype(f32), 0.0))
        extra += mul_nn(jnp.where(hits[j], 1.0, 0.0).astype(bf16), pair.astype(bf16))
    for i, ref in enumerate(send_refs):
        ref[:, :d] = rows_out[i * n_half : (i + 1) * n_half]
        ref[:, d:] = extra[i * n_half : (i + 1) * n_half].astype(bf16)


def spread_kernel(cot_ref, valid_ref, place_ref, send_ref):
    grads = (cot_ref[...] * valid_ref[...]).astype(bf16)
    row = lax.broadcasted_iota(jnp.int32, (send_ref.shape[0], grads.shape[0]), 0)
    hit = (row == place_ref[0:1, :]) | (row == place_ref[1:2, :])
    send_ref[...] = mul_nn(jnp.where(hit, 1.0, 0.0).astype(bf16), grads).astype(bf16)


def picked_rows(place_ref, j, table):
    rows, slots = place_ref.shape[0], table.shape[0]
    slot = lax.broadcasted_iota(jnp.int32, (rows, slots), 1)
    pick = jnp.where(slot == col(place_ref[...], j), 1.0, 0.0).astype(bf16)
    return mul_nn(pick, table)


def gates_back_kernel(
    n_all, back_ref, more_ref, place_ref, routes_ref, scal_ref, hidden_ref, mid_ref, cot_ref, valid_ref, small_ref, wo_ref,
    gmid_ref, gatt_ref, mix_ref, dgain_ref,
):
    n_ffn = n_all - 4
    base = n_all + 4
    scal = scal_ref[...]
    grads = cot_ref[...] * valid_ref[...]
    rows, d = grads.shape
    lane = lane_of(rows)
    hidden = hidden_ref[...].astype(f32)
    small = small_ref[...]
    g_hidden = jnp.sum(grads * hidden, axis=1, keepdims=True)
    high, low = halves(grads)
    g_small = mul_nn(high, small) + mul_nn(low, small)
    table = jnp.concatenate([back_ref[...], more_ref[...]], axis=0)
    grad_hidden = col(scal, base + COEF) * grads
    grad_probs = jnp.zeros((rows, PAIR), f32)
    for j in range(2):
        r = col(routes_ref[...], j)
        came = picked_rows(place_ref, j, table)
        grad_hidden += col(scal, base + GATE + j) * came[:, :d]
        dots = came[:, d : d + 1] + came[:, d + 1 : d + 2]
        dots += jnp.where(r == n_ffn + 1, g_hidden, 0.0)
        for c in range(2):
            whole = col(scal, n_all + 2 * c) * g_hidden + col(scal, n_all + 2 * c + 1) * col(g_small, base + c)
            dots += jnp.where(r == n_ffn + 2 + c, whole, 0.0)
        grad_probs += jnp.where(lane == r, dots, 0.0)
    probs = jnp.where(lane < n_all, scal, 0.0)
    mix = probs * (grad_probs - jnp.sum(probs * grad_probs, axis=1, keepdims=True))
    for c in range(2):
        first, second = col(scal, n_all + 2 * c), col(scal, n_all + 2 * c + 1)
        const = col(scal, base + CONST + c)
        a, b = const * g_hidden, const * col(g_small, base + c)
        inner = first * a + second * b
        mix = jnp.where(lane == n_all + 2 * c, first * (a - inner), mix)
        mix = jnp.where(lane == n_all + 2 * c + 1, second * (b - inner), mix)
    mix_ref[...] = mix
    high, low = halves(mix)
    grad_hidden += mul_nt(high, small) + mul_nt(low, small)
    mid = mid_ref[...]
    back, dgain = rms_backward(mid, rms_scale(mid), gain_row(small_ref, n_all + 7), grad_hidden)
    dgain_ref[...] = dgain
    grad_mid = grads + back
    gmid_ref[...] = grad_mid
    gatt_ref[...] = mul_nt(grad_mid.astype(bf16), wo_ref[...]).astype(bf16)


def out_grads_kernel(
    n_all, block, core_ref, att_ref, gmid_ref, hidden_ref, mix_ref, scal_ref, cot_ref, valid_ref, dgain_ref, keep_ref, give_ref,
):
    d = att_ref.shape[1]
    base = n_all + 4
    upper = core_ref[0] == 1
    dw_out = mul_tn(att_ref[...], gmid_ref[...].astype(bf16))
    keep_ref[:, :d], give_ref[:, :d] = split_rows(upper, dw_out, block)
    hidden = hidden_ref[...]
    high, low = halves(mix_ref[...])
    grads = mul_tn(hidden, high) + mul_tn(hidden, low)
    scal = scal_ref[...]
    lane = lane_of(scal.shape[0])
    vec = jnp.where((lane >= base + VEC) & (lane < base + VEC + 2), scal, 0.0)
    vec_high, vec_low = halves(vec)
    g_high, g_low = halves(cot_ref[...] * valid_ref[...])
    grads += mul_tn(g_high, vec_high) + mul_tn(g_high, vec_low) + mul_tn(g_low, vec_high)
    column = jnp.transpose(jnp.broadcast_to(dgain_ref[...], (8, d)))[:, :1]
    tail = jnp.where(lane_of(d) == base + 2, column, grads)
    keep_ref[:, d:], give_ref[:, d:] = split_rows(upper, tail, block)


def output_kernel(n_all, back_ref, place_ref, scal_ref, hidden_ref, mid_ref, valid_ref, small_ref, out_ref):
    base = n_all + 4
    scal = scal_ref[...]
    lane = lane_of(scal.shape[0])
    vec = jnp.where((lane >= base + VEC) & (lane < base + VEC + 2), scal, 0.0)
    high, low = halves(vec)
    small = small_ref[...]
    total = mid_ref[...] + mul_nt(high, small) + mul_nt(low, small)
    total += col(scal, base + COEF) * hidden_ref[...].astype(f32)
    table = back_ref[...]
    for j in range(2):
        total += col(scal, base + GATE + j) * picked_rows(place_ref, j, table)
    out_ref[...] = total * valid_ref[...]


def local(
    residual_in,
    lengths,
    routes,
    prev_logits,
    cotangent,
    w_qkv,
    w_out,
    attn_gain,
    ffn_gain,
    router,
    const_gate,
    const_vec,
    w_gate,
    w_up,
    w_down,
):
    tok_rows = residual_in.shape[1]
    feat = residual_in.shape[2]
    head_size = feat // HEADS
    score_scale = head_size ** (-0.5)
    n_dp = lax.axis_size("dp")
    n_ctx = lax.axis_size("ctx")
    n_exp = lax.axis_size("exp")
    own_exp = w_gate.shape[0]
    reps = n_dp // own_exp
    n_all = router.shape[1]
    n_ffn = n_all - 4
    cap_rows = tok_rows // 4
    sub_rows = cap_rows // reps
    n_slots = n_ffn * cap_rows
    ctx_rank = lax.axis_index("ctx")
    positions = ctx_rank * tok_rows + jnp.arange(tok_rows, dtype=jnp.int32)
    length = lengths[0]
    valid_rows = (positions < length).astype(f32)[:, None]

    def gather_ctx(rows):
        if n_ctx == 2:
            return swap(rows, "ctx", 1)
        for bit in reversed(bits_of("ctx")):
            other = swap(rows, "ctx", bit)
            upper = (ctx_rank & bit) != 0
            rows = jnp.concatenate([jnp.where(upper, other, rows), jnp.where(upper, rows, other)], axis=0)
        return rows

    def scatter_ctx(rows):
        if n_ctx == 2:
            return swap(rows, "ctx", 1)
        for bit in bits_of("ctx"):
            low, high = jnp.split(rows, 2, axis=0)
            upper = (ctx_rank & bit) != 0
            sent = jnp.where(upper, low, high).astype(bf16)
            rows = jnp.where(upper, high, low).astype(f32) + swap(sent, "ctx", bit).astype(f32)
        return rows

    route_ids = routes[0]
    choose = (route_ids[:, :, None] == jnp.arange(n_all, dtype=jnp.int32)[None, None, :]).astype(f32)
    both = jnp.sum(choose, axis=1)
    before = jnp.arange(tok_rows)
    before = (before[None, :] < before[:, None]).astype(bf16)
    counts = dot32(before, both.astype(bf16))
    slot_ids = jnp.sum(choose * counts[:, None, :], axis=-1).astype(jnp.int32)
    is_ffn = route_ids < n_ffn
    place = (
        ((route_ids % own_exp) * reps + slot_ids // sub_rows) * n_exp + route_ids // own_exp
    ) * sub_rows + slot_ids % sub_rows
    half_rows = sub_rows // 2
    place_half = (
        (place // half_rows % 2) * (n_slots // 2) + place // sub_rows * half_rows + place % half_rows
    )
    place = jnp.where(is_ffn, place, -1)
    place_half = jnp.where(is_ffn, place_half, -1)
    row_ids = jnp.arange(n_slots, dtype=jnp.int32)
    place_rows = jnp.transpose(place)

    def to_experts(rows):
        return lax.all_to_all(
            rows.reshape(n_dp * n_exp, rows.shape[0] // (n_dp * n_exp), -1),
            ("dp", "exp"),
            split_axis=0,
            concat_axis=0,
            tiled=True,
        ).reshape(rows.shape[0], -1)

    width = 2 * feat
    far, mid_a, near = plan_steps(("ctx", "exp"))
    _, mid_b, _ = plan_steps(("exp", "ctx"))
    lane = jnp.arange(PAIR, dtype=jnp.int32)
    half = head_size // 2
    inv_freq = 10000.0 ** (-2.0 * (lane % half).astype(f32) / head_size)
    sign = jnp.where(lane % head_size < half, -1.0, 1.0)

    def turns(where):
        angles = where.astype(f32)[:, None] * inv_freq[None, :]
        return jnp.cos(angles), jnp.sin(angles) * sign[None, :]

    cosine, sine = turns(positions)
    other_start = (1 - ctx_rank) * tok_rows if n_ctx == 2 else 0
    n_other = tok_rows if n_ctx == 2 else tok_rows * n_ctx
    other_cos, other_sin = turns(other_start + jnp.arange(n_other, dtype=jnp.int32))
    other_in = gather_ctx(residual_in[0])
    (rows,) = simple_call(
        rows_kernel, (w_qkv, w_out, router.T, const_gate.T, const_vec.T, attn_gain[None], ffn_gain[None]),
        [((w_out.shape[0], 4 * feat + PAIR), bf16)], 0, "rows",
    )
    packed = pack_expert(w_gate, w_up, w_down, (rows,))
    tables = (cosine, sine, other_cos, other_sin)
    if len(far) == 2:
        whole, placed = gather_far(rows, far, (packed,) + tables)
    else:
        whole, placed = gather_steps(rows, [], far)
    group = trade_far(packed)
    part_a, part_b = whole[..., :width], whole[..., width:]
    placed_a, placed_b = placed, placed
    for i, (step_a, step_b) in enumerate(zip(mid_a, mid_b)):
        meanwhile = (other_in,) if i == 0 else ()
        if i + 1 == len(mid_a):
            (grad_sent,) = simple_call(
                spread_kernel, (cotangent[0], valid_rows, place_rows), [((n_slots, feat), bf16)], 0, "spread", (part_b,)
            )
            meanwhile = (grad_sent,)
        part_a, placed_a = gather_step(part_a, placed_a, *step_a)
        part_b, placed_b = gather_step(part_b, placed_b, *step_b, meanwhile)
    first_part, _ = gather_steps(part_a, placed_a, near)
    second_part, _ = gather_steps(part_b, placed_b, near)
    first_part = first_part.reshape(feat, width)
    second_part = second_part.reshape(feat, 2 * feat + PAIR)

    small_at = 2 * feat // PAIR
    w_v, w_o, small = column(second_part, feat, 0), column(second_part, feat, 1), column(second_part, PAIR, small_at)
    rows_low = ((tok_rows, feat), bf16)
    rows_full = ((tok_rows, feat), f32)
    square = 2 * tok_rows * feat * feat
    hidden_one, queries, own_keys, own_values = simple_call(
        functools.partial(project_kernel, score_scale, n_all + 6),
        (residual_in[0], first_part, w_v, small, cosine, sine), [rows_low] * 4, 3 * square, "project",
    )
    tok_spec = pl.BlockSpec((tok_rows, feat), lambda i: (i, 0))
    turn_spec = pl.BlockSpec((tok_rows, PAIR), lambda i: (i, 0))

    def fixed(rows, cols, index=0):
        return pl.BlockSpec((rows, cols), lambda i: (0, index))

    other_hidden, other_keys, other_values = pl.pallas_call(
        functools.partial(other_project_kernel, n_all + 6),
        grid=(n_other // tok_rows,),
        in_specs=[tok_spec, fixed(feat, feat, 1), fixed(feat, PAIR, small_at), fixed(feat, feat), turn_spec, turn_spec],
        out_specs=[tok_spec] * 3,
        out_shape=[jax.ShapeDtypeStruct((n_other, feat), bf16)] * 3,
        compiler_params=pltpu.CompilerParams(vmem_limit_bytes=VMEM),
        cost_estimate=cost("project_other"),
        name="project_other",
    )(other_in, first_part, second_part, second_part, other_cos, other_sin)
    grad_rows_in = to_experts(hold(grad_sent, group, other_keys))
    info = jnp.stack([ctx_rank * tok_rows, length, ctx_rank]).astype(jnp.int32)
    prev = jnp.pad(prev_logits[0], ((0, 0), (0, PAIR - n_all)))
    attended, attended_low, log_total = attend(
        info, queries, own_keys, own_values, other_keys, other_values, (group, prev, place, place_half)
    )

    mid_rows, hidden, scalars, *sent_rows = simple_call(
        functools.partial(mid_kernel, n_all),
        (attended_low, small, w_o, residual_in[0], prev, route_ids, jnp.transpose(place_half)),
        [rows_full, rows_low, ((tok_rows, PAIR), f32)] + [((n_slots // 2, feat + PAIR), bf16)] * 2, 0, "mid",
    )
    rows_in = [to_experts(hold(sent_rows[0], grad_rows_in)), to_experts(sent_rows[1])]

    steps_near = near_steps(own_exp)
    groups = gather_expert_near([group], steps_near)
    piece_width = group.shape[3]
    if piece_width < PAIR:
        merge = PAIR // piece_width
        whole = jnp.concatenate(groups).reshape(-1, merge, 3, feat, piece_width)
        groups = [jnp.moveaxis(whole, 1, 3).reshape(-1, 3, feat, PAIR)]
    grads_in = grad_rows_in.reshape(n_dp * n_exp, 2, half_rows, feat)
    expert_out = None
    flows, back_grads = [], []
    for part in range(2):
        expert_out, grad_in, *flow = expert_call(part, rows_in[part], grads_in, groups, expert_out, f"expert_{part}")
        back_grads.append(to_experts(grad_in))
        flows.append(flow)
    expert_out = expert_out.reshape(n_slots, feat)
    n_groups = 2 ** len(steps_near)
    act, grad_gate_pre, grad_up_pre, gated_rows, grad_expert_out = zip(*flows)
    flows = (gated_rows, grad_expert_out, act, grad_gate_pre, grad_up_pre)
    simple = piece_width >= PAIR and len(steps_near) == 2
    if simple:
        far_near, far_kept, near_own, kept, expert_out = expert_weights(
            flows, (3, 2, 1, 0), (1, 1, 1, 1), own_exp, piece_width, (bf16,) * 4, "weights_all", expert_out,
            (back_grads[0],),
        )
        far_near = swap(hold(far_near, back_grads[1]), *steps_near[1])
        far_kept = swap(hold(far_kept, back_grads[1]), *steps_near[1])
        near_sent = weights_sent(near_own, far_near)
        near_came = [swap(part, *steps_near[0]) for part in near_sent]
    else:
        step = max(piece_width, PAIR)
        n_steps = act[0].shape[1] // step
        (whole,) = expert_weights(flows, tuple(range(n_steps)), (n_steps,), 1, step, (f32,), "weights_all")
        if piece_width < PAIR:
            whole = jnp.moveaxis(whole.reshape(-1, 3, feat, merge, piece_width), 3, 1)
        whole = whole.reshape(n_groups, own_exp, 3, feat, piece_width)
        expert_sum = scatter_expert_near([whole[i] for i in range(n_groups)], steps_near)
    back_rows = to_experts(expert_out)
    small_shape = ((tok_rows, PAIR), f32)
    grad_mid, grad_attended, grad_mix, grad_gain_two = simple_call(
        functools.partial(gates_back_kernel, n_all),
        (
            *back_grads, place_half, route_ids, scalars, hidden, mid_rows, cotangent[0], valid_rows, small, w_o,
        ),
        [rows_full, rows_low, small_shape, ((1, feat), f32)], 0, "gates_back", tuple(near_sent) if simple else (),
    )
    grad_queries, other_dk, other_dv, delta = grads_other(
        info, queries, other_keys, other_values, grad_attended, attended, log_total, ()
    )
    core = (lax.axis_index("dp") & 1).astype(jnp.int32).reshape(1)
    core_block = feat // (n_dp * n_ctx * n_exp) * row_weight("dp")
    other_gk, other_dh, more_gain = pl.pallas_call(
        other_back_kernel,
        grid=(n_other // tok_rows,),
        in_specs=[tok_spec, tok_spec, fixed(feat, feat, 1), fixed(feat, feat), turn_spec, turn_spec, tok_spec],
        out_specs=[tok_spec, tok_spec, fixed(1, feat)],
        out_shape=[
            jax.ShapeDtypeStruct((n_other, feat), bf16), jax.ShapeDtypeStruct((n_other, feat), bf16),
            jax.ShapeDtypeStruct((1, feat), f32),
        ],
        compiler_params=pltpu.CompilerParams(vmem_limit_bytes=VMEM),
        cost_estimate=cost("back_other"),
        name="back_other",
    )(other_dk, other_dv, first_part, second_part, other_cos, other_sin, other_in)
    more_dh = scatter_ctx(other_dh)
    if simple:
        sum_first = weights_sum(kept, far_kept, near_came[0], 0, (other_dh,))
    else:
        sum_first, sum_rest = jnp.split(expert_sum.astype(bf16), [feat // 3], axis=2)
    back_first = trade_far(sum_first)
    grad_queries, own_dk, own_dv = grads_own(
        info, queries, own_keys, own_values, grad_attended, log_total, delta, grad_queries, (back_rows, sum_first)
    )
    half_rows = feat // 2
    out_keep, out_give = simple_call(
        functools.partial(out_grads_kernel, n_all, core_block),
        (attended_low, grad_mid, hidden, grad_mix, scalars, cotangent[0], valid_rows, grad_gain_two),
        [((half_rows, feat + PAIR), f32), ((half_rows, feat + PAIR), bf16)], 0, "out_grads", (own_dk,), (core,),
    )

    if simple:
        sum_rest = weights_sum(kept, far_kept, near_came[1], feat // 3, (out_keep,))
    back_rest = trade_far(sum_rest)
    own_args = (
        core, grad_queries, own_dk, own_dv, hidden_one, first_part, second_part, cosine, sine, residual_in[0], other_hidden,
        other_gk, other_dv, more_gain,
    )
    own_deps = (sum_rest, back_first)
    token, turn, other = fixed(tok_rows, feat), fixed(tok_rows, PAIR), fixed(n_other, feat)
    q_keep, q_give, k_keep, k_give, v_keep, v_give, grad_hidden_one = pl.pallas_call(
        ordered(functools.partial(own_back_kernel, score_scale, core_block), len(own_args), len(own_deps)),
        grid=(3,),
        in_specs=[pl.BlockSpec(memory_space=pltpu.SMEM)] + [token] * 4
        + [pl.BlockSpec((feat, feat), lambda i: (0, jnp.minimum(i, 1))), fixed(feat, feat), turn, turn, token]
        + [other] * 3 + [fixed(1, feat)] + waits(own_deps),
        out_specs=[fixed(half_rows, feat)] * 4 + [fixed(half_rows, feat + PAIR)] * 2 + [token],
        out_shape=[
            jax.ShapeDtypeStruct((half_rows, feat), f32), jax.ShapeDtypeStruct((half_rows, feat), bf16),
            jax.ShapeDtypeStruct((half_rows, feat), f32), jax.ShapeDtypeStruct((half_rows, feat), bf16),
            jax.ShapeDtypeStruct((half_rows, feat + PAIR), f32), jax.ShapeDtypeStruct((half_rows, feat + PAIR), bf16),
            jax.ShapeDtypeStruct((tok_rows, feat), f32),
        ],
        compiler_params=pltpu.CompilerParams(vmem_limit_bytes=VMEM),
        cost_estimate=cost("back_own"),
        name="back_own",
    )(*own_args, *own_deps)
    def last_rows(sent):
        (output,) = simple_call(
            functools.partial(output_kernel, n_all),
            (back_rows, place, scalars, hidden, mid_rows, valid_rows, small), [rows_full], 0, "output", tuple(sent),
        )
        (grad_x,) = simple_call(
            functools.partial(first_norm_kernel, n_all + 6),
            (grad_hidden_one, more_dh, residual_in[0], small, grad_mid), [rows_full], 0, "first_norm", (output,),
        )
        results.extend([output, grad_x, *unpack_expert(back_first, back_rest, (output, grad_x))])
        return results

    results = []
    dw_qkv, dw_out, *narrow = scatter_parts(
        [
            [(q_keep, q_give, feat, 0), (k_keep, k_give, feat, 0)],
            [(v_keep, v_give, feat + PAIR, 0), (out_keep, out_give, feat + PAIR, 0)],
        ],
        [mid_a, mid_b], far, near, w_out.shape[0], (more_dh,), last_rows, (3 * feat, feat), (n_all, 4, 2, 1, 1),
    )
    output, grad_x, *expert_grads = results
    return (
        output[None],
        grad_x[None],
        dw_qkv,
        dw_out,
        narrow[4][0],
        narrow[3][0],
        narrow[0].T,
        narrow[1].T,
        narrow[2].T,
        expert_grads[0],
        expert_grads[1],
        expert_grads[2],
    )


def solution(mesh):
    in_specs = (
        P(("dp", "exp"), "ctx", None),
        P(("dp", "exp")),
        P(("dp", "exp"), "ctx", None),
        P(("dp", "exp"), "ctx", None),
        P(("dp", "exp"), "ctx", None),
        P(("dp", "ctx", "exp"), None),
        P(("dp", "ctx", "exp"), None),
        P(("dp", "ctx", "exp")),
        P(("dp", "ctx", "exp")),
        P(("dp", "ctx", "exp"), None),
        P(("dp", "ctx", "exp"), None),
        P(("dp", "ctx", "exp"), None),
        P("exp", None, ("dp", "ctx")),
        P("exp", None, ("dp", "ctx")),
        P("exp", ("dp", "ctx"), None),
    )
    out_specs = (
        P(("dp", "exp"), "ctx", None),
        P(("dp", "exp"), "ctx", None),
        P(("dp", "ctx", "exp"), None),
        P(("dp", "ctx", "exp"), None),
        P(("dp", "ctx", "exp")),
        P(("dp", "ctx", "exp")),
        P(("dp", "ctx", "exp"), None),
        P(("dp", "ctx", "exp"), None),
        P(("dp", "ctx", "exp"), None),
        P("exp", None, ("dp", "ctx")),
        P("exp", None, ("dp", "ctx")),
        P("exp", ("dp", "ctx"), None),
    )
    return jax.shard_map(local, mesh=mesh, in_specs=in_specs, out_specs=out_specs, check_vma=False)
```

```python
import functools

import jax
import jax.numpy as jnp
from jax import lax
from jax.experimental import pallas as pl
from jax.experimental.pallas import tpu as pltpu
from jax.sharding import PartitionSpec as P

HEADS = 12

norm_eps = 1e-06
top_precision = lax.Precision.HIGHEST
f32 = jnp.float32
bf16 = jnp.bfloat16


CHUNK = 256
BLOCK = 512
OCHUNK = 512
QCHUNK = 128
PAIR = 128
NEG = -1e30
SCALE = 48
VMEM = 62 << 20
MICROS = {
    "project": 6, "project_other": 5, "spread": 4, "attend": 17, "mid": 9, "expert": 30, "weights_sent": 0,
    "weights_near": 0, "weights_kept": 0, "weights_sum": 0, "gates_back": 0, "grads_other": 0, "back_other": 0, "grads_own": 0,
    "back_own": 0, "out_grads": 0, "output": 6, "first_norm": 4, "weights_all": 26, "pack": 3, "unpack": 4, "combine": 1, "rows": 2, "sums": 1,
}


def cost(name):
    return pl.CostEstimate(flops=MICROS[name] * 1000000000 // SCALE, bytes_accessed=1, transcendentals=0)


def mul_nt(a, b):
    return lax.dot_general(a, b, (((1,), (1,)), ((), ())), preferred_element_type=f32)


def mul_nn(a, b):
    return lax.dot_general(a, b, (((1,), (0,)), ((), ())), preferred_element_type=f32)


def mul_tn(a, b):
    return lax.dot_general(a, b, (((0,), (0,)), ((), ())), preferred_element_type=f32)


def head_part(rows, head):
    lane = lax.broadcasted_iota(jnp.int32, rows.shape, 1)
    return jnp.where((lane >= PAIR // 2) == (head == 1), rows, jnp.zeros_like(rows))


def key_allowed(shape, key_start, length, query_start=None):
    key = key_start + lax.broadcasted_iota(jnp.int32, shape, 0)
    allowed = key < length
    if query_start is not None:
        allowed &= key <= query_start + lax.broadcasted_iota(jnp.int32, shape, 1)
    return allowed


def both_heads(rows, first=0):
    return jnp.concatenate([head_part(rows[first:], head) for head in range(2)], axis=0)


def beside(row_pair):
    return jnp.concatenate([row_pair[0:1], row_pair[1:2]], axis=1)


def split_heads(wide):
    half, t = PAIR // 2, wide.shape[1] // 2
    return jnp.concatenate([wide[:half, :t], wide[half:, t:]], axis=0)


def attend_kernel(info, q_ref, k_ref, v_ref, ok_ref, ov_ref, out_ref, low_ref, log_ref):
    base, length, blocks = info[0], info[1], info[2]
    queries = q_ref[...]
    rows = queries.shape[0]
    half = PAIR // 2
    starts = list(range(0, rows, QCHUNK))
    twice = [both_heads(queries[first : first + QCHUNK]) for first in starts]

    def spread(row):
        n = row.shape[1] // 2
        return jnp.concatenate(
            [jnp.broadcast_to(row[:, :n], (half, n)), jnp.broadcast_to(row[:, n:], (half, n))], axis=0
        )

    scores, tops, states = [], [], []
    for first, part in zip(starts, twice):
        end = first + QCHUNK
        some = mul_nt(k_ref[:end, :], part)
        allowed = key_allowed((end, QCHUNK), base, length, base + first)
        scores.append(jnp.where(jnp.concatenate([allowed, allowed], axis=1), some, NEG))
    for some in scores:
        tops.append(jnp.max(some, axis=0, keepdims=True))
    for first, some, top in zip(starts, scores, tops):
        expo = jnp.exp(some - top)
        total = jnp.sum(expo, axis=0, keepdims=True)
        acc = split_heads(mul_tn(v_ref[: first + QCHUNK, :], expo.astype(bf16)))
        states.append((top, total, acc))

    def step(c, states):
        first = pl.multiple_of(c * BLOCK, BLOCK)
        keys = ok_ref[pl.ds(first, BLOCK), :]
        vals = ov_ref[pl.ds(first, BLOCK), :]
        allowed = key_allowed((BLOCK, 2 * QCHUNK), first, length)
        scores = [jnp.where(allowed, mul_nt(keys, part), NEG) for part in twice]
        new = []
        for some, (top, total, acc) in zip(scores, states):
            new_top = jnp.maximum(top, jnp.max(some, axis=0, keepdims=True))
            expo = jnp.exp(some - new_top)
            factor = jnp.exp(top - new_top)
            total = total * factor + jnp.sum(expo, axis=0, keepdims=True)
            acc = acc * spread(factor) + split_heads(mul_tn(vals, expo.astype(bf16)))
            new.append((new_top, total, acc))
        return tuple(new)

    states = lax.fori_loop(0, blocks, step, tuple(states))
    for first, (top, total, acc) in zip(starts, states):
        there = slice(first, first + QCHUNK)
        out = jnp.transpose(acc / spread(total))
        out_ref[there, :] = out
        low_ref[there, :] = out.astype(bf16)
        log = top + jnp.log(total)
        log_ref[0, 0:1, there] = log[:, :QCHUNK]
        log_ref[0, 1:2, there] = log[:, QCHUNK:]


def pair_grads(keys, vals, twice, grad_twice, log_row, delta_row, allowed):
    probs = jnp.where(allowed, jnp.exp(mul_nt(keys, twice) - log_row), 0.0)
    grad_probs = mul_nt(vals, grad_twice)
    grad_scores = (probs * (grad_probs - delta_row)).astype(bf16)
    return (
        mul_nn(grad_scores, twice),
        mul_nn(probs.astype(bf16), grad_twice),
        split_heads(mul_tn(keys, grad_scores)),
    )


def other_backward(
    info, q_ref, k_ref, v_ref, grad_ref, out_ref, log_ref, dq_ref, dk_ref, dv_ref, delta_ref
):
    length, chunks = info[1], info[2] * (BLOCK // OCHUNK)
    half = PAIR // 2
    queries, grads = q_ref[...], grad_ref[...]
    rows = queries.shape[0]
    product = jnp.transpose(grads.astype(f32) * out_ref[...])
    twice, grad_twice = both_heads(queries), both_heads(grads)
    for head in range(2):
        delta_ref[0, head : head + 1, :] = jnp.sum(
            product[head * half : (head + 1) * half], axis=0, keepdims=True
        )
    log_row, delta_row = beside(log_ref[0]), beside(delta_ref[0])

    def step(c, dq):
        first = pl.multiple_of(c * OCHUNK, OCHUNK)
        keys = k_ref[pl.ds(first, OCHUNK), :]
        vals = v_ref[pl.ds(first, OCHUNK), :]
        allowed = key_allowed((OCHUNK, 2 * rows), first, length)
        dk, dv, more = pair_grads(keys, vals, twice, grad_twice, log_row, delta_row, allowed)
        dk_ref[pl.ds(first, OCHUNK), :] = dk.astype(dk_ref.dtype)
        dv_ref[pl.ds(first, OCHUNK), :] = dv.astype(dv_ref.dtype)
        return dq + more

    dq_ref[...] = lax.fori_loop(0, chunks, step, jnp.zeros((PAIR, rows), f32))

    def clear(c, none):
        first = pl.multiple_of(c * OCHUNK, OCHUNK)
        dk_ref[pl.ds(first, OCHUNK), :] = jnp.zeros((OCHUNK, PAIR), dk_ref.dtype)
        dv_ref[pl.ds(first, OCHUNK), :] = jnp.zeros((OCHUNK, PAIR), dv_ref.dtype)
        return none

    lax.fori_loop(chunks, k_ref.shape[0] // OCHUNK, clear, 0)


def own_backward(
    info, q_ref, k_ref, v_ref, grad_ref, log_ref, delta_ref, before_ref, dq_ref, dk_ref, dv_ref
):
    base, length = info[0], info[1]
    queries, grads = q_ref[...], grad_ref[...]
    rows = queries.shape[0]
    dq = before_ref[...]
    for first in range(0, rows, CHUNK):
        keys = k_ref[first : first + CHUNK, :]
        vals = v_ref[first : first + CHUNK, :]
        allowed = key_allowed((CHUNK, rows - first), base + first, length, base + first)
        dk, dv, more = pair_grads(
            keys,
            vals,
            both_heads(queries, first),
            both_heads(grads, first),
            beside(log_ref[0, :, first:]),
            beside(delta_ref[0, :, first:]),
            jnp.concatenate([allowed, allowed], axis=1),
        )
        dk_ref[first : first + CHUNK, :] = dk.astype(dk_ref.dtype)
        dv_ref[first : first + CHUNK, :] = dv.astype(dv_ref.dtype)
        if first:
            more = jnp.concatenate([jnp.zeros((PAIR, first), f32), more], axis=1)
        dq = dq + more
    dq_ref[...] = jnp.transpose(dq).astype(dq_ref.dtype)


def per_pair(rows):
    return pl.BlockSpec((rows, PAIR), lambda i, info: (0, i))


def turned(cols):
    return pl.BlockSpec((PAIR, cols), lambda i, info: (i, 0))


def stats(cols):
    return pl.BlockSpec((1, 2, cols), lambda i, info: (i, 0, 0))


def ordered(kernel, n_in, n_deps):
    if not n_deps:
        return kernel

    def run(*refs):
        kernel(*refs[:n_in], *refs[n_in + n_deps :])

    return run


def waits(deps):
    return [pl.BlockSpec(memory_space=pl.ANY)] * len(deps)


def attn_call(kernel, info, args, in_specs, outs, out_specs, flops, name, deps=()):
    return pl.pallas_call(
        ordered(kernel, 1 + len(args), len(deps)),
        grid_spec=pltpu.PrefetchScalarGridSpec(
            num_scalar_prefetch=1,
            grid=(HEADS // 2,),
            in_specs=in_specs + waits(deps),
            out_specs=out_specs,
        ),
        out_shape=[jax.ShapeDtypeStruct(s, d) for s, d in outs],
        compiler_params=pltpu.CompilerParams(vmem_limit_bytes=VMEM),
        cost_estimate=cost(name),
        name=name,
    )(info, *args, *deps)


def attend(info, q, k, v, other_k, other_v, deps):
    t, d = q.shape
    st = (HEADS // 2, 2, t)
    n = other_k.shape[0]
    return attn_call(
        attend_kernel, info, (q, k, v, other_k, other_v),
        [per_pair(t)] * 3 + [per_pair(n)] * 2,
        [((t, d), f32), ((t, d), bf16), (st, f32)], [per_pair(t), per_pair(t), stats(t)], 8 * t * t * d, "attend", deps,
    )


def grads_other(info, q, k, v, grad, out, log_total, deps):
    t, d = q.shape
    n = k.shape[0]
    return attn_call(
        other_backward, info, (q, k, v, grad, out, log_total),
        [per_pair(t), per_pair(n), per_pair(n), per_pair(t), per_pair(t), stats(t)],
        [((d, t), f32), ((n, d), bf16), ((n, d), bf16), ((HEADS // 2, 2, t), f32)],
        [turned(t), per_pair(n), per_pair(n), stats(t)], 10 * t * t * d, "grads_other", deps,
    )


def grads_own(info, q, k, v, grad, log_total, delta, before, deps):
    t, d = q.shape
    return attn_call(
        own_backward, info, (q, k, v, grad, log_total, delta, before),
        [per_pair(t)] * 4 + [stats(t)] * 2 + [turned(t)],
        [((t, d), bf16)] * 3, [per_pair(t)] * 3, 10 * t * t * d, "grads_own", deps,
    )


def dot32(a, b, dims=((1,), (0,)), precision=None):
    return lax.dot_general(a, b, (dims, ((), ())), precision=precision, preferred_element_type=f32)


def swap(block, axis, bit):
    return lax.ppermute(block, axis, [(i, i ^ bit) for i in range(lax.axis_size(axis))])


def bits_of(axis, low=1, high=None):
    high = lax.axis_size(axis) if high is None else high
    found = []
    while low < high:
        found.append(low)
        low *= 2
    return found[::-1]


def row_weight(axis):
    x = lax.axis_size("exp")
    c = lax.axis_size("ctx")
    return {"exp": 1, "ctx": x, "dp": x * c}[axis]


def plan_steps(middle):
    far = [("dp", bit) for bit in bits_of("dp", 2)]
    mid = [(axis, bit) for axis in middle for bit in bits_of(axis)]
    near = [("dp", bit) for bit in bits_of("dp", 1, 2)]
    return far, mid, near


def row_bits(steps):
    return sorted([row_weight(axis) * bit for axis, bit in steps], reverse=True)


def nothing(*refs):
    pass


def hold(value, *others):
    return pl.pallas_call(
        nothing,
        in_specs=waits((value,) + others),
        out_specs=waits((value,))[0],
        out_shape=jax.ShapeDtypeStruct(value.shape, value.dtype),
        input_output_aliases={0: 0},
        cost_estimate=pl.CostEstimate(flops=0, bytes_accessed=0, transcendentals=0),
        name="hold",
    )(value, *others)


def rows_kernel(wqkv_ref, wout_ref, *refs):
    out_ref = refs[-1]
    d = wout_ref.shape[1]
    out_ref[:, : 3 * d] = wqkv_ref[...]
    out_ref[:, 3 * d : 4 * d] = wout_ref[...]
    small = jnp.zeros((wout_ref.shape[0], PAIR), f32)
    first = 0
    for ref in refs[:-1]:
        shape = (ref.shape[0], PAIR)
        here = lax.broadcasted_iota(jnp.int32, shape, 0) + first == lax.broadcasted_iota(jnp.int32, shape, 1)
        small += mul_tn(ref[...], jnp.where(here, 1.0, 0.0).astype(bf16))
        first += ref.shape[0]
    out_ref[:, 4 * d :] = small.astype(bf16)


def gather_step(whole, placed, axis, bit, meanwhile=()):
    other = swap(whole, axis, bit)
    if meanwhile:
        whole = hold(whole, *meanwhile)
    upper = (lax.axis_index(axis) & bit) != 0
    weight = row_weight(axis) * bit
    pos = sum(1 for w in placed if w > weight)
    both = [jnp.where(upper, other, whole), jnp.where(upper, whole, other)]
    return jnp.stack(both, axis=pos), placed[:pos] + [weight] + placed[pos:]


def gather_steps(whole, placed, steps):
    for axis, bit in steps:
        whole, placed = gather_step(whole, placed, axis, bit)
    return whole, placed


def gather_far(rows, steps, meanwhile):
    axis = steps[0][0]
    bits = [bit for _, bit in steps]
    parts = [rows] + [swap(rows, axis, mask) for mask in (bits[1], bits[0], bits[0] + bits[1])]
    parts[0] = hold(rows, *meanwhile)
    low, high = [(lax.axis_index(axis) & bit) != 0 for bit in (bits[1], bits[0])]
    parts = [jnp.where(low, parts[i ^ 1], parts[i]) for i in range(4)]
    parts = [jnp.where(high, parts[i ^ 2], parts[i]) for i in range(4)]
    whole = jnp.stack(parts).reshape((2, 2) + rows.shape)
    return whole, [row_weight(axis) * bit for bit in bits]


def scatter_split(part, placed, axis, bit):
    pos = placed.index(row_weight(axis) * bit)
    upper = (lax.axis_index(axis) & bit) != 0
    low = lax.index_in_dim(part, 0, pos, keepdims=False)
    high = lax.index_in_dim(part, 1, pos, keepdims=False)
    sent = jnp.where(upper, low, high).astype(bf16)
    kept = jnp.where(upper, high, low).astype(f32)
    return sent, kept, placed[:pos] + placed[pos + 1 :]


def scatter_step(part, placed, axis, bit):
    sent, kept, placed = scatter_split(part, placed, axis, bit)
    return kept + swap(sent, axis, bit).astype(f32), placed


def combine_kernel(n, block, up_ref, *refs):
    keep_ref, give_ref = refs[2 * n :]
    first = 0
    for kept, came in zip(refs[:n], refs[n : 2 * n]):
        cols = slice(first, first + kept.shape[1])
        total = kept[...] + came[...].astype(f32)
        keep_ref[:, cols], give_ref[:, cols] = split_rows(up_ref[0] == 1, total, block)
        first += kept.shape[1]


def combine(kept, came, placed, axis, bit, rows, deps, steps=2):
    weight = row_weight(axis) * bit
    placed = [w for w in placed if w != weight]
    block = rows * 2 ** sum(1 for w in placed if w < weight)
    upper = ((lax.axis_index(axis) & bit) != 0).astype(jnp.int32).reshape(1)
    n_rows = kept[0][0].shape[0] // steps
    args = [*kept, *came]
    out = pl.BlockSpec((n_rows // 2, sum(arg[1][1] for arg in kept)), lambda i: (i, 0))
    shape = (n_rows // 2 * steps, out.block_shape[1])
    keep, give = pl.pallas_call(
        ordered(functools.partial(combine_kernel, len(kept), block), 1 + len(args), len(deps)),
        grid=(steps,),
        in_specs=[pl.BlockSpec(memory_space=pltpu.SMEM)]
        + [pl.BlockSpec((n_rows, arg[1][1]), lambda i, index=arg[2]: (i, index)) for arg in args]
        + waits(deps),
        out_specs=[out, out],
        out_shape=[jax.ShapeDtypeStruct(shape, f32), jax.ShapeDtypeStruct(shape, bf16)],
        compiler_params=pltpu.CompilerParams(vmem_limit_bytes=VMEM),
        cost_estimate=cost("combine"),
        name="combine",
    )(upper, *[arg[0] for arg in args], *deps)
    return keep, give, placed


def whole_of(array):
    return column(array, array.shape[1], 0)


def scatter_split(part, placed, axis, bit):
    pos = placed.index(row_weight(axis) * bit)
    upper = (lax.axis_index(axis) & bit) != 0
    low = lax.index_in_dim(part, 0, pos, keepdims=False)
    high = lax.index_in_dim(part, 1, pos, keepdims=False)
    sent = jnp.where(upper, low, high).astype(bf16)
    kept = jnp.where(upper, high, low).astype(f32)
    return sent, kept, placed[:pos] + placed[pos + 1 :]


def scatter_parts(parts, orders, far, near, rows, deps, meanwhile, widths, narrow):
    swapped = {}
    for blocks in parts:
        for _, give, _, _ in blocks:
            if id(give) not in swapped:
                swapped[id(give)] = swap(give, *near[0])
    sums, places, gives = [], [], []
    for i, (blocks, order) in enumerate(zip(parts, orders)):
        step, late = order[-1], i == len(parts) - 1
        keep, give, placed = combine(
            [column(keep, width, index) for keep, _, width, index in blocks],
            [column(swapped[id(give)], width, index) for _, give, width, index in blocks],
            row_bits(far + order), *step, rows, () if late else deps,
        )
        gives.append(give)
        sums.append((keep, swap(give, *step)))
        places.append(placed)
    ready = meanwhile(gives)
    sums = [
        (hold(keep, *ready) + came.astype(f32)).reshape((2,) * len(placed) + (-1, keep.shape[1]))
        for (keep, came), placed in zip(sums, places)
    ]
    for steps in zip(*[reversed(order[:-1]) for order in orders]):
        splits = [scatter_split(part, where, *step) for part, where, step in zip(sums, places, steps)]
        places = [split[2] for split in splits]
        sums = [kept + swap(sent, *step).astype(f32) for (sent, kept, _), step in zip(splits, steps)]
    total, placed = jnp.concatenate(sums, axis=-1), places[0]
    for step in reversed(far):
        sent, kept, placed = scatter_split(total, placed, *step)
        came = swap(sent, *step)
        if placed:
            total = kept + came.astype(f32)
    return simple_call(
        sums_kernel, (kept, came), [((rows, width), f32) for width in widths] + [((n, rows), f32) for n in narrow], 0, "sums"
    )


def sums_kernel(kept_ref, came_ref, qkv_ref, out_ref, *refs):
    d = out_ref.shape[1]
    total = kept_ref[...] + came_ref[...].astype(f32)
    qkv_ref[...] = total[:, : 3 * d]
    out_ref[...] = total[:, 3 * d + PAIR : 4 * d + PAIR]
    gain = jnp.transpose(total[:, 3 * d : 3 * d + PAIR])
    small = jnp.transpose(total[:, 4 * d + PAIR :])
    first = 0
    for ref in refs[:-1]:
        ref[...] = small[first : first + ref.shape[0]]
        first += ref.shape[0]
    refs[-1][...] = gain[:1]


def pack_kernel(gate_ref, up_ref, down_ref, out_ref):
    out_ref[0, 0] = gate_ref[0]
    out_ref[0, 1] = up_ref[0]
    out_ref[0, 2] = jnp.transpose(down_ref[0])


def unpack_kernel(first_ref, rest_ref, gate_ref, up_ref, down_ref):
    rows = first_ref.shape[2]
    for ref, there in ((first_ref, slice(0, rows)), (rest_ref, slice(rows, rows + rest_ref.shape[2]))):
        gate_ref[0, there] = ref[0, 0].astype(f32)
        up_ref[0, there] = ref[0, 1].astype(f32)
        down_ref[0, :, there] = jnp.transpose(ref[0, 2].astype(f32))


def one_of(*shape):
    return pl.BlockSpec((1,) + shape, lambda i: (i,) + (0,) * len(shape))


def pack_expert(w_gate, w_up, w_down, deps):
    n, d, f = w_gate.shape
    return pl.pallas_call(
        ordered(pack_kernel, 3, len(deps)),
        grid=(n,),
        in_specs=[one_of(d, f), one_of(d, f), one_of(f, d)] + waits(deps),
        out_specs=one_of(3, d, f),
        out_shape=jax.ShapeDtypeStruct((n, 3, d, f), w_gate.dtype),
        compiler_params=pltpu.CompilerParams(vmem_limit_bytes=VMEM),
        cost_estimate=cost("pack"),
        name="pack",
    )(w_gate, w_up, w_down, *deps)


def unpack_expert(first, rest, deps):
    n, m, d, f = first.shape
    d = d + rest.shape[2]
    outs = (d, f), (d, f), (f, d)
    return pl.pallas_call(
        ordered(unpack_kernel, 2, len(deps)),
        grid=(n,),
        in_specs=[one_of(*part.shape[1:]) for part in (first, rest)] + waits(deps),
        out_specs=[one_of(*shape) for shape in outs],
        out_shape=[jax.ShapeDtypeStruct((n,) + shape, f32) for shape in outs],
        compiler_params=pltpu.CompilerParams(vmem_limit_bytes=VMEM),
        cost_estimate=cost("unpack"),
        name="unpack",
    )(first, rest, *deps)


def trade_far(parts):
    n_own = parts.shape[0]
    reps = lax.axis_size("dp") // n_own
    groups = [[i * reps + r for i in range(n_own)] for r in range(reps)]
    return lax.all_to_all(parts, "dp", 0, 0, axis_index_groups=groups, tiled=True)


def near_steps(n_own):
    reps = lax.axis_size("dp") // n_own
    return [("ctx", bit) for bit in bits_of("ctx")] + [("dp", bit) for bit in bits_of("dp", 1, reps)]


def gather_expert_near(groups, steps):
    for axis, bit in steps:
        groups = groups + [swap(group, axis, bit) for group in groups]
    return groups


def scatter_expert_near(groups, steps):
    for axis, bit in reversed(steps):
        n = len(groups) // 2
        came = [swap(group.astype(bf16), axis, bit) for group in groups[n:]]
        groups = [a.astype(f32) + b.astype(f32) for a, b in zip(groups[:n], came)]
    return groups[0]


def rms_scale(rows):
    return lax.rsqrt(jnp.mean(rows * rows, axis=-1, keepdims=True) + norm_eps)


def rms_backward(in_rows, inv_scale, gain_vec, grad_rows):
    normed = in_rows * inv_scale
    gain_grad = jnp.sum(grad_rows * normed, axis=0, keepdims=True)
    inner_grad = grad_rows * gain_vec
    back_rows = inv_scale * (
        inner_grad - normed * jnp.mean(inner_grad * normed, axis=-1, keepdims=True)
    )
    return (back_rows, gain_grad)


def rope(rows, cos, sin):
    lane = lax.broadcasted_iota(jnp.int32, (rows.shape[0], PAIR), 1)
    low = lane % (PAIR // 2) < PAIR // 4
    parts = []
    for first in range(0, rows.shape[1], PAIR):
        part = rows[:, first : first + PAIR]
        other = jnp.where(low, pltpu.roll(part, PAIR - PAIR // 4, 1), pltpu.roll(part, PAIR // 4, 1))
        parts.append(part * cos + other * sin)
    return jnp.concatenate(parts, axis=1)


def gain_row(small_ref, lane):
    return jnp.transpose(small_ref[...].astype(f32))[lane : lane + 1]


def project_kernel(scale, lane, x_ref, first_ref, wv_ref, small_ref, cos_ref, sin_ref, h_ref, q_ref, k_ref, v_ref):
    rows = x_ref[...].astype(f32)
    d = rows.shape[1]
    hidden = (rows * rms_scale(rows) * gain_row(small_ref, lane)).astype(bf16)
    h_ref[...] = hidden
    cos, sin = cos_ref[...], sin_ref[...]
    k_ref[...] = rope(mul_nn(hidden, first_ref[:, d : 2 * d]), cos, sin).astype(bf16)
    v_ref[...] = mul_nn(hidden, wv_ref[...]).astype(bf16)
    q_ref[...] = (rope(mul_nn(hidden, first_ref[:, :d]), cos, sin) * scale).astype(bf16)


def other_project_kernel(lane, x_ref, wk_ref, small_ref, wv_ref, cos_ref, sin_ref, h_ref, k_ref, v_ref):
    rows = x_ref[...].astype(f32)
    d = rows.shape[1]
    hidden = (rows * rms_scale(rows) * gain_row(small_ref, lane)).astype(bf16)
    h_ref[...] = hidden
    k_ref[...] = rope(mul_nn(hidden, wk_ref[...]), cos_ref[...], sin_ref[...]).astype(bf16)
    v_ref[...] = mul_nn(hidden, wv_ref[...]).astype(bf16)


def other_back_kernel(dk_ref, dv_ref, wk_ref, wv_ref, cos_ref, sin_ref, x_ref, gk_ref, dh_ref, dgain_ref):
    first = pl.program_id(0) == 0
    grad_k = rope(dk_ref[...].astype(f32), cos_ref[...], -sin_ref[...]).astype(bf16)
    gk_ref[...] = grad_k
    rows = x_ref[...].astype(f32)
    dh = mul_nt(grad_k, wk_ref[...]) + mul_nt(dv_ref[...], wv_ref[...])
    dh_ref[...] = dh.astype(bf16)
    dgain = jnp.sum(dh * rows * rms_scale(rows), axis=0, keepdims=True)

    @pl.when(first)
    def _():
        dgain_ref[...] = dgain

    @pl.when(jnp.logical_not(first))
    def _():
        dgain_ref[...] += dgain


def split_rows(upper, rows, block):
    keep, give = [], []
    for first in range(0, rows.shape[0], 2 * block):
        low, high = rows[first : first + block], rows[first + block : first + 2 * block]
        keep.append(jnp.where(upper, high, low))
        give.append(jnp.where(upper, low, high))
    return jnp.concatenate(keep, axis=0), jnp.concatenate(give, axis=0).astype(bf16)


def own_back_kernel(
    scale, block, core_ref, dq_ref, h_ref, first_ref, wv_ref, cos_ref, sin_ref, mgain_ref, dk_hbm, oh_hbm, ok_hbm, dv_hbm, ov_hbm,
    x_hbm, q_keep_ref, q_give_ref, k_keep_ref, k_give_ref, v_keep_ref, v_give_ref, dh_ref, dk_ref, oh_ref, ok_ref, dv_ref, ov_ref,
    x_ref, done,
):
    far = (dk_hbm, oh_hbm, ok_hbm, dv_hbm, ov_hbm, x_hbm)
    near = (dk_ref, oh_ref, ok_ref, dv_ref, ov_ref, x_ref)
    copies = [pltpu.make_async_copy(a, b, done.at[i]) for i, (a, b) in enumerate(zip(far, near))]
    step = pl.program_id(0)
    upper = core_ref[0] == 1
    cos, sin = cos_ref[...], -sin_ref[...]

    def finish(grad, weight, other, keep, give):
        dw = mul_tn(h_ref[...], grad)
        if other is not None:
            dw += mul_tn(oh_ref[...], other)
        keep[...], give[...] = split_rows(upper, dw, block)
        return mul_nt(grad, weight)

    @pl.when(step == 0)
    def _():
        for copy in copies:
            copy.start()
        grad = rope(dq_ref[...].astype(f32) * scale, cos, sin).astype(bf16)
        dh_ref[...] = finish(grad, first_ref[...], None, q_keep_ref, q_give_ref)

    @pl.when(step == 1)
    def _():
        for copy in copies[:3]:
            copy.wait()
        grad = rope(dk_ref[...].astype(f32), cos, sin).astype(bf16)
        dh_ref[...] += finish(grad, first_ref[...], ok_ref[...], k_keep_ref, k_give_ref)

    @pl.when(step == 2)
    def _():
        for copy in copies[3:]:
            copy.wait()
        d = dh_ref.shape[1]
        dh = dh_ref[...] + finish(dv_ref[...], wv_ref[...], ov_ref[...], v_keep_ref.at[:, :d], v_give_ref.at[:, :d])
        dh_ref[...] = dh
        rows = x_ref[...].astype(f32)
        dgain = jnp.sum(dh * rows * rms_scale(rows), axis=0, keepdims=True) + mgain_ref[...]
        column = jnp.transpose(jnp.broadcast_to(dgain, (8, d)))[:, :1]
        small = jnp.where(lane_of(d) == 0, column, 0.0)
        v_keep_ref[:, d:], v_give_ref[:, d:] = split_rows(upper, small, block)


def first_norm_kernel(lane, dh_ref, more_ref, x_ref, small_ref, mid_ref, dx_ref):
    rows = x_ref[...].astype(f32)
    grad = dh_ref[...] + more_ref[...].astype(f32)
    back, _ = rms_backward(rows, rms_scale(rows), gain_row(small_ref, lane), grad)
    dx_ref[...] = mid_ref[...] + back


def column(array, width, index):
    return array, (array.shape[0], width), index


def simple_call(kernel, args, outs, flops, name, deps=(), scalars=()):
    whole = pl.BlockSpec(memory_space=pltpu.VMEM)
    small = pl.BlockSpec(memory_space=pltpu.SMEM)
    specs, arrays = [], []
    for arg in args:
        if isinstance(arg, tuple):
            array, block, index = arg
            specs.append(pl.BlockSpec(block, lambda i, index=index: (0, index)))
            arrays.append(array)
        else:
            specs.append(whole)
            arrays.append(arg)
    return pl.pallas_call(
        ordered(kernel, len(scalars) + len(args), len(deps)),
        grid=(1,),
        in_specs=[small] * len(scalars) + specs + waits(deps),
        out_shape=[jax.ShapeDtypeStruct(s, d) for s, d in outs],
        compiler_params=pltpu.CompilerParams(vmem_limit_bytes=VMEM),
        cost_estimate=cost(name),
        name=name,
    )(*scalars, *arrays, *deps)


def expert_kernel(n_groups, *refs):
    x_ref, g_ref = refs[:2]
    w_refs = refs[2 : 2 + n_groups]
    out_ref, dx_ref, act_ref, dg_ref, du_ref, gx_ref, gg_ref, store, out_sum, back_sum, done = refs[-11:]
    step = pl.program_id(0)
    n, d = out_sum.shape
    copies = [pltpu.make_async_copy(w, store.at[k], done.at[k]) for k, w in enumerate(w_refs)]

    @pl.when(step == 0)
    def _():
        for copy in copies:
            copy.start()
        out_sum[...] = jnp.zeros((n, d), f32)
        back_sum[...] = jnp.zeros((n, d), f32)

    for k, copy in enumerate(copies):
        pl.when(step == k)(copy.wait)
    grads = g_ref[...].reshape(n, d)
    rows = x_ref[:, :d]
    wg, wu, wd = [
        jnp.concatenate([store[step, p, m] for p in range(store.shape[1])], axis=1) for m in range(3)
    ]
    gate_pre = mul_nn(rows, wg)
    up_pre = mul_nn(rows, wu)
    grad_act = mul_nn(grads, wd)
    sig = 1.0 / (1.0 + jnp.exp(-gate_pre))
    silu = gate_pre * sig
    act = (silu * up_pre).astype(bf16)
    act_ref[...] = act
    grad_gate = (grad_act * up_pre * sig * (1.0 + gate_pre * (1.0 - sig))).astype(bf16)
    grad_up = (grad_act * silu).astype(bf16)
    dg_ref[...] = grad_gate
    du_ref[...] = grad_up
    out_sum[...] += mul_nt(act, wd)
    back_sum[...] += mul_nt(grad_gate, wg) + mul_nt(grad_up, wu)

    @pl.when(step == n_groups - 1)
    def _():
        gates = x_ref[:, d : d + 1].astype(f32) + x_ref[:, d + 1 : d + 2].astype(f32)
        gx_ref[...] = jnp.transpose((rows.astype(f32) * gates).astype(bf16))
        gg_ref[...] = jnp.transpose((grads.astype(f32) * gates).astype(bf16))
        low = out_sum[...].astype(bf16)
        out_ref[...] = low.reshape(out_ref.shape)
        dx_ref[:, :d] = back_sum[...].astype(bf16)
        dots = jnp.sum(grads.astype(f32) * low.astype(f32), axis=1, keepdims=True)
        high, rest = halves(dots)
        lane = lax.broadcasted_iota(jnp.int32, (n, PAIR), 1)
        pair = jnp.where(lane == 0, high.astype(f32), jnp.where(lane == 1, rest.astype(f32), 0.0))
        dx_ref[:, d:] = pair.astype(bf16)


def expert_call(part, x, g, groups, outs, name):
    n, wide = x.shape
    d = g.shape[-1]
    group = groups[0].shape
    cols = group[0] * group[3]
    ff = cols * len(groups)
    block = pl.BlockSpec((g.shape[0], 1) + g.shape[2:], lambda i: (0, part, 0, 0))
    passed = [] if outs is None else [outs]

    def whole(*shape):
        return pl.BlockSpec(shape, lambda i: (0,) * len(shape))

    def column(rows):
        return pl.BlockSpec((rows, cols), lambda i: (0, i))

    shapes = [(n, wide), (n, ff), (n, ff), (n, ff), (d, n), (d, n)]
    return pl.pallas_call(
        functools.partial(expert_kernel, len(groups)),
        grid=(len(groups),),
        in_specs=[whole(n, wide), block] + waits(groups) + waits(passed),
        out_specs=[block, whole(n, wide)] + [column(n)] * 3 + [whole(d, n)] * 2,
        out_shape=[jax.ShapeDtypeStruct(g.shape, bf16)] + [jax.ShapeDtypeStruct(shape, bf16) for shape in shapes],
        input_output_aliases={2 + len(groups): 0} if passed else {},
        scratch_shapes=[
            pltpu.VMEM((len(groups),) + group, bf16), pltpu.VMEM((n, d), f32), pltpu.VMEM((n, d), f32),
            pltpu.SemaphoreType.DMA((len(groups),)),
        ],
        compiler_params=pltpu.CompilerParams(vmem_limit_bytes=VMEM),
        cost_estimate=cost("expert"),
        name=name,
    )(x, g, *groups, *passed)


def expert_weights_kernel(plan, n_through, *refs):
    xs, ggs, acts, dgs, dus = [refs[2 * i : 2 * i + 2] for i in range(5)]
    out_refs = refs[10 + n_through :]
    step = pl.program_id(0)
    pieces, _, d, width = out_refs[0].shape
    for m, (left, right) in enumerate([(xs, dgs), (xs, dus), (ggs, acts)]):
        grad = mul_nn(
            jnp.concatenate([half[...] for half in left], axis=1), jnp.concatenate([half[...] for half in right], axis=0)
        )

        def write(ref):
            for p in range(pieces):
                ref[p, m] = grad[:, p * width : (p + 1) * width].astype(ref.dtype)

        first = 0
        for count, ref in zip(plan, out_refs):
            pl.when((step >= first) & (step < first + count))(functools.partial(write, ref))
            first += count


def expert_weights(flows, order, plan, pieces, width, kinds, name, through=None, deps=()):
    d, n = flows[0][0].shape
    cols = pieces * width
    rows = pl.BlockSpec((d, n), lambda i: (0, 0))
    flip = order[0] != 0

    def group(i):
        return len(order) - 1 - i if flip else i

    part = pl.BlockSpec((n, cols), lambda i: (0, group(i)))
    passed = [] if through is None else [through]
    blocks, first = [], 0
    for count in plan:
        blocks.append(
            pl.BlockSpec(
                (pieces, 3, d, width),
                lambda i, first=first, count=count: (jnp.clip(i - first, 0, count - 1), 0, 0, 0),
            )
        )
        first += count
    return pl.pallas_call(
        ordered(functools.partial(expert_weights_kernel, plan, len(passed)), 10 + len(passed), len(deps)),
        grid=(len(order),),
        in_specs=[rows] * 4 + [part] * 6 + waits(passed) + waits(deps),
        out_specs=blocks + waits(passed),
        out_shape=[
            jax.ShapeDtypeStruct((pieces * count, 3, d, width), kind) for count, kind in zip(plan, kinds)
        ]
        + [jax.ShapeDtypeStruct(p.shape, p.dtype) for p in passed],
        input_output_aliases={10: len(plan)} if passed else {},
        compiler_params=pltpu.CompilerParams(vmem_limit_bytes=VMEM),
        cost_estimate=cost(name),
        name=name,
    )(*[half for flow in flows for half in flow], *passed, *deps)


def weights_sent_kernel(near_ref, came_ref, *out_refs):
    first = 0
    for ref in out_refs:
        there = slice(first, first + ref.shape[2])
        ref[...] = near_ref[:, :, there] + came_ref[:, :, there]
        first += ref.shape[2]


def weights_sent(near, came):
    n, m, d, f = near.shape
    whole = pl.BlockSpec((2, m, d, f), lambda i: (i, 0, 0, 0))
    cuts = (d // 3, d - d // 3)
    return pl.pallas_call(
        weights_sent_kernel,
        grid=(n // 2,),
        in_specs=[whole] * 2,
        out_specs=[pl.BlockSpec((2, m, rows, f), lambda i: (i, 0, 0, 0)) for rows in cuts],
        out_shape=[jax.ShapeDtypeStruct((n, m, rows, f), bf16) for rows in cuts],
        compiler_params=pltpu.CompilerParams(vmem_limit_bytes=VMEM),
        cost_estimate=cost("weights_sent"),
        name="weights_sent",
    )(near, came)


def weights_sum_kernel(kept_ref, far_ref, near_ref, out_ref):
    out_ref[...] = (kept_ref[...].astype(f32) + far_ref[...].astype(f32) + near_ref[...].astype(f32)).astype(bf16)


def weights_sum(kept, far, near, first, deps):
    n, m, d, f = near.shape
    unit = kept.shape[2] // 3
    own = pl.BlockSpec((2, m, unit, f), lambda i, j: (i, 0, j, 0))
    some = pl.BlockSpec((2, m, unit, f), lambda i, j: (i, 0, first // unit + j, 0))
    return pl.pallas_call(
        ordered(weights_sum_kernel, 3, len(deps)),
        grid=(n // 2, d // unit),
        in_specs=[some, some, own] + waits(deps),
        out_specs=own,
        out_shape=jax.ShapeDtypeStruct(near.shape, bf16),
        compiler_params=pltpu.CompilerParams(vmem_limit_bytes=VMEM),
        cost_estimate=cost("weights_sum"),
        name="weights_sum",
    )(kept, far, near, *deps)


def lane_of(rows):
    return lax.broadcasted_iota(jnp.int32, (rows, PAIR), 1)


def col(rows, i):
    return rows[:, i : i + 1]


def halves(rows):
    high = rows.astype(bf16)
    return high, (rows - high.astype(f32)).astype(bf16)


VEC, COEF, GATE, CONST = 0, 2, 3, 5


def mid_kernel(
    n_all, att_ref, small_ref, wo_ref, x_ref, prev_ref, routes_ref, place_ref,
    mid_ref, hidden_ref, scal_ref, *send_refs,
):
    n_ffn = n_all - 4
    d = x_ref.shape[1]
    mid = x_ref[...].astype(f32) + mul_nn(att_ref[...], wo_ref[...])
    mid_ref[...] = mid
    hidden = (mid * rms_scale(mid) * gain_row(small_ref, n_all + 7)).astype(bf16)
    hidden_ref[...] = hidden
    rows, d = hidden.shape
    lane = lane_of(rows)
    raw = mul_nn(hidden, small_ref[...])
    logits = jnp.where(lane < n_all, raw + prev_ref[...], NEG)
    expo = jnp.exp(logits - jnp.max(logits, axis=1, keepdims=True))
    probs = jnp.where(lane < n_all, expo / jnp.sum(expo, axis=1, keepdims=True), 0.0)
    ids = [col(routes_ref[...], j) for j in range(2)]
    gates = [jnp.sum(jnp.where(lane == r, probs, 0.0), axis=1, keepdims=True) for r in ids]
    scal = probs
    coef = sum(jnp.where(r == n_ffn + 1, g, 0.0) for r, g in zip(ids, gates))
    base = n_all + 4
    for c in range(2):
        gap = col(raw, n_all + 2 * c + 1) - col(raw, n_all + 2 * c)
        first, second = 1.0 / (1.0 + jnp.exp(gap)), 1.0 / (1.0 + jnp.exp(-gap))
        const = sum(jnp.where(r == n_ffn + 2 + c, g, 0.0) for r, g in zip(ids, gates))
        coef += first * const
        scal = jnp.where(lane == n_all + 2 * c, first, scal)
        scal = jnp.where(lane == n_all + 2 * c + 1, second, scal)
        scal = jnp.where(lane == base + VEC + c, second * const, scal)
        scal = jnp.where(lane == base + CONST + c, const, scal)
        scal = jnp.where(lane == base + GATE + c, gates[c], scal)
    scal_ref[...] = jnp.where(lane == base + COEF, coef, scal)
    n_half = send_refs[0].shape[0]
    slots = n_half * len(send_refs)
    row = lax.broadcasted_iota(jnp.int32, (slots, rows), 0)
    hits = [(row == place_ref[j : j + 1, :]) for j in range(2)]
    both = jnp.where(hits[0] | hits[1], 1.0, 0.0).astype(bf16)
    rows_out = mul_nn(both, hidden).astype(bf16)
    extra = jnp.zeros((slots, PAIR), f32)
    for j in range(2):
        high, low = halves(gates[j])
        pair = jnp.where(lane == 0, high.astype(f32), jnp.where(lane == 1, low.astype(f32), 0.0))
        extra += mul_nn(jnp.where(hits[j], 1.0, 0.0).astype(bf16), pair.astype(bf16))
    for i, ref in enumerate(send_refs):
        ref[:, :d] = rows_out[i * n_half : (i + 1) * n_half]
        ref[:, d:] = extra[i * n_half : (i + 1) * n_half].astype(bf16)


def spread_kernel(cot_ref, valid_ref, place_ref, send_ref):
    grads = (cot_ref[...] * valid_ref[...]).astype(bf16)
    row = lax.broadcasted_iota(jnp.int32, (send_ref.shape[0], grads.shape[0]), 0)
    hit = (row == place_ref[0:1, :]) | (row == place_ref[1:2, :])
    send_ref[...] = mul_nn(jnp.where(hit, 1.0, 0.0).astype(bf16), grads).astype(bf16)


def picked_rows(place_ref, j, table):
    rows, slots = place_ref.shape[0], table.shape[0]
    slot = lax.broadcasted_iota(jnp.int32, (rows, slots), 1)
    pick = jnp.where(slot == col(place_ref[...], j), 1.0, 0.0).astype(bf16)
    return mul_nn(pick, table)


def gates_back_kernel(
    n_all, back_ref, more_ref, place_ref, routes_ref, scal_ref, hidden_ref, mid_ref, cot_ref, valid_ref, small_ref, wo_ref,
    gmid_ref, gatt_ref, mix_ref, dgain_ref,
):
    n_ffn = n_all - 4
    base = n_all + 4
    scal = scal_ref[...]
    grads = cot_ref[...] * valid_ref[...]
    rows, d = grads.shape
    lane = lane_of(rows)
    hidden = hidden_ref[...].astype(f32)
    small = small_ref[...]
    g_hidden = jnp.sum(grads * hidden, axis=1, keepdims=True)
    high, low = halves(grads)
    g_small = mul_nn(high, small) + mul_nn(low, small)
    table = jnp.concatenate([back_ref[...], more_ref[...]], axis=0)
    grad_hidden = col(scal, base + COEF) * grads
    grad_probs = jnp.zeros((rows, PAIR), f32)
    for j in range(2):
        r = col(routes_ref[...], j)
        came = picked_rows(place_ref, j, table)
        grad_hidden += col(scal, base + GATE + j) * came[:, :d]
        dots = came[:, d : d + 1] + came[:, d + 1 : d + 2]
        dots += jnp.where(r == n_ffn + 1, g_hidden, 0.0)
        for c in range(2):
            whole = col(scal, n_all + 2 * c) * g_hidden + col(scal, n_all + 2 * c + 1) * col(g_small, base + c)
            dots += jnp.where(r == n_ffn + 2 + c, whole, 0.0)
        grad_probs += jnp.where(lane == r, dots, 0.0)
    probs = jnp.where(lane < n_all, scal, 0.0)
    mix = probs * (grad_probs - jnp.sum(probs * grad_probs, axis=1, keepdims=True))
    for c in range(2):
        first, second = col(scal, n_all + 2 * c), col(scal, n_all + 2 * c + 1)
        const = col(scal, base + CONST + c)
        a, b = const * g_hidden, const * col(g_small, base + c)
        inner = first * a + second * b
        mix = jnp.where(lane == n_all + 2 * c, first * (a - inner), mix)
        mix = jnp.where(lane == n_all + 2 * c + 1, second * (b - inner), mix)
    mix_ref[...] = mix
    high, low = halves(mix)
    grad_hidden += mul_nt(high, small) + mul_nt(low, small)
    mid = mid_ref[...]
    back, dgain = rms_backward(mid, rms_scale(mid), gain_row(small_ref, n_all + 7), grad_hidden)
    dgain_ref[...] = dgain
    grad_mid = grads + back
    gmid_ref[...] = grad_mid
    gatt_ref[...] = mul_nt(grad_mid.astype(bf16), wo_ref[...]).astype(bf16)


def out_grads_kernel(
    n_all, block, core_ref, att_ref, gmid_ref, hidden_ref, mix_ref, scal_ref, cot_ref, valid_ref, dgain_ref, keep_ref, give_ref,
):
    d = att_ref.shape[1]
    base = n_all + 4
    upper = core_ref[0] == 1
    dw_out = mul_tn(att_ref[...], gmid_ref[...].astype(bf16))
    keep_ref[:, :d], give_ref[:, :d] = split_rows(upper, dw_out, block)
    hidden = hidden_ref[...]
    high, low = halves(mix_ref[...])
    grads = mul_tn(hidden, high) + mul_tn(hidden, low)
    scal = scal_ref[...]
    lane = lane_of(scal.shape[0])
    vec = jnp.where((lane >= base + VEC) & (lane < base + VEC + 2), scal, 0.0)
    vec_high, vec_low = halves(vec)
    g_high, g_low = halves(cot_ref[...] * valid_ref[...])
    grads += mul_tn(g_high, vec_high) + mul_tn(g_high, vec_low) + mul_tn(g_low, vec_high)
    column = jnp.transpose(jnp.broadcast_to(dgain_ref[...], (8, d)))[:, :1]
    tail = jnp.where(lane_of(d) == base + 2, column, grads)
    keep_ref[:, d:], give_ref[:, d:] = split_rows(upper, tail, block)


def output_kernel(n_all, back_ref, place_ref, scal_ref, hidden_ref, mid_ref, valid_ref, small_ref, out_ref):
    base = n_all + 4
    scal = scal_ref[...]
    lane = lane_of(scal.shape[0])
    vec = jnp.where((lane >= base + VEC) & (lane < base + VEC + 2), scal, 0.0)
    high, low = halves(vec)
    small = small_ref[...]
    total = mid_ref[...] + mul_nt(high, small) + mul_nt(low, small)
    total += col(scal, base + COEF) * hidden_ref[...].astype(f32)
    table = back_ref[...]
    for j in range(2):
        total += col(scal, base + GATE + j) * picked_rows(place_ref, j, table)
    out_ref[...] = total * valid_ref[...]


def local(
    residual_in,
    lengths,
    routes,
    prev_logits,
    cotangent,
    w_qkv,
    w_out,
    attn_gain,
    ffn_gain,
    router,
    const_gate,
    const_vec,
    w_gate,
    w_up,
    w_down,
):
    tok_rows = residual_in.shape[1]
    feat = residual_in.shape[2]
    head_size = feat // HEADS
    score_scale = head_size ** (-0.5)
    n_dp = lax.axis_size("dp")
    n_ctx = lax.axis_size("ctx")
    n_exp = lax.axis_size("exp")
    own_exp = w_gate.shape[0]
    reps = n_dp // own_exp
    n_all = router.shape[1]
    n_ffn = n_all - 4
    cap_rows = tok_rows // 4
    sub_rows = cap_rows // reps
    n_slots = n_ffn * cap_rows
    ctx_rank = lax.axis_index("ctx")
    positions = ctx_rank * tok_rows + jnp.arange(tok_rows, dtype=jnp.int32)
    length = lengths[0]
    valid_rows = (positions < length).astype(f32)[:, None]

    def gather_ctx(rows):
        if n_ctx == 2:
            return swap(rows, "ctx", 1)
        for bit in reversed(bits_of("ctx")):
            other = swap(rows, "ctx", bit)
            upper = (ctx_rank & bit) != 0
            rows = jnp.concatenate([jnp.where(upper, other, rows), jnp.where(upper, rows, other)], axis=0)
        return rows

    def scatter_ctx(rows):
        if n_ctx == 2:
            return swap(rows, "ctx", 1)
        for bit in bits_of("ctx"):
            low, high = jnp.split(rows, 2, axis=0)
            upper = (ctx_rank & bit) != 0
            sent = jnp.where(upper, low, high).astype(bf16)
            rows = jnp.where(upper, high, low).astype(f32) + swap(sent, "ctx", bit).astype(f32)
        return rows

    route_ids = routes[0]
    choose = (route_ids[:, :, None] == jnp.arange(n_all, dtype=jnp.int32)[None, None, :]).astype(f32)
    both = jnp.sum(choose, axis=1)
    before = jnp.arange(tok_rows)
    before = (before[None, :] < before[:, None]).astype(bf16)
    counts = dot32(before, both.astype(bf16))
    slot_ids = jnp.sum(choose * counts[:, None, :], axis=-1).astype(jnp.int32)
    is_ffn = route_ids < n_ffn
    place = (
        ((route_ids % own_exp) * reps + slot_ids // sub_rows) * n_exp + route_ids // own_exp
    ) * sub_rows + slot_ids % sub_rows
    half_rows = sub_rows // 2
    place_half = (
        (place // half_rows % 2) * (n_slots // 2) + place // sub_rows * half_rows + place % half_rows
    )
    place = jnp.where(is_ffn, place, -1)
    place_half = jnp.where(is_ffn, place_half, -1)
    row_ids = jnp.arange(n_slots, dtype=jnp.int32)
    place_rows = jnp.transpose(place)

    def to_experts(rows):
        return lax.all_to_all(
            rows.reshape(n_dp * n_exp, rows.shape[0] // (n_dp * n_exp), -1),
            ("dp", "exp"),
            split_axis=0,
            concat_axis=0,
            tiled=True,
        ).reshape(rows.shape[0], -1)

    width = 2 * feat
    far, mid_a, near = plan_steps(("ctx", "exp"))
    _, mid_b, _ = plan_steps(("exp", "ctx"))
    lane = jnp.arange(PAIR, dtype=jnp.int32)
    half = head_size // 2
    inv_freq = 10000.0 ** (-2.0 * (lane % half).astype(f32) / head_size)
    sign = jnp.where(lane % head_size < half, -1.0, 1.0)

    def turns(where):
        angles = where.astype(f32)[:, None] * inv_freq[None, :]
        return jnp.cos(angles), jnp.sin(angles) * sign[None, :]

    cosine, sine = turns(positions)
    other_start = (1 - ctx_rank) * tok_rows if n_ctx == 2 else 0
    n_other = tok_rows if n_ctx == 2 else tok_rows * n_ctx
    other_cos, other_sin = turns(other_start + jnp.arange(n_other, dtype=jnp.int32))
    other_in = gather_ctx(residual_in[0])
    (rows,) = simple_call(
        rows_kernel, (w_qkv, w_out, router.T, const_gate.T, const_vec.T, attn_gain[None], ffn_gain[None]),
        [((w_out.shape[0], 4 * feat + PAIR), bf16)], 0, "rows",
    )
    packed = pack_expert(w_gate, w_up, w_down, (rows,))
    tables = (cosine, sine, other_cos, other_sin)
    if len(far) == 2:
        whole, placed = gather_far(rows, far, (packed,) + tables)
    else:
        whole, placed = gather_steps(rows, [], far)
    group = trade_far(packed)
    part_a, part_b = whole[..., :width], whole[..., width:]
    placed_a, placed_b = placed, placed
    for i, (step_a, step_b) in enumerate(zip(mid_a, mid_b)):
        meanwhile = (other_in,) if i == 0 else ()
        if i + 1 == len(mid_a):
            (grad_sent,) = simple_call(
                spread_kernel, (cotangent[0], valid_rows, place_rows), [((n_slots, feat), bf16)], 0, "spread", (part_b,)
            )
            meanwhile = (grad_sent,)
        part_a, placed_a = gather_step(part_a, placed_a, *step_a)
        part_b, placed_b = gather_step(part_b, placed_b, *step_b, meanwhile)
    first_part, _ = gather_steps(part_a, placed_a, near)
    second_part, _ = gather_steps(part_b, placed_b, near)
    first_part = first_part.reshape(feat, width)
    second_part = second_part.reshape(feat, 2 * feat + PAIR)

    small_at = 2 * feat // PAIR
    w_v, w_o, small = column(second_part, feat, 0), column(second_part, feat, 1), column(second_part, PAIR, small_at)
    rows_low = ((tok_rows, feat), bf16)
    rows_full = ((tok_rows, feat), f32)
    square = 2 * tok_rows * feat * feat
    hidden_one, queries, own_keys, own_values = simple_call(
        functools.partial(project_kernel, score_scale, n_all + 6),
        (residual_in[0], first_part, w_v, small, cosine, sine), [rows_low] * 4, 3 * square, "project",
    )
    tok_spec = pl.BlockSpec((tok_rows, feat), lambda i: (i, 0))
    turn_spec = pl.BlockSpec((tok_rows, PAIR), lambda i: (i, 0))

    def fixed(rows, cols, index=0):
        return pl.BlockSpec((rows, cols), lambda i: (0, index))

    other_hidden, other_keys, other_values = pl.pallas_call(
        functools.partial(other_project_kernel, n_all + 6),
        grid=(n_other // tok_rows,),
        in_specs=[tok_spec, fixed(feat, feat, 1), fixed(feat, PAIR, small_at), fixed(feat, feat), turn_spec, turn_spec],
        out_specs=[tok_spec] * 3,
        out_shape=[jax.ShapeDtypeStruct((n_other, feat), bf16)] * 3,
        compiler_params=pltpu.CompilerParams(vmem_limit_bytes=VMEM),
        cost_estimate=cost("project_other"),
        name="project_other",
    )(other_in, first_part, second_part, second_part, other_cos, other_sin)
    grad_rows_in = to_experts(hold(grad_sent, group, other_keys))
    info = jnp.stack([ctx_rank * tok_rows, length, ctx_rank]).astype(jnp.int32)
    prev = jnp.pad(prev_logits[0], ((0, 0), (0, PAIR - n_all)))
    attended, attended_low, log_total = attend(
        info, queries, own_keys, own_values, other_keys, other_values, (group, prev, place, place_half)
    )

    mid_rows, hidden, scalars, *sent_rows = simple_call(
        functools.partial(mid_kernel, n_all),
        (attended_low, small, w_o, residual_in[0], prev, route_ids, jnp.transpose(place_half)),
        [rows_full, rows_low, ((tok_rows, PAIR), f32)] + [((n_slots // 2, feat + PAIR), bf16)] * 2, 0, "mid",
    )
    rows_in = [to_experts(hold(sent_rows[0], grad_rows_in)), to_experts(sent_rows[1])]

    steps_near = near_steps(own_exp)
    groups = gather_expert_near([group], steps_near)
    piece_width = group.shape[3]
    if piece_width < PAIR:
        merge = PAIR // piece_width
        whole = jnp.concatenate(groups).reshape(-1, merge, 3, feat, piece_width)
        groups = [jnp.moveaxis(whole, 1, 3).reshape(-1, 3, feat, PAIR)]
    grads_in = grad_rows_in.reshape(n_dp * n_exp, 2, half_rows, feat)
    expert_out = None
    flows, back_grads = [], []
    for part in range(2):
        expert_out, grad_in, *flow = expert_call(part, rows_in[part], grads_in, groups, expert_out, f"expert_{part}")
        back_grads.append(to_experts(grad_in))
        flows.append(flow)
    expert_out = expert_out.reshape(n_slots, feat)
    n_groups = 2 ** len(steps_near)
    act, grad_gate_pre, grad_up_pre, gated_rows, grad_expert_out = zip(*flows)
    flows = (gated_rows, grad_expert_out, act, grad_gate_pre, grad_up_pre)
    simple = piece_width >= PAIR and len(steps_near) == 2
    if simple:
        far_near, far_kept, near_own, kept, expert_out = expert_weights(
            flows, (3, 2, 1, 0), (1, 1, 1, 1), own_exp, piece_width, (bf16,) * 4, "weights_all", expert_out,
            (back_grads[0],),
        )
        far_near = swap(hold(far_near, back_grads[1]), *steps_near[1])
        far_kept = swap(hold(far_kept, back_grads[1]), *steps_near[1])
        near_sent = weights_sent(near_own, far_near)
        near_came = [swap(part, *steps_near[0]) for part in near_sent]
    else:
        step = max(piece_width, PAIR)
        n_steps = act[0].shape[1] // step
        (whole,) = expert_weights(flows, tuple(range(n_steps)), (n_steps,), 1, step, (f32,), "weights_all")
        if piece_width < PAIR:
            whole = jnp.moveaxis(whole.reshape(-1, 3, feat, merge, piece_width), 3, 1)
        whole = whole.reshape(n_groups, own_exp, 3, feat, piece_width)
        expert_sum = scatter_expert_near([whole[i] for i in range(n_groups)], steps_near)
    back_rows = to_experts(expert_out)
    small_shape = ((tok_rows, PAIR), f32)
    grad_mid, grad_attended, grad_mix, grad_gain_two = simple_call(
        functools.partial(gates_back_kernel, n_all),
        (
            *back_grads, place_half, route_ids, scalars, hidden, mid_rows, cotangent[0], valid_rows, small, w_o,
        ),
        [rows_full, rows_low, small_shape, ((1, feat), f32)], 0, "gates_back", tuple(near_sent) if simple else (),
    )
    grad_queries, other_dk, other_dv, delta = grads_other(
        info, queries, other_keys, other_values, grad_attended, attended, log_total, ()
    )
    core = (lax.axis_index("dp") & 1).astype(jnp.int32).reshape(1)
    core_block = feat // (n_dp * n_ctx * n_exp) * row_weight("dp")
    other_gk, other_dh, more_gain = pl.pallas_call(
        other_back_kernel,
        grid=(n_other // tok_rows,),
        in_specs=[tok_spec, tok_spec, fixed(feat, feat, 1), fixed(feat, feat), turn_spec, turn_spec, tok_spec],
        out_specs=[tok_spec, tok_spec, fixed(1, feat)],
        out_shape=[
            jax.ShapeDtypeStruct((n_other, feat), bf16), jax.ShapeDtypeStruct((n_other, feat), bf16),
            jax.ShapeDtypeStruct((1, feat), f32),
        ],
        compiler_params=pltpu.CompilerParams(vmem_limit_bytes=VMEM),
        cost_estimate=cost("back_other"),
        name="back_other",
    )(other_dk, other_dv, first_part, second_part, other_cos, other_sin, other_in)
    more_dh = scatter_ctx(other_dh)
    if simple:
        sum_first = weights_sum(kept, far_kept, near_came[0], 0, (other_dh,))
    else:
        sum_first, sum_rest = jnp.split(expert_sum.astype(bf16), [feat // 3], axis=2)
    back_first = trade_far(sum_first)
    grad_queries, own_dk, own_dv = grads_own(
        info, queries, own_keys, own_values, grad_attended, log_total, delta, grad_queries, (back_rows, sum_first)
    )
    half_rows = feat // 2
    out_keep, out_give = simple_call(
        functools.partial(out_grads_kernel, n_all, core_block),
        (attended_low, grad_mid, hidden, grad_mix, scalars, cotangent[0], valid_rows, grad_gain_two),
        [((half_rows, feat + PAIR), f32), ((half_rows, feat + PAIR), bf16)], 0, "out_grads", (own_dk,), (core,),
    )

    if simple:
        sum_rest = weights_sum(kept, far_kept, near_came[1], feat // 3, (out_keep,))
    back_rest = trade_far(sum_rest)
    own_args = (
        core, grad_queries, hidden_one, first_part, second_part, cosine, sine, more_gain, own_dk, other_hidden, other_gk, own_dv,
        other_dv, residual_in[0],
    )
    own_deps = (sum_rest, back_first)
    token, turn = fixed(tok_rows, feat), fixed(tok_rows, PAIR)
    q_keep, q_give, k_keep, k_give, v_keep, v_give, grad_hidden_one = pl.pallas_call(
        ordered(functools.partial(own_back_kernel, score_scale, core_block), len(own_args), len(own_deps)),
        grid=(3,),
        in_specs=[pl.BlockSpec(memory_space=pltpu.SMEM)] + [token] * 2
        + [pl.BlockSpec((feat, feat), lambda i: (0, jnp.minimum(i, 1))), fixed(feat, feat), turn, turn, fixed(1, feat)]
        + waits(own_args[-6:]) + waits(own_deps),
        scratch_shapes=[pltpu.VMEM(arg.shape, bf16) for arg in own_args[-6:]] + [pltpu.SemaphoreType.DMA((6,))],
        out_specs=[fixed(half_rows, feat)] * 4 + [fixed(half_rows, feat + PAIR)] * 2 + [token],
        out_shape=[
            jax.ShapeDtypeStruct((half_rows, feat), f32), jax.ShapeDtypeStruct((half_rows, feat), bf16),
            jax.ShapeDtypeStruct((half_rows, feat), f32), jax.ShapeDtypeStruct((half_rows, feat), bf16),
            jax.ShapeDtypeStruct((half_rows, feat + PAIR), f32), jax.ShapeDtypeStruct((half_rows, feat + PAIR), bf16),
            jax.ShapeDtypeStruct((tok_rows, feat), f32),
        ],
        compiler_params=pltpu.CompilerParams(vmem_limit_bytes=VMEM),
        cost_estimate=cost("back_own"),
        name="back_own",
    )(*own_args, *own_deps)
    def last_rows(sent):
        (output,) = simple_call(
            functools.partial(output_kernel, n_all),
            (back_rows, place, scalars, hidden, mid_rows, valid_rows, small), [rows_full], 0, "output", tuple(sent),
        )
        (grad_x,) = simple_call(
            functools.partial(first_norm_kernel, n_all + 6),
            (grad_hidden_one, more_dh, residual_in[0], small, grad_mid), [rows_full], 0, "first_norm", (output,),
        )
        results.extend([output, grad_x, *unpack_expert(back_first, back_rest, (output, grad_x))])
        return results

    results = []
    dw_qkv, dw_out, *narrow = scatter_parts(
        [
            [(q_keep, q_give, feat, 0), (k_keep, k_give, feat, 0)],
            [(v_keep, v_give, feat + PAIR, 0), (out_keep, out_give, feat + PAIR, 0)],
        ],
        [mid_a, mid_b], far, near, w_out.shape[0], (more_dh,), last_rows, (3 * feat, feat), (n_all, 4, 2, 1, 1),
    )
    output, grad_x, *expert_grads = results
    return (
        output[None],
        grad_x[None],
        dw_qkv,
        dw_out,
        narrow[4][0],
        narrow[3][0],
        narrow[0].T,
        narrow[1].T,
        narrow[2].T,
        expert_grads[0],
        expert_grads[1],
        expert_grads[2],
    )


def solution(mesh):
    in_specs = (
        P(("dp", "exp"), "ctx", None),
        P(("dp", "exp")),
        P(("dp", "exp"), "ctx", None),
        P(("dp", "exp"), "ctx", None),
        P(("dp", "exp"), "ctx", None),
        P(("dp", "ctx", "exp"), None),
        P(("dp", "ctx", "exp"), None),
        P(("dp", "ctx", "exp")),
        P(("dp", "ctx", "exp")),
        P(("dp", "ctx", "exp"), None),
        P(("dp", "ctx", "exp"), None),
        P(("dp", "ctx", "exp"), None),
        P("exp", None, ("dp", "ctx")),
        P("exp", None, ("dp", "ctx")),
        P("exp", ("dp", "ctx"), None),
    )
    out_specs = (
        P(("dp", "exp"), "ctx", None),
        P(("dp", "exp"), "ctx", None),
        P(("dp", "ctx", "exp"), None),
        P(("dp", "ctx", "exp"), None),
        P(("dp", "ctx", "exp")),
        P(("dp", "ctx", "exp")),
        P(("dp", "ctx", "exp"), None),
        P(("dp", "ctx", "exp"), None),
        P(("dp", "ctx", "exp"), None),
        P("exp", None, ("dp", "ctx")),
        P("exp", None, ("dp", "ctx")),
        P("exp", ("dp", "ctx"), None),
    )
    return jax.shard_map(local, mesh=mesh, in_specs=in_specs, out_specs=out_specs, check_vma=False)
```

```python
import functools

import jax
import jax.numpy as jnp
from jax import lax
from jax.experimental import pallas as pl
from jax.experimental.pallas import tpu as pltpu
from jax.sharding import PartitionSpec as P

HEADS = 12

norm_eps = 1e-06
top_precision = lax.Precision.HIGHEST
f32 = jnp.float32
bf16 = jnp.bfloat16


CHUNK = 256
BLOCK = 512
OCHUNK = 512
QCHUNK = 128
PAIR = 128
NEG = -1e30
SCALE = 48
VMEM = 62 << 20
MICROS = {
    "project": 6, "project_other": 5, "spread": 4, "attend": 17, "mid": 9, "expert": 30, "weights_sent": 0,
    "weights_near": 0, "weights_kept": 0, "weights_sum": 0, "gates_back": 0, "grads_other": 0, "back_other": 0, "grads_own": 0,
    "back_own": 0, "out_grads": 0, "output": 6, "first_norm": 4, "weights_all": 26, "pack": 3, "unpack": 4, "combine": 1, "rows": 2, "sums": 1,
}


def cost(name):
    return pl.CostEstimate(flops=MICROS[name] * 1000000000 // SCALE, bytes_accessed=1, transcendentals=0)


def mul_nt(a, b):
    return lax.dot_general(a, b, (((1,), (1,)), ((), ())), preferred_element_type=f32)


def mul_nn(a, b):
    return lax.dot_general(a, b, (((1,), (0,)), ((), ())), preferred_element_type=f32)


def mul_tn(a, b):
    return lax.dot_general(a, b, (((0,), (0,)), ((), ())), preferred_element_type=f32)


def head_part(rows, head):
    lane = lax.broadcasted_iota(jnp.int32, rows.shape, 1)
    return jnp.where((lane >= PAIR // 2) == (head == 1), rows, jnp.zeros_like(rows))


def key_allowed(shape, key_start, length, query_start=None):
    key = key_start + lax.broadcasted_iota(jnp.int32, shape, 0)
    allowed = key < length
    if query_start is not None:
        allowed &= key <= query_start + lax.broadcasted_iota(jnp.int32, shape, 1)
    return allowed


def both_heads(rows, first=0):
    return jnp.concatenate([head_part(rows[first:], head) for head in range(2)], axis=0)


def beside(row_pair):
    return jnp.concatenate([row_pair[0:1], row_pair[1:2]], axis=1)


def split_heads(wide):
    half, t = PAIR // 2, wide.shape[1] // 2
    return jnp.concatenate([wide[:half, :t], wide[half:, t:]], axis=0)


def attend_kernel(info, q_ref, k_ref, v_ref, ok_ref, ov_ref, out_ref, low_ref, log_ref):
    base, length, blocks = info[0], info[1], info[2]
    queries = q_ref[...]
    rows = queries.shape[0]
    half = PAIR // 2
    starts = list(range(0, rows, QCHUNK))
    twice = [both_heads(queries[first : first + QCHUNK]) for first in starts]

    def spread(row):
        n = row.shape[1] // 2
        return jnp.concatenate(
            [jnp.broadcast_to(row[:, :n], (half, n)), jnp.broadcast_to(row[:, n:], (half, n))], axis=0
        )

    scores, tops, states = [], [], []
    for first, part in zip(starts, twice):
        end = first + QCHUNK
        some = mul_nt(k_ref[:end, :], part)
        allowed = key_allowed((end, QCHUNK), base, length, base + first)
        scores.append(jnp.where(jnp.concatenate([allowed, allowed], axis=1), some, NEG))
    for some in scores:
        tops.append(jnp.max(some, axis=0, keepdims=True))
    for first, some, top in zip(starts, scores, tops):
        expo = jnp.exp(some - top)
        total = jnp.sum(expo, axis=0, keepdims=True)
        acc = split_heads(mul_tn(v_ref[: first + QCHUNK, :], expo.astype(bf16)))
        states.append((top, total, acc))

    def step(c, states):
        first = pl.multiple_of(c * BLOCK, BLOCK)
        keys = ok_ref[pl.ds(first, BLOCK), :]
        vals = ov_ref[pl.ds(first, BLOCK), :]
        allowed = key_allowed((BLOCK, 2 * QCHUNK), first, length)
        scores = [jnp.where(allowed, mul_nt(keys, part), NEG) for part in twice]
        new = []
        for some, (top, total, acc) in zip(scores, states):
            new_top = jnp.maximum(top, jnp.max(some, axis=0, keepdims=True))
            expo = jnp.exp(some - new_top)
            factor = jnp.exp(top - new_top)
            total = total * factor + jnp.sum(expo, axis=0, keepdims=True)
            acc = acc * spread(factor) + split_heads(mul_tn(vals, expo.astype(bf16)))
            new.append((new_top, total, acc))
        return tuple(new)

    states = lax.fori_loop(0, blocks, step, tuple(states))
    for first, (top, total, acc) in zip(starts, states):
        there = slice(first, first + QCHUNK)
        out = jnp.transpose(acc / spread(total))
        out_ref[there, :] = out
        low_ref[there, :] = out.astype(bf16)
        log = top + jnp.log(total)
        log_ref[0, 0:1, there] = log[:, :QCHUNK]
        log_ref[0, 1:2, there] = log[:, QCHUNK:]


def pair_grads(keys, vals, twice, grad_twice, log_row, delta_row, allowed):
    probs = jnp.where(allowed, jnp.exp(mul_nt(keys, twice) - log_row), 0.0)
    grad_probs = mul_nt(vals, grad_twice)
    grad_scores = (probs * (grad_probs - delta_row)).astype(bf16)
    return (
        mul_nn(grad_scores, twice),
        mul_nn(probs.astype(bf16), grad_twice),
        split_heads(mul_tn(keys, grad_scores)),
    )


def other_backward(
    info, q_ref, k_ref, v_ref, grad_ref, out_ref, log_ref, dq_ref, dk_ref, dv_ref, delta_ref
):
    length, chunks = info[1], info[2] * (BLOCK // OCHUNK)
    half = PAIR // 2
    queries, grads = q_ref[...], grad_ref[...]
    rows = queries.shape[0]
    product = jnp.transpose(grads.astype(f32) * out_ref[...])
    twice, grad_twice = both_heads(queries), both_heads(grads)
    for head in range(2):
        delta_ref[0, head : head + 1, :] = jnp.sum(
            product[head * half : (head + 1) * half], axis=0, keepdims=True
        )
    log_row, delta_row = beside(log_ref[0]), beside(delta_ref[0])

    def step(c, dq):
        first = pl.multiple_of(c * OCHUNK, OCHUNK)
        keys = k_ref[pl.ds(first, OCHUNK), :]
        vals = v_ref[pl.ds(first, OCHUNK), :]
        allowed = key_allowed((OCHUNK, 2 * rows), first, length)
        dk, dv, more = pair_grads(keys, vals, twice, grad_twice, log_row, delta_row, allowed)
        dk_ref[pl.ds(first, OCHUNK), :] = dk.astype(dk_ref.dtype)
        dv_ref[pl.ds(first, OCHUNK), :] = dv.astype(dv_ref.dtype)
        return dq + more

    dq_ref[...] = lax.fori_loop(0, chunks, step, jnp.zeros((PAIR, rows), f32))

    def clear(c, none):
        first = pl.multiple_of(c * OCHUNK, OCHUNK)
        dk_ref[pl.ds(first, OCHUNK), :] = jnp.zeros((OCHUNK, PAIR), dk_ref.dtype)
        dv_ref[pl.ds(first, OCHUNK), :] = jnp.zeros((OCHUNK, PAIR), dv_ref.dtype)
        return none

    lax.fori_loop(chunks, k_ref.shape[0] // OCHUNK, clear, 0)


def own_backward(
    info, q_ref, k_ref, v_ref, grad_ref, log_ref, delta_ref, before_ref, dq_ref, dk_ref, dv_ref
):
    base, length = info[0], info[1]
    queries, grads = q_ref[...], grad_ref[...]
    rows = queries.shape[0]
    dq = before_ref[...]
    for first in range(0, rows, CHUNK):
        keys = k_ref[first : first + CHUNK, :]
        vals = v_ref[first : first + CHUNK, :]
        allowed = key_allowed((CHUNK, rows - first), base + first, length, base + first)
        dk, dv, more = pair_grads(
            keys,
            vals,
            both_heads(queries, first),
            both_heads(grads, first),
            beside(log_ref[0, :, first:]),
            beside(delta_ref[0, :, first:]),
            jnp.concatenate([allowed, allowed], axis=1),
        )
        dk_ref[first : first + CHUNK, :] = dk.astype(dk_ref.dtype)
        dv_ref[first : first + CHUNK, :] = dv.astype(dv_ref.dtype)
        if first:
            more = jnp.concatenate([jnp.zeros((PAIR, first), f32), more], axis=1)
        dq = dq + more
    dq_ref[...] = jnp.transpose(dq).astype(dq_ref.dtype)


def per_pair(rows):
    return pl.BlockSpec((rows, PAIR), lambda i, info: (0, i))


def turned(cols):
    return pl.BlockSpec((PAIR, cols), lambda i, info: (i, 0))


def stats(cols):
    return pl.BlockSpec((1, 2, cols), lambda i, info: (i, 0, 0))


def ordered(kernel, n_in, n_deps):
    if not n_deps:
        return kernel

    def run(*refs):
        kernel(*refs[:n_in], *refs[n_in + n_deps :])

    return run


def waits(deps):
    return [pl.BlockSpec(memory_space=pl.ANY)] * len(deps)


def attn_call(kernel, info, args, in_specs, outs, out_specs, flops, name, deps=()):
    return pl.pallas_call(
        ordered(kernel, 1 + len(args), len(deps)),
        grid_spec=pltpu.PrefetchScalarGridSpec(
            num_scalar_prefetch=1,
            grid=(HEADS // 2,),
            in_specs=in_specs + waits(deps),
            out_specs=out_specs,
        ),
        out_shape=[jax.ShapeDtypeStruct(s, d) for s, d in outs],
        compiler_params=pltpu.CompilerParams(vmem_limit_bytes=VMEM),
        cost_estimate=cost(name),
        name=name,
    )(info, *args, *deps)


def attend(info, q, k, v, other_k, other_v, deps):
    t, d = q.shape
    st = (HEADS // 2, 2, t)
    n = other_k.shape[0]
    return attn_call(
        attend_kernel, info, (q, k, v, other_k, other_v),
        [per_pair(t)] * 3 + [per_pair(n)] * 2,
        [((t, d), f32), ((t, d), bf16), (st, f32)], [per_pair(t), per_pair(t), stats(t)], 8 * t * t * d, "attend", deps,
    )


def grads_other(info, q, k, v, grad, out, log_total, deps):
    t, d = q.shape
    n = k.shape[0]
    return attn_call(
        other_backward, info, (q, k, v, grad, out, log_total),
        [per_pair(t), per_pair(n), per_pair(n), per_pair(t), per_pair(t), stats(t)],
        [((d, t), f32), ((n, d), bf16), ((n, d), bf16), ((HEADS // 2, 2, t), f32)],
        [turned(t), per_pair(n), per_pair(n), stats(t)], 10 * t * t * d, "grads_other", deps,
    )


def grads_own(info, q, k, v, grad, log_total, delta, before, deps):
    t, d = q.shape
    return attn_call(
        own_backward, info, (q, k, v, grad, log_total, delta, before),
        [per_pair(t)] * 4 + [stats(t)] * 2 + [turned(t)],
        [((t, d), bf16)] * 3, [per_pair(t)] * 3, 10 * t * t * d, "grads_own", deps,
    )


def dot32(a, b, dims=((1,), (0,)), precision=None):
    return lax.dot_general(a, b, (dims, ((), ())), precision=precision, preferred_element_type=f32)


def swap(block, axis, bit):
    return lax.ppermute(block, axis, [(i, i ^ bit) for i in range(lax.axis_size(axis))])


def bits_of(axis, low=1, high=None):
    high = lax.axis_size(axis) if high is None else high
    found = []
    while low < high:
        found.append(low)
        low *= 2
    return found[::-1]


def row_weight(axis):
    x = lax.axis_size("exp")
    c = lax.axis_size("ctx")
    return {"exp": 1, "ctx": x, "dp": x * c}[axis]


def plan_steps(middle):
    far = [("dp", bit) for bit in bits_of("dp", 2)]
    mid = [(axis, bit) for axis in middle for bit in bits_of(axis)]
    near = [("dp", bit) for bit in bits_of("dp", 1, 2)]
    return far, mid, near


def row_bits(steps):
    return sorted([row_weight(axis) * bit for axis, bit in steps], reverse=True)


def nothing(*refs):
    pass


def hold(value, *others):
    return pl.pallas_call(
        nothing,
        in_specs=waits((value,) + others),
        out_specs=waits((value,))[0],
        out_shape=jax.ShapeDtypeStruct(value.shape, value.dtype),
        input_output_aliases={0: 0},
        cost_estimate=pl.CostEstimate(flops=0, bytes_accessed=0, transcendentals=0),
        name="hold",
    )(value, *others)


def rows_kernel(wqkv_ref, wout_ref, *refs):
    out_ref = refs[-1]
    d = wout_ref.shape[1]
    out_ref[:, : 3 * d] = wqkv_ref[...]
    out_ref[:, 3 * d : 4 * d] = wout_ref[...]
    small = jnp.zeros((wout_ref.shape[0], PAIR), f32)
    first = 0
    for ref in refs[:-1]:
        shape = (ref.shape[0], PAIR)
        here = lax.broadcasted_iota(jnp.int32, shape, 0) + first == lax.broadcasted_iota(jnp.int32, shape, 1)
        small += mul_tn(ref[...], jnp.where(here, 1.0, 0.0).astype(bf16))
        first += ref.shape[0]
    out_ref[:, 4 * d :] = small.astype(bf16)


def gather_step(whole, placed, axis, bit, meanwhile=()):
    other = swap(whole, axis, bit)
    if meanwhile:
        whole = hold(whole, *meanwhile)
    upper = (lax.axis_index(axis) & bit) != 0
    weight = row_weight(axis) * bit
    pos = sum(1 for w in placed if w > weight)
    both = [jnp.where(upper, other, whole), jnp.where(upper, whole, other)]
    return jnp.stack(both, axis=pos), placed[:pos] + [weight] + placed[pos:]


def gather_steps(whole, placed, steps):
    for axis, bit in steps:
        whole, placed = gather_step(whole, placed, axis, bit)
    return whole, placed


def gather_far(rows, steps, meanwhile):
    axis = steps[0][0]
    bits = [bit for _, bit in steps]
    parts = [rows] + [swap(rows, axis, mask) for mask in (bits[1], bits[0], bits[0] + bits[1])]
    parts[0] = hold(rows, *meanwhile)
    low, high = [(lax.axis_index(axis) & bit) != 0 for bit in (bits[1], bits[0])]
    parts = [jnp.where(low, parts[i ^ 1], parts[i]) for i in range(4)]
    parts = [jnp.where(high, parts[i ^ 2], parts[i]) for i in range(4)]
    whole = jnp.stack(parts).reshape((2, 2) + rows.shape)
    return whole, [row_weight(axis) * bit for bit in bits]


def scatter_split(part, placed, axis, bit):
    pos = placed.index(row_weight(axis) * bit)
    upper = (lax.axis_index(axis) & bit) != 0
    low = lax.index_in_dim(part, 0, pos, keepdims=False)
    high = lax.index_in_dim(part, 1, pos, keepdims=False)
    sent = jnp.where(upper, low, high).astype(bf16)
    kept = jnp.where(upper, high, low).astype(f32)
    return sent, kept, placed[:pos] + placed[pos + 1 :]


def scatter_step(part, placed, axis, bit):
    sent, kept, placed = scatter_split(part, placed, axis, bit)
    return kept + swap(sent, axis, bit).astype(f32), placed


def combine_kernel(n, block, up_ref, *refs):
    keep_ref, give_ref = refs[2 * n :]
    first = 0
    for kept, came in zip(refs[:n], refs[n : 2 * n]):
        cols = slice(first, first + kept.shape[1])
        total = kept[...] + came[...].astype(f32)
        keep_ref[:, cols], give_ref[:, cols] = split_rows(up_ref[0] == 1, total, block)
        first += kept.shape[1]


def combine(kept, came, placed, axis, bit, rows, deps, steps=2):
    weight = row_weight(axis) * bit
    placed = [w for w in placed if w != weight]
    block = rows * 2 ** sum(1 for w in placed if w < weight)
    upper = ((lax.axis_index(axis) & bit) != 0).astype(jnp.int32).reshape(1)
    n_rows = kept[0][0].shape[0] // steps
    args = [*kept, *came]
    out = pl.BlockSpec((n_rows // 2, sum(arg[1][1] for arg in kept)), lambda i: (i, 0))
    shape = (n_rows // 2 * steps, out.block_shape[1])
    keep, give = pl.pallas_call(
        ordered(functools.partial(combine_kernel, len(kept), block), 1 + len(args), len(deps)),
        grid=(steps,),
        in_specs=[pl.BlockSpec(memory_space=pltpu.SMEM)]
        + [pl.BlockSpec((n_rows, arg[1][1]), lambda i, index=arg[2]: (i, index)) for arg in args]
        + waits(deps),
        out_specs=[out, out],
        out_shape=[jax.ShapeDtypeStruct(shape, f32), jax.ShapeDtypeStruct(shape, bf16)],
        compiler_params=pltpu.CompilerParams(vmem_limit_bytes=VMEM),
        cost_estimate=cost("combine"),
        name="combine",
    )(upper, *[arg[0] for arg in args], *deps)
    return keep, give, placed


def whole_of(array):
    return column(array, array.shape[1], 0)


def scatter_split(part, placed, axis, bit):
    pos = placed.index(row_weight(axis) * bit)
    upper = (lax.axis_index(axis) & bit) != 0
    low = lax.index_in_dim(part, 0, pos, keepdims=False)
    high = lax.index_in_dim(part, 1, pos, keepdims=False)
    sent = jnp.where(upper, low, high).astype(bf16)
    kept = jnp.where(upper, high, low).astype(f32)
    return sent, kept, placed[:pos] + placed[pos + 1 :]


def scatter_parts(parts, orders, far, near, rows, deps, meanwhile, widths, narrow):
    swapped = {}
    for blocks in parts:
        for _, give, _, _ in blocks:
            if id(give) not in swapped:
                swapped[id(give)] = swap(give, *near[0])
    sums, places, gives = [], [], []
    for i, (blocks, order) in enumerate(zip(parts, orders)):
        step, late = order[-1], i == len(parts) - 1
        keep, give, placed = combine(
            [column(keep, width, index) for keep, _, width, index in blocks],
            [column(swapped[id(give)], width, index) for _, give, width, index in blocks],
            row_bits(far + order), *step, rows, () if late else deps,
        )
        gives.append(give)
        sums.append((keep, swap(give, *step)))
        places.append(placed)
    ready = meanwhile(gives)
    sums = [
        (hold(keep, *ready) + came.astype(f32)).reshape((2,) * len(placed) + (-1, keep.shape[1]))
        for (keep, came), placed in zip(sums, places)
    ]
    for steps in zip(*[reversed(order[:-1]) for order in orders]):
        splits = [scatter_split(part, where, *step) for part, where, step in zip(sums, places, steps)]
        places = [split[2] for split in splits]
        sums = [kept + swap(sent, *step).astype(f32) for (sent, kept, _), step in zip(splits, steps)]
    total, placed = jnp.concatenate(sums, axis=-1), places[0]
    for step in reversed(far):
        sent, kept, placed = scatter_split(total, placed, *step)
        came = swap(sent, *step)
        if placed:
            total = kept + came.astype(f32)
    return simple_call(
        sums_kernel, (kept, came), [((rows, width), f32) for width in widths] + [((n, rows), f32) for n in narrow], 0, "sums"
    )


def sums_kernel(kept_ref, came_ref, qkv_ref, out_ref, *refs):
    d = out_ref.shape[1]
    total = kept_ref[...] + came_ref[...].astype(f32)
    qkv_ref[...] = total[:, : 3 * d]
    out_ref[...] = total[:, 3 * d + PAIR : 4 * d + PAIR]
    gain = jnp.transpose(total[:, 3 * d : 3 * d + PAIR])
    small = jnp.transpose(total[:, 4 * d + PAIR :])
    first = 0
    for ref in refs[:-1]:
        ref[...] = small[first : first + ref.shape[0]]
        first += ref.shape[0]
    refs[-1][...] = gain[:1]


def pack_kernel(gate_ref, up_ref, down_ref, out_ref):
    out_ref[0, 0] = gate_ref[0]
    out_ref[0, 1] = up_ref[0]
    out_ref[0, 2] = jnp.transpose(down_ref[0])


def unpack_kernel(first_ref, rest_ref, gate_ref, up_ref, down_ref):
    rows = first_ref.shape[2]
    for ref, there in ((first_ref, slice(0, rows)), (rest_ref, slice(rows, rows + rest_ref.shape[2]))):
        gate_ref[0, there] = ref[0, 0].astype(f32)
        up_ref[0, there] = ref[0, 1].astype(f32)
        down_ref[0, :, there] = jnp.transpose(ref[0, 2].astype(f32))


def one_of(*shape):
    return pl.BlockSpec((1,) + shape, lambda i: (i,) + (0,) * len(shape))


def pack_expert(w_gate, w_up, w_down, deps):
    n, d, f = w_gate.shape
    return pl.pallas_call(
        ordered(pack_kernel, 3, len(deps)),
        grid=(n,),
        in_specs=[one_of(d, f), one_of(d, f), one_of(f, d)] + waits(deps),
        out_specs=one_of(3, d, f),
        out_shape=jax.ShapeDtypeStruct((n, 3, d, f), w_gate.dtype),
        compiler_params=pltpu.CompilerParams(vmem_limit_bytes=VMEM),
        cost_estimate=cost("pack"),
        name="pack",
    )(w_gate, w_up, w_down, *deps)


def unpack_expert(first, rest, deps):
    n, m, d, f = first.shape
    d = d + rest.shape[2]
    outs = (d, f), (d, f), (f, d)
    return pl.pallas_call(
        ordered(unpack_kernel, 2, len(deps)),
        grid=(n,),
        in_specs=[one_of(*part.shape[1:]) for part in (first, rest)] + waits(deps),
        out_specs=[one_of(*shape) for shape in outs],
        out_shape=[jax.ShapeDtypeStruct((n,) + shape, f32) for shape in outs],
        compiler_params=pltpu.CompilerParams(vmem_limit_bytes=VMEM),
        cost_estimate=cost("unpack"),
        name="unpack",
    )(first, rest, *deps)


def trade_far(parts):
    n_own = parts.shape[0]
    reps = lax.axis_size("dp") // n_own
    groups = [[i * reps + r for i in range(n_own)] for r in range(reps)]
    return lax.all_to_all(parts, "dp", 0, 0, axis_index_groups=groups, tiled=True)


def near_steps(n_own):
    reps = lax.axis_size("dp") // n_own
    return [("ctx", bit) for bit in bits_of("ctx")] + [("dp", bit) for bit in bits_of("dp", 1, reps)]


def gather_expert_near(groups, steps):
    for axis, bit in steps:
        groups = groups + [swap(group, axis, bit) for group in groups]
    return groups


def scatter_expert_near(groups, steps):
    for axis, bit in reversed(steps):
        n = len(groups) // 2
        came = [swap(group.astype(bf16), axis, bit) for group in groups[n:]]
        groups = [a.astype(f32) + b.astype(f32) for a, b in zip(groups[:n], came)]
    return groups[0]


def rms_scale(rows):
    return lax.rsqrt(jnp.mean(rows * rows, axis=-1, keepdims=True) + norm_eps)


def rms_backward(in_rows, inv_scale, gain_vec, grad_rows):
    normed = in_rows * inv_scale
    gain_grad = jnp.sum(grad_rows * normed, axis=0, keepdims=True)
    inner_grad = grad_rows * gain_vec
    back_rows = inv_scale * (
        inner_grad - normed * jnp.mean(inner_grad * normed, axis=-1, keepdims=True)
    )
    return (back_rows, gain_grad)


def rope(rows, cos, sin):
    lane = lax.broadcasted_iota(jnp.int32, (rows.shape[0], PAIR), 1)
    low = lane % (PAIR // 2) < PAIR // 4
    parts = []
    for first in range(0, rows.shape[1], PAIR):
        part = rows[:, first : first + PAIR]
        other = jnp.where(low, pltpu.roll(part, PAIR - PAIR // 4, 1), pltpu.roll(part, PAIR // 4, 1))
        parts.append(part * cos + other * sin)
    return jnp.concatenate(parts, axis=1)


def gain_row(small_ref, lane):
    return jnp.transpose(small_ref[...].astype(f32))[lane : lane + 1]


def project_kernel(scale, lane, x_ref, first_ref, wv_ref, small_ref, cos_ref, sin_ref, h_ref, q_ref, k_ref, v_ref):
    rows = x_ref[...].astype(f32)
    d = rows.shape[1]
    hidden = (rows * rms_scale(rows) * gain_row(small_ref, lane)).astype(bf16)
    h_ref[...] = hidden
    cos, sin = cos_ref[...], sin_ref[...]
    k_ref[...] = rope(mul_nn(hidden, first_ref[:, d : 2 * d]), cos, sin).astype(bf16)
    v_ref[...] = mul_nn(hidden, wv_ref[...]).astype(bf16)
    q_ref[...] = (rope(mul_nn(hidden, first_ref[:, :d]), cos, sin) * scale).astype(bf16)


def other_project_kernel(lane, x_ref, wk_ref, small_ref, wv_ref, cos_ref, sin_ref, h_ref, k_ref, v_ref):
    rows = x_ref[...].astype(f32)
    d = rows.shape[1]
    hidden = (rows * rms_scale(rows) * gain_row(small_ref, lane)).astype(bf16)
    h_ref[...] = hidden
    k_ref[...] = rope(mul_nn(hidden, wk_ref[...]), cos_ref[...], sin_ref[...]).astype(bf16)
    v_ref[...] = mul_nn(hidden, wv_ref[...]).astype(bf16)


def other_back_kernel(dk_ref, dv_ref, wk_ref, wv_ref, cos_ref, sin_ref, x_ref, gk_ref, dh_ref, dgain_ref):
    first = pl.program_id(0) == 0
    grad_k = rope(dk_ref[...].astype(f32), cos_ref[...], -sin_ref[...]).astype(bf16)
    gk_ref[...] = grad_k
    rows = x_ref[...].astype(f32)
    dh = mul_nt(grad_k, wk_ref[...]) + mul_nt(dv_ref[...], wv_ref[...])
    dh_ref[...] = dh.astype(bf16)
    dgain = jnp.sum(dh * rows * rms_scale(rows), axis=0, keepdims=True)

    @pl.when(first)
    def _():
        dgain_ref[...] = dgain

    @pl.when(jnp.logical_not(first))
    def _():
        dgain_ref[...] += dgain


def split_rows(upper, rows, block):
    keep, give = [], []
    for first in range(0, rows.shape[0], 2 * block):
        low, high = rows[first : first + block], rows[first + block : first + 2 * block]
        keep.append(jnp.where(upper, high, low))
        give.append(jnp.where(upper, low, high))
    return jnp.concatenate(keep, axis=0), jnp.concatenate(give, axis=0).astype(bf16)


def own_back_kernel(
    scale, block, core_ref, dq_ref, h_ref, first_ref, wv_ref, cos_ref, sin_ref, mgain_ref, dk_hbm, oh_hbm, ok_hbm, dv_hbm, ov_hbm,
    x_hbm, q_keep_ref, q_give_ref, k_keep_ref, k_give_ref, v_keep_ref, v_give_ref, dh_ref, dk_ref, oh_ref, ok_ref, dv_ref, ov_ref,
    x_ref, done,
):
    far = (dk_hbm, oh_hbm, ok_hbm, dv_hbm, ov_hbm, x_hbm)
    near = (dk_ref, oh_ref, ok_ref, dv_ref, ov_ref, x_ref)
    copies = [pltpu.make_async_copy(a, b, done.at[i]) for i, (a, b) in enumerate(zip(far, near))]
    step = pl.program_id(0)
    upper = core_ref[0] == 1
    cos, sin = cos_ref[...], -sin_ref[...]

    def finish(grad, weight, other, keep, give):
        dw = mul_tn(h_ref[...], grad)
        if other is not None:
            dw += mul_tn(oh_ref[...], other)
        keep[...], give[...] = split_rows(upper, dw, block)
        return mul_nt(grad, weight)

    @pl.when(step == 0)
    def _():
        for copy in copies:
            copy.start()
        grad = rope(dq_ref[...].astype(f32) * scale, cos, sin).astype(bf16)
        dh_ref[...] = finish(grad, first_ref[...], None, q_keep_ref, q_give_ref)

    @pl.when(step == 1)
    def _():
        for copy in copies[:3]:
            copy.wait()
        grad = rope(dk_ref[...].astype(f32), cos, sin).astype(bf16)
        dh_ref[...] += finish(grad, first_ref[...], ok_ref[...], k_keep_ref, k_give_ref)

    @pl.when(step == 2)
    def _():
        for copy in copies[3:]:
            copy.wait()
        d = dh_ref.shape[1]
        dh = dh_ref[...] + finish(dv_ref[...], wv_ref[...], ov_ref[...], v_keep_ref.at[:, :d], v_give_ref.at[:, :d])
        dh_ref[...] = dh
        rows = x_ref[...].astype(f32)
        dgain = jnp.sum(dh * rows * rms_scale(rows), axis=0, keepdims=True) + mgain_ref[...]
        column = jnp.transpose(jnp.broadcast_to(dgain, (8, d)))[:, :1]
        small = jnp.where(lane_of(d) == 0, column, 0.0)
        v_keep_ref[:, d:], v_give_ref[:, d:] = split_rows(upper, small, block)


def first_norm_kernel(lane, dh_ref, more_ref, x_ref, small_ref, mid_ref, dx_ref):
    rows = x_ref[...].astype(f32)
    grad = dh_ref[...] + more_ref[...].astype(f32)
    back, _ = rms_backward(rows, rms_scale(rows), gain_row(small_ref, lane), grad)
    dx_ref[...] = mid_ref[...] + back


def column(array, width, index):
    return array, (array.shape[0], width), index


def simple_call(kernel, args, outs, flops, name, deps=(), scalars=()):
    whole = pl.BlockSpec(memory_space=pltpu.VMEM)
    small = pl.BlockSpec(memory_space=pltpu.SMEM)
    specs, arrays = [], []
    for arg in args:
        if isinstance(arg, tuple):
            array, block, index = arg
            specs.append(pl.BlockSpec(block, lambda i, index=index: (0, index)))
            arrays.append(array)
        else:
            specs.append(whole)
            arrays.append(arg)
    return pl.pallas_call(
        ordered(kernel, len(scalars) + len(args), len(deps)),
        grid=(1,),
        in_specs=[small] * len(scalars) + specs + waits(deps),
        out_shape=[jax.ShapeDtypeStruct(s, d) for s, d in outs],
        compiler_params=pltpu.CompilerParams(vmem_limit_bytes=VMEM),
        cost_estimate=cost(name),
        name=name,
    )(*scalars, *arrays, *deps)


def expert_kernel(n_groups, *refs):
    x_ref, g_ref = refs[:2]
    w_refs = refs[2 : 2 + n_groups]
    out_ref, dx_ref, act_ref, dg_ref, du_ref, gx_ref, gg_ref, store, out_sum, back_sum, done = refs[-11:]
    step = pl.program_id(0)
    n, d = out_sum.shape
    copies = [pltpu.make_async_copy(w, store.at[k], done.at[k]) for k, w in enumerate(w_refs)]

    @pl.when(step == 0)
    def _():
        for copy in copies:
            copy.start()
        out_sum[...] = jnp.zeros((n, d), f32)
        back_sum[...] = jnp.zeros((n, d), f32)

    for k, copy in enumerate(copies):
        pl.when(step == k)(copy.wait)
    grads = g_ref[...].reshape(n, d)
    rows = x_ref[:, :d]
    wg, wu, wd = [
        jnp.concatenate([store[step, p, m] for p in range(store.shape[1])], axis=1) for m in range(3)
    ]
    gate_pre = mul_nn(rows, wg)
    up_pre = mul_nn(rows, wu)
    grad_act = mul_nn(grads, wd)
    sig = 1.0 / (1.0 + jnp.exp(-gate_pre))
    silu = gate_pre * sig
    act = (silu * up_pre).astype(bf16)
    act_ref[...] = act
    grad_gate = (grad_act * up_pre * sig * (1.0 + gate_pre * (1.0 - sig))).astype(bf16)
    grad_up = (grad_act * silu).astype(bf16)
    dg_ref[...] = grad_gate
    du_ref[...] = grad_up
    out_sum[...] += mul_nt(act, wd)
    back_sum[...] += mul_nt(grad_gate, wg) + mul_nt(grad_up, wu)

    @pl.when(step == n_groups - 1)
    def _():
        gates = x_ref[:, d : d + 1].astype(f32) + x_ref[:, d + 1 : d + 2].astype(f32)
        gx_ref[...] = jnp.transpose((rows.astype(f32) * gates).astype(bf16))
        gg_ref[...] = jnp.transpose((grads.astype(f32) * gates).astype(bf16))
        low = out_sum[...].astype(bf16)
        out_ref[...] = low.reshape(out_ref.shape)
        dx_ref[:, :d] = back_sum[...].astype(bf16)
        dots = jnp.sum(grads.astype(f32) * low.astype(f32), axis=1, keepdims=True)
        high, rest = halves(dots)
        lane = lax.broadcasted_iota(jnp.int32, (n, PAIR), 1)
        pair = jnp.where(lane == 0, high.astype(f32), jnp.where(lane == 1, rest.astype(f32), 0.0))
        dx_ref[:, d:] = pair.astype(bf16)


def expert_call(part, x, g, groups, outs, name):
    n, wide = x.shape
    d = g.shape[-1]
    group = groups[0].shape
    cols = group[0] * group[3]
    ff = cols * len(groups)
    block = pl.BlockSpec((g.shape[0], 1) + g.shape[2:], lambda i: (0, part, 0, 0))
    passed = [] if outs is None else [outs]

    def whole(*shape):
        return pl.BlockSpec(shape, lambda i: (0,) * len(shape))

    def column(rows):
        return pl.BlockSpec((rows, cols), lambda i: (0, i))

    shapes = [(n, wide), (n, ff), (n, ff), (n, ff), (d, n), (d, n)]
    return pl.pallas_call(
        functools.partial(expert_kernel, len(groups)),
        grid=(len(groups),),
        in_specs=[whole(n, wide), block] + waits(groups) + waits(passed),
        out_specs=[block, whole(n, wide)] + [column(n)] * 3 + [whole(d, n)] * 2,
        out_shape=[jax.ShapeDtypeStruct(g.shape, bf16)] + [jax.ShapeDtypeStruct(shape, bf16) for shape in shapes],
        input_output_aliases={2 + len(groups): 0} if passed else {},
        scratch_shapes=[
            pltpu.VMEM((len(groups),) + group, bf16), pltpu.VMEM((n, d), f32), pltpu.VMEM((n, d), f32),
            pltpu.SemaphoreType.DMA((len(groups),)),
        ],
        compiler_params=pltpu.CompilerParams(vmem_limit_bytes=VMEM),
        cost_estimate=cost("expert"),
        name=name,
    )(x, g, *groups, *passed)


def expert_weights_kernel(plan, n_through, *refs):
    xs, ggs, acts, dgs, dus = [refs[2 * i : 2 * i + 2] for i in range(5)]
    out_refs = refs[10 + n_through :]
    step = pl.program_id(0)
    pieces, _, d, width = out_refs[0].shape
    for m, (left, right) in enumerate([(xs, dgs), (xs, dus), (ggs, acts)]):
        grad = mul_nn(
            jnp.concatenate([half[...] for half in left], axis=1), jnp.concatenate([half[...] for half in right], axis=0)
        )

        def write(ref):
            for p in range(pieces):
                ref[p, m] = grad[:, p * width : (p + 1) * width].astype(ref.dtype)

        first = 0
        for count, ref in zip(plan, out_refs):
            pl.when((step >= first) & (step < first + count))(functools.partial(write, ref))
            first += count


def expert_weights(flows, order, plan, pieces, width, kinds, name, through=None, deps=()):
    d, n = flows[0][0].shape
    cols = pieces * width
    rows = pl.BlockSpec((d, n), lambda i: (0, 0))
    flip = order[0] != 0

    def group(i):
        return len(order) - 1 - i if flip else i

    part = pl.BlockSpec((n, cols), lambda i: (0, group(i)))
    passed = [] if through is None else [through]
    blocks, first = [], 0
    for count in plan:
        blocks.append(
            pl.BlockSpec(
                (pieces, 3, d, width),
                lambda i, first=first, count=count: (jnp.clip(i - first, 0, count - 1), 0, 0, 0),
            )
        )
        first += count
    return pl.pallas_call(
        ordered(functools.partial(expert_weights_kernel, plan, len(passed)), 10 + len(passed), len(deps)),
        grid=(len(order),),
        in_specs=[rows] * 4 + [part] * 6 + waits(passed) + waits(deps),
        out_specs=blocks + waits(passed),
        out_shape=[
            jax.ShapeDtypeStruct((pieces * count, 3, d, width), kind) for count, kind in zip(plan, kinds)
        ]
        + [jax.ShapeDtypeStruct(p.shape, p.dtype) for p in passed],
        input_output_aliases={10: len(plan)} if passed else {},
        compiler_params=pltpu.CompilerParams(vmem_limit_bytes=VMEM),
        cost_estimate=cost(name),
        name=name,
    )(*[half for flow in flows for half in flow], *passed, *deps)


def weights_sent_kernel(near_ref, came_ref, *out_refs):
    first = 0
    for ref in out_refs:
        there = slice(first, first + ref.shape[2])
        ref[...] = near_ref[:, :, there] + came_ref[:, :, there]
        first += ref.shape[2]


def weights_sent(near, came):
    n, m, d, f = near.shape
    whole = pl.BlockSpec((2, m, d, f), lambda i: (i, 0, 0, 0))
    cuts = (d // 3, d - d // 3)
    return pl.pallas_call(
        weights_sent_kernel,
        grid=(n // 2,),
        in_specs=[whole] * 2,
        out_specs=[pl.BlockSpec((2, m, rows, f), lambda i: (i, 0, 0, 0)) for rows in cuts],
        out_shape=[jax.ShapeDtypeStruct((n, m, rows, f), bf16) for rows in cuts],
        compiler_params=pltpu.CompilerParams(vmem_limit_bytes=VMEM),
        cost_estimate=cost("weights_sent"),
        name="weights_sent",
    )(near, came)


def weights_sum_kernel(kept_ref, far_ref, near_ref, out_ref):
    out_ref[...] = (kept_ref[...].astype(f32) + far_ref[...].astype(f32) + near_ref[...].astype(f32)).astype(bf16)


def weights_sum(kept, far, near, first, deps):
    n, m, d, f = near.shape
    unit = kept.shape[2] // 3
    own = pl.BlockSpec((4, m, unit, f), lambda i, j: (i, 0, j, 0))
    some = pl.BlockSpec((4, m, unit, f), lambda i, j: (i, 0, first // unit + j, 0))
    return pl.pallas_call(
        ordered(weights_sum_kernel, 3, len(deps)),
        grid=(n // 4, d // unit),
        in_specs=[some, some, own] + waits(deps),
        out_specs=own,
        out_shape=jax.ShapeDtypeStruct(near.shape, bf16),
        compiler_params=pltpu.CompilerParams(vmem_limit_bytes=VMEM),
        cost_estimate=cost("weights_sum"),
        name="weights_sum",
    )(kept, far, near, *deps)


def lane_of(rows):
    return lax.broadcasted_iota(jnp.int32, (rows, PAIR), 1)


def col(rows, i):
    return rows[:, i : i + 1]


def halves(rows):
    high = rows.astype(bf16)
    return high, (rows - high.astype(f32)).astype(bf16)


VEC, COEF, GATE, CONST = 0, 2, 3, 5


def mid_kernel(
    n_all, att_ref, small_ref, wo_ref, x_ref, prev_ref, routes_ref, place_ref,
    mid_ref, hidden_ref, scal_ref, *send_refs,
):
    n_ffn = n_all - 4
    d = x_ref.shape[1]
    mid = x_ref[...].astype(f32) + mul_nn(att_ref[...], wo_ref[...])
    mid_ref[...] = mid
    hidden = (mid * rms_scale(mid) * gain_row(small_ref, n_all + 7)).astype(bf16)
    hidden_ref[...] = hidden
    rows, d = hidden.shape
    lane = lane_of(rows)
    raw = mul_nn(hidden, small_ref[...])
    logits = jnp.where(lane < n_all, raw + prev_ref[...], NEG)
    expo = jnp.exp(logits - jnp.max(logits, axis=1, keepdims=True))
    probs = jnp.where(lane < n_all, expo / jnp.sum(expo, axis=1, keepdims=True), 0.0)
    ids = [col(routes_ref[...], j) for j in range(2)]
    gates = [jnp.sum(jnp.where(lane == r, probs, 0.0), axis=1, keepdims=True) for r in ids]
    scal = probs
    coef = sum(jnp.where(r == n_ffn + 1, g, 0.0) for r, g in zip(ids, gates))
    base = n_all + 4
    for c in range(2):
        gap = col(raw, n_all + 2 * c + 1) - col(raw, n_all + 2 * c)
        first, second = 1.0 / (1.0 + jnp.exp(gap)), 1.0 / (1.0 + jnp.exp(-gap))
        const = sum(jnp.where(r == n_ffn + 2 + c, g, 0.0) for r, g in zip(ids, gates))
        coef += first * const
        scal = jnp.where(lane == n_all + 2 * c, first, scal)
        scal = jnp.where(lane == n_all + 2 * c + 1, second, scal)
        scal = jnp.where(lane == base + VEC + c, second * const, scal)
        scal = jnp.where(lane == base + CONST + c, const, scal)
        scal = jnp.where(lane == base + GATE + c, gates[c], scal)
    scal_ref[...] = jnp.where(lane == base + COEF, coef, scal)
    n_half = send_refs[0].shape[0]
    slots = n_half * len(send_refs)
    row = lax.broadcasted_iota(jnp.int32, (slots, rows), 0)
    hits = [(row == place_ref[j : j + 1, :]) for j in range(2)]
    both = jnp.where(hits[0] | hits[1], 1.0, 0.0).astype(bf16)
    rows_out = mul_nn(both, hidden).astype(bf16)
    extra = jnp.zeros((slots, PAIR), f32)
    for j in range(2):
        high, low = halves(gates[j])
        pair = jnp.where(lane == 0, high.astype(f32), jnp.where(lane == 1, low.astype(f32), 0.0))
        extra += mul_nn(jnp.where(hits[j], 1.0, 0.0).astype(bf16), pair.astype(bf16))
    for i, ref in enumerate(send_refs):
        ref[:, :d] = rows_out[i * n_half : (i + 1) * n_half]
        ref[:, d:] = extra[i * n_half : (i + 1) * n_half].astype(bf16)


def spread_kernel(cot_ref, valid_ref, place_ref, send_ref):
    grads = (cot_ref[...] * valid_ref[...]).astype(bf16)
    row = lax.broadcasted_iota(jnp.int32, (send_ref.shape[0], grads.shape[0]), 0)
    hit = (row == place_ref[0:1, :]) | (row == place_ref[1:2, :])
    send_ref[...] = mul_nn(jnp.where(hit, 1.0, 0.0).astype(bf16), grads).astype(bf16)


def picked_rows(place_ref, j, table):
    rows, slots = place_ref.shape[0], table.shape[0]
    slot = lax.broadcasted_iota(jnp.int32, (rows, slots), 1)
    pick = jnp.where(slot == col(place_ref[...], j), 1.0, 0.0).astype(bf16)
    return mul_nn(pick, table)


def gates_back_kernel(
    n_all, back_ref, more_ref, place_ref, routes_ref, scal_ref, hidden_ref, mid_ref, cot_ref, valid_ref, small_ref, wo_ref,
    gmid_ref, gatt_ref, mix_ref, dgain_ref,
):
    n_ffn = n_all - 4
    base = n_all + 4
    scal = scal_ref[...]
    grads = cot_ref[...] * valid_ref[...]
    rows, d = grads.shape
    lane = lane_of(rows)
    hidden = hidden_ref[...].astype(f32)
    small = small_ref[...]
    g_hidden = jnp.sum(grads * hidden, axis=1, keepdims=True)
    high, low = halves(grads)
    g_small = mul_nn(high, small) + mul_nn(low, small)
    table = jnp.concatenate([back_ref[...], more_ref[...]], axis=0)
    grad_hidden = col(scal, base + COEF) * grads
    grad_probs = jnp.zeros((rows, PAIR), f32)
    for j in range(2):
        r = col(routes_ref[...], j)
        came = picked_rows(place_ref, j, table)
        grad_hidden += col(scal, base + GATE + j) * came[:, :d]
        dots = came[:, d : d + 1] + came[:, d + 1 : d + 2]
        dots += jnp.where(r == n_ffn + 1, g_hidden, 0.0)
        for c in range(2):
            whole = col(scal, n_all + 2 * c) * g_hidden + col(scal, n_all + 2 * c + 1) * col(g_small, base + c)
            dots += jnp.where(r == n_ffn + 2 + c, whole, 0.0)
        grad_probs += jnp.where(lane == r, dots, 0.0)
    probs = jnp.where(lane < n_all, scal, 0.0)
    mix = probs * (grad_probs - jnp.sum(probs * grad_probs, axis=1, keepdims=True))
    for c in range(2):
        first, second = col(scal, n_all + 2 * c), col(scal, n_all + 2 * c + 1)
        const = col(scal, base + CONST + c)
        a, b = const * g_hidden, const * col(g_small, base + c)
        inner = first * a + second * b
        mix = jnp.where(lane == n_all + 2 * c, first * (a - inner), mix)
        mix = jnp.where(lane == n_all + 2 * c + 1, second * (b - inner), mix)
    mix_ref[...] = mix
    high, low = halves(mix)
    grad_hidden += mul_nt(high, small) + mul_nt(low, small)
    mid = mid_ref[...]
    back, dgain = rms_backward(mid, rms_scale(mid), gain_row(small_ref, n_all + 7), grad_hidden)
    dgain_ref[...] = dgain
    grad_mid = grads + back
    gmid_ref[...] = grad_mid
    gatt_ref[...] = mul_nt(grad_mid.astype(bf16), wo_ref[...]).astype(bf16)


def out_grads_kernel(
    n_all, block, core_ref, att_ref, gmid_ref, hidden_ref, mix_ref, scal_ref, cot_ref, valid_ref, dgain_ref, keep_ref, give_ref,
):
    d = att_ref.shape[1]
    base = n_all + 4
    upper = core_ref[0] == 1
    dw_out = mul_tn(att_ref[...], gmid_ref[...].astype(bf16))
    keep_ref[:, :d], give_ref[:, :d] = split_rows(upper, dw_out, block)
    hidden = hidden_ref[...]
    high, low = halves(mix_ref[...])
    grads = mul_tn(hidden, high) + mul_tn(hidden, low)
    scal = scal_ref[...]
    lane = lane_of(scal.shape[0])
    vec = jnp.where((lane >= base + VEC) & (lane < base + VEC + 2), scal, 0.0)
    vec_high, vec_low = halves(vec)
    g_high, g_low = halves(cot_ref[...] * valid_ref[...])
    grads += mul_tn(g_high, vec_high) + mul_tn(g_high, vec_low) + mul_tn(g_low, vec_high)
    column = jnp.transpose(jnp.broadcast_to(dgain_ref[...], (8, d)))[:, :1]
    tail = jnp.where(lane_of(d) == base + 2, column, grads)
    keep_ref[:, d:], give_ref[:, d:] = split_rows(upper, tail, block)


def output_kernel(n_all, back_ref, place_ref, scal_ref, hidden_ref, mid_ref, valid_ref, small_ref, out_ref):
    base = n_all + 4
    scal = scal_ref[...]
    lane = lane_of(scal.shape[0])
    vec = jnp.where((lane >= base + VEC) & (lane < base + VEC + 2), scal, 0.0)
    high, low = halves(vec)
    small = small_ref[...]
    total = mid_ref[...] + mul_nt(high, small) + mul_nt(low, small)
    total += col(scal, base + COEF) * hidden_ref[...].astype(f32)
    table = back_ref[...]
    for j in range(2):
        total += col(scal, base + GATE + j) * picked_rows(place_ref, j, table)
    out_ref[...] = total * valid_ref[...]


def local(
    residual_in,
    lengths,
    routes,
    prev_logits,
    cotangent,
    w_qkv,
    w_out,
    attn_gain,
    ffn_gain,
    router,
    const_gate,
    const_vec,
    w_gate,
    w_up,
    w_down,
):
    tok_rows = residual_in.shape[1]
    feat = residual_in.shape[2]
    head_size = feat // HEADS
    score_scale = head_size ** (-0.5)
    n_dp = lax.axis_size("dp")
    n_ctx = lax.axis_size("ctx")
    n_exp = lax.axis_size("exp")
    own_exp = w_gate.shape[0]
    reps = n_dp // own_exp
    n_all = router.shape[1]
    n_ffn = n_all - 4
    cap_rows = tok_rows // 4
    sub_rows = cap_rows // reps
    n_slots = n_ffn * cap_rows
    ctx_rank = lax.axis_index("ctx")
    positions = ctx_rank * tok_rows + jnp.arange(tok_rows, dtype=jnp.int32)
    length = lengths[0]
    valid_rows = (positions < length).astype(f32)[:, None]

    def gather_ctx(rows):
        if n_ctx == 2:
            return swap(rows, "ctx", 1)
        for bit in reversed(bits_of("ctx")):
            other = swap(rows, "ctx", bit)
            upper = (ctx_rank & bit) != 0
            rows = jnp.concatenate([jnp.where(upper, other, rows), jnp.where(upper, rows, other)], axis=0)
        return rows

    def scatter_ctx(rows):
        if n_ctx == 2:
            return swap(rows, "ctx", 1)
        for bit in bits_of("ctx"):
            low, high = jnp.split(rows, 2, axis=0)
            upper = (ctx_rank & bit) != 0
            sent = jnp.where(upper, low, high).astype(bf16)
            rows = jnp.where(upper, high, low).astype(f32) + swap(sent, "ctx", bit).astype(f32)
        return rows

    route_ids = routes[0]
    choose = (route_ids[:, :, None] == jnp.arange(n_all, dtype=jnp.int32)[None, None, :]).astype(f32)
    both = jnp.sum(choose, axis=1)
    before = jnp.arange(tok_rows)
    before = (before[None, :] < before[:, None]).astype(bf16)
    counts = dot32(before, both.astype(bf16))
    slot_ids = jnp.sum(choose * counts[:, None, :], axis=-1).astype(jnp.int32)
    is_ffn = route_ids < n_ffn
    place = (
        ((route_ids % own_exp) * reps + slot_ids // sub_rows) * n_exp + route_ids // own_exp
    ) * sub_rows + slot_ids % sub_rows
    half_rows = sub_rows // 2
    place_half = (
        (place // half_rows % 2) * (n_slots // 2) + place // sub_rows * half_rows + place % half_rows
    )
    place = jnp.where(is_ffn, place, -1)
    place_half = jnp.where(is_ffn, place_half, -1)
    row_ids = jnp.arange(n_slots, dtype=jnp.int32)
    place_rows = jnp.transpose(place)

    def to_experts(rows):
        return lax.all_to_all(
            rows.reshape(n_dp * n_exp, rows.shape[0] // (n_dp * n_exp), -1),
            ("dp", "exp"),
            split_axis=0,
            concat_axis=0,
            tiled=True,
        ).reshape(rows.shape[0], -1)

    width = 2 * feat
    far, mid_a, near = plan_steps(("ctx", "exp"))
    _, mid_b, _ = plan_steps(("exp", "ctx"))
    lane = jnp.arange(PAIR, dtype=jnp.int32)
    half = head_size // 2
    inv_freq = 10000.0 ** (-2.0 * (lane % half).astype(f32) / head_size)
    sign = jnp.where(lane % head_size < half, -1.0, 1.0)

    def turns(where):
        angles = where.astype(f32)[:, None] * inv_freq[None, :]
        return jnp.cos(angles), jnp.sin(angles) * sign[None, :]

    cosine, sine = turns(positions)
    other_start = (1 - ctx_rank) * tok_rows if n_ctx == 2 else 0
    n_other = tok_rows if n_ctx == 2 else tok_rows * n_ctx
    other_cos, other_sin = turns(other_start + jnp.arange(n_other, dtype=jnp.int32))
    other_in = gather_ctx(residual_in[0])
    (rows,) = simple_call(
        rows_kernel, (w_qkv, w_out, router.T, const_gate.T, const_vec.T, attn_gain[None], ffn_gain[None]),
        [((w_out.shape[0], 4 * feat + PAIR), bf16)], 0, "rows",
    )
    packed = pack_expert(w_gate, w_up, w_down, (rows,))
    tables = (cosine, sine, other_cos, other_sin)
    if len(far) == 2:
        whole, placed = gather_far(rows, far, (packed,) + tables)
    else:
        whole, placed = gather_steps(rows, [], far)
    group = trade_far(packed)
    part_a, part_b = whole[..., :width], whole[..., width:]
    placed_a, placed_b = placed, placed
    for i, (step_a, step_b) in enumerate(zip(mid_a, mid_b)):
        meanwhile = (other_in,) if i == 0 else ()
        if i + 1 == len(mid_a):
            (grad_sent,) = simple_call(
                spread_kernel, (cotangent[0], valid_rows, place_rows), [((n_slots, feat), bf16)], 0, "spread", (part_b,)
            )
            meanwhile = (grad_sent,)
        part_a, placed_a = gather_step(part_a, placed_a, *step_a)
        part_b, placed_b = gather_step(part_b, placed_b, *step_b, meanwhile)
    first_part, _ = gather_steps(part_a, placed_a, near)
    second_part, _ = gather_steps(part_b, placed_b, near)
    first_part = first_part.reshape(feat, width)
    second_part = second_part.reshape(feat, 2 * feat + PAIR)

    small_at = 2 * feat // PAIR
    w_v, w_o, small = column(second_part, feat, 0), column(second_part, feat, 1), column(second_part, PAIR, small_at)
    rows_low = ((tok_rows, feat), bf16)
    rows_full = ((tok_rows, feat), f32)
    square = 2 * tok_rows * feat * feat
    hidden_one, queries, own_keys, own_values = simple_call(
        functools.partial(project_kernel, score_scale, n_all + 6),
        (residual_in[0], first_part, w_v, small, cosine, sine), [rows_low] * 4, 3 * square, "project",
    )
    tok_spec = pl.BlockSpec((tok_rows, feat), lambda i: (i, 0))
    turn_spec = pl.BlockSpec((tok_rows, PAIR), lambda i: (i, 0))

    def fixed(rows, cols, index=0):
        return pl.BlockSpec((rows, cols), lambda i: (0, index))

    other_hidden, other_keys, other_values = pl.pallas_call(
        functools.partial(other_project_kernel, n_all + 6),
        grid=(n_other // tok_rows,),
        in_specs=[tok_spec, fixed(feat, feat, 1), fixed(feat, PAIR, small_at), fixed(feat, feat), turn_spec, turn_spec],
        out_specs=[tok_spec] * 3,
        out_shape=[jax.ShapeDtypeStruct((n_other, feat), bf16)] * 3,
        compiler_params=pltpu.CompilerParams(vmem_limit_bytes=VMEM),
        cost_estimate=cost("project_other"),
        name="project_other",
    )(other_in, first_part, second_part, second_part, other_cos, other_sin)
    grad_rows_in = to_experts(hold(grad_sent, group, other_keys))
    info = jnp.stack([ctx_rank * tok_rows, length, ctx_rank]).astype(jnp.int32)
    prev = jnp.pad(prev_logits[0], ((0, 0), (0, PAIR - n_all)))
    attended, attended_low, log_total = attend(
        info, queries, own_keys, own_values, other_keys, other_values, (group, prev, place, place_half)
    )

    mid_rows, hidden, scalars, *sent_rows = simple_call(
        functools.partial(mid_kernel, n_all),
        (attended_low, small, w_o, residual_in[0], prev, route_ids, jnp.transpose(place_half)),
        [rows_full, rows_low, ((tok_rows, PAIR), f32)] + [((n_slots // 2, feat + PAIR), bf16)] * 2, 0, "mid",
    )
    rows_in = [to_experts(hold(sent_rows[0], grad_rows_in)), to_experts(sent_rows[1])]

    steps_near = near_steps(own_exp)
    groups = gather_expert_near([group], steps_near)
    piece_width = group.shape[3]
    if piece_width < PAIR:
        merge = PAIR // piece_width
        whole = jnp.concatenate(groups).reshape(-1, merge, 3, feat, piece_width)
        groups = [jnp.moveaxis(whole, 1, 3).reshape(-1, 3, feat, PAIR)]
    grads_in = grad_rows_in.reshape(n_dp * n_exp, 2, half_rows, feat)
    expert_out = None
    flows, back_grads = [], []
    for part in range(2):
        expert_out, grad_in, *flow = expert_call(part, rows_in[part], grads_in, groups, expert_out, f"expert_{part}")
        back_grads.append(to_experts(grad_in))
        flows.append(flow)
    expert_out = expert_out.reshape(n_slots, feat)
    n_groups = 2 ** len(steps_near)
    act, grad_gate_pre, grad_up_pre, gated_rows, grad_expert_out = zip(*flows)
    flows = (gated_rows, grad_expert_out, act, grad_gate_pre, grad_up_pre)
    simple = piece_width >= PAIR and len(steps_near) == 2
    if simple:
        far_near, far_kept, near_own, kept, expert_out = expert_weights(
            flows, (3, 2, 1, 0), (1, 1, 1, 1), own_exp, piece_width, (bf16,) * 4, "weights_all", expert_out,
            (back_grads[0],),
        )
        far_near = swap(hold(far_near, back_grads[1]), *steps_near[1])
        far_kept = swap(hold(far_kept, back_grads[1]), *steps_near[1])
        near_sent = weights_sent(near_own, far_near)
        near_came = [swap(part, *steps_near[0]) for part in near_sent]
    else:
        step = max(piece_width, PAIR)
        n_steps = act[0].shape[1] // step
        (whole,) = expert_weights(flows, tuple(range(n_steps)), (n_steps,), 1, step, (f32,), "weights_all")
        if piece_width < PAIR:
            whole = jnp.moveaxis(whole.reshape(-1, 3, feat, merge, piece_width), 3, 1)
        whole = whole.reshape(n_groups, own_exp, 3, feat, piece_width)
        expert_sum = scatter_expert_near([whole[i] for i in range(n_groups)], steps_near)
    back_rows = to_experts(expert_out)
    small_shape = ((tok_rows, PAIR), f32)
    grad_mid, grad_attended, grad_mix, grad_gain_two = simple_call(
        functools.partial(gates_back_kernel, n_all),
        (
            *back_grads, place_half, route_ids, scalars, hidden, mid_rows, cotangent[0], valid_rows, small, w_o,
        ),
        [rows_full, rows_low, small_shape, ((1, feat), f32)], 0, "gates_back", tuple(near_sent) if simple else (),
    )
    grad_queries, other_dk, other_dv, delta = grads_other(
        info, queries, other_keys, other_values, grad_attended, attended, log_total, ()
    )
    core = (lax.axis_index("dp") & 1).astype(jnp.int32).reshape(1)
    core_block = feat // (n_dp * n_ctx * n_exp) * row_weight("dp")
    other_gk, other_dh, more_gain = pl.pallas_call(
        other_back_kernel,
        grid=(n_other // tok_rows,),
        in_specs=[tok_spec, tok_spec, fixed(feat, feat, 1), fixed(feat, feat), turn_spec, turn_spec, tok_spec],
        out_specs=[tok_spec, tok_spec, fixed(1, feat)],
        out_shape=[
            jax.ShapeDtypeStruct((n_other, feat), bf16), jax.ShapeDtypeStruct((n_other, feat), bf16),
            jax.ShapeDtypeStruct((1, feat), f32),
        ],
        compiler_params=pltpu.CompilerParams(vmem_limit_bytes=VMEM),
        cost_estimate=cost("back_other"),
        name="back_other",
    )(other_dk, other_dv, first_part, second_part, other_cos, other_sin, other_in)
    more_dh = scatter_ctx(other_dh)
    if simple:
        sum_first = weights_sum(kept, far_kept, near_came[0], 0, (other_dh,))
    else:
        sum_first, sum_rest = jnp.split(expert_sum.astype(bf16), [feat // 3], axis=2)
    back_first = trade_far(sum_first)
    grad_queries, own_dk, own_dv = grads_own(
        info, queries, own_keys, own_values, grad_attended, log_total, delta, grad_queries, (back_rows, sum_first)
    )
    half_rows = feat // 2
    out_keep, out_give = simple_call(
        functools.partial(out_grads_kernel, n_all, core_block),
        (attended_low, grad_mid, hidden, grad_mix, scalars, cotangent[0], valid_rows, grad_gain_two),
        [((half_rows, feat + PAIR), f32), ((half_rows, feat + PAIR), bf16)], 0, "out_grads", (own_dk,), (core,),
    )

    if simple:
        sum_rest = weights_sum(kept, far_kept, near_came[1], feat // 3, (out_keep,))
    back_rest = trade_far(sum_rest)
    own_args = (
        core, grad_queries, hidden_one, first_part, second_part, cosine, sine, more_gain, own_dk, other_hidden, other_gk, own_dv,
        other_dv, residual_in[0],
    )
    own_deps = (sum_rest, back_first)
    token, turn = fixed(tok_rows, feat), fixed(tok_rows, PAIR)
    q_keep, q_give, k_keep, k_give, v_keep, v_give, grad_hidden_one = pl.pallas_call(
        ordered(functools.partial(own_back_kernel, score_scale, core_block), len(own_args), len(own_deps)),
        grid=(3,),
        in_specs=[pl.BlockSpec(memory_space=pltpu.SMEM)] + [token] * 2
        + [pl.BlockSpec((feat, feat), lambda i: (0, jnp.minimum(i, 1))), fixed(feat, feat), turn, turn, fixed(1, feat)]
        + waits(own_args[-6:]) + waits(own_deps),
        scratch_shapes=[pltpu.VMEM(arg.shape, bf16) for arg in own_args[-6:]] + [pltpu.SemaphoreType.DMA((6,))],
        out_specs=[fixed(half_rows, feat)] * 4 + [fixed(half_rows, feat + PAIR)] * 2 + [token],
        out_shape=[
            jax.ShapeDtypeStruct((half_rows, feat), f32), jax.ShapeDtypeStruct((half_rows, feat), bf16),
            jax.ShapeDtypeStruct((half_rows, feat), f32), jax.ShapeDtypeStruct((half_rows, feat), bf16),
            jax.ShapeDtypeStruct((half_rows, feat + PAIR), f32), jax.ShapeDtypeStruct((half_rows, feat + PAIR), bf16),
            jax.ShapeDtypeStruct((tok_rows, feat), f32),
        ],
        compiler_params=pltpu.CompilerParams(vmem_limit_bytes=VMEM),
        cost_estimate=cost("back_own"),
        name="back_own",
    )(*own_args, *own_deps)
    def last_rows(sent):
        (output,) = simple_call(
            functools.partial(output_kernel, n_all),
            (back_rows, place, scalars, hidden, mid_rows, valid_rows, small), [rows_full], 0, "output", tuple(sent),
        )
        (grad_x,) = simple_call(
            functools.partial(first_norm_kernel, n_all + 6),
            (grad_hidden_one, more_dh, residual_in[0], small, grad_mid), [rows_full], 0, "first_norm", (output,),
        )
        results.extend([output, grad_x, *unpack_expert(back_first, back_rest, (output, grad_x))])
        return results

    results = []
    dw_qkv, dw_out, *narrow = scatter_parts(
        [
            [(q_keep, q_give, feat, 0), (k_keep, k_give, feat, 0)],
            [(v_keep, v_give, feat + PAIR, 0), (out_keep, out_give, feat + PAIR, 0)],
        ],
        [mid_a, mid_b], far, near, w_out.shape[0], (more_dh,), last_rows, (3 * feat, feat), (n_all, 4, 2, 1, 1),
    )
    output, grad_x, *expert_grads = results
    return (
        output[None],
        grad_x[None],
        dw_qkv,
        dw_out,
        narrow[4][0],
        narrow[3][0],
        narrow[0].T,
        narrow[1].T,
        narrow[2].T,
        expert_grads[0],
        expert_grads[1],
        expert_grads[2],
    )


def solution(mesh):
    in_specs = (
        P(("dp", "exp"), "ctx", None),
        P(("dp", "exp")),
        P(("dp", "exp"), "ctx", None),
        P(("dp", "exp"), "ctx", None),
        P(("dp", "exp"), "ctx", None),
        P(("dp", "ctx", "exp"), None),
        P(("dp", "ctx", "exp"), None),
        P(("dp", "ctx", "exp")),
        P(("dp", "ctx", "exp")),
        P(("dp", "ctx", "exp"), None),
        P(("dp", "ctx", "exp"), None),
        P(("dp", "ctx", "exp"), None),
        P("exp", None, ("dp", "ctx")),
        P("exp", None, ("dp", "ctx")),
        P("exp", ("dp", "ctx"), None),
    )
    out_specs = (
        P(("dp", "exp"), "ctx", None),
        P(("dp", "exp"), "ctx", None),
        P(("dp", "ctx", "exp"), None),
        P(("dp", "ctx", "exp"), None),
        P(("dp", "ctx", "exp")),
        P(("dp", "ctx", "exp")),
        P(("dp", "ctx", "exp"), None),
        P(("dp", "ctx", "exp"), None),
        P(("dp", "ctx", "exp"), None),
        P("exp", None, ("dp", "ctx")),
        P("exp", None, ("dp", "ctx")),
        P("exp", ("dp", "ctx"), None),
    )
    return jax.shard_map(local, mesh=mesh, in_specs=in_specs, out_specs=out_specs, check_vma=False)
```
